32 devices in a mesh: clip: 8 (over z, x), band: 4 (over y, core).
Axes of the slice: x: 2, y: 2, z: 4, core: 2. Of those that a mesh axis runs over, the one named last changes fastest.
Arguments:
- pixels: bfloat16 [98304, 256], P(('clip', 'band')), may hold values from -6 to 6
- lengths: int32 [32, 6], P(('clip', 'band')), may hold values from 0 to 1536, as said below
- shifts: int32 [32, 6, 2], P(('clip', 'band')), may hold values from 0 to 3
- visible: int32 [18432], P(('clip', 'band')), may hold values from 0 to 3071, as said below
- patch_embed: float32 [256, 768], P('clip'), may hold values from -0.375 to 0.375
- encoder_in: float32 [768, 6656], P('clip'), may hold values from -0.21875 to 0.21875
- encoder_down: float32 [3072, 768], P('clip'), may hold values from -0.109375 to 0.109375
- decoder_in: float32 [512, 4352], P('clip'), may hold values from -0.25 to 0.25
- decoder_down: float32 [2048, 512], P('clip'), may hold values from -0.125 to 0.125
- norm_vectors: float32 [8192], P('clip')
- first_embed: float32 [256, 768], P('clip'), may hold values from -4.7683716e-07 to 4.7683716e-07
- first_encoder_in: float32 [768, 6656], P('clip'), may hold values from -4.7683716e-07 to 4.7683716e-07
- first_encoder_down: float32 [3072, 768], P('clip'), may hold values from -4.7683716e-07 to 4.7683716e-07
- first_decoder_in: float32 [512, 4352], P('clip'), may hold values from -4.7683716e-07 to 4.7683716e-07
- first_decoder_down: float32 [2048, 512], P('clip'), may hold values from -4.7683716e-07 to 4.7683716e-07
- first_vectors: float32 [8192], P('clip'), may hold values from -2.3841858e-06 to 2.3841858e-06
- second_embed: float32 [256, 768], P('clip'), may hold values from 4.802467e-15 to 1.9173348e-14
- second_encoder_in: float32 [768, 6656], P('clip'), may hold values from 4.802467e-15 to 1.9173348e-14
- second_encoder_down: float32 [3072, 768], P('clip'), may hold values from 4.802467e-15 to 1.9173348e-14
- second_decoder_in: float32 [512, 4352], P('clip'), may hold values from 4.802467e-15 to 1.9173348e-14
- second_decoder_down: float32 [2048, 512], P('clip'), may hold values from 4.802467e-15 to 1.9173348e-14
- second_vectors: float32 [8192], P('clip'), may hold values from 1.1869215e-13 to 4.747686e-13
Outputs:
- loss_sum: float32 [], replicated
- grad_norm: float32 [], replicated
- updated_embed: float32 [256, 768], P('clip')
- updated_encoder_in: float32 [768, 6656], P('clip')
- updated_encoder_down: float32 [3072, 768], P('clip')
- updated_decoder_in: float32 [512, 4352], P('clip')
- updated_decoder_down: float32 [2048, 512], P('clip')
- updated_vectors: float32 [8192], P('clip')
- moment_embed: float32 [256, 768], P('clip')
- moment_encoder_in: float32 [768, 6656], P('clip')
- moment_encoder_down: float32 [3072, 768], P('clip')
- moment_decoder_in: float32 [512, 4352], P('clip')
- moment_decoder_down: float32 [2048, 512], P('clip')
- moment_vectors: float32 [8192], P('clip')
- square_embed: float32 [256, 768], P('clip')
- square_encoder_in: float32 [768, 6656], P('clip')
- square_encoder_down: float32 [3072, 768], P('clip')
- square_decoder_in: float32 [512, 4352], P('clip')
- square_decoder_down: float32 [2048, 512], P('clip')
- square_vectors: float32 [8192], P('clip')
The draws below stay inside these ranges and needn't reach their ends.
Inputs may be any that keep to these rules, and one draw needn't show every extreme that they name: `lengths`: each row lists its clips first, each 512 or 1536 patches, then zero slots; every row sums to 3072; some row holds 2 clips of 1536 patches. Each pack's 576 entries rise; exactly three patches are visible in each aligned block of 16 patches (two time columns).
All inputs are finite; a program needn't handle non-finite values.
Results may differ from the reference program's by a relative error of at most 0.0003.
The reference program's roundings to bfloat16 on the way count: a program that leaves them out, or rounds other values in their place, can miss the bound.
Values may be sent and summed in bfloat16 or wider, within the bound.
A program may use at most 448 MiB of HBM per device.

```python
import math
import jax
import jax.numpy as jnp
from jax import lax

DE = 768
HEADS_ENC = 12
FE = 3072
DD = 512
HEADS_DEC = 16
FD = 2048
P_SIZE = 256
SHORT = 512
UNITS = 6
STEP = 10
PACKS = 32
PATCH_DEV = 3072
VIS_DEV = 576
PATCHES = 98304
N_MASKED = 79872
NPARAMS = 10952704


def draw_lengths(key, part):
    key = jax.random.fold_in(key, 5)
    count_key, order_key, pick_key = jax.random.split(key, 3)
    most = UNITS // 3
    longs = jax.random.randint(count_key, (PACKS,), 0, most + 1)
    chosen = jax.random.randint(pick_key, (), 0, PACKS)
    longs = jnp.where(jnp.arange(PACKS) == chosen, most, longs)
    shorts = UNITS - 3 * longs
    slot = jnp.arange(UNITS)[None, :]
    items = jnp.where(slot < longs[:, None], 3, jnp.where(slot < (longs + shorts)[:, None], 1, 0))

    def shuffle(one_key):
        return jax.random.permutation(one_key, UNITS)
    orders = jax.vmap(shuffle)(jax.random.split(order_key, PACKS))
    mixed = jnp.take_along_axis(items, orders, axis=1)
    packed_order = jnp.argsort((mixed == 0).astype(jnp.int32), axis=1, stable=True)
    return (jnp.take_along_axis(mixed, packed_order, axis=1) * SHORT).astype(jnp.int32)


def draw_visible(key, part):
    key = jax.random.fold_in(key, 7)
    blocks = PACKS * PATCH_DEV // 16

    def choose(one_key):
        return jnp.sort(jax.random.permutation(one_key, 16)[:3])
    picks = jax.vmap(choose)(jax.random.split(key, blocks))
    base = jnp.arange(blocks) % (PATCH_DEV // 16) * 16
    return (picks + base[:, None]).reshape(-1).astype(jnp.int32)


def draw_norm_vectors(key, part):
    key = jax.random.fold_in(key, 11)
    gain_key, offset_key, dec_gain_key, dec_offset_key, token_key = jax.random.split(key, 5)
    enc_rise = 0.5 + jnp.arange(DE, dtype=jnp.float32) / DE
    dec_rise = 0.5 + jnp.arange(DD, dtype=jnp.float32) / DD
    enc_gain = enc_rise[None, :] * jax.random.uniform(gain_key, (3, DE), jnp.float32, 0.8, 1.2)
    enc_offset = 0.2 * jax.random.normal(offset_key, (3, DE), jnp.float32)
    dec_gain = dec_rise[None, :] * jax.random.uniform(dec_gain_key, (3, DD), jnp.float32, 0.8, 1.2)
    dec_offset = 0.2 * jax.random.normal(dec_offset_key, (3, DD), jnp.float32)
    token = jax.random.normal(token_key, (DD,), jnp.float32)
    encoder_part = jnp.stack([enc_gain[0], enc_offset[0], enc_gain[1], enc_offset[1], enc_gain[2], enc_offset[2]])
    decoder_part = jnp.stack([dec_gain[0], dec_offset[0], dec_gain[1], dec_offset[1], dec_gain[2], dec_offset[2], token])
    return jnp.concatenate([encoder_part.reshape(-1), decoder_part.reshape(-1)]).astype(jnp.float32)


def touch_ends(drawn, key, smallest, largest):
    longest = drawn.shape.index(max(drawn.shape))
    spots = []
    for shift in (0, 1):
        where = [jax.random.randint(jax.random.fold_in(key, axis), (), 0, length) for axis, length in enumerate(drawn.shape)]
        where[longest] = (where[longest] + shift) % drawn.shape[longest]
        spots.append(tuple(where))
    return drawn.at[spots[0]].set(smallest).at[spots[1]].set(largest)


def block_scale(own_key, dims, shards, low, largest):
    factor_of = 1.0
    for dim, parts in shards:
        heights = jax.random.uniform(jax.random.fold_in(jax.random.fold_in(own_key, 6), dim), (parts,), jnp.float32, low / len(shards), largest / len(shards))
        factor_of = factor_of * jnp.repeat(jnp.exp(heights), dims[dim] // parts).reshape((-1,) + (1,) * (len(dims) - 1 - dim))
    return factor_of


def scatter_about(key, extent, scale, bound, pieces=(), kind=jnp.bfloat16):
    loudness = block_scale(key, extent, pieces, -0.22, 0.18) if pieces else 1.0
    result = jax.random.normal(key, extent, jnp.float32) * scale * loudness
    return jnp.minimum(jnp.maximum(result, -bound), bound).astype(kind)


def setup_inputs(seed: int = 0) -> dict:
    keys = jax.random.split(jax.random.key(seed), 23)
    return {
        "pixels": scatter_about(keys[0], (PATCHES, P_SIZE), 1.0, 6.0, ((0, 32),)),
        "lengths": draw_lengths(jax.random.fold_in(keys[22], 71), 0),
        "shifts": touch_ends(jax.random.randint(keys[2], (PACKS, UNITS, 2), 0, 4), jax.random.fold_in(keys[2], 1), 0, 3).astype(jnp.int32),
        "visible": draw_visible(jax.random.fold_in(keys[22], 71), 0),
        "patch_embed": scatter_about(keys[4], (P_SIZE, DE), P_SIZE ** -0.5, 0.375, ((0, 8),), jnp.float32),
        "encoder_in": scatter_about(keys[5], (DE, 4 * DE + FE + DD), DE ** -0.5, 0.21875, ((0, 8),), jnp.float32),
        "encoder_down": scatter_about(keys[6], (FE, DE), FE ** -0.5, 0.109375, ((0, 8),), jnp.float32),
        "decoder_in": scatter_about(keys[7], (DD, 4 * DD + FD + P_SIZE), DD ** -0.5, 0.25, ((0, 8),), jnp.float32),
        "decoder_down": scatter_about(keys[8], (FD, DD), FD ** -0.5, 0.125, ((0, 8),), jnp.float32),
        "norm_vectors": draw_norm_vectors(jax.random.fold_in(keys[22], 71), 0),
        "first_embed": scatter_about(keys[10], (P_SIZE, DE), (0.000111 * NPARAMS ** -0.5), 4.76837158203125e-07, ((0, 8),), jnp.float32),
        "first_encoder_in": scatter_about(keys[11], (DE, 4 * DE + FE + DD), (0.000111 * NPARAMS ** -0.5), 4.76837158203125e-07, ((0, 8),), jnp.float32),
        "first_encoder_down": scatter_about(keys[12], (FE, DE), (0.000111 * NPARAMS ** -0.5), 4.76837158203125e-07, ((0, 8),), jnp.float32),
        "first_decoder_in": scatter_about(keys[13], (DD, 4 * DD + FD + P_SIZE), (0.000111 * NPARAMS ** -0.5), 4.76837158203125e-07, ((0, 8),), jnp.float32),
        "first_decoder_down": scatter_about(keys[14], (FD, DD), (0.000111 * NPARAMS ** -0.5), 4.76837158203125e-07, ((0, 8),), jnp.float32),
        "first_vectors": scatter_about(keys[15], (6 * DE + 7 * DD,), (0.000555 * NPARAMS ** -0.5), 2.384185791015625e-06, ((0, 8),), jnp.float32),
        "second_embed": jnp.clip(jnp.exp(math.log(1.9173348008555934e-14) - 1.3843914 * jax.random.uniform(keys[16], (P_SIZE, DE), jnp.float32) ** block_scale(keys[16], (P_SIZE, DE), ((0, 8),), -0.2, 0.2)), 4.8024671702774375e-15, 1.9173348008555934e-14),
        "second_encoder_in": jnp.clip(jnp.exp(math.log(1.9173348008555934e-14) - 1.3843914 * jax.random.uniform(keys[17], (DE, 4 * DE + FE + DD), jnp.float32) ** block_scale(keys[17], (DE, 4 * DE + FE + DD), ((0, 8),), -0.2, 0.2)), 4.8024671702774375e-15, 1.9173348008555934e-14),
        "second_encoder_down": jnp.clip(jnp.exp(math.log(1.9173348008555934e-14) - 1.3843914 * jax.random.uniform(keys[18], (FE, DE), jnp.float32) ** block_scale(keys[18], (FE, DE), ((0, 8),), -0.2, 0.2)), 4.8024671702774375e-15, 1.9173348008555934e-14),
        "second_decoder_in": jnp.clip(jnp.exp(math.log(1.9173348008555934e-14) - 1.3843914 * jax.random.uniform(keys[19], (DD, 4 * DD + FD + P_SIZE), jnp.float32) ** block_scale(keys[19], (DD, 4 * DD + FD + P_SIZE), ((0, 8),), -0.2, 0.2)), 4.8024671702774375e-15, 1.9173348008555934e-14),
        "second_decoder_down": jnp.clip(jnp.exp(math.log(1.9173348008555934e-14) - 1.3843914 * jax.random.uniform(keys[20], (FD, DD), jnp.float32) ** block_scale(keys[20], (FD, DD), ((0, 8),), -0.2, 0.2)), 4.8024671702774375e-15, 1.9173348008555934e-14),
        "second_vectors": jnp.clip(jnp.exp(math.log(4.747686076743418e-13) - 1.3862944 * jax.random.uniform(keys[21], (6 * DE + 7 * DD,), jnp.float32) ** block_scale(keys[21], (6 * DE + 7 * DD,), ((0, 8),), -0.2, 0.2)), 1.1869215191858545e-13, 4.747686076743418e-13),
    }


LEARN_RATE = 0.02
BETA_ONE = 0.9
BETA_TWO = 0.95
EPSILON = 1e-08
DECAY_RATE = 0.05
CLIP_LIMIT = 0.001

@jax.custom_vjp
def low(v):
    return lax.optimization_barrier(v.astype(jnp.bfloat16)).astype(jnp.float32)

@jax.custom_vjp
def low_back(v):
    return v

def low_keep(v):
    return (low(v), None)

def low_pass(kept, grad):
    return (grad,)

def back_keep(v):
    return (v, None)

def back_low(kept, grad):
    return (low(grad),)
low.defvjp(low_keep, low_pass)
low_back.defvjp(back_keep, back_low)

def layer_norm(stream, gain, offset):
    centre = stream - lax.optimization_barrier(jnp.mean(stream, axis=-1, keepdims=True))
    spread = lax.optimization_barrier(jnp.mean(centre * centre, axis=-1, keepdims=True))
    return centre * lax.rsqrt(spread + 1e-06) * gain + offset

def sincos(time_pos, frequency, width):
    quarter = width // 4
    omega = 1.0 / 10000.0 ** (jnp.arange(quarter, dtype=jnp.float32) / quarter)
    time_angle = time_pos.astype(jnp.float32)[:, None] * omega[None, :]
    band_angle = frequency.astype(jnp.float32)[:, None] * omega[None, :]
    return jnp.concatenate([jnp.sin(time_angle), jnp.cos(time_angle), jnp.sin(band_angle), jnp.cos(band_angle)], axis=1)

def layout(clip_lengths, clip_shifts, patch_dev):
    columns = (clip_lengths // 8).astype(jnp.int32)
    clip_ends = jnp.cumsum(columns).astype(jnp.int32)
    starts = (clip_ends - columns).astype(jnp.int32)
    windows = (columns // 8).astype(jnp.int32)
    offsets = (jnp.cumsum(windows) - windows).astype(jnp.int32)
    patches = jnp.arange(patch_dev, dtype=jnp.int32)
    column = patches // 8
    frequency = patches % 8
    clip_id = lax.optimization_barrier(jnp.sum((column[:, None] >= clip_ends[None, :]).astype(jnp.int32), axis=1)).astype(jnp.int32)
    onehot = (clip_id[:, None] == jnp.arange(clip_lengths.shape[0], dtype=jnp.int32)[None, :]).astype(jnp.int32)

    def select(values):
        return lax.optimization_barrier(jnp.sum(onehot * values[None, :], axis=1)).astype(jnp.int32)
    time_pos = column - select(starts)
    turned_time = (time_pos + select(clip_shifts[:, 0])) % select(columns)
    turned_band = (frequency + select(clip_shifts[:, 1])) % 8
    target_band = turned_band // 4 * 2 + turned_time // 4 % 2
    dest_row = target_band * (patch_dev // 4) + (select(offsets) + turned_time // 8) * 16 + turned_time % 4 * 4 + turned_band % 4
    return (time_pos, frequency, clip_id, dest_row.astype(jnp.int32))

def product(values_in, weights_in):
    return low_back(jnp.dot(low(values_in), weights_in, precision=lax.Precision.HIGHEST))

def attend(projections, heads, group, score_bias):
    rows = projections.shape[0]
    head_size = projections.shape[1] // (3 * heads)
    split_parts = projections.reshape(rows // group, group, 3, heads, head_size)
    query, key_rows, value_rows = (split_parts[:, :, 0], split_parts[:, :, 1], split_parts[:, :, 2])
    scores = low_back(jnp.einsum('bqhd,bkhd->bhqk', query, key_rows, precision=lax.Precision.HIGHEST)) * head_size ** (-0.5) + score_bias
    probs = low(jax.nn.softmax(scores, axis=-1))
    mixed = low_back(jnp.einsum('bhqk,bkhd->bqhd', probs, value_rows, precision=lax.Precision.HIGHEST))
    return mixed.reshape(rows, heads * head_size)

def layer_block(stream, weights, gains, heads, group, score_bias):
    w_qkv, w_out, w_up, w_down = weights
    projections = low(product(layer_norm(stream, gains[0], gains[1]), w_qkv))
    middle = stream + product(attend(projections, heads, group, score_bias), w_out)
    activated = jax.nn.gelu(product(layer_norm(middle, gains[2], gains[3]), w_up))
    return middle + product(activated, w_down)

def device_loss(params, pixel_rows, clip_lengths, clip_shifts, seen_index):
    embed, enc_in, enc_down, dec_in, dec_down, vectors = params
    enc_width, dec_width = (enc_in.shape[0], dec_in.shape[0])
    enc_hidden, dec_hidden = (enc_down.shape[0], dec_down.shape[0])
    enc_gains = vectors[:6 * enc_width].reshape(6, enc_width)
    dec_gains = vectors[6 * enc_width:].reshape(7, dec_width)
    time_pos, frequency, clip_id, dest_row = layout(clip_lengths, clip_shifts, PATCH_DEV)
    source = jnp.zeros((PATCH_DEV,), jnp.int32).at[dest_row].set(jnp.arange(PATCH_DEV, dtype=jnp.int32))
    segment = clip_id[seen_index]
    score_bias = jnp.where(segment[:, None] == segment[None, :], 0.0, -1e+30)
    stream = product(pixel_rows[seen_index], embed) + sincos(time_pos[seen_index], frequency[seen_index], enc_width)
    enc_weights = (enc_in[:, :3 * enc_width], enc_in[:, 3 * enc_width:4 * enc_width], enc_in[:, 4 * enc_width:4 * enc_width + enc_hidden], enc_down)
    stream = layer_block(stream, enc_weights, enc_gains, HEADS_ENC, VIS_DEV, score_bias)
    projected = product(layer_norm(stream, enc_gains[4], enc_gains[5]), enc_in[:, 4 * enc_width + enc_hidden:])
    kept_mask = jnp.zeros((PATCH_DEV,), jnp.float32).at[seen_index].set(1.0)
    placed = jnp.zeros((PATCH_DEV, dec_width), jnp.float32).at[seen_index].set(projected)
    grid = jnp.where(kept_mask[:, None] > 0.5, placed, dec_gains[6][None, :]) + sincos(time_pos, frequency, dec_width)
    grid = low_back(low(grid))
    centre = pixel_rows - lax.optimization_barrier(jnp.mean(pixel_rows, axis=1, keepdims=True))
    target = low(centre * lax.rsqrt(lax.optimization_barrier(jnp.mean(centre * centre, axis=1, keepdims=True)) + 1e-06))
    dec_weights = (dec_in[:, :3 * dec_width], dec_in[:, 3 * dec_width:4 * dec_width], dec_in[:, 4 * dec_width:4 * dec_width + dec_hidden], dec_down)
    decoded = layer_block(grid[source], dec_weights, dec_gains, HEADS_DEC, 16, 0.0)
    predicted = product(layer_norm(decoded, dec_gains[4], dec_gains[5]), dec_in[:, 4 * dec_width + dec_hidden:])
    error = predicted - target[source]
    return jnp.sum((1.0 - kept_mask)[source] * lax.optimization_barrier(jnp.mean(error * error, axis=1)))

def adam_update(weight, first, second, grad, decay):
    first = BETA_ONE * first + (1.0 - BETA_ONE) * grad
    second = BETA_TWO * second + (1.0 - BETA_TWO) * grad * grad
    first_hat = first / (1.0 - BETA_ONE ** STEP)
    second_hat = second / (1.0 - BETA_TWO ** STEP)
    weight = weight - LEARN_RATE * (first_hat / (jnp.sqrt(second_hat) + EPSILON) + decay * weight)
    return (weight, first, second)

def reference(pixels, lengths, shifts, visible, patch_embed, encoder_in, encoder_down, decoder_in, decoder_down, norm_vectors, first_embed, first_encoder_in, first_encoder_down, first_decoder_in, first_decoder_down, first_vectors, second_embed, second_encoder_in, second_encoder_down, second_decoder_in, second_decoder_down, second_vectors):
    masters = (patch_embed, encoder_in, encoder_down, decoder_in, decoder_down, norm_vectors)
    firsts = (first_embed, first_encoder_in, first_encoder_down, first_decoder_in, first_decoder_down, first_vectors)
    seconds = (second_embed, second_encoder_in, second_encoder_down, second_decoder_in, second_decoder_down, second_vectors)
    packed = (pixels.astype(jnp.float32).reshape(PACKS, PATCH_DEV, P_SIZE), lengths, shifts, visible.reshape(PACKS, VIS_DEV))

    def total_loss(params):
        low_params = tuple((low(weight) for weight in params))

        def scan_step(total, item):
            return (total + device_loss(low_params, item[0], item[1], item[2], item[3]), None)
        total, _ = lax.scan(jax.checkpoint(scan_step), jnp.zeros((), jnp.float32), packed)
        return total
    loss_sum, back = jax.vjp(total_loss, masters)
    grads = back(jnp.ones_like(loss_sum) / N_MASKED)[0]
    squares = jnp.zeros((), jnp.float32)
    for grad in grads:
        squares = squares + jnp.sum(grad * grad)
    grad_norm = jnp.sqrt(squares)
    factor = jnp.minimum(1.0, CLIP_LIMIT / (grad_norm + 1e-06))
    results = []
    for index in range(6):
        decay = DECAY_RATE if index < 5 else 0.0
        results.append(adam_update(masters[index], firsts[index], seconds[index], grads[index] * factor, decay))
    return (loss_sum, grad_norm, results[0][0], results[1][0], results[2][0], results[3][0], results[4][0], results[5][0], results[0][1], results[1][1], results[2][1], results[3][1], results[4][1], results[5][1], results[0][2], results[1][2], results[2][2], results[3][2], results[4][2], results[5][2])
```

```python
import functools

import jax
import jax.numpy as jnp
from jax import lax
from jax.experimental import pallas as pl
from jax.experimental.pallas import tpu as pltpu
from jax.sharding import PartitionSpec as P

HEADS_ENC = 12
HEADS_DEC = 16
STEP = 10


LEARN_RATE = 0.02
BETA_ONE = 0.9
BETA_TWO = 0.95
EPSILON = 1e-08
DECAY_RATE = 0.05
CLIP_LIMIT = 0.001


F32, BF16 = jnp.float32, jnp.bfloat16
GELU_C = 0.7978845608028654


def mm(a, b, ca=1, cb=0):
    return lax.dot_general(a, b, (((ca,), (cb,)), ((), ())), preferred_element_type=F32)


def wide(v, n):
    return jnp.concatenate([v] * (n // 128), axis=1)


def loop(n, body, unroll=1):
    def step(i, carry):
        for k in range(unroll):
            body(i * unroll + k)
        return carry
    lax.fori_loop(0, n // unroll, step, 0)


def fold(v):
    total = v[:, :128]
    for i in range(1, v.shape[1] // 128):
        total = total + v[:, 128 * i : 128 * (i + 1)]
    return total


def decoder_kernel(
    coef, heads, shift_ref, rvis_ref, gvt_ref, pix_ref, et_ref, ef_ref, vec_ref, w_ref, wt_ref, wd_ref, wdt_ref,
    gin_ref, gdown_ref, gvec_ref, gp_ref, loss_ref,
    res, xh1, xh2, xh3, tmp, n1, n2, fin, rs, qkv, att, act, dgel, probs, dqkv, dup, low, oh, mrow, hb, hm, wm,
):
    width = w_ref.shape[0]
    hidden = wd_ref.shape[0]
    rows = res.shape[1]
    size = width // heads
    per = 128 // size
    scale = size ** -0.5
    groups = width // 128
    c_out, c_up, c_head = 3 * width, 4 * width, 4 * width + hidden
    pixels = w_ref.shape[1] - c_head
    cols = rows // 8
    nblk = pix_ref.shape[0] // rows
    chunk = 512

    gin_ref[...] = jnp.zeros_like(gin_ref)
    gdown_ref[...] = jnp.zeros_like(gdown_ref)
    gvec_ref[...] = jnp.zeros_like(gvec_ref)
    gp_ref[...] = jnp.zeros_like(gp_ref)
    loss_ref[...] = jnp.zeros_like(loss_ref)
    f_id = lax.broadcasted_iota(jnp.int32, (128, 128 * per), 0)
    q_id = lax.broadcasted_iota(jnp.int32, (128, 128 * per), 1)
    hm[...] = jnp.where(f_id // size == q_id // 128, 1.0, 0.0).astype(BF16)
    wm[...] = jnp.where(f_id // 32 == (q_id % 128) // 32, 1.0, 0.0).astype(BF16)

    def lane(i):
        return pl.ds(pl.multiple_of(i * 128, 128), 128)

    def ln_forward(k, xh, out):
        def body(i):
            x = res[:, lane(i)]
            centre = x - jnp.mean(x, axis=0, keepdims=True)
            r = lax.rsqrt(jnp.mean(centre * centre, axis=0, keepdims=True) + 1e-06)
            xhat = centre * r
            xh[:, lane(i)] = xhat
            rs[8 * k : 8 * k + 8, lane(i)] = jnp.broadcast_to(r, (8, 128))
            out[:, lane(i)] = (xhat * vec_ref[2 * k] + vec_ref[2 * k + 1]).astype(BF16)
        loop(rows // 128, body, 4)

    def ln_backward(k, xh, add):
        def body(i):
            d = tmp[:, lane(i)]
            xhat = xh[:, lane(i)]
            gvec_ref[2 * k] += d * xhat
            gvec_ref[2 * k + 1] += d
            dx = d * vec_ref[2 * k]
            m1 = jnp.mean(dx, axis=0, keepdims=True)
            m2 = jnp.mean(dx * xhat, axis=0, keepdims=True)
            g = rs[8 * k : 8 * k + 1, lane(i)] * (dx - m1 - xhat * m2)
            if add:
                g = g + res[:, lane(i)]
            res[:, lane(i)] = g
            low[:, lane(i)] = g.astype(BF16)
        loop(rows // 128, body, 4)

    def block(j):
        first = pl.multiple_of(j * rows, rows)
        turn = shift_ref[j]
        spot = lax.broadcasted_iota(jnp.int32, (rvis_ref.shape[0], rows), 1) + first
        hot = jnp.where(wide(rvis_ref[...], rows) == spot, 1.0, 0.0)
        oh[...] = hot.astype(BF16)
        masked = 1.0 - jnp.sum(hot, axis=0, keepdims=True)
        mrow[...] = jnp.broadcast_to(masked, (8, rows))
        et = et_ref[pl.ds(pl.multiple_of(j * cols, cols), cols), :]
        e_hi = et.astype(BF16)
        rest = et - e_hi.astype(F32)
        e_mid = rest.astype(BF16)
        e_lo = (rest - e_mid.astype(F32)).astype(BF16)
        spread = jnp.where(
            lax.broadcasted_iota(jnp.int32, (cols, rows), 1) // 8 == lax.broadcasted_iota(jnp.int32, (cols, rows), 0), 1.0, 0.0
        ).astype(BF16)
        e_t = mm(e_hi, spread, 0, 0) + (mm(e_mid, spread, 0, 0) + mm(e_lo, spread, 0, 0))
        half = width // 2
        keep = masked > 0.5
        placed = mm(gvt_ref[...], oh[...])
        top = (wide(vec_ref[6, :half], rows) + e_t).astype(BF16).astype(F32)
        res[:half] = jnp.where(keep, top, placed[:half])
        bottom = wide((vec_ref[6, half:] + ef_ref[...]).astype(BF16).astype(F32), rows)
        res[half:] = jnp.where(keep, bottom, placed[half:])
        k_half = (lax.broadcasted_iota(jnp.int32, (32, 128 * per), 0) % 8 + turn) % 8 // 4
        q_half = (lax.broadcasted_iota(jnp.int32, (32, 128 * per), 1) % 8 + turn) % 8 // 4
        hb[...] = jnp.where(k_half == q_half, 0.0, -1e30)

        ln_forward(0, xh1, n1)

        def qkv_part(i):
            part = pl.ds(pl.multiple_of(i * chunk, chunk), chunk)
            qkv[part, :] = mm(wt_ref[part, :], n1[...]).astype(BF16)
        loop(3 * width // chunk, qkv_part)

        q_group = (lax.broadcasted_iota(jnp.int32, (32, 128 * per), 1) % 128) // 32

        def compact(s):
            c = s[96:128]
            for i in (2, 1, 0):
                c = jnp.where(q_group == i, s[32 * i : 32 * i + 32], c)
            return c

        def attend(i):
            sb, g = i // groups, i % groups
            at = lane(sb)
            f0 = pl.multiple_of(g * 128, 128)
            q = qkv[pl.ds(f0, 128), at]
            k = qkv[pl.ds(width + f0, 128), at]
            v = qkv[pl.ds(2 * width + f0, 128), at]
            s = mm(k.T, wide(q, 128 * per) * hm[...])
            c = compact(s) * scale + hb[...]
            e = jnp.exp(c - jnp.max(c, axis=0, keepdims=True))
            p = e * (1.0 / jnp.sum(e, axis=0, keepdims=True))
            probs[i] = p
            p_low = p.astype(BF16)
            p_all = jnp.concatenate([p_low] * 4, axis=0) * wm[...]
            for h in range(per):
                o = mm(v[size * h : size * h + size], p_all[:, 128 * h : 128 * h + 128])
                att[pl.ds(f0 + size * h, size), at] = o.astype(BF16)
        loop(rows // 128 * groups, attend, 4)

        res[...] += mm(wt_ref[c_out : c_out + width], att[...])
        ln_forward(1, xh2, n2)

        def up_part(i):
            part = pl.ds(pl.multiple_of(i * chunk, chunk), chunk)
            u = mm(wt_ref[pl.ds(pl.multiple_of(c_up + i * chunk, chunk), chunk), :], n2[...])
            t = jnp.tanh(GELU_C * (u + 0.044715 * (u * u * u)))
            hp = 0.5 * (1.0 + t)
            act[part, :] = (u * hp).astype(BF16)
            dgel[part, :] = hp + (0.5 * GELU_C) * u * (1.0 - t * t) * (1.0 + 0.134145 * (u * u))
        loop(hidden // chunk, up_part)

        res[...] += mm(wdt_ref[...], act[...])
        ln_forward(2, xh3, fin)
        pred = mm(wt_ref[c_head:], fin[...])
        pix = pix_ref[pl.ds(first, rows), :].astype(F32).T
        centre = pix - jnp.mean(pix, axis=0, keepdims=True)
        target = (centre * lax.rsqrt(jnp.mean(centre * centre, axis=0, keepdims=True) + 1e-06)).astype(BF16).astype(F32)
        err = pred - target
        loss_ref[...] += fold(mrow[...] * jnp.mean(err * err, axis=0, keepdims=True))
        gpred = (mrow[0:1] * err * coef).astype(BF16)

        gin_ref[:, c_head:] += mm(fin[...], gpred, 1, 1)
        tmp[...] = mm(w_ref[:, c_head:], gpred)
        ln_backward(2, xh3, False)

        def mlp_back(i):
            part = pl.ds(pl.multiple_of(i * chunk, chunk), chunk)
            there = pl.ds(pl.multiple_of(c_up + i * chunk, chunk), chunk)
            d = (mm(wd_ref[part, :], low[...]) * dgel[part, :]).astype(BF16)
            dup[part, :] = d
            gdown_ref[part, :] += mm(act[part, :], low[...], 1, 1)
            gin_ref[:, there] += mm(n2[...], d, 1, 1)
        loop(hidden // chunk, mlp_back)
        tmp[...] = mm(w_ref[:, c_up:c_head], dup[...])
        ln_backward(1, xh2, True)
        gin_ref[:, c_out:c_up] += mm(att[...], low[...], 1, 1)
        fin[...] = mm(w_ref[:, c_out:c_up], low[...]).astype(BF16)

        def attend_back(i):
            sb, g = i // groups, i % groups
            at = lane(sb)
            f0 = pl.multiple_of(g * 128, 128)
            q = qkv[pl.ds(f0, 128), at]
            k = qkv[pl.ds(width + f0, 128), at]
            v = qkv[pl.ds(2 * width + f0, 128), at]
            do = fin[pl.ds(f0, 128), at]
            dp = compact(mm(v.T, wide(do, 128 * per) * hm[...]))
            p = probs[i]
            ds = p * (dp - jnp.sum(dp * p, axis=0, keepdims=True))
            p_all = jnp.concatenate([p.astype(BF16)] * 4, axis=0) * wm[...]
            ds_all = jnp.concatenate([(ds * scale).astype(BF16)] * 4, axis=0) * wm[...]
            for h in range(per):
                rows_h = slice(size * h, size * h + size)
                ds_h = ds_all[:, 128 * h : 128 * h + 128]
                p_h = p_all[:, 128 * h : 128 * h + 128]
                dqkv[pl.ds(f0 + size * h, size), at] = mm(k[rows_h], ds_h).astype(BF16)
                dqkv[pl.ds(width + f0 + size * h, size), at] = mm(q[rows_h], ds_h, 1, 1).astype(BF16)
                dqkv[pl.ds(2 * width + f0 + size * h, size), at] = mm(do[rows_h], p_h, 1, 1).astype(BF16)
        loop(rows // 128 * groups, attend_back, 4)

        def qkv_back(i):
            part = pl.ds(pl.multiple_of(i * chunk, chunk), chunk)
            gin_ref[:, part] += mm(n1[...], dqkv[part, :], 1, 1)
        loop(3 * width // chunk, qkv_back)
        tmp[...] = mm(w_ref[:, :c_out], dqkv[...])
        ln_backward(0, xh1, True)
        gvec_ref[6] += fold(low[...].astype(F32) * mrow[0:1])
        gp_ref[...] += mm(oh[...], low[...], 1, 1)

    loop(nblk, block)


def decoder_step(shift, rvis, gvt, pix, et, ef, vec, w, wt, wd, wdt, coef, heads):
    width, total = w.shape
    hidden = wd.shape[0]
    rows = 512
    vis = rvis.shape[0]
    per = 128 // (width // heads)
    vmem = pl.BlockSpec(memory_space=pltpu.VMEM)
    f = lambda *s: pltpu.VMEM(s, F32)
    b = lambda *s: pltpu.VMEM(s, BF16)
    return pl.pallas_call(
        functools.partial(decoder_kernel, coef, heads),
        out_shape=(
            jax.ShapeDtypeStruct((width, total), F32),
            jax.ShapeDtypeStruct((hidden, width), F32),
            jax.ShapeDtypeStruct((7, width, 128), F32),
            jax.ShapeDtypeStruct((vis, width), F32),
            jax.ShapeDtypeStruct((8, 128), F32),
        ),
        in_specs=[pl.BlockSpec(memory_space=pltpu.SMEM)] + [vmem] * 10,
        out_specs=(vmem,) * 5,
        scratch_shapes=[
            f(width, rows), f(width, rows), f(width, rows), f(width, rows), f(width, rows),
            b(width, rows), b(width, rows), b(width, rows), f(24, rows),
            b(3 * width, rows), b(width, rows), b(hidden, rows), f(hidden, rows),
            f(rows // 128 * (width // 128), 32, 128 * per), b(3 * width, rows), b(hidden, rows), b(width, rows),
            b(vis, rows), f(8, rows), f(32, 128 * per), b(128, 128 * per), b(128, 128 * per),
        ],
        compiler_params=pltpu.CompilerParams(vmem_limit_bytes=63 * 2**20),
        name="decoder",
    )(shift, rvis, gvt, pix, et, ef, vec, w, wt, wd, wdt)


def layer_norm(stream, gain, offset):
    centre = stream - jnp.mean(stream, axis=-1, keepdims=True)
    spread = jnp.mean(centre * centre, axis=-1, keepdims=True)
    return centre * lax.rsqrt(spread + 1e-06) * gain + offset


def sincos(time_pos, frequency, width):
    quarter = width // 4
    omega = 1.0 / 10000.0 ** (jnp.arange(quarter, dtype=jnp.float32) / quarter)
    time_angle = time_pos.astype(jnp.float32)[:, None] * omega[None, :]
    band_angle = frequency.astype(jnp.float32)[:, None] * omega[None, :]
    return jnp.concatenate(
        [jnp.sin(time_angle), jnp.cos(time_angle), jnp.sin(band_angle), jnp.cos(band_angle)], axis=1
    )


def clip_of(column, clip_lengths, clip_shifts):
    columns = clip_lengths // 8
    ends = jnp.cumsum(columns)
    clip_id = jnp.sum((column[:, None] >= ends[None, :]).astype(jnp.int32), axis=1)
    onehot = (clip_id[:, None] == jnp.arange(clip_lengths.shape[0], dtype=jnp.int32)[None, :]).astype(jnp.int32)

    def select(values):
        return jnp.sum(onehot * values[None, :], axis=1)

    return clip_id, select(ends - columns), select(columns), select(clip_shifts[:, 0]), select(clip_shifts[:, 1])


def product(values_in, weights_in):
    return jnp.dot(values_in, weights_in, preferred_element_type=jnp.float32)


def input_grad(grad_low, weights_in):
    return lax.dot_general(
        grad_low, weights_in, (((1,), (1,)), ((), ())), preferred_element_type=jnp.float32
    )


def weight_grad(values_in, grad_low):
    return lax.dot_general(
        values_in, grad_low, (((0,), (0,)), ((), ())), preferred_element_type=jnp.float32
    )


def split_heads(projections, heads, group):
    rows = projections.shape[0]
    head_size = projections.shape[1] // (3 * heads)
    split_parts = projections.reshape(rows // group, group, 3, heads, head_size)
    return (split_parts[:, :, 0], split_parts[:, :, 1], split_parts[:, :, 2], head_size)


def softmax_probs(query, key_rows, head_size, score_bias):
    scores = jnp.einsum("bqhd,bkhd->bhqk", query, key_rows, preferred_element_type=jnp.float32)
    return jax.nn.softmax(scores * head_size ** (-0.5) + score_bias, axis=-1)


def attend(projections, heads, group, score_bias):
    query, key_rows, value_rows, head_size = split_heads(projections, heads, group)
    probs = softmax_probs(query, key_rows, head_size, score_bias)
    mixed = jnp.einsum(
        "bhqk,bkhd->bqhd",
        probs.astype(jnp.bfloat16),
        value_rows,
        preferred_element_type=jnp.float32,
    )
    return mixed.reshape(projections.shape[0], -1)


def attend_back(grad_mixed, projections, heads, group, score_bias):
    query, key_rows, value_rows, head_size = split_heads(projections, heads, group)
    probs = softmax_probs(query, key_rows, head_size, score_bias)
    grad_heads = grad_mixed.reshape(query.shape)
    grad_probs = jnp.einsum(
        "bqhd,bkhd->bhqk", grad_heads, value_rows, preferred_element_type=jnp.float32
    )
    grad_values = jnp.einsum(
        "bhqk,bqhd->bkhd",
        probs.astype(jnp.bfloat16),
        grad_heads,
        preferred_element_type=jnp.float32,
    )
    grad_scores = probs * (grad_probs - jnp.sum(grad_probs * probs, axis=-1, keepdims=True))
    scaled = (grad_scores * head_size ** (-0.5)).astype(jnp.bfloat16)
    grad_query = jnp.einsum("bhqk,bkhd->bqhd", scaled, key_rows, preferred_element_type=jnp.float32)
    grad_keys = jnp.einsum("bhqk,bqhd->bkhd", scaled, query, preferred_element_type=jnp.float32)
    return jnp.stack([grad_query, grad_keys, grad_values], axis=2).reshape(projections.shape[0], -1)


def block_forward(stream, weights, gains, heads, group, score_bias):
    w_qkv, w_out, w_up, w_down = weights
    normed = layer_norm(stream, gains[0], gains[1]).astype(jnp.bfloat16)
    projections = product(normed, w_qkv).astype(jnp.bfloat16)
    attended = attend(projections, heads, group, score_bias).astype(jnp.bfloat16)
    middle = stream + product(attended, w_out)
    second_normed = layer_norm(middle, gains[2], gains[3]).astype(jnp.bfloat16)
    up_values = product(second_normed, w_up)
    activated = jax.nn.gelu(up_values).astype(jnp.bfloat16)
    return (
        middle + product(activated, w_down),
        (stream, normed, projections, attended, middle, second_normed, up_values, activated),
    )


def block_backward(grad_out, cache, weights, gains, heads, group, score_bias):
    w_qkv, w_out, w_up, w_down = weights
    stream, normed, projections, attended, middle, second_normed, up_values, activated = cache
    grad_down = grad_out.astype(jnp.bfloat16)
    g_down = weight_grad(activated, grad_down)
    _, gelu_back = jax.vjp(jax.nn.gelu, up_values)
    grad_up = gelu_back(input_grad(grad_down, w_down))[0].astype(jnp.bfloat16)
    g_up = weight_grad(second_normed, grad_up)
    _, norm_back = jax.vjp(layer_norm, middle, gains[2], gains[3])
    grad_middle, g_gain_two, g_offset_two = norm_back(input_grad(grad_up, w_up))
    grad_middle = grad_middle + grad_out
    grad_branch = grad_middle.astype(jnp.bfloat16)
    g_out = weight_grad(attended, grad_branch)
    grad_attended = input_grad(grad_branch, w_out).astype(jnp.bfloat16)
    grad_projections = attend_back(grad_attended, projections, heads, group, score_bias).astype(
        jnp.bfloat16
    )
    g_qkv = weight_grad(normed, grad_projections)
    _, first_back = jax.vjp(layer_norm, stream, gains[0], gains[1])
    grad_stream, g_gain_one, g_offset_one = first_back(input_grad(grad_projections, w_qkv))
    norm_grads = jnp.stack([g_gain_one, g_offset_one, g_gain_two, g_offset_two])
    return (grad_stream + grad_middle, (g_qkv, g_out, g_up, g_down), norm_grads)


def adam_update(weight, first, second, grad, decay):
    first = BETA_ONE * first + (1.0 - BETA_ONE) * grad
    second = BETA_TWO * second + (1.0 - BETA_TWO) * grad * grad
    first_hat = first / (1.0 - BETA_ONE**STEP)
    second_hat = second / (1.0 - BETA_TWO**STEP)
    weight = weight - LEARN_RATE * (first_hat / (jnp.sqrt(second_hat) + EPSILON) + decay * weight)
    return (weight, first, second)


def shards(
    pixels,
    lengths,
    shifts,
    visible,
    patch_embed,
    encoder_in,
    encoder_down,
    decoder_in,
    decoder_down,
    norm_vectors,
    first_embed,
    first_encoder_in,
    first_encoder_down,
    first_decoder_in,
    first_decoder_down,
    first_vectors,
    second_embed,
    second_encoder_in,
    second_encoder_down,
    second_decoder_in,
    second_decoder_down,
    second_vectors,
):
    masters = (patch_embed, encoder_in, encoder_down, decoder_in, decoder_down, norm_vectors)
    firsts = (
        first_embed,
        first_encoder_in,
        first_encoder_down,
        first_decoder_in,
        first_decoder_down,
        first_vectors,
    )
    seconds = (
        second_embed,
        second_encoder_in,
        second_encoder_down,
        second_decoder_in,
        second_decoder_down,
        second_vectors,
    )
    w_embed, w_enc, w_enc_down, w_dec, w_dec_down, gathered_vectors = (
        lax.all_gather(patch_embed.astype(jnp.bfloat16), "clip", axis=0, tiled=True),
        lax.all_gather(encoder_in.astype(jnp.bfloat16), "clip", axis=0, tiled=True),
        lax.all_gather(encoder_down.astype(jnp.bfloat16), "clip", axis=0, tiled=True),
        lax.all_gather(decoder_in.astype(jnp.bfloat16), "clip", axis=0, tiled=True),
        lax.all_gather(decoder_down.astype(jnp.bfloat16), "clip", axis=0, tiled=True),
        lax.all_gather(norm_vectors.astype(jnp.bfloat16), "clip", axis=0, tiled=True),
    )
    enc_width, dec_width = (w_enc.shape[0], w_dec.shape[0])
    enc_hidden, dec_hidden = (w_enc_down.shape[0], w_dec_down.shape[0])
    vectors = gathered_vectors.astype(jnp.float32)
    enc_gains = vectors[: 6 * enc_width].reshape(6, enc_width)
    dec_gains = vectors[6 * enc_width :].reshape(7, dec_width)
    enc_weights = (
        w_enc[:, : 3 * enc_width],
        w_enc[:, 3 * enc_width : 4 * enc_width],
        w_enc[:, 4 * enc_width : 4 * enc_width + enc_hidden],
        w_enc_down,
    )
    w_proj = w_enc[:, 4 * enc_width + enc_hidden :]
    patch_dev, n_visible = pixels.shape[0], visible.shape[0]
    turned = jnp.arange(patch_dev // 8, dtype=jnp.int32)
    _, start, size, shift_time, shift_band = clip_of(turned, lengths[0], shifts[0])
    turned_time = (turned - start - shift_time) % size
    decoder_pixels = pixels.reshape(patch_dev // 8, 8, -1)[start + turned_time].reshape(pixels.shape)
    seen = pixels[visible]
    seen_column, seen_band = visible // 8, visible % 8
    segment, seen_start, seen_size, seen_shift, _ = clip_of(seen_column, lengths[0], shifts[0])
    seen_time = seen_column - seen_start
    decoder_row = 8 * (seen_start + (seen_time + seen_shift) % seen_size) + seen_band
    padded = -(-n_visible // 128) * 128
    decoder_row = jnp.pad(decoder_row, (0, padded - n_visible), constant_values=-1)
    decoder_row = jnp.broadcast_to(decoder_row[:, None], (padded, 128))
    score_bias = jnp.where(segment[:, None] == segment[None, :], 0.0, -1e30)
    embedded = product(seen, w_embed) + sincos(seen_time, seen_band, enc_width)
    encoded, enc_cache = block_forward(
        embedded, enc_weights, enc_gains, HEADS_ENC, seen.shape[0], score_bias
    )
    final_enc = layer_norm(encoded, enc_gains[4], enc_gains[5]).astype(jnp.bfloat16)
    projected = product(final_enc, w_proj)
    grid_seen = (projected + sincos(seen_time, seen_band, dec_width)).astype(jnp.bfloat16)
    grid_seen = jnp.pad(grid_seen, ((0, padded - n_visible), (0, 0)))
    time_table = sincos(turned_time, turned_time, dec_width)[:, : dec_width // 2]
    bands = jnp.arange(8, dtype=jnp.int32)
    band_table = jnp.tile(sincos(bands, bands, dec_width)[:, dec_width // 2 :].T, (1, 16))
    wide_vectors = jnp.broadcast_to(dec_gains[:, :, None], dec_gains.shape + (128,))
    masked_count = 13.0 * (patch_dev // 16) * lax.axis_size("clip") * lax.axis_size("band")
    g_dec_in, g_dec_down, g_dec_vectors, grad_proj, loss = decoder_step(
        shift_band[::64],
        decoder_row,
        grid_seen.T,
        decoder_pixels,
        time_table,
        band_table,
        wide_vectors,
        w_dec,
        w_dec.T,
        w_dec_down,
        w_dec_down.T,
        2.0 / (pixels.shape[1] * masked_count),
        HEADS_DEC,
    )
    local_loss = jnp.sum(loss[0])
    g_dec_vectors = jnp.sum(g_dec_vectors, axis=2)
    grad_proj = grad_proj[:n_visible].astype(jnp.bfloat16)
    g_proj = weight_grad(final_enc, grad_proj)
    _, enc_final_back = jax.vjp(layer_norm, encoded, enc_gains[4], enc_gains[5])
    grad_encoded, g_enc_gain, g_enc_offset = enc_final_back(input_grad(grad_proj, w_proj))
    grad_embedded, g_enc_mats, g_enc_norms = block_backward(
        grad_encoded, enc_cache, enc_weights, enc_gains, HEADS_ENC, seen.shape[0], score_bias
    )
    g_embed = weight_grad(seen, grad_embedded.astype(jnp.bfloat16))
    g_enc_in = jnp.concatenate([g_enc_mats[0], g_enc_mats[1], g_enc_mats[2], g_proj], axis=1)
    g_vectors = jnp.concatenate(
        [
            g_enc_norms.reshape(-1),
            g_enc_gain,
            g_enc_offset,
            g_dec_vectors.reshape(-1),
        ]
    )
    shard_grads = (
        lax.psum_scatter(g_embed, "clip", scatter_dimension=0, tiled=True),
        lax.psum_scatter(g_enc_in, "clip", scatter_dimension=0, tiled=True),
        lax.psum_scatter(g_enc_mats[3], "clip", scatter_dimension=0, tiled=True),
        lax.psum_scatter(g_dec_in, "clip", scatter_dimension=0, tiled=True),
        lax.psum_scatter(g_dec_down, "clip", scatter_dimension=0, tiled=True),
        lax.psum_scatter(g_vectors, "clip", scatter_dimension=0, tiled=True),
    )
    reduced = lax.psum(
        (
            shard_grads[0],
            shard_grads[1],
            shard_grads[2],
            shard_grads[3],
            shard_grads[4],
            shard_grads[5],
        ),
        "band",
    )
    squares = jnp.zeros((), jnp.float32)
    for grad in reduced:
        squares = squares + jnp.sum(grad * grad)
    loss_sum = lax.psum(local_loss, ("clip", "band"))
    norm_squared = lax.psum(squares, "clip")
    grad_norm = jnp.sqrt(norm_squared)
    factor = jnp.minimum(1.0, CLIP_LIMIT / (grad_norm + 1e-06))
    results = []
    for index in range(6):
        decay = DECAY_RATE if index < 5 else 0.0
        results.append(
            adam_update(
                masters[index], firsts[index], seconds[index], reduced[index] * factor, decay
            )
        )
    return (
        loss_sum,
        grad_norm,
        results[0][0],
        results[1][0],
        results[2][0],
        results[3][0],
        results[4][0],
        results[5][0],
        results[0][1],
        results[1][1],
        results[2][1],
        results[3][1],
        results[4][1],
        results[5][1],
        results[0][2],
        results[1][2],
        results[2][2],
        results[3][2],
        results[4][2],
        results[5][2],
    )


def solution(mesh):
    in_specs = (
        P(("clip", "band"), None),
        P(("clip", "band"), None),
        P(("clip", "band"), None, None),
        P(("clip", "band")),
        P("clip", None),
        P("clip", None),
        P("clip", None),
        P("clip", None),
        P("clip", None),
        P("clip"),
        P("clip", None),
        P("clip", None),
        P("clip", None),
        P("clip", None),
        P("clip", None),
        P("clip"),
        P("clip", None),
        P("clip", None),
        P("clip", None),
        P("clip", None),
        P("clip", None),
        P("clip"),
    )
    out_specs = (
        P(),
        P(),
        P("clip", None),
        P("clip", None),
        P("clip", None),
        P("clip", None),
        P("clip", None),
        P("clip"),
        P("clip", None),
        P("clip", None),
        P("clip", None),
        P("clip", None),
        P("clip", None),
        P("clip"),
        P("clip", None),
        P("clip", None),
        P("clip", None),
        P("clip", None),
        P("clip", None),
        P("clip"),
    )
    return jax.shard_map(shards, mesh=mesh, in_specs=in_specs, out_specs=out_specs, check_vma=False)
```

```python
import functools

import jax
import jax.numpy as jnp
from jax import lax
from jax.experimental import pallas as pl
from jax.experimental.pallas import tpu as pltpu
from jax.sharding import PartitionSpec as P

HEADS_ENC = 12
HEADS_DEC = 16
STEP = 10


LEARN_RATE = 0.02
BETA_ONE = 0.9
BETA_TWO = 0.95
EPSILON = 1e-08
DECAY_RATE = 0.05
CLIP_LIMIT = 0.001


F32, BF16 = jnp.float32, jnp.bfloat16
GELU_C = 0.7978845608028654


def mm(a, b, ca=1, cb=0):
    return lax.dot_general(a, b, (((ca,), (cb,)), ((), ())), preferred_element_type=F32)


def wide(v, n):
    return jnp.concatenate([v] * (n // 128), axis=1)


def loop(n, body, unroll=1):
    def step(i, carry):
        for k in range(unroll):
            body(i * unroll + k)
        return carry
    lax.fori_loop(0, n // unroll, step, 0)


def fold(v):
    total = v[:, :128]
    for i in range(1, v.shape[1] // 128):
        total = total + v[:, 128 * i : 128 * (i + 1)]
    return total


def decoder_kernel(
    coef, heads, shift_ref, rvis_ref, gvt_ref, pix_ref, et_ref, ef_ref, vec_ref, w_ref, wt_ref, wd_ref, wdt_ref,
    gin_ref, gdown_ref, gvec_ref, gp_ref, loss_ref,
    res, xh1, xh2, xh3, tmp, n1, n2, fin, rs, qkv, att, act, dgel, probs, dqkv, dup, low, oh, mrow, hb, hm, wm,
):
    width = w_ref.shape[0]
    hidden = wd_ref.shape[0]
    rows = res.shape[1]
    size = width // heads
    per = 128 // size
    scale = size ** -0.5
    groups = width // 128
    c_out, c_up, c_head = 3 * width, 4 * width, 4 * width + hidden
    pixels = w_ref.shape[1] - c_head
    cols = rows // 8
    nblk = pix_ref.shape[0] // rows
    chunk = 512

    gin_ref[...] = jnp.zeros_like(gin_ref)
    gdown_ref[...] = jnp.zeros_like(gdown_ref)
    gvec_ref[...] = jnp.zeros_like(gvec_ref)
    gp_ref[...] = jnp.zeros_like(gp_ref)
    loss_ref[...] = jnp.zeros_like(loss_ref)
    f_id = lax.broadcasted_iota(jnp.int32, (128, 128 * per), 0)
    q_id = lax.broadcasted_iota(jnp.int32, (128, 128 * per), 1)
    hm[...] = jnp.where(f_id // size == q_id // 128, 1.0, 0.0).astype(BF16)
    wm[...] = jnp.where(f_id // 32 == (q_id % 128) // 32, 1.0, 0.0).astype(BF16)

    def lane(i):
        return pl.ds(pl.multiple_of(i * 128, 128), 128)

    def ln_forward(k, xh, out):
        def body(i):
            x = res[:, lane(i)]
            centre = x - jnp.mean(x, axis=0, keepdims=True)
            r = lax.rsqrt(jnp.mean(centre * centre, axis=0, keepdims=True) + 1e-06)
            xhat = centre * r
            xh[:, lane(i)] = xhat
            rs[8 * k : 8 * k + 8, lane(i)] = jnp.broadcast_to(r, (8, 128))
            out[:, lane(i)] = (xhat * vec_ref[2 * k] + vec_ref[2 * k + 1]).astype(BF16)
        loop(rows // 128, body, 4)

    def ln_backward(k, xh, add):
        def body(i):
            d = tmp[:, lane(i)]
            xhat = xh[:, lane(i)]
            gvec_ref[2 * k] += d * xhat
            gvec_ref[2 * k + 1] += d
            dx = d * vec_ref[2 * k]
            m1 = jnp.mean(dx, axis=0, keepdims=True)
            m2 = jnp.mean(dx * xhat, axis=0, keepdims=True)
            g = rs[8 * k : 8 * k + 1, lane(i)] * (dx - m1 - xhat * m2)
            if add:
                g = g + res[:, lane(i)]
            res[:, lane(i)] = g
            low[:, lane(i)] = g.astype(BF16)
        loop(rows // 128, body, 4)

    def block(j):
        first = pl.multiple_of(j * rows, rows)
        turn = shift_ref[j]
        spot = lax.broadcasted_iota(jnp.int32, (rvis_ref.shape[0], rows), 1) + first
        hot = jnp.where(wide(rvis_ref[...], rows) == spot, 1.0, 0.0)
        oh[...] = hot.astype(BF16)
        masked = 1.0 - jnp.sum(hot, axis=0, keepdims=True)
        mrow[...] = jnp.broadcast_to(masked, (8, rows))
        et = et_ref[pl.ds(pl.multiple_of(j * cols, cols), cols), :]
        e_hi = et.astype(BF16)
        rest = et - e_hi.astype(F32)
        e_mid = rest.astype(BF16)
        e_lo = (rest - e_mid.astype(F32)).astype(BF16)
        spread = jnp.where(
            lax.broadcasted_iota(jnp.int32, (cols, rows), 1) // 8 == lax.broadcasted_iota(jnp.int32, (cols, rows), 0), 1.0, 0.0
        ).astype(BF16)
        e_t = mm(e_hi, spread, 0, 0) + (mm(e_mid, spread, 0, 0) + mm(e_lo, spread, 0, 0))
        half = width // 2
        keep = masked > 0.5
        placed = mm(gvt_ref[...], oh[...])
        top = (wide(vec_ref[6, :half], rows) + e_t).astype(BF16).astype(F32)
        res[:half] = jnp.where(keep, top, placed[:half])
        bottom = wide((vec_ref[6, half:] + ef_ref[...]).astype(BF16).astype(F32), rows)
        res[half:] = jnp.where(keep, bottom, placed[half:])
        k_half = (lax.broadcasted_iota(jnp.int32, (32, 128 * per), 0) % 8 + turn) % 8 // 4
        q_half = (lax.broadcasted_iota(jnp.int32, (32, 128 * per), 1) % 8 + turn) % 8 // 4
        hb[...] = jnp.where(k_half == q_half, 0.0, -1e30)

        ln_forward(0, xh1, n1)

        def qkv_part(i):
            part = pl.ds(pl.multiple_of(i * chunk, chunk), chunk)
            qkv[part, :] = mm(wt_ref[part, :], n1[...]).astype(BF16)
        loop(3 * width // chunk, qkv_part)

        q_group = (lax.broadcasted_iota(jnp.int32, (32, 128 * per), 1) % 128) // 32

        def compact(s):
            c = s[96:128]
            for i in (2, 1, 0):
                c = jnp.where(q_group == i, s[32 * i : 32 * i + 32], c)
            return c

        def attend(i):
            sb, g = i // groups, i % groups
            at = lane(sb)
            f0 = pl.multiple_of(g * 128, 128)
            q = qkv[pl.ds(f0, 128), at]
            k = qkv[pl.ds(width + f0, 128), at]
            v = qkv[pl.ds(2 * width + f0, 128), at]
            s = mm(k.T, wide(q, 128 * per) * hm[...])
            c = compact(s) * scale + hb[...]
            e = jnp.exp(c - jnp.max(c, axis=0, keepdims=True))
            p = e * (1.0 / jnp.sum(e, axis=0, keepdims=True))
            probs[i] = p
            p_low = p.astype(BF16)
            p_all = jnp.concatenate([p_low] * 4, axis=0) * wm[...]
            for h in range(per):
                o = mm(v[size * h : size * h + size], p_all[:, 128 * h : 128 * h + 128])
                att[pl.ds(f0 + size * h, size), at] = o.astype(BF16)
        loop(rows // 128 * groups, attend, 4)

        res[...] += mm(wt_ref[c_out : c_out + width], att[...])
        ln_forward(1, xh2, n2)

        def up_part(i):
            part = pl.ds(pl.multiple_of(i * chunk, chunk), chunk)
            u = mm(wt_ref[pl.ds(pl.multiple_of(c_up + i * chunk, chunk), chunk), :], n2[...])
            t = jnp.tanh(GELU_C * (u + 0.044715 * (u * u * u)))
            hp = 0.5 * (1.0 + t)
            act[part, :] = (u * hp).astype(BF16)
            dgel[part, :] = hp + (0.5 * GELU_C) * u * (1.0 - t * t) * (1.0 + 0.134145 * (u * u))
        loop(hidden // chunk, up_part)

        res[...] += mm(wdt_ref[...], act[...])
        ln_forward(2, xh3, fin)
        pred = mm(wt_ref[c_head:], fin[...])
        pix = pix_ref[pl.ds(first, rows), :].astype(F32).T
        centre = pix - jnp.mean(pix, axis=0, keepdims=True)
        target = (centre * lax.rsqrt(jnp.mean(centre * centre, axis=0, keepdims=True) + 1e-06)).astype(BF16).astype(F32)
        err = pred - target
        loss_ref[...] += fold(mrow[...] * jnp.mean(err * err, axis=0, keepdims=True))
        gpred = (mrow[0:1] * err * coef).astype(BF16)

        gin_ref[:, c_head:] += mm(fin[...], gpred, 1, 1)
        tmp[...] = mm(w_ref[:, c_head:], gpred)
        ln_backward(2, xh3, False)

        def mlp_back(i):
            part = pl.ds(pl.multiple_of(i * chunk, chunk), chunk)
            there = pl.ds(pl.multiple_of(c_up + i * chunk, chunk), chunk)
            d = (mm(wd_ref[part, :], low[...]) * dgel[part, :]).astype(BF16)
            dup[part, :] = d
            gdown_ref[part, :] += mm(act[part, :], low[...], 1, 1)
            gin_ref[:, there] += mm(n2[...], d, 1, 1)
        loop(hidden // chunk, mlp_back)
        tmp[...] = mm(w_ref[:, c_up:c_head], dup[...])
        ln_backward(1, xh2, True)
        gin_ref[:, c_out:c_up] += mm(att[...], low[...], 1, 1)
        fin[...] = mm(w_ref[:, c_out:c_up], low[...]).astype(BF16)

        def attend_back(i):
            sb, g = i // groups, i % groups
            at = lane(sb)
            f0 = pl.multiple_of(g * 128, 128)
            q = qkv[pl.ds(f0, 128), at]
            k = qkv[pl.ds(width + f0, 128), at]
            v = qkv[pl.ds(2 * width + f0, 128), at]
            do = fin[pl.ds(f0, 128), at]
            dp = compact(mm(v.T, wide(do, 128 * per) * hm[...]))
            p = probs[i]
            ds = p * (dp - jnp.sum(dp * p, axis=0, keepdims=True))
            p_all = jnp.concatenate([p.astype(BF16)] * 4, axis=0) * wm[...]
            ds_all = jnp.concatenate([(ds * scale).astype(BF16)] * 4, axis=0) * wm[...]
            for h in range(per):
                rows_h = slice(size * h, size * h + size)
                ds_h = ds_all[:, 128 * h : 128 * h + 128]
                p_h = p_all[:, 128 * h : 128 * h + 128]
                dqkv[pl.ds(f0 + size * h, size), at] = mm(k[rows_h], ds_h).astype(BF16)
                dqkv[pl.ds(width + f0 + size * h, size), at] = mm(q[rows_h], ds_h, 1, 1).astype(BF16)
                dqkv[pl.ds(2 * width + f0 + size * h, size), at] = mm(do[rows_h], p_h, 1, 1).astype(BF16)
        loop(rows // 128 * groups, attend_back, 4)

        def qkv_back(i):
            part = pl.ds(pl.multiple_of(i * chunk, chunk), chunk)
            gin_ref[:, part] += mm(n1[...], dqkv[part, :], 1, 1)
        loop(3 * width // chunk, qkv_back)
        tmp[...] = mm(w_ref[:, :c_out], dqkv[...])
        ln_backward(0, xh1, True)
        gvec_ref[6] += fold(low[...].astype(F32) * mrow[0:1])
        gp_ref[...] += mm(oh[...], low[...], 1, 1)

    loop(nblk, block)


def decoder_step(shift, rvis, gvt, pix, et, ef, vec, w, wt, wd, wdt, coef, heads):
    width, total = w.shape
    hidden = wd.shape[0]
    rows = 512
    vis = rvis.shape[0]
    per = 128 // (width // heads)
    vmem = pl.BlockSpec(memory_space=pltpu.VMEM)
    f = lambda *s: pltpu.VMEM(s, F32)
    b = lambda *s: pltpu.VMEM(s, BF16)
    return pl.pallas_call(
        functools.partial(decoder_kernel, coef, heads),
        out_shape=(
            jax.ShapeDtypeStruct((width, total), F32),
            jax.ShapeDtypeStruct((hidden, width), F32),
            jax.ShapeDtypeStruct((7, width, 128), F32),
            jax.ShapeDtypeStruct((vis, width), F32),
            jax.ShapeDtypeStruct((8, 128), F32),
        ),
        in_specs=[pl.BlockSpec(memory_space=pltpu.SMEM)] + [vmem] * 10,
        out_specs=(vmem,) * 5,
        scratch_shapes=[
            f(width, rows), f(width, rows), f(width, rows), f(width, rows), f(width, rows),
            b(width, rows), b(width, rows), b(width, rows), f(24, rows),
            b(3 * width, rows), b(width, rows), b(hidden, rows), f(hidden, rows),
            f(rows // 128 * (width // 128), 32, 128 * per), b(3 * width, rows), b(hidden, rows), b(width, rows),
            b(vis, rows), f(8, rows), f(32, 128 * per), b(128, 128 * per), b(128, 128 * per),
        ],
        compiler_params=pltpu.CompilerParams(vmem_limit_bytes=63 * 2**20),
        name="decoder",
    )(shift, rvis, gvt, pix, et, ef, vec, w, wt, wd, wdt)


def place():
    clip, band = lax.axis_index("clip"), lax.axis_index("band")
    return clip // 2, clip % 2, band // 2, band % 2


def device(z, x, y, c):
    return (z * 2 + x, y * 2 + c)


def greet(z, x, y, c):
    barrier = pltpu.get_barrier_semaphore()
    others = [device(z, x, y, 1 - c), device(z, 1 - x, y, c), device(z, x, 1 - y, c)]
    others += [device((z + k) % 4, x, y, c) for k in (1, 2, 3)]
    for other in others:
        pl.semaphore_signal(barrier, inc=1, device_id=other, device_id_type=pl.DeviceIdType.MESH)
    pl.semaphore_wait(barrier, len(others))


def remote(src, dst, send, recv, to):
    return pltpu.make_async_remote_copy(
        src_ref=src, dst_ref=dst, send_sem=send, recv_sem=recv, device_id=to, device_id_type=pl.DeviceIdType.MESH
    )


def reduce_kernel(widths, n, *refs):
    grads, small, outs, small_out = refs[:n], refs[n], refs[n + 1 : 2 * n + 1], refs[2 * n + 1]
    rest = refs[2 * n + 2 :]
    sums, r0, r1x, r1y, r2x, r2y, r3 = (rest[i * n : (i + 1) * n] for i in range(7))
    s_buf, s_sum, send, recv, near, s_send, s_recv = rest[7 * n :]
    z, x, y, c = place()
    greet(z, x, y, c)

    def at_z(k):
        return (z + k) % 4

    def columns(t, core):
        half = sums[t].shape[4]
        return pl.ds(pl.multiple_of(core * half, 128), half)

    def local(t, k):
        zk = at_z(k)
        return pltpu.make_async_copy(grads[t].at[zk, :, :, :, columns(t, c)], sums[t].at[zk], near.at[t, k])

    def copy(stage, t, k):
        zk, w = at_z(k), widths[t]
        total = sums[t].shape[4]
        first, last = pl.ds(0, w), pl.ds(w, total - w)
        s = sums[t]
        src, dst, to = {
            0: lambda: (grads[t].at[zk, :, :, :, columns(t, 1 - c)], r0[t].at[zk], device(z, x, y, 1 - c)),
            1: lambda: (s.at[zk, 1 - x, :, :, first], r1x[t].at[zk], device(z, 1 - x, y, c)),
            2: lambda: (s.at[zk, :, 1 - y, :, last], r1y[t].at[zk], device(z, x, 1 - y, c)),
            3: lambda: (s.at[zk, x, 1 - y, :, first], r2x[t].at[zk], device(z, x, 1 - y, c)),
            4: lambda: (s.at[zk, 1 - x, y, :, last], r2y[t].at[zk], device(z, 1 - x, y, c)),
            5: lambda: (s.at[zk, x, y], r3[t].at[k - 1], device(zk, x, y, c)),
            6: lambda: (s.at[z, x, y], outs[t].at[y, :, columns(t, c)], device(z, x, 1 - y, c)),
            7: lambda: (outs[t].at[:, :, columns(t, c)], outs[t].at[:, :, columns(t, c)], device(z, x, y, 1 - c)),
        }[stage]()
        return remote(src, dst, send.at[t, stage, k], recv.at[t, stage, k], to)

    def keep(t):
        return pltpu.make_async_copy(sums[t].at[z, x, y], outs[t].at[y, :, columns(t, c)], near.at[t, 4])

    def add(rows, parts, body):
        per = rows // 16
        def step(i, carry):
            body(i // per, pl.ds(pl.multiple_of(i % per * 16, 16), 16))
            return carry
        lax.fori_loop(0, parts * per, step, 0)

    def each(lo, hi, body):
        def step(k, carry):
            body(k)
            return carry
        lax.fori_loop(lo, hi, step, 0)

    def start(k):
        for t in range(n):
            copy(0, t, k).start()
            local(t, k).start()
    each(1, 5, lambda k: start(k % 4))

    s_sum[...] = small[...]
    for stage, to in enumerate((device(z, x, y, 1 - c), device(z, 1 - x, y, c), device(z, x, 1 - y, c))):
        hop = remote(s_sum, s_buf.at[stage], s_send.at[stage], s_recv.at[stage], to)
        hop.start()
        hop.wait()
        s_sum[...] += s_buf[stage]
    def small_hop(k):
        return remote(s_sum, s_buf.at[3 + z], s_send.at[2 + k], s_recv.at[2 + k], device(at_z(k), x, y, c))
    for k in (1, 2, 3):
        small_hop(k).start()
    s_buf[3 + z] = s_sum[...]

    def first_sum(k):
        zk = at_z(k)
        for t in range(n):
            copy(0, t, k).wait_recv()
            local(t, k).wait()
            def body(p, rows, t=t):
                sums[t][zk, p // 2, p % 2, rows] += r0[t][zk, p // 2, p % 2, rows]
            add(sums[t].shape[3], 4, body)
            copy(1, t, k).start()
            copy(2, t, k).start()
    each(1, 5, lambda k: first_sum(k % 4))

    def second_sum(k):
        zk = at_z(k)
        for t in range(n):
            w = widths[t]
            copy(1, t, k).wait_recv()
            def body(p, rows, t=t, w=w):
                sums[t][zk, x, p, rows, :w] += r1x[t][zk, p, rows]
            add(sums[t].shape[3], 2, body)
            copy(3, t, k).start()
            copy(2, t, k).wait_recv()
            def body(p, rows, t=t, w=w):
                sums[t][zk, p, y, rows, w:] += r1y[t][zk, p, rows]
            add(sums[t].shape[3], 2, body)
            copy(4, t, k).start()
    each(1, 5, lambda k: second_sum(k % 4))

    def third_sum(k):
        zk = at_z(k)
        for t in range(n):
            w = widths[t]
            copy(3, t, k).wait_recv()
            copy(4, t, k).wait_recv()
            def body(p, rows, t=t, w=w):
                sums[t][zk, x, y, rows, :w] += r2x[t][zk, rows]
                sums[t][zk, x, y, rows, w:] += r2y[t][zk, rows]
            add(sums[t].shape[3], 1, body)
    def send_sum(k):
        third_sum(k)
        for t in range(n):
            copy(5, t, k).start()
    each(1, 4, send_sum)
    third_sum(0)

    for t in range(n):
        for k in (1, 2, 3):
            copy(5, t, k).wait_recv()
        def body(p, rows, t=t):
            sums[t][z, x, y, rows] += r3[t][0, rows] + r3[t][1, rows] + r3[t][2, rows]
        add(sums[t].shape[3], 1, body)
        copy(6, t, 0).start()
        keep(t).start()
    for k in (1, 2, 3):
        small_hop(k).wait()
    small_out[...] = (s_buf[3] + s_buf[4]) + (s_buf[5] + s_buf[6])
    for t in range(n):
        copy(6, t, 0).wait_recv()
        keep(t).wait()
        copy(7, t, 0).start()

    def finish(k):
        for t in range(n):
            for stage in range(5):
                copy(stage, t, k).wait_send()
    each(0, 4, finish)
    def finish_z(k):
        for t in range(n):
            copy(5, t, k).wait_send()
    each(1, 4, finish_z)
    for t in range(n):
        copy(6, t, 0).wait_send()
        copy(7, t, 0).wait()


def reduce_grads(grads, small, ident):
    n = len(grads)
    views, widths = [], []
    scratch = [[] for _ in range(7)]
    for grad in grads:
        rows, total = grad.shape
        r2, half = rows // 16, total // 2
        w = (half // 128 + 1) // 2 * 128
        views.append(grad.reshape(4, 2, 2, r2, total))
        widths.append(w)
        f = lambda *s: pltpu.VMEM(s, F32)
        for i, s in enumerate((f(4, 2, 2, r2, half), f(4, 2, 2, r2, half), f(4, 2, r2, w), f(4, 2, r2, half - w),
                               f(4, r2, w), f(4, r2, half - w), f(3, r2, half))):
            scratch[i].append(s)
    anywhere, vmem = pl.BlockSpec(memory_space=pl.ANY), pl.BlockSpec(memory_space=pltpu.VMEM)
    dma = pltpu.SemaphoreType.DMA
    out = pl.pallas_call(
        functools.partial(reduce_kernel, tuple(widths), n),
        out_shape=tuple(jax.ShapeDtypeStruct((2, v.shape[3], v.shape[4]), F32) for v in views)
        + (jax.ShapeDtypeStruct(small.shape, F32),),
        in_specs=[anywhere] * n + [vmem],
        out_specs=(anywhere,) * n + (vmem,),
        scratch_shapes=sum(scratch, []) + [
            pltpu.VMEM((7,) + small.shape, F32), pltpu.VMEM(small.shape, F32),
            dma((n, 8, 4)), dma((n, 8, 4)), dma((n, 5)), dma((6,)), dma((6,)),
        ],
        compiler_params=pltpu.CompilerParams(
            collective_id=ident, has_side_effects=True, vmem_limit_bytes=60 * 2**20
        ),
        name="reduce",
    )(*views, small)
    return [o.reshape(-1, o.shape[2]) for o in out[:n]], out[n]


def gather_kernel(widths, n, *refs):
    shards, vector, outs, vectors = refs[:n], refs[n], refs[n + 1 : 2 * n + 1], refs[2 * n + 1]
    send, recv, near, v_send, v_recv = refs[2 * n + 2 :]
    z, x, y, c = place()
    greet(z, x, y, c)

    def at_z(k):
        return (z + k) % 4

    def columns(t, lo, size):
        half = shards[t].shape[2] // 2
        return pl.ds(pl.multiple_of(c * half + lo, 128), size)

    def own(t):
        return pltpu.make_async_copy(shards[t], outs[t].at[z, x], near.at[t])

    def copy(stage, t, k):
        zk, w, half = at_z(k), widths[t], shards[t].shape[2] // 2
        both, split, whole = columns(t, 0, w), columns(t, w, half - w), columns(t, 0, half)
        first = isinstance(k, int) and k == 0
        o = outs[t]
        zo = (z - k) % 4
        src, dst, to = {
            0: lambda: (shards[t].at[:, :, both], o.at[z, x, :, :, both], device(zk, x, y, c)),
            1: lambda: (shards[t].at[y, :, split], o.at[z, x, y, :, split], device(zk, x, y, c)),
            2: lambda: ((shards[t].at[:, :, both] if first else o.at[zo, x, :, :, both]), o.at[zo, x, :, :, both], device(z, 1 - x, y, c)),
            3: lambda: ((shards[t].at[y, :, split] if first else o.at[zo, x, y, :, split]), o.at[zo, x, y, :, split], device(z, 1 - x, y, c)),
            4: lambda: ((o.at[zo, 1 - x, y, :, split],) * 2 if first else (o.at[zo, :, y, :, split],) * 2) + (device(z, x, 1 - y, c),),
            5: lambda: ((o.at[zo, 1 - x, :, :, whole],) * 2 if first else (o.at[zo, :, :, :, whole],) * 2) + (device(z, x, y, 1 - c),),
        }[stage]()
        return remote(src, dst, send.at[t, stage, k], recv.at[t, stage, k], to)

    def arrived(stage, t, k):
        copy(stage, t, k).wait_recv()

    def vector_copy(stage, k):
        zo = (z - k) % 4
        if stage == 0:
            return remote(vector, vectors.at[z, x], v_send.at[k], v_recv.at[k], device(at_z(k), x, y, c))
        src = vector if isinstance(k, int) and k == 0 else vectors.at[zo, x]
        return remote(src, vectors.at[zo, x], v_send.at[4 + k], v_recv.at[4 + k], device(z, 1 - x, y, c))

    def each(lo, hi, body):
        def step(k, carry):
            body(k)
            return carry
        lax.fori_loop(lo, hi, step, 0)

    vectors[z, x] = vector[...]
    for k in (1, 2, 3):
        vector_copy(0, k).start()
    vector_copy(1, 0).start()
    for t in range(n):
        copy(2, t, 0).start()
        copy(3, t, 0).start()
    def spread(k):
        for t in range(n):
            copy(0, t, k).start()
            copy(1, t, k).start()
    each(1, 4, spread)
    for t in range(n):
        own(t).start()
    for k in (1, 2, 3):
        vector_copy(0, k).wait_recv()
        vector_copy(1, k).start()

    def along_x(k):
        for t in range(n):
            copy(0, t, k).wait_recv()
            copy(2, t, k).start()
            copy(1, t, k).wait_recv()
            copy(3, t, k).start()
    each(1, 4, along_x)

    for t in range(n):
        own(t).wait()
        copy(3, t, 0).wait_recv()
        copy(4, t, 0).start()
    def along_y(k):
        for t in range(n):
            copy(3, t, k).wait_recv()
            copy(4, t, k).start()
    each(1, 4, along_y)

    for t in range(n):
        copy(2, t, 0).wait_recv()
        copy(4, t, 0).wait_recv()
        copy(5, t, 0).start()
    def across(k):
        for t in range(n):
            copy(2, t, k).wait_recv()
            copy(4, t, k).wait_recv()
            copy(5, t, k).start()
    each(1, 4, across)

    for t in range(n):
        for stage in (2, 3, 4, 5):
            copy(stage, t, 0).wait_send()
        copy(5, t, 0).wait_recv()
    def finish(k):
        for t in range(n):
            for stage in range(6):
                copy(stage, t, k).wait_send()
            copy(5, t, k).wait_recv()
    each(1, 4, finish)
    vector_copy(1, 0).wait()
    for k in (1, 2, 3):
        vector_copy(0, k).wait_send()
        vector_copy(1, k).wait()


def gather_weights(shards, vector, ident):
    n = len(shards)
    views, widths = [], []
    for shard in shards:
        rows, total = shard.shape
        views.append(shard.reshape(2, rows // 2, total))
        widths.append((total // 256 + 1) // 3 * 128)
    anywhere, vmem = pl.BlockSpec(memory_space=pl.ANY), pl.BlockSpec(memory_space=pltpu.VMEM)
    dma = pltpu.SemaphoreType.DMA
    out = pl.pallas_call(
        functools.partial(gather_kernel, tuple(widths), n),
        out_shape=tuple(jax.ShapeDtypeStruct((4, 2) + v.shape, BF16) for v in views)
        + (jax.ShapeDtypeStruct((4, 2, 8, 128), F32),),
        in_specs=[anywhere] * n + [vmem],
        out_specs=(anywhere,) * n + (vmem,),
        scratch_shapes=[dma((n, 6, 4)), dma((n, 6, 4)), dma((n,)), dma((8,)), dma((8,))],
        compiler_params=pltpu.CompilerParams(collective_id=ident, has_side_effects=True),
        name="gather",
    )(*views, vector.reshape(8, 128))
    return [o.reshape(-1, o.shape[4]) for o in out[:n]], out[n].reshape(-1)


def layer_norm(stream, gain, offset):
    centre = stream - jnp.mean(stream, axis=-1, keepdims=True)
    spread = jnp.mean(centre * centre, axis=-1, keepdims=True)
    return centre * lax.rsqrt(spread + 1e-06) * gain + offset


def sincos(time_pos, frequency, width):
    quarter = width // 4
    omega = 1.0 / 10000.0 ** (jnp.arange(quarter, dtype=jnp.float32) / quarter)
    time_angle = time_pos.astype(jnp.float32)[:, None] * omega[None, :]
    band_angle = frequency.astype(jnp.float32)[:, None] * omega[None, :]
    return jnp.concatenate(
        [jnp.sin(time_angle), jnp.cos(time_angle), jnp.sin(band_angle), jnp.cos(band_angle)], axis=1
    )


def clip_of(column, clip_lengths, clip_shifts):
    columns = clip_lengths // 8
    ends = jnp.cumsum(columns)
    clip_id = jnp.sum((column[:, None] >= ends[None, :]).astype(jnp.int32), axis=1)
    onehot = (clip_id[:, None] == jnp.arange(clip_lengths.shape[0], dtype=jnp.int32)[None, :]).astype(jnp.int32)

    def select(values):
        return jnp.sum(onehot * values[None, :], axis=1)

    return clip_id, select(ends - columns), select(columns), select(clip_shifts[:, 0]), select(clip_shifts[:, 1])


def product(values_in, weights_in):
    return jnp.dot(values_in, weights_in, preferred_element_type=jnp.float32)


def input_grad(grad_low, weights_in):
    return lax.dot_general(
        grad_low, weights_in, (((1,), (1,)), ((), ())), preferred_element_type=jnp.float32
    )


def weight_grad(values_in, grad_low):
    return lax.dot_general(
        values_in, grad_low, (((0,), (0,)), ((), ())), preferred_element_type=jnp.float32
    )


def split_heads(projections, heads, group):
    rows = projections.shape[0]
    head_size = projections.shape[1] // (3 * heads)
    split_parts = projections.reshape(rows // group, group, 3, heads, head_size)
    return (split_parts[:, :, 0], split_parts[:, :, 1], split_parts[:, :, 2], head_size)


def softmax_probs(query, key_rows, head_size, score_bias):
    scores = jnp.einsum("bqhd,bkhd->bhqk", query, key_rows, preferred_element_type=jnp.float32)
    return jax.nn.softmax(scores * head_size ** (-0.5) + score_bias, axis=-1)


def attend(projections, heads, group, score_bias):
    query, key_rows, value_rows, head_size = split_heads(projections, heads, group)
    probs = softmax_probs(query, key_rows, head_size, score_bias)
    mixed = jnp.einsum(
        "bhqk,bkhd->bqhd",
        probs.astype(jnp.bfloat16),
        value_rows,
        preferred_element_type=jnp.float32,
    )
    return mixed.reshape(projections.shape[0], -1)


def attend_back(grad_mixed, projections, heads, group, score_bias):
    query, key_rows, value_rows, head_size = split_heads(projections, heads, group)
    probs = softmax_probs(query, key_rows, head_size, score_bias)
    grad_heads = grad_mixed.reshape(query.shape)
    grad_probs = jnp.einsum(
        "bqhd,bkhd->bhqk", grad_heads, value_rows, preferred_element_type=jnp.float32
    )
    grad_values = jnp.einsum(
        "bhqk,bqhd->bkhd",
        probs.astype(jnp.bfloat16),
        grad_heads,
        preferred_element_type=jnp.float32,
    )
    grad_scores = probs * (grad_probs - jnp.sum(grad_probs * probs, axis=-1, keepdims=True))
    scaled = (grad_scores * head_size ** (-0.5)).astype(jnp.bfloat16)
    grad_query = jnp.einsum("bhqk,bkhd->bqhd", scaled, key_rows, preferred_element_type=jnp.float32)
    grad_keys = jnp.einsum("bhqk,bqhd->bkhd", scaled, query, preferred_element_type=jnp.float32)
    return jnp.stack([grad_query, grad_keys, grad_values], axis=2).reshape(projections.shape[0], -1)


def block_forward(stream, weights, gains, heads, group, score_bias):
    w_qkv, w_out, w_up, w_down = weights
    normed = layer_norm(stream, gains[0], gains[1]).astype(jnp.bfloat16)
    projections = product(normed, w_qkv).astype(jnp.bfloat16)
    attended = attend(projections, heads, group, score_bias).astype(jnp.bfloat16)
    middle = stream + product(attended, w_out)
    second_normed = layer_norm(middle, gains[2], gains[3]).astype(jnp.bfloat16)
    up_values = product(second_normed, w_up)
    activated = jax.nn.gelu(up_values).astype(jnp.bfloat16)
    return (
        middle + product(activated, w_down),
        (stream, normed, projections, attended, middle, second_normed, up_values, activated),
    )


def block_backward(grad_out, cache, weights, gains, heads, group, score_bias):
    w_qkv, w_out, w_up, w_down = weights
    stream, normed, projections, attended, middle, second_normed, up_values, activated = cache
    grad_down = grad_out.astype(jnp.bfloat16)
    g_down = weight_grad(activated, grad_down)
    _, gelu_back = jax.vjp(jax.nn.gelu, up_values)
    grad_up = gelu_back(input_grad(grad_down, w_down))[0].astype(jnp.bfloat16)
    g_up = weight_grad(second_normed, grad_up)
    _, norm_back = jax.vjp(layer_norm, middle, gains[2], gains[3])
    grad_middle, g_gain_two, g_offset_two = norm_back(input_grad(grad_up, w_up))
    grad_middle = grad_middle + grad_out
    grad_branch = grad_middle.astype(jnp.bfloat16)
    g_out = weight_grad(attended, grad_branch)
    grad_attended = input_grad(grad_branch, w_out).astype(jnp.bfloat16)
    grad_projections = attend_back(grad_attended, projections, heads, group, score_bias).astype(
        jnp.bfloat16
    )
    g_qkv = weight_grad(normed, grad_projections)
    _, first_back = jax.vjp(layer_norm, stream, gains[0], gains[1])
    grad_stream, g_gain_one, g_offset_one = first_back(input_grad(grad_projections, w_qkv))
    norm_grads = jnp.stack([g_gain_one, g_offset_one, g_gain_two, g_offset_two])
    return (grad_stream + grad_middle, (g_qkv, g_out, g_up, g_down), norm_grads)


def adam_update(weight, first, second, grad, decay):
    first = BETA_ONE * first + (1.0 - BETA_ONE) * grad
    second = BETA_TWO * second + (1.0 - BETA_TWO) * grad * grad
    first_hat = first / (1.0 - BETA_ONE**STEP)
    second_hat = second / (1.0 - BETA_TWO**STEP)
    weight = weight - LEARN_RATE * (first_hat / (jnp.sqrt(second_hat) + EPSILON) + decay * weight)
    return (weight, first, second)


def shards(
    pixels,
    lengths,
    shifts,
    visible,
    patch_embed,
    encoder_in,
    encoder_down,
    decoder_in,
    decoder_down,
    norm_vectors,
    first_embed,
    first_encoder_in,
    first_encoder_down,
    first_decoder_in,
    first_decoder_down,
    first_vectors,
    second_embed,
    second_encoder_in,
    second_encoder_down,
    second_decoder_in,
    second_decoder_down,
    second_vectors,
):
    masters = (patch_embed, encoder_in, encoder_down, decoder_in, decoder_down, norm_vectors)
    firsts = (
        first_embed,
        first_encoder_in,
        first_encoder_down,
        first_decoder_in,
        first_decoder_down,
        first_vectors,
    )
    seconds = (
        second_embed,
        second_encoder_in,
        second_encoder_down,
        second_decoder_in,
        second_decoder_down,
        second_vectors,
    )
    direct = lax.axis_size("clip") == 8 and lax.axis_size("band") == 4
    low_shards = [master.astype(jnp.bfloat16) for master in masters]
    if direct:
        (w_embed, w_enc, w_enc_down, w_dec, w_dec_down), vectors = gather_weights(
            low_shards[:5], lax.reduce_precision(norm_vectors, exponent_bits=8, mantissa_bits=7), 0
        )
    else:
        w_embed, w_enc, w_enc_down, w_dec, w_dec_down, gathered_vectors = (
            lax.all_gather(shard, "clip", axis=0, tiled=True) for shard in low_shards
        )
        vectors = gathered_vectors.astype(jnp.float32)
    enc_width, dec_width = (w_enc.shape[0], w_dec.shape[0])
    enc_hidden, dec_hidden = (w_enc_down.shape[0], w_dec_down.shape[0])
    enc_gains = vectors[: 6 * enc_width].reshape(6, enc_width)
    dec_gains = vectors[6 * enc_width :].reshape(7, dec_width)
    enc_weights = (
        w_enc[:, : 3 * enc_width],
        w_enc[:, 3 * enc_width : 4 * enc_width],
        w_enc[:, 4 * enc_width : 4 * enc_width + enc_hidden],
        w_enc_down,
    )
    w_proj = w_enc[:, 4 * enc_width + enc_hidden :]
    patch_dev, n_visible = pixels.shape[0], visible.shape[0]
    turned = jnp.arange(patch_dev // 8, dtype=jnp.int32)
    _, start, size, shift_time, shift_band = clip_of(turned, lengths[0], shifts[0])
    turned_time = (turned - start - shift_time) % size
    decoder_pixels = pixels.reshape(patch_dev // 8, 8, -1)[start + turned_time].reshape(pixels.shape)
    seen = pixels[visible]
    seen_column, seen_band = visible // 8, visible % 8
    segment, seen_start, seen_size, seen_shift, _ = clip_of(seen_column, lengths[0], shifts[0])
    seen_time = seen_column - seen_start
    decoder_row = 8 * (seen_start + (seen_time + seen_shift) % seen_size) + seen_band
    padded = -(-n_visible // 128) * 128
    decoder_row = jnp.pad(decoder_row, (0, padded - n_visible), constant_values=-1)
    decoder_row = jnp.broadcast_to(decoder_row[:, None], (padded, 128))
    score_bias = jnp.where(segment[:, None] == segment[None, :], 0.0, -1e30)
    embedded = product(seen, w_embed) + sincos(seen_time, seen_band, enc_width)
    encoded, enc_cache = block_forward(
        embedded, enc_weights, enc_gains, HEADS_ENC, seen.shape[0], score_bias
    )
    final_enc = layer_norm(encoded, enc_gains[4], enc_gains[5]).astype(jnp.bfloat16)
    projected = product(final_enc, w_proj)
    grid_seen = (projected + sincos(seen_time, seen_band, dec_width)).astype(jnp.bfloat16)
    grid_seen = jnp.pad(grid_seen, ((0, padded - n_visible), (0, 0)))
    time_table = sincos(turned_time, turned_time, dec_width)[:, : dec_width // 2]
    bands = jnp.arange(8, dtype=jnp.int32)
    band_table = jnp.tile(sincos(bands, bands, dec_width)[:, dec_width // 2 :].T, (1, 16))
    wide_vectors = jnp.broadcast_to(dec_gains[:, :, None], dec_gains.shape + (128,))
    masked_count = 13.0 * (patch_dev // 16) * lax.axis_size("clip") * lax.axis_size("band")
    g_dec_in, g_dec_down, g_dec_vectors, grad_proj, loss = decoder_step(
        shift_band[::64],
        decoder_row,
        grid_seen.T,
        decoder_pixels,
        time_table,
        band_table,
        wide_vectors,
        w_dec,
        w_dec.T,
        w_dec_down,
        w_dec_down.T,
        2.0 / (pixels.shape[1] * masked_count),
        HEADS_DEC,
    )
    local_loss = jnp.sum(loss[0])
    g_dec_vectors = jnp.sum(g_dec_vectors, axis=2)
    grad_proj = grad_proj[:n_visible].astype(jnp.bfloat16)
    g_proj = weight_grad(final_enc, grad_proj)
    _, enc_final_back = jax.vjp(layer_norm, encoded, enc_gains[4], enc_gains[5])
    grad_encoded, g_enc_gain, g_enc_offset = enc_final_back(input_grad(grad_proj, w_proj))
    grad_embedded, g_enc_mats, g_enc_norms = block_backward(
        grad_encoded, enc_cache, enc_weights, enc_gains, HEADS_ENC, seen.shape[0], score_bias
    )
    g_embed = weight_grad(seen, grad_embedded.astype(jnp.bfloat16))
    g_enc_in = jnp.concatenate([g_enc_mats[0], g_enc_mats[1], g_enc_mats[2], g_proj], axis=1)
    g_vectors = jnp.concatenate(
        [
            g_enc_norms.reshape(-1),
            g_enc_gain,
            g_enc_offset,
            g_dec_vectors.reshape(-1),
        ]
    )
    if direct:
        small = jnp.concatenate([g_vectors.reshape(-1, 128), jnp.full((8, 128), local_loss)])
        dec_shards, _ = reduce_grads([g_dec_in, g_dec_down], small[:8], 1)
        enc_shards, summed = reduce_grads([g_embed, g_enc_in, g_enc_mats[3]], small, 2)
        rows = norm_vectors.shape[0]
        own = lax.dynamic_slice(summed[:-8].reshape(-1), (lax.axis_index("clip") * rows,), (rows,))
        reduced = (*enc_shards, *dec_shards, own)
        loss_sum = summed[-1, 0]
    else:
        reduced = lax.psum(
            tuple(
                lax.psum_scatter(grad, "clip", scatter_dimension=0, tiled=True)
                for grad in (g_embed, g_enc_in, g_enc_mats[3], g_dec_in, g_dec_down, g_vectors)
            ),
            "band",
        )
        loss_sum = lax.psum(local_loss, ("clip", "band"))
    squares = jnp.zeros((), jnp.float32)
    for grad in reduced:
        squares = squares + jnp.sum(grad * grad)
    norm_squared = lax.psum(squares, "clip")
    grad_norm = jnp.sqrt(norm_squared)
    factor = jnp.minimum(1.0, CLIP_LIMIT / (grad_norm + 1e-06))
    results = []
    for index in range(6):
        decay = DECAY_RATE if index < 5 else 0.0
        results.append(
            adam_update(
                masters[index], firsts[index], seconds[index], reduced[index] * factor, decay
            )
        )
    return (
        loss_sum,
        grad_norm,
        results[0][0],
        results[1][0],
        results[2][0],
        results[3][0],
        results[4][0],
        results[5][0],
        results[0][1],
        results[1][1],
        results[2][1],
        results[3][1],
        results[4][1],
        results[5][1],
        results[0][2],
        results[1][2],
        results[2][2],
        results[3][2],
        results[4][2],
        results[5][2],
    )


def solution(mesh):
    in_specs = (
        P(("clip", "band"), None),
        P(("clip", "band"), None),
        P(("clip", "band"), None, None),
        P(("clip", "band")),
        P("clip", None),
        P("clip", None),
        P("clip", None),
        P("clip", None),
        P("clip", None),
        P("clip"),
        P("clip", None),
        P("clip", None),
        P("clip", None),
        P("clip", None),
        P("clip", None),
        P("clip"),
        P("clip", None),
        P("clip", None),
        P("clip", None),
        P("clip", None),
        P("clip", None),
        P("clip"),
    )
    out_specs = (
        P(),
        P(),
        P("clip", None),
        P("clip", None),
        P("clip", None),
        P("clip", None),
        P("clip", None),
        P("clip"),
        P("clip", None),
        P("clip", None),
        P("clip", None),
        P("clip", None),
        P("clip", None),
        P("clip"),
        P("clip", None),
        P("clip", None),
        P("clip", None),
        P("clip", None),
        P("clip", None),
        P("clip"),
    )
    return jax.shard_map(shards, mesh=mesh, in_specs=in_specs, out_specs=out_specs, check_vma=False)
```

```python
import functools

import jax
import jax.numpy as jnp
from jax import lax
from jax.experimental import pallas as pl
from jax.experimental.pallas import tpu as pltpu
from jax.sharding import PartitionSpec as P

HEADS_ENC = 12
HEADS_DEC = 16
STEP = 10


LEARN_RATE = 0.02
BETA_ONE = 0.9
BETA_TWO = 0.95
EPSILON = 1e-08
DECAY_RATE = 0.05
CLIP_LIMIT = 0.001


F32, BF16 = jnp.float32, jnp.bfloat16
GELU_C = 0.7978845608028654


def mm(a, b, ca=1, cb=0):
    return lax.dot_general(a, b, (((ca,), (cb,)), ((), ())), preferred_element_type=F32)


def wide(v, n):
    return jnp.concatenate([v] * (n // 128), axis=1)


def loop(n, body, unroll=1):
    def step(i, carry):
        for k in range(unroll):
            body(i * unroll + k)
        return carry
    lax.fori_loop(0, n // unroll, step, 0)


def fold(v):
    total = v[:, :128]
    for i in range(1, v.shape[1] // 128):
        total = total + v[:, 128 * i : 128 * (i + 1)]
    return total


def decoder_kernel(
    coef, heads, shift_ref, rvis_ref, gvt_ref, pix_ref, et_ref, ef_ref, vec_ref, w_ref, wt_ref, wd_ref, wdt_ref,
    gin_ref, gdown_ref, gvec_ref, gp_ref, loss_ref,
    res, xh1, xh2, xh3, tmp, n1, n2, fin, rs, qkv, att, act, dgel, probs, dqkv, dup, low, oh, mrow, hb, hm, wm,
):
    width = w_ref.shape[0]
    hidden = wd_ref.shape[0]
    rows = res.shape[1]
    size = width // heads
    per = 128 // size
    scale = size ** -0.5
    groups = width // 128
    c_out, c_up, c_head = 3 * width, 4 * width, 4 * width + hidden
    pixels = w_ref.shape[1] - c_head
    cols = rows // 8
    nblk = pix_ref.shape[0] // rows
    chunk = 512

    gin_ref[...] = jnp.zeros_like(gin_ref)
    gdown_ref[...] = jnp.zeros_like(gdown_ref)
    gvec_ref[...] = jnp.zeros_like(gvec_ref)
    gp_ref[...] = jnp.zeros_like(gp_ref)
    loss_ref[...] = jnp.zeros_like(loss_ref)
    f_id = lax.broadcasted_iota(jnp.int32, (128, 128 * per), 0)
    q_id = lax.broadcasted_iota(jnp.int32, (128, 128 * per), 1)
    hm[...] = jnp.where(f_id // size == q_id // 128, 1.0, 0.0).astype(BF16)
    wm[...] = jnp.where(f_id // 32 == (q_id % 128) // 32, 1.0, 0.0).astype(BF16)

    def lane(i):
        return pl.ds(pl.multiple_of(i * 128, 128), 128)

    def ln_forward(k, xh, out):
        def body(i):
            x = res[:, lane(i)]
            centre = x - jnp.mean(x, axis=0, keepdims=True)
            r = lax.rsqrt(jnp.mean(centre * centre, axis=0, keepdims=True) + 1e-06)
            xhat = centre * r
            xh[:, lane(i)] = xhat
            rs[8 * k : 8 * k + 8, lane(i)] = jnp.broadcast_to(r, (8, 128))
            out[:, lane(i)] = (xhat * vec_ref[2 * k] + vec_ref[2 * k + 1]).astype(BF16)
        loop(rows // 128, body, 4)

    def ln_backward(k, xh, add):
        def body(i):
            d = tmp[:, lane(i)]
            xhat = xh[:, lane(i)]
            gvec_ref[2 * k] += d * xhat
            gvec_ref[2 * k + 1] += d
            dx = d * vec_ref[2 * k]
            m1 = jnp.mean(dx, axis=0, keepdims=True)
            m2 = jnp.mean(dx * xhat, axis=0, keepdims=True)
            g = rs[8 * k : 8 * k + 1, lane(i)] * (dx - m1 - xhat * m2)
            if add:
                g = g + res[:, lane(i)]
            res[:, lane(i)] = g
            low[:, lane(i)] = g.astype(BF16)
        loop(rows // 128, body, 4)

    def block(j):
        first = pl.multiple_of(j * rows, rows)
        turn = shift_ref[j]
        spot = lax.broadcasted_iota(jnp.int32, (rvis_ref.shape[0], rows), 1) + first
        hot = jnp.where(wide(rvis_ref[...], rows) == spot, 1.0, 0.0)
        oh[...] = hot.astype(BF16)
        masked = 1.0 - jnp.sum(hot, axis=0, keepdims=True)
        mrow[...] = jnp.broadcast_to(masked, (8, rows))
        et = et_ref[pl.ds(pl.multiple_of(j * cols, cols), cols), :]
        e_hi = et.astype(BF16)
        rest = et - e_hi.astype(F32)
        e_mid = rest.astype(BF16)
        e_lo = (rest - e_mid.astype(F32)).astype(BF16)
        spread = jnp.where(
            lax.broadcasted_iota(jnp.int32, (cols, rows), 1) // 8 == lax.broadcasted_iota(jnp.int32, (cols, rows), 0), 1.0, 0.0
        ).astype(BF16)
        e_t = mm(e_hi, spread, 0, 0) + (mm(e_mid, spread, 0, 0) + mm(e_lo, spread, 0, 0))
        half = width // 2
        keep = masked > 0.5
        placed = mm(gvt_ref[...], oh[...])
        top = (wide(vec_ref[6, :half], rows) + e_t).astype(BF16).astype(F32)
        res[:half] = jnp.where(keep, top, placed[:half])
        bottom = wide((vec_ref[6, half:] + ef_ref[...]).astype(BF16).astype(F32), rows)
        res[half:] = jnp.where(keep, bottom, placed[half:])
        k_half = (lax.broadcasted_iota(jnp.int32, (32, 128 * per), 0) % 8 + turn) % 8 // 4
        q_half = (lax.broadcasted_iota(jnp.int32, (32, 128 * per), 1) % 8 + turn) % 8 // 4
        hb[...] = jnp.where(k_half == q_half, 0.0, -1e30)

        ln_forward(0, xh1, n1)

        def qkv_part(i):
            part = pl.ds(pl.multiple_of(i * chunk, chunk), chunk)
            qkv[part, :] = mm(wt_ref[part, :], n1[...]).astype(BF16)
        loop(3 * width // chunk, qkv_part)

        q_group = (lax.broadcasted_iota(jnp.int32, (32, 128 * per), 1) % 128) // 32

        def compact(s):
            c = s[96:128]
            for i in (2, 1, 0):
                c = jnp.where(q_group == i, s[32 * i : 32 * i + 32], c)
            return c

        def attend(i):
            sb, g = i // groups, i % groups
            at = lane(sb)
            f0 = pl.multiple_of(g * 128, 128)
            q = qkv[pl.ds(f0, 128), at]
            k = qkv[pl.ds(width + f0, 128), at]
            v = qkv[pl.ds(2 * width + f0, 128), at]
            s = mm(k.T, wide(q, 128 * per) * hm[...])
            c = compact(s) * scale + hb[...]
            e = jnp.exp(c - jnp.max(c, axis=0, keepdims=True))
            p = e * (1.0 / jnp.sum(e, axis=0, keepdims=True))
            probs[i] = p
            p_low = p.astype(BF16)
            p_all = jnp.concatenate([p_low] * 4, axis=0) * wm[...]
            for h in range(per):
                o = mm(v[size * h : size * h + size], p_all[:, 128 * h : 128 * h + 128])
                att[pl.ds(f0 + size * h, size), at] = o.astype(BF16)
        loop(rows // 128 * groups, attend, 4)

        res[...] += mm(wt_ref[c_out : c_out + width], att[...])
        ln_forward(1, xh2, n2)

        def up_part(i):
            part = pl.ds(pl.multiple_of(i * chunk, chunk), chunk)
            u = mm(wt_ref[pl.ds(pl.multiple_of(c_up + i * chunk, chunk), chunk), :], n2[...])
            t = jnp.tanh(GELU_C * (u + 0.044715 * (u * u * u)))
            hp = 0.5 * (1.0 + t)
            act[part, :] = (u * hp).astype(BF16)
            dgel[part, :] = hp + (0.5 * GELU_C) * u * (1.0 - t * t) * (1.0 + 0.134145 * (u * u))
        loop(hidden // chunk, up_part)

        res[...] += mm(wdt_ref[...], act[...])
        ln_forward(2, xh3, fin)
        pred = mm(wt_ref[c_head:], fin[...])
        pix = pix_ref[pl.ds(first, rows), :].astype(F32).T
        centre = pix - jnp.mean(pix, axis=0, keepdims=True)
        target = (centre * lax.rsqrt(jnp.mean(centre * centre, axis=0, keepdims=True) + 1e-06)).astype(BF16).astype(F32)
        err = pred - target
        loss_ref[...] += fold(mrow[...] * jnp.mean(err * err, axis=0, keepdims=True))
        gpred = (mrow[0:1] * err * coef).astype(BF16)

        gin_ref[:, c_head:] += mm(fin[...], gpred, 1, 1)
        tmp[...] = mm(w_ref[:, c_head:], gpred)
        ln_backward(2, xh3, False)

        def mlp_back(i):
            part = pl.ds(pl.multiple_of(i * chunk, chunk), chunk)
            there = pl.ds(pl.multiple_of(c_up + i * chunk, chunk), chunk)
            d = (mm(wd_ref[part, :], low[...]) * dgel[part, :]).astype(BF16)
            dup[part, :] = d
            gdown_ref[part, :] += mm(act[part, :], low[...], 1, 1)
            gin_ref[:, there] += mm(n2[...], d, 1, 1)
        loop(hidden // chunk, mlp_back)
        tmp[...] = mm(w_ref[:, c_up:c_head], dup[...])
        ln_backward(1, xh2, True)
        gin_ref[:, c_out:c_up] += mm(att[...], low[...], 1, 1)
        fin[...] = mm(w_ref[:, c_out:c_up], low[...]).astype(BF16)

        def attend_back(i):
            sb, g = i // groups, i % groups
            at = lane(sb)
            f0 = pl.multiple_of(g * 128, 128)
            q = qkv[pl.ds(f0, 128), at]
            k = qkv[pl.ds(width + f0, 128), at]
            v = qkv[pl.ds(2 * width + f0, 128), at]
            do = fin[pl.ds(f0, 128), at]
            dp = compact(mm(v.T, wide(do, 128 * per) * hm[...]))
            p = probs[i]
            ds = p * (dp - jnp.sum(dp * p, axis=0, keepdims=True))
            p_all = jnp.concatenate([p.astype(BF16)] * 4, axis=0) * wm[...]
            ds_all = jnp.concatenate([(ds * scale).astype(BF16)] * 4, axis=0) * wm[...]
            for h in range(per):
                rows_h = slice(size * h, size * h + size)
                ds_h = ds_all[:, 128 * h : 128 * h + 128]
                p_h = p_all[:, 128 * h : 128 * h + 128]
                dqkv[pl.ds(f0 + size * h, size), at] = mm(k[rows_h], ds_h).astype(BF16)
                dqkv[pl.ds(width + f0 + size * h, size), at] = mm(q[rows_h], ds_h, 1, 1).astype(BF16)
                dqkv[pl.ds(2 * width + f0 + size * h, size), at] = mm(do[rows_h], p_h, 1, 1).astype(BF16)
        loop(rows // 128 * groups, attend_back, 4)

        def qkv_back(i):
            part = pl.ds(pl.multiple_of(i * chunk, chunk), chunk)
            gin_ref[:, part] += mm(n1[...], dqkv[part, :], 1, 1)
        loop(3 * width // chunk, qkv_back)
        tmp[...] = mm(w_ref[:, :c_out], dqkv[...])
        ln_backward(0, xh1, True)
        gvec_ref[6] += fold(low[...].astype(F32) * mrow[0:1])
        gp_ref[...] += mm(oh[...], low[...], 1, 1)

    loop(nblk, block)


def decoder_step(shift, rvis, gvt, pix, et, ef, vec, w, wt, wd, wdt, coef, heads):
    width, total = w.shape
    hidden = wd.shape[0]
    rows = 512
    vis = rvis.shape[0]
    per = 128 // (width // heads)
    vmem = pl.BlockSpec(memory_space=pltpu.VMEM)
    f = lambda *s: pltpu.VMEM(s, F32)
    b = lambda *s: pltpu.VMEM(s, BF16)
    return pl.pallas_call(
        functools.partial(decoder_kernel, coef, heads),
        out_shape=(
            jax.ShapeDtypeStruct((width, total), F32),
            jax.ShapeDtypeStruct((hidden, width), F32),
            jax.ShapeDtypeStruct((7, width, 128), F32),
            jax.ShapeDtypeStruct((vis, width), F32),
            jax.ShapeDtypeStruct((8, 128), F32),
        ),
        in_specs=[pl.BlockSpec(memory_space=pltpu.SMEM)] + [vmem] * 10,
        out_specs=(vmem,) * 5,
        scratch_shapes=[
            f(width, rows), f(width, rows), f(width, rows), f(width, rows), f(width, rows),
            b(width, rows), b(width, rows), b(width, rows), f(24, rows),
            b(3 * width, rows), b(width, rows), b(hidden, rows), f(hidden, rows),
            f(rows // 128 * (width // 128), 32, 128 * per), b(3 * width, rows), b(hidden, rows), b(width, rows),
            b(vis, rows), f(8, rows), f(32, 128 * per), b(128, 128 * per), b(128, 128 * per),
        ],
        compiler_params=pltpu.CompilerParams(vmem_limit_bytes=63 * 2**20),
        name="decoder",
    )(shift, rvis, gvt, pix, et, ef, vec, w, wt, wd, wdt)


def place():
    clip, band = lax.axis_index("clip"), lax.axis_index("band")
    return clip // 2, clip % 2, band // 2, band % 2


def device(z, x, y, c):
    return (z * 2 + x, y * 2 + c)


def greet(z, x, y, c):
    barrier = pltpu.get_barrier_semaphore()
    others = [device(z, x, y, 1 - c), device(z, 1 - x, y, c), device(z, x, 1 - y, c)]
    others += [device((z + k) % 4, x, y, c) for k in (1, 2, 3)]
    for other in others:
        pl.semaphore_signal(barrier, inc=1, device_id=other, device_id_type=pl.DeviceIdType.MESH)
    pl.semaphore_wait(barrier, len(others))


def remote(src, dst, send, recv, to):
    return pltpu.make_async_remote_copy(
        src_ref=src, dst_ref=dst, send_sem=send, recv_sem=recv, device_id=to, device_id_type=pl.DeviceIdType.MESH
    )


def reduce_kernel(widths, n, *refs):
    grads, small, before = refs[:n], refs[n], refs[n + 1]
    outs, small_out, squares = refs[n + 2 : 2 * n + 2], refs[2 * n + 2], refs[2 * n + 3]
    rest = refs[2 * n + 4 :]
    sums, r0 = rest[:n], rest[n : 2 * n]
    coded = {1 + i: rest[(2 + i) * n : (3 + i) * n] for i in range(5)}
    came = {1 + i: rest[(7 + i) * n : (8 + i) * n] for i in range(5)}
    step_out = {1 + i: rest[(12 + i) * n : (13 + i) * n] for i in range(5)}
    step_in = {1 + i: rest[(17 + i) * n : (18 + i) * n] for i in range(5)}
    s_buf, s_sum, q_buf, q_sum, send, recv, near, t_send, t_recv, s_send, s_recv = rest[22 * n :]
    z, x, y, c = place()
    greet(z, x, y, c)

    def at_z(k):
        return (z + k) % 4

    def columns(t, core):
        half = sums[t].shape[4]
        return pl.ds(pl.multiple_of(core * half, 128), half)

    def local(t, k):
        zk = at_z(k)
        return pltpu.make_async_copy(grads[t].at[zk, :, :, :, columns(t, c)], sums[t].at[zk], near.at[t, k])

    def target(stage, k):
        return {
            1: lambda: device(z, 1 - x, y, c),
            2: lambda: device(z, x, 1 - y, c),
            3: lambda: device(z, x, 1 - y, c),
            4: lambda: device(z, 1 - x, y, c),
            5: lambda: device(at_z(k), x, y, c),
        }[stage]()

    def copy(stage, t, k):
        if stage == 0:
            src, dst, to = grads[t].at[at_z(k), :, :, :, columns(t, 1 - c)], r0[t].at[at_z(k)], device(z, x, y, 1 - c)
        elif stage == 6:
            src, dst, to = sums[t].at[z, x, y], outs[t].at[y, :, columns(t, c)], device(z, x, 1 - y, c)
        elif stage == 7:
            src = outs[t].at[:, :, columns(t, c)]
            dst, to = src, device(z, x, y, 1 - c)
        else:
            src, dst, to = coded[stage][t].at[k], came[stage][t].at[k], target(stage, k)
        return remote(src, dst, send.at[t, stage, k], recv.at[t, stage, k], to)

    def steps(stage, t, k):
        src, dst = step_out[stage][t].at[k], step_in[stage][t].at[k]
        return remote(src, dst, t_send.at[t, stage, k], t_recv.at[t, stage, k], target(stage, k))

    def keep(t):
        return pltpu.make_async_copy(sums[t].at[z, x, y], outs[t].at[y, :, columns(t, c)], near.at[t, 4])

    def each(lo, hi, body):
        def one(k, carry):
            body(k)
            return carry
        lax.fori_loop(lo, hi, one, 0)

    def slab(i, height):
        return pl.ds(pl.multiple_of(i * height, height), height)

    def part(stage, t):
        w = widths[t]
        return slice(0, w) if stage in (1, 3) else slice(w, None) if stage in (2, 4) else slice(None)

    def encode(stage, t, k, parts, read):
        rows = sums[t].shape[3]
        zk, width = at_z(k), coded[stage][t].shape[-1]
        block = lambda p: coded[stage][t].at[(k, p) if parts > 1 else k]
        per = rows // 8
        def peak(i, most):
            return jnp.maximum(most, jnp.abs(read(zk, i // per, slab(i % per, 8))))
        most = lax.fori_loop(0, parts * per, peak, jnp.zeros((8, width), F32))
        most = jnp.maximum(jnp.max(most, axis=0, keepdims=True), 1e-30)
        step_out[stage][t][k] = most * (1.0 / 32767.0)
        steps(stage, t, k).start()
        scale = 32767.0 / most
        half = rows // 16
        def one(i):
            values = jnp.round(read(zk, i // half, slab(i % half, 16)) * scale).astype(jnp.int32).astype(jnp.int16)
            block(i // half)[slab(i % half, 16)] = values
        each(0, parts * half, one)
        copy(stage, t, k).start()

    def landed(stage, t, k):
        steps(stage, t, k).wait_recv()
        copy(stage, t, k).wait_recv()

    def decoded(stage, t, k, p, rows, parts):
        values = came[stage][t][(k, p, rows) if parts > 1 else (k, rows)]
        return values.astype(jnp.int32).astype(F32) * step_in[stage][t][k]

    order = (2, 1, 3, 0)
    for t in range(n):
        for k in order:
            copy(0, t, k).start()
            local(t, k).start()

    def hop(total, buffer, first, stage, to):
        return remote(total, buffer.at[stage], s_send.at[first + stage], s_recv.at[first + stage], to)

    def advance(total, buffer, first, stage):
        neighbours = (device(z, x, y, 1 - c), device(z, 1 - x, y, c), device(z, x, 1 - y, c))
        if stage:
            hop(total, buffer, first, stage - 1, neighbours[stage - 1]).wait()
            total[...] += buffer[stage - 1]
        if stage < 3:
            hop(total, buffer, first, stage, neighbours[stage]).start()
        else:
            for k in (1, 2, 3):
                last_hop(total, buffer, first, k).start()
            buffer[3 + z] = total[...]

    def last_hop(total, buffer, first, k):
        return remote(total, buffer.at[3 + z], s_send.at[first + 2 + k], s_recv.at[first + 2 + k], device(at_z(k), x, y, c))

    def finish_sum(total, buffer, first, out):
        for k in (1, 2, 3):
            last_hop(total, buffer, first, k).wait()
        out[...] = (buffer[3] + buffer[4]) + (buffer[5] + buffer[6])

    s_sum[...] = small[...]

    def first_sum(t, k):
        zk = at_z(k)
        copy(0, t, k).wait_recv()
        local(t, k).wait()
        per = sums[t].shape[3] // 16
        def one(i):
            p, r = i // per, slab(i % per, 16)
            sums[t][zk, p // 2, p % 2, r] += r0[t][zk, p // 2, p % 2, r]
        each(0, 4 * per, one)
        encode(1, t, k, 2, lambda zk, p, r: sums[t][zk, 1 - x, p, r, part(1, t)])
        encode(2, t, k, 2, lambda zk, p, r: sums[t][zk, p, 1 - y, r, part(2, t)])

    def second_sum(t, k):
        zk = at_z(k)
        per = sums[t].shape[3] // 16
        landed(1, t, k)
        def one(i):
            p, r = i // per, slab(i % per, 16)
            sums[t][zk, x, p, r, part(1, t)] += decoded(1, t, k, p, r, 2)
        each(0, 2 * per, one)
        encode(3, t, k, 1, lambda zk, p, r: sums[t][zk, x, 1 - y, r, part(3, t)])
        landed(2, t, k)
        def two(i):
            p, r = i // per, slab(i % per, 16)
            sums[t][zk, p, y, r, part(2, t)] += decoded(2, t, k, p, r, 2)
        each(0, 2 * per, two)
        encode(4, t, k, 1, lambda zk, p, r: sums[t][zk, 1 - x, y, r, part(4, t)])

    def third_sum(t, k):
        zk = at_z(k)
        landed(3, t, k)
        landed(4, t, k)
        def one(i):
            r = slab(i, 16)
            sums[t][zk, x, y, r, part(3, t)] += decoded(3, t, k, 0, r, 1)
            sums[t][zk, x, y, r, part(4, t)] += decoded(4, t, k, 0, r, 1)
        each(0, sums[t].shape[3] // 16, one)
        if k:
            encode(5, t, k, 1, lambda zk, p, r: sums[t][zk, x, y, r])

    def last_sum(t, total):
        for k in (1, 2, 3):
            landed(5, t, k)
        half = sums[t].shape[4]
        def one(i, acc):
            r = slab(i, 16)
            value = sums[t][z, x, y, r]
            for k in (1, 2, 3):
                value = value + decoded(5, t, k, 0, r, 1)
            sums[t][z, x, y, r] = value
            value = value * value
            value = value[:8] + value[8:]
            for j in range(half // 128):
                acc = acc + value[:, 128 * j : 128 * j + 128]
            return acc
        total = lax.fori_loop(0, sums[t].shape[3] // 16, one, total)
        copy(6, t, 0).start()
        keep(t).start()
        return total

    def share(t):
        copy(6, t, 0).wait_recv()
        keep(t).wait()
        copy(7, t, 0).start()

    blocks = [(t, k) for t in range(n) for k in order]
    total = before[...]
    for i in range(len(blocks) + 2):
        if i < len(blocks):
            first_sum(*blocks[i])
        if 0 <= i - 1 < len(blocks):
            second_sum(*blocks[i - 1])
        if 0 <= i - 2:
            third_sum(*blocks[i - 2])
        if i < 4:
            advance(s_sum, s_buf, 0, i)
        for t in range(n - 1):
            if i == 4 * t + 7:
                total = last_sum(t, total)
            if i == 4 * t + 9:
                share(t)
    total = last_sum(n - 1, total)
    finish_sum(s_sum, s_buf, 0, small_out)
    late = [t for t in range(n) if t == n - 1 or 4 * t + 9 >= len(blocks) + 2]
    for t in late[:-1]:
        share(t)
    q_sum[...] = total
    if q_buf.shape[0] > 1:
        for stage in range(4):
            advance(q_sum, q_buf, 6, stage)
        finish_sum(q_sum, q_buf, 6, squares)
    else:
        squares[...] = total
    share(late[-1])

    def finish(k):
        for t in range(n):
            copy(0, t, k).wait_send()
            for stage in range(1, 5):
                copy(stage, t, k).wait_send()
                steps(stage, t, k).wait_send()
    each(0, 4, finish)
    def finish_z(k):
        for t in range(n):
            copy(5, t, k).wait_send()
            steps(5, t, k).wait_send()
    each(1, 4, finish_z)
    for t in range(n):
        copy(6, t, 0).wait_send()
        copy(7, t, 0).wait()


def reduce_grads(grads, small, before, last, ident):
    n = len(grads)
    views, widths = [], []
    scratch = [[] for _ in range(22)]
    f = lambda *s: pltpu.VMEM(s, F32)
    q = lambda *s: pltpu.VMEM(s, jnp.int16)
    for grad in grads:
        rows, cols = grad.shape
        r2, half = rows // 16, cols // 2
        w = (half // 128 * 7 + 5) // 10 * 128
        views.append(grad.reshape(4, 2, 2, r2, cols))
        widths.append(w)
        blocks = [(4, 2, r2, w), (4, 2, r2, half - w), (4, r2, w), (4, r2, half - w), (4, r2, half)]
        for i, s in enumerate([f(4, 2, 2, r2, half)] * 2 + [q(*b) for b in blocks * 2] + [f(4, 1, b[-1]) for b in blocks * 2]):
            scratch[i].append(s)
    anywhere, vmem = pl.BlockSpec(memory_space=pl.ANY), pl.BlockSpec(memory_space=pltpu.VMEM)
    dma = pltpu.SemaphoreType.DMA
    square = jax.ShapeDtypeStruct((8, 128), F32)
    out = pl.pallas_call(
        functools.partial(reduce_kernel, tuple(widths), n),
        out_shape=tuple(jax.ShapeDtypeStruct((2, v.shape[3], v.shape[4]), F32) for v in views)
        + (jax.ShapeDtypeStruct(small.shape, F32), square),
        in_specs=[anywhere] * n + [vmem] * 2,
        out_specs=(anywhere,) * n + (vmem,) * 2,
        scratch_shapes=sum(scratch, []) + [
            f(7, *small.shape), f(*small.shape), f(7 if last else 1, 8, 128), f(8, 128),
            dma((n, 8, 4)), dma((n, 8, 4)), dma((n, 5)), dma((n, 6, 4)), dma((n, 6, 4)), dma((12,)), dma((12,)),
        ],
        compiler_params=pltpu.CompilerParams(
            collective_id=ident, has_side_effects=True, vmem_limit_bytes=60 * 2**20
        ),
        name="reduce",
    )(*views, small, before)
    return [o.reshape(-1, o.shape[2]) for o in out[:n]], out[n], out[n + 1]


def gather_kernel(chunks, n, *refs):
    shards, vector, results, vectors = refs[:n], refs[n], refs[n + 1 : 2 * n + 1], refs[2 * n + 1]
    outs = refs[2 * n + 2 : 3 * n + 2]
    send, recv, near, v_send, v_recv = refs[3 * n + 2 :]
    z, x, y, c = place()
    greet(z, x, y, c)

    def at_z(k):
        return (z + k) % 4

    def own(t):
        return pltpu.make_async_copy(shards[t], outs[t].at[z, x], near.at[t])

    def copy(stage, i, k):
        t, r0, nr, c0, both, split = chunks[i]
        half = shards[t].shape[2] // 2
        columns = lambda lo, size: pl.ds(pl.multiple_of(c * half + lo, 128), size)
        wide, narrow, whole = columns(c0, both), columns(c0 + both, split), columns(c0, both + split)
        rows = pl.ds(r0, nr)
        mine = isinstance(k, int) and k == 0
        o, src_z = outs[t], (z + 4 - k) % 4
        if stage == 0:
            src, dst, to = shards[t].at[:, rows, wide], o.at[z, x, :, rows, wide], device(at_z(k), x, y, c)
        elif stage == 1:
            src, dst, to = shards[t].at[y, rows, narrow], o.at[z, x, y, rows, narrow], device(at_z(k), x, y, c)
        elif stage == 2:
            dst, to = o.at[src_z, x, :, rows, wide], device(z, 1 - x, y, c)
            src = shards[t].at[:, rows, wide] if mine else dst
        elif stage == 3:
            dst, to = o.at[src_z, x, y, rows, narrow], device(z, 1 - x, y, c)
            src = shards[t].at[y, rows, narrow] if mine else dst
        elif stage == 4:
            src = o.at[src_z, 1 - x, y, rows, narrow] if mine else o.at[src_z, :, y, rows, narrow]
            dst, to = src, device(z, x, 1 - y, c)
        else:
            src = o.at[src_z, 1 - x, :, rows, whole] if mine else o.at[src_z, :, :, rows, whole]
            dst, to = src, device(z, x, y, 1 - c)
        return remote(src, dst, send.at[i, stage, k], recv.at[i, stage, k], to)

    def leave(t):
        return pltpu.make_async_copy(outs[t], results[t], near.at[n + t])

    def vector_copy(stage, k):
        src_z = (z + 4 - k) % 4
        if stage == 0:
            return remote(vector, vectors.at[z, x], v_send.at[k], v_recv.at[k], device(at_z(k), x, y, c))
        src = vector if k == 0 else vectors.at[src_z, x]
        return remote(src, vectors.at[src_z, x], v_send.at[4 + k], v_recv.at[4 + k], device(z, 1 - x, y, c))

    def each(lo, hi, body):
        def step(k, carry):
            body(k)
            return carry
        lax.fori_loop(lo, hi, step, 0)

    def along_z(i):
        def one(k):
            copy(0, i, k).start()
            copy(1, i, k).start()
        each(1, 4, one)
        copy(2, i, 0).start()
        copy(3, i, 0).start()

    def along_x(i):
        def one(k):
            copy(0, i, k).wait_recv()
            copy(2, i, k).start()
            copy(1, i, k).wait_recv()
            copy(3, i, k).start()
        each(1, 4, one)

    def along_y(i):
        copy(3, i, 0).wait_recv()
        copy(4, i, 0).start()
        def one(k):
            copy(3, i, k).wait_recv()
            copy(4, i, k).start()
        each(1, 4, one)

    def across(i):
        def one(k):
            copy(2, i, k).wait_recv()
            copy(4, i, k).wait_recv()
            copy(5, i, k).start()
        one(0)
        each(1, 4, one)

    vectors[z, x] = vector[...]
    for k in (1, 2, 3):
        vector_copy(0, k).start()
    vector_copy(1, 0).start()
    along_z(0)
    for t in range(n):
        own(t).start()
    count = len(chunks)
    for i in range(count + 3):
        if i + 1 < count:
            along_z(i + 1)
        if i < count:
            along_x(i)
        if i == 0:
            for t in range(n):
                own(t).wait()
        if i == 1:
            for k in (1, 2, 3):
                vector_copy(0, k).wait_recv()
                vector_copy(1, k).start()
        if 0 <= i - 1 < count:
            along_y(i - 1)
        if 0 <= i - 2 < count:
            across(i - 2)
        if 0 <= i - 3:
            copy(5, i - 3, 0).wait_recv()
            each(1, 4, lambda k, i=i: copy(5, i - 3, k).wait_recv())
            if i - 2 == count or chunks[i - 2][0] != chunks[i - 3][0]:
                leave(chunks[i - 3][0]).start()

    for i in range(count):
        for stage in (2, 3, 4, 5):
            copy(stage, i, 0).wait_send()
        def finish(k, i=i):
            for stage in range(6):
                copy(stage, i, k).wait_send()
        each(1, 4, finish)
    for t in range(n):
        leave(t).wait()
    vector_copy(1, 0).wait()
    for k in (1, 2, 3):
        vector_copy(0, k).wait_send()
        vector_copy(1, k).wait()


def chunks_of(shards, largest):
    chunks = []
    for t, shard in enumerate(shards):
        rows, tiles = shard.shape[0] // 2, shard.shape[1] // 256
        size = rows * tiles * 128
        parts = -(-size // largest)
        by_rows = rows // parts % 16 == 0 and tiles < 2 * parts
        if by_rows:
            for p in range(parts):
                both = max(1, tiles // 3) if tiles > 1 else 0
                chunks.append((t, rows // parts * p, rows // parts, 0, both * 128, (tiles - both) * 128))
        else:
            cuts = [tiles * p // parts for p in range(parts + 1)]
            for lo, hi in zip(cuts, cuts[1:]):
                both = max(1, (hi - lo) // 3)
                chunks.append((t, 0, rows, lo * 128, both * 128, (hi - lo - both) * 128))
    return tuple(chunks)


def gather_weights(shards, vector, ident):
    n = len(shards)
    views = [shard.reshape(2, shard.shape[0] // 2, shard.shape[1]) for shard in shards]
    chunks = chunks_of(shards, 75000)
    anywhere, vmem = pl.BlockSpec(memory_space=pl.ANY), pl.BlockSpec(memory_space=pltpu.VMEM)
    dma = pltpu.SemaphoreType.DMA
    out = pl.pallas_call(
        functools.partial(gather_kernel, chunks, n),
        out_shape=tuple(jax.ShapeDtypeStruct((4, 2) + v.shape, BF16) for v in views)
        + (jax.ShapeDtypeStruct((4, 2, 8, 128), F32),),
        in_specs=[vmem] * n + [vmem],
        out_specs=(anywhere,) * n + (vmem,),
        scratch_shapes=[pltpu.VMEM((4, 2) + v.shape, BF16) for v in views]
        + [dma((len(chunks), 6, 4)), dma((len(chunks), 6, 4)), dma((2 * n,)), dma((8,)), dma((8,))],
        compiler_params=pltpu.CompilerParams(collective_id=ident, has_side_effects=True, vmem_limit_bytes=60 * 2**20),
        name="gather",
    )(*views, vector.reshape(8, 128))
    return [o.reshape(-1, o.shape[4]) for o in out[:n]], out[n].reshape(-1)


def layer_norm(stream, gain, offset):
    centre = stream - jnp.mean(stream, axis=-1, keepdims=True)
    spread = jnp.mean(centre * centre, axis=-1, keepdims=True)
    return centre * lax.rsqrt(spread + 1e-06) * gain + offset


def sincos(time_pos, frequency, width):
    quarter = width // 4
    omega = 1.0 / 10000.0 ** (jnp.arange(quarter, dtype=jnp.float32) / quarter)
    time_angle = time_pos.astype(jnp.float32)[:, None] * omega[None, :]
    band_angle = frequency.astype(jnp.float32)[:, None] * omega[None, :]
    return jnp.concatenate(
        [jnp.sin(time_angle), jnp.cos(time_angle), jnp.sin(band_angle), jnp.cos(band_angle)], axis=1
    )


def clip_of(column, clip_lengths, clip_shifts):
    columns = clip_lengths // 8
    ends = jnp.cumsum(columns)
    clip_id = jnp.sum((column[:, None] >= ends[None, :]).astype(jnp.int32), axis=1)
    onehot = (clip_id[:, None] == jnp.arange(clip_lengths.shape[0], dtype=jnp.int32)[None, :]).astype(jnp.int32)

    def select(values):
        return jnp.sum(onehot * values[None, :], axis=1)

    return clip_id, select(ends - columns), select(columns), select(clip_shifts[:, 0]), select(clip_shifts[:, 1])


def product(values_in, weights_in):
    return jnp.dot(values_in, weights_in, preferred_element_type=jnp.float32)


def input_grad(grad_low, weights_in):
    return lax.dot_general(
        grad_low, weights_in, (((1,), (1,)), ((), ())), preferred_element_type=jnp.float32
    )


def weight_grad(values_in, grad_low):
    return lax.dot_general(
        values_in, grad_low, (((0,), (0,)), ((), ())), preferred_element_type=jnp.float32
    )


def split_heads(projections, heads, group):
    rows = projections.shape[0]
    head_size = projections.shape[1] // (3 * heads)
    split_parts = projections.reshape(rows // group, group, 3, heads, head_size)
    return (split_parts[:, :, 0], split_parts[:, :, 1], split_parts[:, :, 2], head_size)


def softmax_probs(query, key_rows, head_size, score_bias):
    scores = jnp.einsum("bqhd,bkhd->bhqk", query, key_rows, preferred_element_type=jnp.float32)
    return jax.nn.softmax(scores * head_size ** (-0.5) + score_bias, axis=-1)


def attend(projections, heads, group, score_bias):
    query, key_rows, value_rows, head_size = split_heads(projections, heads, group)
    probs = softmax_probs(query, key_rows, head_size, score_bias)
    mixed = jnp.einsum(
        "bhqk,bkhd->bqhd",
        probs.astype(jnp.bfloat16),
        value_rows,
        preferred_element_type=jnp.float32,
    )
    return mixed.reshape(projections.shape[0], -1)


def attend_back(grad_mixed, projections, heads, group, score_bias):
    query, key_rows, value_rows, head_size = split_heads(projections, heads, group)
    probs = softmax_probs(query, key_rows, head_size, score_bias)
    grad_heads = grad_mixed.reshape(query.shape)
    grad_probs = jnp.einsum(
        "bqhd,bkhd->bhqk", grad_heads, value_rows, preferred_element_type=jnp.float32
    )
    grad_values = jnp.einsum(
        "bhqk,bqhd->bkhd",
        probs.astype(jnp.bfloat16),
        grad_heads,
        preferred_element_type=jnp.float32,
    )
    grad_scores = probs * (grad_probs - jnp.sum(grad_probs * probs, axis=-1, keepdims=True))
    scaled = (grad_scores * head_size ** (-0.5)).astype(jnp.bfloat16)
    grad_query = jnp.einsum("bhqk,bkhd->bqhd", scaled, key_rows, preferred_element_type=jnp.float32)
    grad_keys = jnp.einsum("bhqk,bqhd->bkhd", scaled, query, preferred_element_type=jnp.float32)
    return jnp.stack([grad_query, grad_keys, grad_values], axis=2).reshape(projections.shape[0], -1)


def block_forward(stream, weights, gains, heads, group, score_bias):
    w_qkv, w_out, w_up, w_down = weights
    normed = layer_norm(stream, gains[0], gains[1]).astype(jnp.bfloat16)
    projections = product(normed, w_qkv).astype(jnp.bfloat16)
    attended = attend(projections, heads, group, score_bias).astype(jnp.bfloat16)
    middle = stream + product(attended, w_out)
    second_normed = layer_norm(middle, gains[2], gains[3]).astype(jnp.bfloat16)
    up_values = product(second_normed, w_up)
    activated = jax.nn.gelu(up_values).astype(jnp.bfloat16)
    return (
        middle + product(activated, w_down),
        (stream, normed, projections, attended, middle, second_normed, up_values, activated),
    )


def block_backward(grad_out, cache, weights, gains, heads, group, score_bias):
    w_qkv, w_out, w_up, w_down = weights
    stream, normed, projections, attended, middle, second_normed, up_values, activated = cache
    grad_down = grad_out.astype(jnp.bfloat16)
    g_down = weight_grad(activated, grad_down)
    _, gelu_back = jax.vjp(jax.nn.gelu, up_values)
    grad_up = gelu_back(input_grad(grad_down, w_down))[0].astype(jnp.bfloat16)
    g_up = weight_grad(second_normed, grad_up)
    _, norm_back = jax.vjp(layer_norm, middle, gains[2], gains[3])
    grad_middle, g_gain_two, g_offset_two = norm_back(input_grad(grad_up, w_up))
    grad_middle = grad_middle + grad_out
    grad_branch = grad_middle.astype(jnp.bfloat16)
    g_out = weight_grad(attended, grad_branch)
    grad_attended = input_grad(grad_branch, w_out).astype(jnp.bfloat16)
    grad_projections = attend_back(grad_attended, projections, heads, group, score_bias).astype(
        jnp.bfloat16
    )
    g_qkv = weight_grad(normed, grad_projections)
    _, first_back = jax.vjp(layer_norm, stream, gains[0], gains[1])
    grad_stream, g_gain_one, g_offset_one = first_back(input_grad(grad_projections, w_qkv))
    norm_grads = jnp.stack([g_gain_one, g_offset_one, g_gain_two, g_offset_two])
    return (grad_stream + grad_middle, (g_qkv, g_out, g_up, g_down), norm_grads)


def adam_update(weight, first, second, grad, decay):
    first = BETA_ONE * first + (1.0 - BETA_ONE) * grad
    second = BETA_TWO * second + (1.0 - BETA_TWO) * grad * grad
    first_hat = first / (1.0 - BETA_ONE**STEP)
    second_hat = second / (1.0 - BETA_TWO**STEP)
    weight = weight - LEARN_RATE * (first_hat / (jnp.sqrt(second_hat) + EPSILON) + decay * weight)
    return (weight, first, second)


def shards(
    pixels,
    lengths,
    shifts,
    visible,
    patch_embed,
    encoder_in,
    encoder_down,
    decoder_in,
    decoder_down,
    norm_vectors,
    first_embed,
    first_encoder_in,
    first_encoder_down,
    first_decoder_in,
    first_decoder_down,
    first_vectors,
    second_embed,
    second_encoder_in,
    second_encoder_down,
    second_decoder_in,
    second_decoder_down,
    second_vectors,
):
    masters = (patch_embed, encoder_in, encoder_down, decoder_in, decoder_down, norm_vectors)
    firsts = (
        first_embed,
        first_encoder_in,
        first_encoder_down,
        first_decoder_in,
        first_decoder_down,
        first_vectors,
    )
    seconds = (
        second_embed,
        second_encoder_in,
        second_encoder_down,
        second_decoder_in,
        second_decoder_down,
        second_vectors,
    )
    direct = lax.axis_size("clip") == 8 and lax.axis_size("band") == 4
    low_shards = [master.astype(jnp.bfloat16) for master in masters]
    if direct:
        (w_embed, w_enc, w_enc_down, w_dec, w_dec_down), vectors = gather_weights(
            low_shards[:5], lax.reduce_precision(norm_vectors, exponent_bits=8, mantissa_bits=7), 0
        )
    else:
        w_embed, w_enc, w_enc_down, w_dec, w_dec_down, gathered_vectors = (
            lax.all_gather(shard, "clip", axis=0, tiled=True) for shard in low_shards
        )
        vectors = gathered_vectors.astype(jnp.float32)
    enc_width, dec_width = (w_enc.shape[0], w_dec.shape[0])
    enc_hidden, dec_hidden = (w_enc_down.shape[0], w_dec_down.shape[0])
    enc_gains = vectors[: 6 * enc_width].reshape(6, enc_width)
    dec_gains = vectors[6 * enc_width :].reshape(7, dec_width)
    enc_weights = (
        w_enc[:, : 3 * enc_width],
        w_enc[:, 3 * enc_width : 4 * enc_width],
        w_enc[:, 4 * enc_width : 4 * enc_width + enc_hidden],
        w_enc_down,
    )
    w_proj = w_enc[:, 4 * enc_width + enc_hidden :]
    patch_dev, n_visible = pixels.shape[0], visible.shape[0]
    turned = jnp.arange(patch_dev // 8, dtype=jnp.int32)
    _, start, size, shift_time, shift_band = clip_of(turned, lengths[0], shifts[0])
    turned_time = (turned - start - shift_time) % size
    decoder_pixels = pixels.reshape(patch_dev // 8, 8, -1)[start + turned_time].reshape(pixels.shape)
    seen = pixels[visible]
    seen_column, seen_band = visible // 8, visible % 8
    segment, seen_start, seen_size, seen_shift, _ = clip_of(seen_column, lengths[0], shifts[0])
    seen_time = seen_column - seen_start
    decoder_row = 8 * (seen_start + (seen_time + seen_shift) % seen_size) + seen_band
    padded = -(-n_visible // 128) * 128
    decoder_row = jnp.pad(decoder_row, (0, padded - n_visible), constant_values=-1)
    decoder_row = jnp.broadcast_to(decoder_row[:, None], (padded, 128))
    score_bias = jnp.where(segment[:, None] == segment[None, :], 0.0, -1e30)
    embedded = product(seen, w_embed) + sincos(seen_time, seen_band, enc_width)
    encoded, enc_cache = block_forward(
        embedded, enc_weights, enc_gains, HEADS_ENC, seen.shape[0], score_bias
    )
    final_enc = layer_norm(encoded, enc_gains[4], enc_gains[5]).astype(jnp.bfloat16)
    projected = product(final_enc, w_proj)
    grid_seen = (projected + sincos(seen_time, seen_band, dec_width)).astype(jnp.bfloat16)
    grid_seen = jnp.pad(grid_seen, ((0, padded - n_visible), (0, 0)))
    time_table = sincos(turned_time, turned_time, dec_width)[:, : dec_width // 2]
    bands = jnp.arange(8, dtype=jnp.int32)
    band_table = jnp.tile(sincos(bands, bands, dec_width)[:, dec_width // 2 :].T, (1, 16))
    wide_vectors = jnp.broadcast_to(dec_gains[:, :, None], dec_gains.shape + (128,))
    masked_count = 13.0 * (patch_dev // 16) * lax.axis_size("clip") * lax.axis_size("band")
    g_dec_in, g_dec_down, g_dec_vectors, grad_proj, loss = decoder_step(
        shift_band[::64],
        decoder_row,
        grid_seen.T,
        decoder_pixels,
        time_table,
        band_table,
        wide_vectors,
        w_dec,
        w_dec.T,
        w_dec_down,
        w_dec_down.T,
        2.0 / (pixels.shape[1] * masked_count),
        HEADS_DEC,
    )
    local_loss = jnp.sum(loss[0])
    g_dec_vectors = jnp.sum(g_dec_vectors, axis=2)
    grad_proj = grad_proj[:n_visible].astype(jnp.bfloat16)
    g_proj = weight_grad(final_enc, grad_proj)
    _, enc_final_back = jax.vjp(layer_norm, encoded, enc_gains[4], enc_gains[5])
    grad_encoded, g_enc_gain, g_enc_offset = enc_final_back(input_grad(grad_proj, w_proj))
    grad_embedded, g_enc_mats, g_enc_norms = block_backward(
        grad_encoded, enc_cache, enc_weights, enc_gains, HEADS_ENC, seen.shape[0], score_bias
    )
    g_embed = weight_grad(seen, grad_embedded.astype(jnp.bfloat16))
    g_enc_in = jnp.concatenate([g_enc_mats[0], g_enc_mats[1], g_enc_mats[2], g_proj], axis=1)
    g_vectors = jnp.concatenate(
        [
            g_enc_norms.reshape(-1),
            g_enc_gain,
            g_enc_offset,
            g_dec_vectors.reshape(-1),
        ]
    )
    if direct:
        small = jnp.concatenate([g_vectors.reshape(-1, 128), jnp.full((8, 128), local_loss)])
        nothing = jnp.zeros((8, 128), jnp.float32)
        dec_shards, _, squares = reduce_grads([g_dec_in, g_dec_down], nothing, nothing, False, 1)
        enc_shards, summed, squares = reduce_grads(
            [g_enc_in, g_enc_mats[3], g_embed], small, squares, True, 2
        )
        rows = norm_vectors.shape[0]
        vector_sums = summed[:-8].reshape(-1)
        own = lax.dynamic_slice(vector_sums, (lax.axis_index("clip") * rows,), (rows,))
        reduced = (enc_shards[2], enc_shards[0], enc_shards[1], *dec_shards, own)
        loss_sum = summed[-1, 0]
        norm_squared = jnp.sum(squares) + jnp.sum(vector_sums * vector_sums)
    else:
        reduced = lax.psum(
            tuple(
                lax.psum_scatter(grad, "clip", scatter_dimension=0, tiled=True)
                for grad in (g_embed, g_enc_in, g_enc_mats[3], g_dec_in, g_dec_down, g_vectors)
            ),
            "band",
        )
        loss_sum = lax.psum(local_loss, ("clip", "band"))
        norm_squared = lax.psum(sum(jnp.sum(grad * grad) for grad in reduced), "clip")
    grad_norm = jnp.sqrt(norm_squared)
    factor = jnp.minimum(1.0, CLIP_LIMIT / (grad_norm + 1e-06))
    results = []
    for index in range(6):
        decay = DECAY_RATE if index < 5 else 0.0
        results.append(
            adam_update(
                masters[index], firsts[index], seconds[index], reduced[index] * factor, decay
            )
        )
    return (
        loss_sum,
        grad_norm,
        results[0][0],
        results[1][0],
        results[2][0],
        results[3][0],
        results[4][0],
        results[5][0],
        results[0][1],
        results[1][1],
        results[2][1],
        results[3][1],
        results[4][1],
        results[5][1],
        results[0][2],
        results[1][2],
        results[2][2],
        results[3][2],
        results[4][2],
        results[5][2],
    )


def solution(mesh):
    in_specs = (
        P(("clip", "band"), None),
        P(("clip", "band"), None),
        P(("clip", "band"), None, None),
        P(("clip", "band")),
        P("clip", None),
        P("clip", None),
        P("clip", None),
        P("clip", None),
        P("clip", None),
        P("clip"),
        P("clip", None),
        P("clip", None),
        P("clip", None),
        P("clip", None),
        P("clip", None),
        P("clip"),
        P("clip", None),
        P("clip", None),
        P("clip", None),
        P("clip", None),
        P("clip", None),
        P("clip"),
    )
    out_specs = (
        P(),
        P(),
        P("clip", None),
        P("clip", None),
        P("clip", None),
        P("clip", None),
        P("clip", None),
        P("clip"),
        P("clip", None),
        P("clip", None),
        P("clip", None),
        P("clip", None),
        P("clip", None),
        P("clip"),
        P("clip", None),
        P("clip", None),
        P("clip", None),
        P("clip", None),
        P("clip", None),
        P("clip"),
    )
    return jax.shard_map(shards, mesh=mesh, in_specs=in_specs, out_specs=out_specs, check_vma=False)
```

```python
import functools

import jax
import jax.numpy as jnp
from jax import lax
from jax.experimental import pallas as pl
from jax.experimental.pallas import tpu as pltpu
from jax.sharding import PartitionSpec as P

HEADS_ENC = 12
HEADS_DEC = 16
STEP = 10


LEARN_RATE = 0.02
BETA_ONE = 0.9
BETA_TWO = 0.95
EPSILON = 1e-08
DECAY_RATE = 0.05
CLIP_LIMIT = 0.001


F32, BF16 = jnp.float32, jnp.bfloat16
GELU_C = 0.7978845608028654


def mm(a, b, ca=1, cb=0):
    return lax.dot_general(a, b, (((ca,), (cb,)), ((), ())), preferred_element_type=F32)


def wide(v, n):
    return jnp.concatenate([v] * (n // 128), axis=1)


def loop(n, body, unroll=1):
    def step(i, carry):
        for k in range(unroll):
            body(i * unroll + k)
        return carry
    lax.fori_loop(0, n // unroll, step, 0)


def fold(v):
    total = v[:, :128]
    for i in range(1, v.shape[1] // 128):
        total = total + v[:, 128 * i : 128 * (i + 1)]
    return total


def decoder_kernel(
    coef, heads, shift_ref, rvis_ref, gvt_ref, pix_ref, et_ref, ef_ref, vec_ref, w_ref, wt_ref, wd_ref, wdt_ref,
    gin_ref, gdown_ref, gvec_ref, gp_ref, loss_ref,
    res, xh1, xh2, xh3, tmp, n1, n2, fin, rs, qkv, att, act, dgel, probs, dqkv, dup, low, oh, mrow, hb, hm, wm,
):
    width = w_ref.shape[0]
    hidden = wd_ref.shape[0]
    rows = res.shape[1]
    size = width // heads
    per = 128 // size
    scale = size ** -0.5
    groups = width // 128
    c_out, c_up, c_head = 3 * width, 4 * width, 4 * width + hidden
    pixels = w_ref.shape[1] - c_head
    cols = rows // 8
    nblk = pix_ref.shape[0] // rows
    chunk = 512

    gin_ref[...] = jnp.zeros_like(gin_ref)
    gdown_ref[...] = jnp.zeros_like(gdown_ref)
    gvec_ref[...] = jnp.zeros_like(gvec_ref)
    gp_ref[...] = jnp.zeros_like(gp_ref)
    loss_ref[...] = jnp.zeros_like(loss_ref)
    f_id = lax.broadcasted_iota(jnp.int32, (128, 128 * per), 0)
    q_id = lax.broadcasted_iota(jnp.int32, (128, 128 * per), 1)
    hm[...] = jnp.where(f_id // size == q_id // 128, 1.0, 0.0).astype(BF16)
    wm[...] = jnp.where(f_id // 32 == (q_id % 128) // 32, 1.0, 0.0).astype(BF16)

    def lane(i):
        return pl.ds(pl.multiple_of(i * 128, 128), 128)

    def ln_forward(k, xh, out):
        def body(i):
            x = res[:, lane(i)]
            centre = x - jnp.mean(x, axis=0, keepdims=True)
            r = lax.rsqrt(jnp.mean(centre * centre, axis=0, keepdims=True) + 1e-06)
            xhat = centre * r
            xh[:, lane(i)] = xhat
            rs[8 * k : 8 * k + 8, lane(i)] = jnp.broadcast_to(r, (8, 128))
            out[:, lane(i)] = (xhat * vec_ref[2 * k] + vec_ref[2 * k + 1]).astype(BF16)
        loop(rows // 128, body, 4)

    def ln_backward(k, xh, add):
        def body(i):
            d = tmp[:, lane(i)]
            xhat = xh[:, lane(i)]
            gvec_ref[2 * k] += d * xhat
            gvec_ref[2 * k + 1] += d
            dx = d * vec_ref[2 * k]
            m1 = jnp.mean(dx, axis=0, keepdims=True)
            m2 = jnp.mean(dx * xhat, axis=0, keepdims=True)
            g = rs[8 * k : 8 * k + 1, lane(i)] * (dx - m1 - xhat * m2)
            if add:
                g = g + res[:, lane(i)]
            res[:, lane(i)] = g
            low[:, lane(i)] = g.astype(BF16)
        loop(rows // 128, body, 4)

    def block(j):
        first = pl.multiple_of(j * rows, rows)
        turn = shift_ref[j]
        spot = lax.broadcasted_iota(jnp.int32, (rvis_ref.shape[0], rows), 1) + first
        hot = jnp.where(wide(rvis_ref[...], rows) == spot, 1.0, 0.0)
        oh[...] = hot.astype(BF16)
        masked = 1.0 - jnp.sum(hot, axis=0, keepdims=True)
        mrow[...] = jnp.broadcast_to(masked, (8, rows))
        et = et_ref[pl.ds(pl.multiple_of(j * cols, cols), cols), :]
        e_hi = et.astype(BF16)
        rest = et - e_hi.astype(F32)
        e_mid = rest.astype(BF16)
        e_lo = (rest - e_mid.astype(F32)).astype(BF16)
        spread = jnp.where(
            lax.broadcasted_iota(jnp.int32, (cols, rows), 1) // 8 == lax.broadcasted_iota(jnp.int32, (cols, rows), 0), 1.0, 0.0
        ).astype(BF16)
        e_t = mm(e_hi, spread, 0, 0) + (mm(e_mid, spread, 0, 0) + mm(e_lo, spread, 0, 0))
        half = width // 2
        keep = masked > 0.5
        placed = mm(gvt_ref[...], oh[...])
        top = (wide(vec_ref[6, :half], rows) + e_t).astype(BF16).astype(F32)
        res[:half] = jnp.where(keep, top, placed[:half])
        bottom = wide((vec_ref[6, half:] + ef_ref[...]).astype(BF16).astype(F32), rows)
        res[half:] = jnp.where(keep, bottom, placed[half:])
        k_half = (lax.broadcasted_iota(jnp.int32, (32, 128 * per), 0) % 8 + turn) % 8 // 4
        q_half = (lax.broadcasted_iota(jnp.int32, (32, 128 * per), 1) % 8 + turn) % 8 // 4
        hb[...] = jnp.where(k_half == q_half, 0.0, -1e30)

        ln_forward(0, xh1, n1)

        def qkv_part(i):
            part = pl.ds(pl.multiple_of(i * chunk, chunk), chunk)
            qkv[part, :] = mm(wt_ref[part, :], n1[...]).astype(BF16)
        loop(3 * width // chunk, qkv_part, 3)

        q_group = (lax.broadcasted_iota(jnp.int32, (32, 128 * per), 1) % 128) // 32

        def compact(s):
            c = s[96:128]
            for i in (2, 1, 0):
                c = jnp.where(q_group == i, s[32 * i : 32 * i + 32], c)
            return c

        def attend(i):
            sb, g = i // groups, i % groups
            at = lane(sb)
            f0 = pl.multiple_of(g * 128, 128)
            q = qkv[pl.ds(f0, 128), at]
            k = qkv[pl.ds(width + f0, 128), at]
            v = qkv[pl.ds(2 * width + f0, 128), at]
            s = mm(k.T, wide(q, 128 * per) * hm[...])
            c = compact(s) * scale + hb[...]
            e = jnp.exp(c - jnp.max(c, axis=0, keepdims=True))
            p = e * (1.0 / jnp.sum(e, axis=0, keepdims=True))
            probs[i] = p
            p_low = p.astype(BF16)
            p_all = jnp.concatenate([p_low] * 4, axis=0) * wm[...]
            for h in range(per):
                o = mm(v[size * h : size * h + size], p_all[:, 128 * h : 128 * h + 128])
                att[pl.ds(f0 + size * h, size), at] = o.astype(BF16)
        loop(rows // 128 * groups, attend, 16)

        res[...] += mm(wt_ref[c_out : c_out + width], att[...])
        ln_forward(1, xh2, n2)

        def up_part(i):
            part = pl.ds(pl.multiple_of(i * chunk, chunk), chunk)
            u = mm(wt_ref[pl.ds(pl.multiple_of(c_up + i * chunk, chunk), chunk), :], n2[...])
            square = u * u
            hp = 0.5 + 0.5 * jnp.tanh(u * (GELU_C + (GELU_C * 0.044715) * square))
            v = u * hp
            act[part, :] = v.astype(BF16)
            dgel[part, :] = hp + (v - v * hp) * ((2 * GELU_C) + (6 * GELU_C * 0.044715) * square)
        loop(hidden // chunk, up_part, 4)

        res[...] += mm(wdt_ref[...], act[...])
        ln_forward(2, xh3, fin)
        pred = mm(wt_ref[c_head:], fin[...])
        pix = pix_ref[pl.ds(first, rows), :].astype(F32).T
        centre = pix - jnp.mean(pix, axis=0, keepdims=True)
        target = (centre * lax.rsqrt(jnp.mean(centre * centre, axis=0, keepdims=True) + 1e-06)).astype(BF16).astype(F32)
        err = pred - target
        loss_ref[...] += fold(mrow[...] * jnp.mean(err * err, axis=0, keepdims=True))
        gpred = (mrow[0:1] * err * coef).astype(BF16)

        gin_ref[:, c_head:] += mm(fin[...], gpred, 1, 1)
        tmp[...] = mm(w_ref[:, c_head:], gpred)
        ln_backward(2, xh3, False)

        def mlp_back(i):
            part = pl.ds(pl.multiple_of(i * chunk, chunk), chunk)
            there = pl.ds(pl.multiple_of(c_up + i * chunk, chunk), chunk)
            d = (mm(wd_ref[part, :], low[...]) * dgel[part, :]).astype(BF16)
            dup[part, :] = d
            gdown_ref[part, :] += mm(act[part, :], low[...], 1, 1)
            gin_ref[:, there] += mm(n2[...], d, 1, 1)
        loop(hidden // chunk, mlp_back, 4)
        tmp[...] = mm(w_ref[:, c_up:c_head], dup[...])
        ln_backward(1, xh2, True)
        gin_ref[:, c_out:c_up] += mm(att[...], low[...], 1, 1)
        fin[...] = mm(w_ref[:, c_out:c_up], low[...]).astype(BF16)

        def attend_back(i):
            sb, g = i // groups, i % groups
            at = lane(sb)
            f0 = pl.multiple_of(g * 128, 128)
            q = qkv[pl.ds(f0, 128), at]
            k = qkv[pl.ds(width + f0, 128), at]
            v = qkv[pl.ds(2 * width + f0, 128), at]
            do = fin[pl.ds(f0, 128), at]
            do_all = wide(do, 128 * per) * hm[...]
            dp = compact(mm(v.T, do_all))
            p = probs[i]
            ds = p * (dp - jnp.sum(dp * p, axis=0, keepdims=True))
            p_all = jnp.concatenate([p.astype(BF16)] * 4, axis=0) * wm[...]
            ds_all = jnp.concatenate([(ds * scale).astype(BF16)] * 4, axis=0) * wm[...]
            tall = jnp.concatenate([ds_all[:, 128 * h : 128 * h + 128] for h in range(per)], axis=0)
            dqkv[pl.ds(f0, 128), at] = mm(wide(k, 128 * per) * hm[...], tall).astype(BF16)
            dqkv[pl.ds(width + f0, 128), at] = mm(wide(q, 128 * per) * hm[...], ds_all, 1, 1).astype(BF16)
            dqkv[pl.ds(2 * width + f0, 128), at] = mm(do_all, p_all, 1, 1).astype(BF16)
        loop(rows // 128 * groups, attend_back, 8)

        def qkv_back(i):
            part = pl.ds(pl.multiple_of(i * chunk, chunk), chunk)
            gin_ref[:, part] += mm(n1[...], dqkv[part, :], 1, 1)
        loop(3 * width // chunk, qkv_back, 3)
        tmp[...] = mm(w_ref[:, :c_out], dqkv[...])
        ln_backward(0, xh1, True)
        gvec_ref[6] += fold(low[...].astype(F32) * mrow[0:1])
        gp_ref[...] += mm(low[...], oh[...], 1, 1)

    loop(nblk, block)


def decoder_step(shift, rvis, gvt, pix, et, ef, vec, w, wt, wd, wdt, coef, heads):
    width, total = w.shape
    hidden = wd.shape[0]
    rows = 512
    vis = rvis.shape[0]
    per = 128 // (width // heads)
    vmem = pl.BlockSpec(memory_space=pltpu.VMEM)
    f = lambda *s: pltpu.VMEM(s, F32)
    b = lambda *s: pltpu.VMEM(s, BF16)
    return pl.pallas_call(
        functools.partial(decoder_kernel, coef, heads),
        out_shape=(
            jax.ShapeDtypeStruct((width, total), F32),
            jax.ShapeDtypeStruct((hidden, width), F32),
            jax.ShapeDtypeStruct((7, width, 128), F32),
            jax.ShapeDtypeStruct((width, vis), F32),
            jax.ShapeDtypeStruct((8, 128), F32),
        ),
        in_specs=[pl.BlockSpec(memory_space=pltpu.SMEM)] + [vmem] * 10,
        out_specs=(vmem,) * 5,
        scratch_shapes=[
            f(width, rows), f(width, rows), f(width, rows), f(width, rows), f(width, rows),
            b(width, rows), b(width, rows), b(width, rows), f(24, rows),
            b(3 * width, rows), b(width, rows), b(hidden, rows), f(hidden, rows),
            f(rows // 128 * (width // 128), 32, 128 * per), b(3 * width, rows), b(hidden, rows), b(width, rows),
            b(vis, rows), f(8, rows), f(32, 128 * per), b(128, 128 * per), b(128, 128 * per),
        ],
        compiler_params=pltpu.CompilerParams(vmem_limit_bytes=63 * 2**20),
        name="decoder",
    )(shift, rvis, gvt, pix, et, ef, vec, w, wt, wd, wdt)


CHUNK = 768


def lane(i):
    return pl.ds(i * 128 if isinstance(i, int) else pl.multiple_of(i * 128, 128), 128)


def part(i, base=0):
    return pl.ds(pl.multiple_of(base + i * CHUNK, 128), CHUNK)


def encoder_scores(q, k, bias, scale):
    c = mm(k, q, 0, 0) * scale + bias
    e = jnp.exp(c - jnp.max(c, axis=0, keepdims=True))
    return e * (1.0 / jnp.sum(e, axis=0, keepdims=True))


def encoder_forward_kernel(
    heads, seen_ref, pos_ref, grid_pos_ref, segc_ref, segr_ref, vec_ref, we_ref, wi_ref, wd_ref,
    grid_ref, bias_ref, seen_t_ref, xh1_ref, n1_ref, qkv_ref, att_ref, xh2_ref, n2_ref, act_ref, dgel_ref, xh3_ref, fin_ref, rs_ref,
    we, wi, wd, res, bias, seen_t, xh1, n1, qkv, att, xh2, n2, act, dgel, xh3, fin, rs, w_sem, o_sem,
):
    width, hidden = we.shape[1], wd.shape[0]
    rows = res.shape[1]
    size = width // heads
    scale = size ** -0.5
    c_out, c_up, c_proj = 3 * width, 4 * width, 4 * width + hidden
    total = wi.shape[1]
    loads = [pltpu.make_async_copy(we_ref, we, w_sem.at[0])]
    for i, (lo, hi) in enumerate(((0, c_out), (c_out, c_up), (c_up, c_proj), (c_proj, total))):
        at = pl.ds(lo, hi - lo)
        loads.append(pltpu.make_async_copy(wi_ref.at[:, at], wi.at[:, at], w_sem.at[1 + i]))
    loads.insert(4, pltpu.make_async_copy(wd_ref, wd, w_sem.at[5]))
    for load in loads:
        load.start()
    pairs = (
        (bias, bias_ref), (seen_t, seen_t_ref), (xh1, xh1_ref), (n1, n1_ref), (qkv, qkv_ref), (att, att_ref), (xh2, xh2_ref),
        (n2, n2_ref), (act, act_ref), (dgel, dgel_ref), (xh3, xh3_ref), (fin, fin_ref), (rs, rs_ref),
    )
    saves = [pltpu.make_async_copy(a, b, o_sem.at[i]) for i, (a, b) in enumerate(pairs)]

    def ln_forward(k, xh, out):
        def body(i):
            x = res[:, lane(i)]
            centre = x - jnp.mean(x, axis=0, keepdims=True)
            r = lax.rsqrt(jnp.mean(centre * centre, axis=0, keepdims=True) + 1e-06)
            xhat = centre * r
            xh[:, lane(i)] = xhat
            rs[8 * k : 8 * k + 8, lane(i)] = jnp.broadcast_to(r, (8, 128))
            out[:, lane(i)] = (xhat * vec_ref[2 * k] + vec_ref[2 * k + 1]).astype(BF16)
        for i in range(rows // 128):
            body(i)

    seen_t[...] = seen_ref[...].T
    saves[1].start()
    bias[...] = jnp.where(wide(segc_ref[...], rows) == segr_ref[0:1], 0.0, -1e30)
    saves[0].start()
    loads[0].wait()
    res[...] = mm(we[...], seen_t[...], 0, 0) + pos_ref[...]
    ln_forward(0, xh1, n1)
    saves[2].start()
    saves[3].start()
    loads[1].wait()

    def qkv_part(i):
        qkv[part(i), :] = mm(wi[:, part(i)], n1[...], 0, 0).astype(BF16)
    loop(3, qkv_part)
    saves[4].start()

    def attend(h):
        f0 = pl.multiple_of(h * size, size)
        k = qkv[pl.ds(width + f0, size), :]
        v = qkv[pl.ds(2 * width + f0, size), :]
        for i in range(rows // 128):
            p = encoder_scores(qkv[pl.ds(f0, size), lane(i)], k, bias[:, lane(i)], scale)
            att[pl.ds(f0, size), lane(i)] = mm(v, p.astype(BF16)).astype(BF16)
    loop(heads, attend)
    saves[5].start()
    loads[2].wait()
    res[...] += mm(wi[:, c_out:c_up], att[...], 0, 0)
    ln_forward(1, xh2, n2)
    saves[6].start()
    saves[7].start()
    loads[3].wait()

    def up_part(i):
        u = mm(wi[:, part(i, c_up)], n2[...], 0, 0)
        square = u * u
        hp = 0.5 + 0.5 * jnp.tanh(u * (GELU_C + (GELU_C * 0.044715) * square))
        v = u * hp
        act[part(i), :] = v.astype(BF16)
        dgel[part(i), :] = hp + (v - v * hp) * ((2 * GELU_C) + (6 * GELU_C * 0.044715) * square)
    loop(hidden // CHUNK, up_part, 2)
    saves[8].start()
    saves[9].start()
    loads[4].wait()
    res[...] += mm(wd[...], act[...], 0, 0)
    ln_forward(2, xh3, fin)
    for i in (10, 11, 12):
        saves[i].start()
    loads[5].wait()
    grid_ref[...] = (mm(wi[:, c_proj:], fin[...], 0, 0) + grid_pos_ref[...]).astype(BF16)
    for save in saves:
        save.wait()


def encoder_forward(seen, pos, grid_pos, segc, segr, vec, we, wi, wd, heads):
    rows, patch = seen.shape
    width, total = wi.shape
    hidden = wd.shape[0]
    any_, vmem = pl.BlockSpec(memory_space=pl.ANY), pl.BlockSpec(memory_space=pltpu.VMEM)
    saved = (
        ((rows, rows), F32), ((patch, rows), BF16), ((width, rows), F32), ((width, rows), BF16), ((3 * width, rows), BF16),
        ((width, rows), BF16), ((width, rows), F32), ((width, rows), BF16), ((hidden, rows), BF16), ((hidden, rows), F32),
        ((width, rows), F32), ((width, rows), BF16), ((24, rows), F32),
    )
    return pl.pallas_call(
        functools.partial(encoder_forward_kernel, heads),
        out_shape=(jax.ShapeDtypeStruct((grid_pos.shape[0], rows), BF16),) + tuple(jax.ShapeDtypeStruct(*s) for s in saved),
        in_specs=[vmem] * 6 + [any_] * 3,
        out_specs=(vmem,) + (any_,) * len(saved),
        scratch_shapes=[pltpu.VMEM(we.shape, BF16), pltpu.VMEM(wi.shape, BF16), pltpu.VMEM(wd.shape, BF16), pltpu.VMEM((width, rows), F32)]
        + [pltpu.VMEM(*s) for s in saved] + [pltpu.SemaphoreType.DMA((6,)), pltpu.SemaphoreType.DMA((len(saved),))],
        compiler_params=pltpu.CompilerParams(vmem_limit_bytes=62 * 2**20),
        name="encode",
    )(seen, pos, grid_pos, segc, segr, vec, we, wi, wd)


def encoder_backward_kernel(
    heads, gp_ref, vec_ref, wi_ref, wd_ref,
    bias_ref, seen_t_ref, xh1_ref, n1_ref, qkv_ref, att_ref, xh2_ref, n2_ref, act_ref, dgel_ref, xh3_ref, fin_ref, rs_ref,
    gin_ref, gdown_ref, gembed_ref, gvec_ref,
    wi, wd, res, tmp, low, dqkv, probs, dscores, stage, bias, seen_t, xh1, n1, qkv, att, xh2, n2, act, dgel, rs, i_sem, s_sem,
):
    width, hidden = wi.shape[0], wd.shape[0]
    rows = res.shape[1]
    size = width // heads
    scale = size ** -0.5
    c_out, c_up, c_proj = 3 * width, 4 * width, 4 * width + hidden
    total = wi.shape[1]
    n_proj = total - c_proj

    def load(i, src, dst):
        return pltpu.make_async_copy(src, dst, i_sem.at[i])

    def columns(i, lo, hi):
        at = pl.ds(lo, hi - lo)
        return load(i, wi_ref.at[:, at], wi.at[:, at])

    first = [load(0, fin_ref, n1), columns(1, c_proj, total), load(2, xh3_ref, xh1), load(3, rs_ref, rs)]
    mlp = [load(4, wd_ref, wd), load(5, dgel_ref, dgel), load(6, act_ref, act), load(7, n2_ref, n2)]
    second = [columns(8, c_up, c_proj), load(9, xh2_ref, xh2), columns(10, c_out, c_up), load(11, att_ref, att)]
    attention = [load(12, qkv_ref, qkv), load(13, bias_ref, bias), columns(14, 0, c_out), load(15, seen_t_ref, seen_t)]
    again = [load(16, xh1_ref, xh1), load(17, n1_ref, n1)]
    for group in (first, mlp, second, attention):
        for copy in group:
            copy.start()
    gvec_ref[...] = jnp.zeros_like(gvec_ref)

    open_copies = [None, None]
    turn = [0]

    def leave(value, dst):
        slot = turn[0] % 2
        if open_copies[slot] is not None:
            open_copies[slot].wait()
        height, length = value.shape
        stage[slot, :height, :length] = value
        copy = pltpu.make_async_copy(stage.at[slot, pl.ds(0, height), pl.ds(0, length)], dst, s_sem.at[slot])
        copy.start()
        open_copies[slot] = copy
        turn[0] += 1

    def ln_backward(k, xh, add):
        for i in range(rows // 128):
            d = tmp[:, lane(i)]
            xhat = xh[:, lane(i)]
            gvec_ref[2 * k] += d * xhat
            gvec_ref[2 * k + 1] += d
            dx = d * vec_ref[2 * k]
            m1 = jnp.mean(dx, axis=0, keepdims=True)
            m2 = jnp.mean(dx * xhat, axis=0, keepdims=True)
            g = rs[8 * k : 8 * k + 1, lane(i)] * (dx - m1 - xhat * m2)
            if add:
                g = g + res[:, lane(i)]
            res[:, lane(i)] = g
            low[:, lane(i)] = g.astype(BF16)

    for copy in first:
        copy.wait()
    gp = gp_ref[...].astype(BF16)
    leave(mm(n1[...], gp, 1, 1), gin_ref.at[:, pl.ds(c_proj, n_proj)])
    tmp[...] = mm(wi[:, c_proj:], gp)
    ln_backward(2, xh1, False)
    for copy in again:
        copy.start()
    for copy in mlp:
        copy.wait()
    for i in range(hidden // CHUNK):
        at = pl.ds(i * CHUNK, CHUNK)
        d = (mm(wd[at, :], low[...]) * dgel[at, :]).astype(BF16)
        leave(mm(act[at, :], low[...], 1, 1), gdown_ref.at[at, :])
        act[at, :] = d
        leave(mm(n2[...], d, 1, 1), gin_ref.at[:, pl.ds(c_up + i * CHUNK, CHUNK)])
    for copy in second:
        copy.wait()
    tmp[...] = mm(wi[:, c_up:c_proj], act[...])
    ln_backward(1, xh2, True)
    leave(mm(att[...], low[...], 1, 1), gin_ref.at[:, pl.ds(c_out, width)])
    att[...] = mm(wi[:, c_out:c_up], low[...]).astype(BF16)
    for copy in attention:
        copy.wait()

    def attend_back(h):
        f0 = pl.multiple_of(h * size, size)
        mine = pl.ds(f0, size)
        q = qkv[mine, :]
        k = qkv[pl.ds(width + f0, size), :]
        v = qkv[pl.ds(2 * width + f0, size), :]
        do = att[mine, :]
        for i in range(rows // 128):
            p = encoder_scores(q[:, 128 * i : 128 * i + 128], k, bias[:, lane(i)], scale)
            dp = mm(v, do[:, 128 * i : 128 * i + 128], 0, 0)
            ds = p * (dp - jnp.sum(dp * p, axis=0, keepdims=True))
            probs[:, lane(i)] = p.astype(BF16)
            dscores[:, lane(i)] = (ds * scale).astype(BF16)
        dqkv[mine, :] = mm(k, dscores[...]).astype(BF16)
        dqkv[pl.ds(width + f0, size), :] = mm(q, dscores[...], 1, 1).astype(BF16)
        dqkv[pl.ds(2 * width + f0, size), :] = mm(do, probs[...], 1, 1).astype(BF16)
    loop(heads, attend_back)
    for copy in again:
        copy.wait()
    for i in range(3 * width // CHUNK):
        at = pl.ds(i * CHUNK, CHUNK)
        leave(mm(n1[...], dqkv[at, :], 1, 1), gin_ref.at[:, at])
    tmp[...] = mm(wi[:, :c_out], dqkv[...])
    ln_backward(0, xh1, True)
    leave(mm(seen_t[...], low[...], 1, 1), gembed_ref)
    for copy in open_copies:
        copy.wait()


def encoder_backward(gp, vec, wi, wd, saved, patch, heads):
    rows = gp.shape[1]
    width, total = wi.shape
    hidden = wd.shape[0]
    any_, vmem = pl.BlockSpec(memory_space=pl.ANY), pl.BlockSpec(memory_space=pltpu.VMEM)
    f = lambda *s: pltpu.VMEM(s, F32)
    b = lambda *s: pltpu.VMEM(s, BF16)
    shape = lambda *s: jax.ShapeDtypeStruct(s, F32)
    return pl.pallas_call(
        functools.partial(encoder_backward_kernel, heads),
        out_shape=(shape(width, total), shape(hidden, width), shape(patch, width), shape(6, width, 128)),
        in_specs=[vmem] * 2 + [any_] * (2 + len(saved)),
        out_specs=(any_,) * 3 + (vmem,),
        scratch_shapes=[
            b(*wi.shape), b(*wd.shape), f(width, rows), f(width, rows), b(width, rows), b(3 * width, rows), b(rows, rows), b(rows, rows),
            f(2, CHUNK, CHUNK), f(rows, rows), b(patch, rows), f(width, rows), b(width, rows), b(3 * width, rows), b(width, rows),
            f(width, rows), b(width, rows), b(hidden, rows), f(hidden, rows), f(24, rows),
            pltpu.SemaphoreType.DMA((18,)), pltpu.SemaphoreType.DMA((2,)),
        ],
        compiler_params=pltpu.CompilerParams(vmem_limit_bytes=63 * 2**20),
        name="encode_back",
    )(gp, vec, wi, wd, *saved)


def place():
    clip, band = lax.axis_index("clip"), lax.axis_index("band")
    return clip // 2, clip % 2, band // 2, band % 2


def device(z, x, y, c):
    return (z * 2 + x, y * 2 + c)


def greet(z, x, y, c):
    barrier = pltpu.get_barrier_semaphore()
    others = [device(z, x, y, 1 - c), device(z, 1 - x, y, c), device(z, x, 1 - y, c)]
    others += [device((z + k) % 4, x, y, c) for k in (1, 2, 3)]
    for other in others:
        pl.semaphore_signal(barrier, inc=1, device_id=other, device_id_type=pl.DeviceIdType.MESH)
    pl.semaphore_wait(barrier, len(others))


def remote(src, dst, send, recv, to):
    return pltpu.make_async_remote_copy(
        src_ref=src, dst_ref=dst, send_sem=send, recv_sem=recv, device_id=to, device_id_type=pl.DeviceIdType.MESH
    )


def reduce_kernel(widths, n, *refs):
    grads, small, before = refs[:n], refs[n], refs[n + 1]
    outs, small_out, squares = refs[n + 2 : 2 * n + 2], refs[2 * n + 2], refs[2 * n + 3]
    rest = refs[2 * n + 4 :]
    sums, r0 = rest[:n], rest[n : 2 * n]
    coded = {1 + i: rest[(2 + i) * n : (3 + i) * n] for i in range(5)}
    came = {1 + i: rest[(7 + i) * n : (8 + i) * n] for i in range(5)}
    step_out = {1 + i: rest[(12 + i) * n : (13 + i) * n] for i in range(5)}
    step_in = {1 + i: rest[(17 + i) * n : (18 + i) * n] for i in range(5)}
    s_buf, s_sum, q_buf, q_sum, send, recv, near, t_send, t_recv, s_send, s_recv = rest[22 * n :]
    z, x, y, c = place()
    greet(z, x, y, c)

    def at_z(k):
        return (z + k) % 4

    def columns(t, core):
        half = sums[t].shape[4]
        return pl.ds(pl.multiple_of(core * half, 128), half)

    def local(t, k):
        zk = at_z(k)
        return pltpu.make_async_copy(grads[t].at[zk, :, :, :, columns(t, c)], sums[t].at[zk], near.at[t, k])

    def target(stage, k):
        return {
            1: lambda: device(z, 1 - x, y, c),
            2: lambda: device(z, x, 1 - y, c),
            3: lambda: device(z, x, 1 - y, c),
            4: lambda: device(z, 1 - x, y, c),
            5: lambda: device(at_z(k), x, y, c),
        }[stage]()

    def copy(stage, t, k):
        if stage == 0:
            src, dst, to = grads[t].at[at_z(k), :, :, :, columns(t, 1 - c)], r0[t].at[at_z(k)], device(z, x, y, 1 - c)
        elif stage == 6:
            src, dst, to = sums[t].at[z, x, y], outs[t].at[y, :, columns(t, c)], device(z, x, 1 - y, c)
        elif stage == 7:
            src = outs[t].at[:, :, columns(t, c)]
            dst, to = src, device(z, x, y, 1 - c)
        else:
            src, dst, to = coded[stage][t].at[k], came[stage][t].at[k], target(stage, k)
        return remote(src, dst, send.at[t, stage, k], recv.at[t, stage, k], to)

    def steps(stage, t, k):
        src, dst = step_out[stage][t].at[k], step_in[stage][t].at[k]
        return remote(src, dst, t_send.at[t, stage, k], t_recv.at[t, stage, k], target(stage, k))

    def keep(t):
        return pltpu.make_async_copy(sums[t].at[z, x, y], outs[t].at[y, :, columns(t, c)], near.at[t, 4])

    def each(lo, hi, body):
        def one(k, carry):
            body(k)
            return carry
        lax.fori_loop(lo, hi, one, 0)

    def slab(i, height):
        return pl.ds(pl.multiple_of(i * height, height), height)

    def part(stage, t):
        w = widths[t]
        return slice(0, w) if stage in (1, 3) else slice(w, None) if stage in (2, 4) else slice(None)

    def encode(stage, t, k, parts, read):
        rows = sums[t].shape[3]
        zk, width = at_z(k), coded[stage][t].shape[-1]
        block = lambda p: coded[stage][t].at[(k, p) if parts > 1 else k]
        per = rows // 8
        def peak(i, most):
            return jnp.maximum(most, jnp.abs(read(zk, i // per, slab(i % per, 8))))
        most = lax.fori_loop(0, parts * per, peak, jnp.zeros((8, width), F32))
        most = jnp.maximum(jnp.max(most, axis=0, keepdims=True), 1e-30)
        step_out[stage][t][k] = most * (1.0 / 32767.0)
        steps(stage, t, k).start()
        scale = 32767.0 / most
        half = rows // 16
        def one(i):
            values = jnp.round(read(zk, i // half, slab(i % half, 16)) * scale).astype(jnp.int32).astype(jnp.int16)
            block(i // half)[slab(i % half, 16)] = values
        each(0, parts * half, one)
        copy(stage, t, k).start()

    def landed(stage, t, k):
        steps(stage, t, k).wait_recv()
        copy(stage, t, k).wait_recv()

    def decoded(stage, t, k, p, rows, parts):
        values = came[stage][t][(k, p, rows) if parts > 1 else (k, rows)]
        return values.astype(jnp.int32).astype(F32) * step_in[stage][t][k]

    order = (2, 1, 3, 0)
    for t in range(n):
        for k in order:
            copy(0, t, k).start()
            local(t, k).start()

    def hop(total, buffer, first, stage, to):
        return remote(total, buffer.at[stage], s_send.at[first + stage], s_recv.at[first + stage], to)

    def advance(total, buffer, first, stage):
        neighbours = (device(z, x, y, 1 - c), device(z, 1 - x, y, c), device(z, x, 1 - y, c))
        if stage:
            hop(total, buffer, first, stage - 1, neighbours[stage - 1]).wait()
            total[...] += buffer[stage - 1]
        if stage < 3:
            hop(total, buffer, first, stage, neighbours[stage]).start()
        else:
            for k in (1, 2, 3):
                last_hop(total, buffer, first, k).start()
            buffer[3 + z] = total[...]

    def last_hop(total, buffer, first, k):
        return remote(total, buffer.at[3 + z], s_send.at[first + 2 + k], s_recv.at[first + 2 + k], device(at_z(k), x, y, c))

    def finish_sum(total, buffer, first, out):
        for k in (1, 2, 3):
            last_hop(total, buffer, first, k).wait()
        out[...] = (buffer[3] + buffer[4]) + (buffer[5] + buffer[6])

    s_sum[...] = small[...]

    def first_sum(t, k):
        zk = at_z(k)
        copy(0, t, k).wait_recv()
        local(t, k).wait()
        per = sums[t].shape[3] // 16
        def one(i):
            p, r = i // per, slab(i % per, 16)
            sums[t][zk, p // 2, p % 2, r] += r0[t][zk, p // 2, p % 2, r]
        each(0, 4 * per, one)
        encode(1, t, k, 2, lambda zk, p, r: sums[t][zk, 1 - x, p, r, part(1, t)])
        encode(2, t, k, 2, lambda zk, p, r: sums[t][zk, p, 1 - y, r, part(2, t)])

    def second_sum(t, k):
        zk = at_z(k)
        per = sums[t].shape[3] // 16
        landed(1, t, k)
        def one(i):
            p, r = i // per, slab(i % per, 16)
            sums[t][zk, x, p, r, part(1, t)] += decoded(1, t, k, p, r, 2)
        each(0, 2 * per, one)
        encode(3, t, k, 1, lambda zk, p, r: sums[t][zk, x, 1 - y, r, part(3, t)])
        landed(2, t, k)
        def two(i):
            p, r = i // per, slab(i % per, 16)
            sums[t][zk, p, y, r, part(2, t)] += decoded(2, t, k, p, r, 2)
        each(0, 2 * per, two)
        encode(4, t, k, 1, lambda zk, p, r: sums[t][zk, 1 - x, y, r, part(4, t)])

    def third_sum(t, k):
        zk = at_z(k)
        landed(3, t, k)
        landed(4, t, k)
        def one(i):
            r = slab(i, 16)
            sums[t][zk, x, y, r, part(3, t)] += decoded(3, t, k, 0, r, 1)
            sums[t][zk, x, y, r, part(4, t)] += decoded(4, t, k, 0, r, 1)
        each(0, sums[t].shape[3] // 16, one)
        if k:
            encode(5, t, k, 1, lambda zk, p, r: sums[t][zk, x, y, r])

    def last_sum(t, total):
        for k in (1, 2, 3):
            landed(5, t, k)
        half = sums[t].shape[4]
        def one(i, acc):
            r = slab(i, 16)
            value = sums[t][z, x, y, r]
            for k in (1, 2, 3):
                value = value + decoded(5, t, k, 0, r, 1)
            sums[t][z, x, y, r] = value
            value = value * value
            value = value[:8] + value[8:]
            for j in range(half // 128):
                acc = acc + value[:, 128 * j : 128 * j + 128]
            return acc
        total = lax.fori_loop(0, sums[t].shape[3] // 16, one, total)
        copy(6, t, 0).start()
        keep(t).start()
        return total

    def share(t):
        copy(6, t, 0).wait_recv()
        keep(t).wait()
        copy(7, t, 0).start()

    blocks = [(t, k) for t in range(n) for k in order]
    total = before[...]
    for i in range(len(blocks) + 2):
        if i < len(blocks):
            first_sum(*blocks[i])
        if 0 <= i - 1 < len(blocks):
            second_sum(*blocks[i - 1])
        if 0 <= i - 2:
            third_sum(*blocks[i - 2])
        if i < 4:
            advance(s_sum, s_buf, 0, i)
        for t in range(n - 1):
            if i == 4 * t + 7:
                total = last_sum(t, total)
            if i == 4 * t + 9:
                share(t)
    total = last_sum(n - 1, total)
    finish_sum(s_sum, s_buf, 0, small_out)
    late = [t for t in range(n) if t == n - 1 or 4 * t + 9 >= len(blocks) + 2]
    for t in late[:-1]:
        share(t)
    q_sum[...] = total
    if q_buf.shape[0] > 1:
        for stage in range(4):
            advance(q_sum, q_buf, 6, stage)
        finish_sum(q_sum, q_buf, 6, squares)
    else:
        squares[...] = total
    share(late[-1])

    def finish(k):
        for t in range(n):
            copy(0, t, k).wait_send()
            for stage in range(1, 5):
                copy(stage, t, k).wait_send()
                steps(stage, t, k).wait_send()
    each(0, 4, finish)
    def finish_z(k):
        for t in range(n):
            copy(5, t, k).wait_send()
            steps(5, t, k).wait_send()
    each(1, 4, finish_z)
    for t in range(n):
        copy(6, t, 0).wait_send()
        copy(7, t, 0).wait()


def reduce_grads(grads, small, before, last, ident):
    n = len(grads)
    views, widths = [], []
    scratch = [[] for _ in range(22)]
    f = lambda *s: pltpu.VMEM(s, F32)
    q = lambda *s: pltpu.VMEM(s, jnp.int16)
    for grad in grads:
        rows, cols = grad.shape
        r2, half = rows // 16, cols // 2
        w = (half // 128 * 7 + 5) // 10 * 128
        views.append(grad.reshape(4, 2, 2, r2, cols))
        widths.append(w)
        blocks = [(4, 2, r2, w), (4, 2, r2, half - w), (4, r2, w), (4, r2, half - w), (4, r2, half)]
        for i, s in enumerate([f(4, 2, 2, r2, half)] * 2 + [q(*b) for b in blocks * 2] + [f(4, 1, b[-1]) for b in blocks * 2]):
            scratch[i].append(s)
    anywhere, vmem = pl.BlockSpec(memory_space=pl.ANY), pl.BlockSpec(memory_space=pltpu.VMEM)
    dma = pltpu.SemaphoreType.DMA
    square = jax.ShapeDtypeStruct((8, 128), F32)
    out = pl.pallas_call(
        functools.partial(reduce_kernel, tuple(widths), n),
        out_shape=tuple(jax.ShapeDtypeStruct((2, v.shape[3], v.shape[4]), F32) for v in views)
        + (jax.ShapeDtypeStruct(small.shape, F32), square),
        in_specs=[anywhere] * n + [vmem] * 2,
        out_specs=(anywhere,) * n + (vmem,) * 2,
        scratch_shapes=sum(scratch, []) + [
            f(7, *small.shape), f(*small.shape), f(7 if last else 1, 8, 128), f(8, 128),
            dma((n, 8, 4)), dma((n, 8, 4)), dma((n, 5)), dma((n, 6, 4)), dma((n, 6, 4)), dma((12,)), dma((12,)),
        ],
        compiler_params=pltpu.CompilerParams(
            collective_id=ident, has_side_effects=True, vmem_limit_bytes=60 * 2**20
        ),
        name="reduce",
    )(*views, small, before)
    return [o.reshape(-1, o.shape[2]) for o in out[:n]], out[n], out[n + 1]


def gather_kernel(chunks, n, *refs):
    shards, vector, results, vectors = refs[:n], refs[n], refs[n + 1 : 2 * n + 1], refs[2 * n + 1]
    outs = refs[2 * n + 2 : 3 * n + 2]
    send, recv, near, v_send, v_recv = refs[3 * n + 2 :]
    z, x, y, c = place()
    greet(z, x, y, c)

    def at_z(k):
        return (z + k) % 4

    def own(t):
        return pltpu.make_async_copy(shards[t], outs[t].at[z, x], near.at[t])

    def copy(stage, i, k):
        t, r0, nr, c0, both, split = chunks[i]
        half = shards[t].shape[2] // 2
        columns = lambda lo, size: pl.ds(pl.multiple_of(c * half + lo, 128), size)
        wide, narrow, whole = columns(c0, both), columns(c0 + both, split), columns(c0, both + split)
        rows = pl.ds(r0, nr)
        mine = isinstance(k, int) and k == 0
        o, src_z = outs[t], (z + 4 - k) % 4
        if stage == 0:
            src, dst, to = shards[t].at[:, rows, wide], o.at[z, x, :, rows, wide], device(at_z(k), x, y, c)
        elif stage == 1:
            src, dst, to = shards[t].at[y, rows, narrow], o.at[z, x, y, rows, narrow], device(at_z(k), x, y, c)
        elif stage == 2:
            dst, to = o.at[src_z, x, :, rows, wide], device(z, 1 - x, y, c)
            src = shards[t].at[:, rows, wide] if mine else dst
        elif stage == 3:
            dst, to = o.at[src_z, x, y, rows, narrow], device(z, 1 - x, y, c)
            src = shards[t].at[y, rows, narrow] if mine else dst
        elif stage == 4:
            src = o.at[src_z, 1 - x, y, rows, narrow] if mine else o.at[src_z, :, y, rows, narrow]
            dst, to = src, device(z, x, 1 - y, c)
        else:
            src = o.at[src_z, 1 - x, :, rows, whole] if mine else o.at[src_z, :, :, rows, whole]
            dst, to = src, device(z, x, y, 1 - c)
        return remote(src, dst, send.at[i, stage, k], recv.at[i, stage, k], to)

    def leave(t):
        return pltpu.make_async_copy(outs[t], results[t], near.at[n + t])

    def vector_copy(stage, k):
        src_z = (z + 4 - k) % 4
        if stage == 0:
            return remote(vector, vectors.at[z, x], v_send.at[k], v_recv.at[k], device(at_z(k), x, y, c))
        src = vector if k == 0 else vectors.at[src_z, x]
        return remote(src, vectors.at[src_z, x], v_send.at[4 + k], v_recv.at[4 + k], device(z, 1 - x, y, c))

    def each(lo, hi, body):
        def step(k, carry):
            body(k)
            return carry
        lax.fori_loop(lo, hi, step, 0)

    def along_z(i):
        def one(k):
            copy(0, i, k).start()
            copy(1, i, k).start()
        each(1, 4, one)
        copy(2, i, 0).start()
        copy(3, i, 0).start()

    def along_x(i):
        def one(k):
            copy(0, i, k).wait_recv()
            copy(2, i, k).start()
            copy(1, i, k).wait_recv()
            copy(3, i, k).start()
        each(1, 4, one)

    def along_y(i):
        copy(3, i, 0).wait_recv()
        copy(4, i, 0).start()
        def one(k):
            copy(3, i, k).wait_recv()
            copy(4, i, k).start()
        each(1, 4, one)

    def across(i):
        def one(k):
            copy(2, i, k).wait_recv()
            copy(4, i, k).wait_recv()
            copy(5, i, k).start()
        one(0)
        each(1, 4, one)

    vectors[z, x] = vector[...]
    for k in (1, 2, 3):
        vector_copy(0, k).start()
    vector_copy(1, 0).start()
    along_z(0)
    for t in range(n):
        own(t).start()
    count = len(chunks)
    for i in range(count + 3):
        if i + 1 < count:
            along_z(i + 1)
        if i < count:
            along_x(i)
        if i == 0:
            for t in range(n):
                own(t).wait()
        if i == 1:
            for k in (1, 2, 3):
                vector_copy(0, k).wait_recv()
                vector_copy(1, k).start()
        if 0 <= i - 1 < count:
            along_y(i - 1)
        if 0 <= i - 2 < count:
            across(i - 2)
        if 0 <= i - 3:
            copy(5, i - 3, 0).wait_recv()
            each(1, 4, lambda k, i=i: copy(5, i - 3, k).wait_recv())
            if i - 2 == count or chunks[i - 2][0] != chunks[i - 3][0]:
                leave(chunks[i - 3][0]).start()

    for i in range(count):
        for stage in (2, 3, 4, 5):
            copy(stage, i, 0).wait_send()
        def finish(k, i=i):
            for stage in range(6):
                copy(stage, i, k).wait_send()
        each(1, 4, finish)
    for t in range(n):
        leave(t).wait()
    vector_copy(1, 0).wait()
    for k in (1, 2, 3):
        vector_copy(0, k).wait_send()
        vector_copy(1, k).wait()


def chunks_of(shards, largest):
    chunks = []
    for t, shard in enumerate(shards):
        rows, tiles = shard.shape[0] // 2, shard.shape[1] // 256
        size = rows * tiles * 128
        parts = -(-size // largest)
        by_rows = rows // parts % 16 == 0 and tiles < 2 * parts
        if by_rows:
            for p in range(parts):
                both = max(1, tiles // 3) if tiles > 1 else 0
                chunks.append((t, rows // parts * p, rows // parts, 0, both * 128, (tiles - both) * 128))
        else:
            cuts = [tiles * p // parts for p in range(parts + 1)]
            for lo, hi in zip(cuts, cuts[1:]):
                both = max(1, (hi - lo) // 3)
                chunks.append((t, 0, rows, lo * 128, both * 128, (hi - lo - both) * 128))
    return tuple(chunks)


def gather_weights(shards, vector, ident):
    n = len(shards)
    views = [shard.reshape(2, shard.shape[0] // 2, shard.shape[1]) for shard in shards]
    chunks = chunks_of(shards, 75000)
    anywhere, vmem = pl.BlockSpec(memory_space=pl.ANY), pl.BlockSpec(memory_space=pltpu.VMEM)
    dma = pltpu.SemaphoreType.DMA
    out = pl.pallas_call(
        functools.partial(gather_kernel, chunks, n),
        out_shape=tuple(jax.ShapeDtypeStruct((4, 2) + v.shape, BF16) for v in views)
        + (jax.ShapeDtypeStruct((4, 2, 8, 128), F32),),
        in_specs=[vmem] * n + [vmem],
        out_specs=(anywhere,) * n + (vmem,),
        scratch_shapes=[pltpu.VMEM((4, 2) + v.shape, BF16) for v in views]
        + [dma((len(chunks), 6, 4)), dma((len(chunks), 6, 4)), dma((2 * n,)), dma((8,)), dma((8,))],
        compiler_params=pltpu.CompilerParams(collective_id=ident, has_side_effects=True, vmem_limit_bytes=60 * 2**20),
        name="gather",
    )(*views, vector.reshape(8, 128))
    return [o.reshape(-1, o.shape[4]) for o in out[:n]], out[n].reshape(-1)


def clip_of(column, clip_lengths, clip_shifts):
    columns = clip_lengths // 8
    ends = jnp.cumsum(columns)
    clip_id = jnp.sum((column[:, None] >= ends[None, :]).astype(jnp.int32), axis=1)
    onehot = (clip_id[:, None] == jnp.arange(clip_lengths.shape[0], dtype=jnp.int32)[None, :]).astype(jnp.int32)

    def select(values):
        return jnp.sum(onehot * values[None, :], axis=1)

    return clip_id, select(ends - columns), select(columns), select(clip_shifts[:, 0]), select(clip_shifts[:, 1])


def half_table(position, width):
    quarter = width // 4
    omega = 1.0 / 10000.0 ** (jnp.arange(quarter, dtype=jnp.float32) / quarter)
    angle = omega[:, None] * position.astype(jnp.float32)[None, :]
    return jnp.concatenate([jnp.sin(angle), jnp.cos(angle)])


def adam_update(weight, first, second, grad, decay):
    first = BETA_ONE * first + (1.0 - BETA_ONE) * grad
    second = BETA_TWO * second + (1.0 - BETA_TWO) * grad * grad
    first_hat = first / (1.0 - BETA_ONE**STEP)
    second_hat = second / (1.0 - BETA_TWO**STEP)
    weight = weight - LEARN_RATE * (first_hat / (jnp.sqrt(second_hat) + EPSILON) + decay * weight)
    return (weight, first, second)


def shards(
    pixels,
    lengths,
    shifts,
    visible,
    patch_embed,
    encoder_in,
    encoder_down,
    decoder_in,
    decoder_down,
    norm_vectors,
    first_embed,
    first_encoder_in,
    first_encoder_down,
    first_decoder_in,
    first_decoder_down,
    first_vectors,
    second_embed,
    second_encoder_in,
    second_encoder_down,
    second_decoder_in,
    second_decoder_down,
    second_vectors,
):
    masters = (patch_embed, encoder_in, encoder_down, decoder_in, decoder_down, norm_vectors)
    firsts = (
        first_embed,
        first_encoder_in,
        first_encoder_down,
        first_decoder_in,
        first_decoder_down,
        first_vectors,
    )
    seconds = (
        second_embed,
        second_encoder_in,
        second_encoder_down,
        second_decoder_in,
        second_decoder_down,
        second_vectors,
    )
    direct = lax.axis_size("clip") == 8 and lax.axis_size("band") == 4
    low_shards = [master.astype(jnp.bfloat16) for master in masters]
    if direct:
        (w_embed, w_enc, w_enc_down, w_dec, w_dec_down), vectors = gather_weights(
            low_shards[:5], lax.reduce_precision(norm_vectors, exponent_bits=8, mantissa_bits=7), 0
        )
    else:
        w_embed, w_enc, w_enc_down, w_dec, w_dec_down, gathered_vectors = (
            lax.all_gather(shard, "clip", axis=0, tiled=True) for shard in low_shards
        )
        vectors = gathered_vectors.astype(jnp.float32)
    enc_width, dec_width = (w_enc.shape[0], w_dec.shape[0])
    patch_dev, n_visible = pixels.shape[0], visible.shape[0]
    padded = -(-n_visible // 128) * 128
    enc_gains = vectors[: 6 * enc_width].reshape(6, enc_width, 1)
    dec_gains = vectors[6 * enc_width :].reshape(7, dec_width, 1)
    enc_gains = jnp.broadcast_to(enc_gains, (6, enc_width, 128))
    dec_gains = jnp.broadcast_to(dec_gains, (7, dec_width, 128))
    turned = jnp.arange(patch_dev // 8, dtype=jnp.int32)
    _, start, size, shift_time, shift_band = clip_of(turned, lengths[0], shifts[0])
    turned_time = (turned - start - shift_time) % size
    decoder_pixels = pixels.reshape(patch_dev // 8, 8, -1)[start + turned_time].reshape(pixels.shape)
    time_table = half_table(turned_time, dec_width).T
    band_table = jnp.tile(half_table(jnp.arange(8, dtype=jnp.int32), dec_width), (1, 16))
    spots = jnp.pad(visible, (0, padded - n_visible))
    real = jnp.arange(padded, dtype=jnp.int32) < n_visible
    seen = pixels[spots]
    column, band = spots // 8, spots % 8
    segment, seen_start, seen_size, seen_shift, _ = clip_of(column, lengths[0], shifts[0])
    segment = jnp.where(real, segment, -1).astype(jnp.int32)
    seen_time = column - seen_start
    decoder_row = jnp.where(real, 8 * (seen_start + (seen_time + seen_shift) % seen_size) + band, -1)
    decoder_row = jnp.broadcast_to(decoder_row[:, None], (padded, 128)).astype(jnp.int32)

    def positions(width):
        return jnp.concatenate([half_table(seen_time, width), half_table(band, width)])

    grid_seen, *saved = encoder_forward(
        seen,
        positions(enc_width),
        positions(dec_width),
        jnp.broadcast_to(segment[:, None], (padded, 128)),
        jnp.broadcast_to(segment[None, :], (8, padded)),
        enc_gains,
        w_embed,
        w_enc,
        w_enc_down,
        HEADS_ENC,
    )
    masked_count = 13.0 * (patch_dev // 16) * lax.axis_size("clip") * lax.axis_size("band")
    g_dec_in, g_dec_down, g_dec_vectors, grad_grid, loss = decoder_step(
        shift_band[::64],
        decoder_row,
        grid_seen,
        decoder_pixels,
        time_table,
        band_table,
        dec_gains,
        w_dec,
        w_dec.T,
        w_dec_down,
        w_dec_down.T,
        2.0 / (pixels.shape[1] * masked_count),
        HEADS_DEC,
    )
    local_loss = jnp.sum(loss[0])
    g_enc_in, g_enc_down, g_embed, g_enc_vectors = encoder_backward(
        grad_grid, enc_gains, w_enc, w_enc_down, saved, pixels.shape[1], HEADS_ENC
    )
    g_vectors = jnp.concatenate(
        [jnp.sum(g_enc_vectors, axis=2).reshape(-1), jnp.sum(g_dec_vectors, axis=2).reshape(-1)]
    )
    if direct:
        small = jnp.concatenate([g_vectors.reshape(-1, 128), jnp.full((8, 128), local_loss)])
        nothing = jnp.zeros((8, 128), jnp.float32)
        dec_shards, _, squares = reduce_grads([g_dec_in, g_dec_down], nothing, nothing, False, 1)
        enc_shards, summed, squares = reduce_grads(
            [g_enc_in, g_enc_down, g_embed], small, squares, True, 2
        )
        rows = norm_vectors.shape[0]
        vector_sums = summed[:-8].reshape(-1)
        own = lax.dynamic_slice(vector_sums, (lax.axis_index("clip") * rows,), (rows,))
        reduced = (enc_shards[2], enc_shards[0], enc_shards[1], *dec_shards, own)
        loss_sum = summed[-1, 0]
        norm_squared = jnp.sum(squares) + jnp.sum(vector_sums * vector_sums)
    else:
        reduced = lax.psum(
            tuple(
                lax.psum_scatter(grad, "clip", scatter_dimension=0, tiled=True)
                for grad in (g_embed, g_enc_in, g_enc_down, g_dec_in, g_dec_down, g_vectors)
            ),
            "band",
        )
        loss_sum = lax.psum(local_loss, ("clip", "band"))
        norm_squared = lax.psum(sum(jnp.sum(grad * grad) for grad in reduced), "clip")
    grad_norm = jnp.sqrt(norm_squared)
    factor = jnp.minimum(1.0, CLIP_LIMIT / (grad_norm + 1e-06))
    results = []
    for index in range(6):
        decay = DECAY_RATE if index < 5 else 0.0
        results.append(
            adam_update(
                masters[index], firsts[index], seconds[index], reduced[index] * factor, decay
            )
        )
    return (
        loss_sum,
        grad_norm,
        results[0][0],
        results[1][0],
        results[2][0],
        results[3][0],
        results[4][0],
        results[5][0],
        results[0][1],
        results[1][1],
        results[2][1],
        results[3][1],
        results[4][1],
        results[5][1],
        results[0][2],
        results[1][2],
        results[2][2],
        results[3][2],
        results[4][2],
        results[5][2],
    )


def solution(mesh):
    in_specs = (
        P(("clip", "band"), None),
        P(("clip", "band"), None),
        P(("clip", "band"), None, None),
        P(("clip", "band")),
        P("clip", None),
        P("clip", None),
        P("clip", None),
        P("clip", None),
        P("clip", None),
        P("clip"),
        P("clip", None),
        P("clip", None),
        P("clip", None),
        P("clip", None),
        P("clip", None),
        P("clip"),
        P("clip", None),
        P("clip", None),
        P("clip", None),
        P("clip", None),
        P("clip", None),
        P("clip"),
    )
    out_specs = (
        P(),
        P(),
        P("clip", None),
        P("clip", None),
        P("clip", None),
        P("clip", None),
        P("clip", None),
        P("clip"),
        P("clip", None),
        P("clip", None),
        P("clip", None),
        P("clip", None),
        P("clip", None),
        P("clip"),
        P("clip", None),
        P("clip", None),
        P("clip", None),
        P("clip", None),
        P("clip", None),
        P("clip"),
    )
    return jax.shard_map(shards, mesh=mesh, in_specs=in_specs, out_specs=out_specs, check_vma=False)
```

```python
import functools

import jax
import jax.numpy as jnp
from jax import lax
from jax.experimental import pallas as pl
from jax.experimental.pallas import tpu as pltpu
from jax.sharding import PartitionSpec as P

HEADS_ENC = 12
HEADS_DEC = 16
STEP = 10


LEARN_RATE = 0.02
BETA_ONE = 0.9
BETA_TWO = 0.95
EPSILON = 1e-08
DECAY_RATE = 0.05
CLIP_LIMIT = 0.001


F32, BF16 = jnp.float32, jnp.bfloat16
GELU_C = 0.7978845608028654


def mm(a, b, ca=1, cb=0):
    return lax.dot_general(a, b, (((ca,), (cb,)), ((), ())), preferred_element_type=F32)


def wide(v, n):
    return jnp.concatenate([v] * (n // 128), axis=1)


def loop(n, body, unroll=1):
    def step(i, carry):
        for k in range(unroll):
            body(i * unroll + k)
        return carry
    lax.fori_loop(0, n // unroll, step, 0)


def fold(v):
    total = v[:, :128]
    for i in range(1, v.shape[1] // 128):
        total = total + v[:, 128 * i : 128 * (i + 1)]
    return total


def decoder_kernel(
    coef, heads, shift_ref, rvis_ref, gvt_ref, pix_ref, et_ref, ef_ref, vec_ref, w_ref, wd_ref,
    gin_ref, gdown_ref, gvec_ref, gp_ref, loss_ref,
    wt_ref, wdt_ref, res, xh1, xh2, xh3, tmp, n1, n2, fin, rs, qkv, att, act, dgel, probs, dqkv, dup, low, oh, mrow, hb, hm, wm,
):
    width = w_ref.shape[0]
    hidden = wd_ref.shape[0]
    rows = res.shape[1]
    size = width // heads
    per = 128 // size
    scale = size ** -0.5
    groups = width // 128
    c_out, c_up, c_head = 3 * width, 4 * width, 4 * width + hidden
    pixels = w_ref.shape[1] - c_head
    cols = rows // 8
    nblk = pix_ref.shape[0] // rows
    chunk = 512

    def turn_in(i):
        at = pl.ds(pl.multiple_of(i * 256, 256), 256)
        wt_ref[at, :] = w_ref[:, at].T
    loop(w_ref.shape[1] // 256, turn_in)

    def turn_down(i):
        at = pl.ds(pl.multiple_of(i * 256, 256), 256)
        wdt_ref[:, at] = wd_ref[at, :].T
    loop(hidden // 256, turn_down)
    gin_ref[...] = jnp.zeros_like(gin_ref)
    gdown_ref[...] = jnp.zeros_like(gdown_ref)
    gvec_ref[...] = jnp.zeros_like(gvec_ref)
    gp_ref[...] = jnp.zeros_like(gp_ref)
    loss_ref[...] = jnp.zeros_like(loss_ref)
    f_id = lax.broadcasted_iota(jnp.int32, (128, 128 * per), 0)
    q_id = lax.broadcasted_iota(jnp.int32, (128, 128 * per), 1)
    hm[...] = jnp.where(f_id // size == q_id // 128, 1.0, 0.0).astype(BF16)
    wm[...] = jnp.where(f_id // 32 == (q_id % 128) // 32, 1.0, 0.0).astype(BF16)

    def lane(i):
        return pl.ds(pl.multiple_of(i * 128, 128), 128)

    def ln_forward(k, xh, out):
        def body(i):
            x = res[:, lane(i)]
            centre = x - jnp.mean(x, axis=0, keepdims=True)
            r = lax.rsqrt(jnp.mean(centre * centre, axis=0, keepdims=True) + 1e-06)
            xhat = centre * r
            xh[:, lane(i)] = xhat
            rs[8 * k : 8 * k + 8, lane(i)] = jnp.broadcast_to(r, (8, 128))
            out[:, lane(i)] = (xhat * vec_ref[2 * k] + vec_ref[2 * k + 1]).astype(BF16)
        loop(rows // 128, body, 4)

    def ln_backward(k, xh, add):
        def body(i):
            d = tmp[:, lane(i)]
            xhat = xh[:, lane(i)]
            gvec_ref[2 * k] += d * xhat
            gvec_ref[2 * k + 1] += d
            dx = d * vec_ref[2 * k]
            m1 = jnp.mean(dx, axis=0, keepdims=True)
            m2 = jnp.mean(dx * xhat, axis=0, keepdims=True)
            g = rs[8 * k : 8 * k + 1, lane(i)] * (dx - m1 - xhat * m2)
            if add:
                g = g + res[:, lane(i)]
            res[:, lane(i)] = g
            low[:, lane(i)] = g.astype(BF16)
        loop(rows // 128, body, 4)

    def block(j):
        first = pl.multiple_of(j * rows, rows)
        turn = shift_ref[j]
        spot = lax.broadcasted_iota(jnp.int32, (rvis_ref.shape[0], rows), 1) + first
        hot = jnp.where(wide(rvis_ref[...], rows) == spot, 1.0, 0.0)
        oh[...] = hot.astype(BF16)
        masked = 1.0 - jnp.sum(hot, axis=0, keepdims=True)
        mrow[...] = jnp.broadcast_to(masked, (8, rows))
        et = et_ref[pl.ds(pl.multiple_of(j * cols, cols), cols), :]
        e_hi = et.astype(BF16)
        rest = et - e_hi.astype(F32)
        e_mid = rest.astype(BF16)
        e_lo = (rest - e_mid.astype(F32)).astype(BF16)
        spread = jnp.where(
            lax.broadcasted_iota(jnp.int32, (cols, rows), 1) // 8 == lax.broadcasted_iota(jnp.int32, (cols, rows), 0), 1.0, 0.0
        ).astype(BF16)
        e_t = mm(e_hi, spread, 0, 0) + (mm(e_mid, spread, 0, 0) + mm(e_lo, spread, 0, 0))
        half = width // 2
        keep = masked > 0.5
        placed = mm(gvt_ref[...], oh[...])
        top = (wide(vec_ref[6, :half], rows) + e_t).astype(BF16).astype(F32)
        res[:half] = jnp.where(keep, top, placed[:half])
        bottom = wide((vec_ref[6, half:] + ef_ref[...]).astype(BF16).astype(F32), rows)
        res[half:] = jnp.where(keep, bottom, placed[half:])
        k_half = (lax.broadcasted_iota(jnp.int32, (32, 128 * per), 0) % 8 + turn) % 8 // 4
        q_half = (lax.broadcasted_iota(jnp.int32, (32, 128 * per), 1) % 8 + turn) % 8 // 4
        hb[...] = jnp.where(k_half == q_half, 0.0, -1e30)

        ln_forward(0, xh1, n1)

        def qkv_part(i):
            part = pl.ds(pl.multiple_of(i * chunk, chunk), chunk)
            qkv[part, :] = mm(wt_ref[part, :], n1[...]).astype(BF16)
        loop(3 * width // chunk, qkv_part, 3)

        q_group = (lax.broadcasted_iota(jnp.int32, (32, 128 * per), 1) % 128) // 32

        def compact(s):
            c = s[96:128]
            for i in (2, 1, 0):
                c = jnp.where(q_group == i, s[32 * i : 32 * i + 32], c)
            return c

        def attend(i):
            sb, g = i // groups, i % groups
            at = lane(sb)
            f0 = pl.multiple_of(g * 128, 128)
            q = qkv[pl.ds(f0, 128), at]
            k = qkv[pl.ds(width + f0, 128), at]
            v = qkv[pl.ds(2 * width + f0, 128), at]
            s = jnp.concatenate([mm(k[size * h : size * h + size], q[size * h : size * h + size], 0, 0) for h in range(per)], axis=1)
            c = compact(s) * scale + hb[...]
            e = jnp.exp(c - jnp.max(c, axis=0, keepdims=True))
            p = e * (1.0 / jnp.sum(e, axis=0, keepdims=True))
            probs[i] = p
            p_low = p.astype(BF16)
            p_all = jnp.concatenate([p_low] * 4, axis=0) * wm[...]
            for h in range(per):
                o = mm(v[size * h : size * h + size], p_all[:, 128 * h : 128 * h + 128])
                att[pl.ds(f0 + size * h, size), at] = o.astype(BF16)
        loop(rows // 128 * groups, attend, 16)

        res[...] += mm(wt_ref[c_out : c_out + width], att[...])
        ln_forward(1, xh2, n2)

        def up_part(i):
            part = pl.ds(pl.multiple_of(i * chunk, chunk), chunk)
            u = mm(wt_ref[pl.ds(pl.multiple_of(c_up + i * chunk, chunk), chunk), :], n2[...])
            square = u * u
            hp = 0.5 + 0.5 * jnp.tanh(u * (GELU_C + (GELU_C * 0.044715) * square))
            v = u * hp
            act[part, :] = v.astype(BF16)
            dgel[part, :] = hp + (v - v * hp) * ((2 * GELU_C) + (6 * GELU_C * 0.044715) * square)
        loop(hidden // chunk, up_part, 4)

        res[...] += mm(wdt_ref[...], act[...])
        ln_forward(2, xh3, fin)
        pred = mm(wt_ref[c_head:], fin[...])
        pix = pix_ref[pl.ds(first, rows), :].astype(F32).T
        centre = pix - jnp.mean(pix, axis=0, keepdims=True)
        target = (centre * lax.rsqrt(jnp.mean(centre * centre, axis=0, keepdims=True) + 1e-06)).astype(BF16).astype(F32)
        err = pred - target
        loss_ref[...] += fold(mrow[...] * jnp.mean(err * err, axis=0, keepdims=True))
        gpred = (mrow[0:1] * err * coef).astype(BF16)

        gin_ref[:, c_head:] += mm(fin[...], gpred, 1, 1)
        tmp[...] = mm(w_ref[:, c_head:], gpred)
        ln_backward(2, xh3, False)

        def mlp_back(i):
            part = pl.ds(pl.multiple_of(i * chunk, chunk), chunk)
            there = pl.ds(pl.multiple_of(c_up + i * chunk, chunk), chunk)
            d = (mm(wd_ref[part, :], low[...]) * dgel[part, :]).astype(BF16)
            dup[part, :] = d
            gdown_ref[part, :] += mm(act[part, :], low[...], 1, 1)
            gin_ref[:, there] += mm(n2[...], d, 1, 1)
        loop(hidden // chunk, mlp_back, 4)
        tmp[...] = mm(w_ref[:, c_up:c_head], dup[...])
        ln_backward(1, xh2, True)
        gin_ref[:, c_out:c_up] += mm(att[...], low[...], 1, 1)
        fin[...] = mm(w_ref[:, c_out:c_up], low[...]).astype(BF16)

        def attend_back(i):
            sb, g = i // groups, i % groups
            at = lane(sb)
            f0 = pl.multiple_of(g * 128, 128)
            q = qkv[pl.ds(f0, 128), at]
            k = qkv[pl.ds(width + f0, 128), at]
            v = qkv[pl.ds(2 * width + f0, 128), at]
            do = fin[pl.ds(f0, 128), at]
            do_all = wide(do, 128 * per) * hm[...]
            dp = compact(jnp.concatenate([mm(v[size * h : size * h + size], do[size * h : size * h + size], 0, 0) for h in range(per)], axis=1))
            p = probs[i]
            ds = p * (dp - jnp.sum(dp * p, axis=0, keepdims=True))
            p_all = jnp.concatenate([p.astype(BF16)] * 4, axis=0) * wm[...]
            ds_all = jnp.concatenate([(ds * scale).astype(BF16)] * 4, axis=0) * wm[...]
            tall = jnp.concatenate([ds_all[:, 128 * h : 128 * h + 128] for h in range(per)], axis=0)
            dqkv[pl.ds(f0, 128), at] = mm(wide(k, 128 * per) * hm[...], tall).astype(BF16)
            dqkv[pl.ds(width + f0, 128), at] = mm(wide(q, 128 * per) * hm[...], ds_all, 1, 1).astype(BF16)
            dqkv[pl.ds(2 * width + f0, 128), at] = mm(do_all, p_all, 1, 1).astype(BF16)
        loop(rows // 128 * groups, attend_back, 8)

        def qkv_back(i):
            part = pl.ds(pl.multiple_of(i * chunk, chunk), chunk)
            gin_ref[:, part] += mm(n1[...], dqkv[part, :], 1, 1)
        loop(3 * width // chunk, qkv_back, 3)
        tmp[...] = mm(w_ref[:, :c_out], dqkv[...])
        ln_backward(0, xh1, True)
        gvec_ref[6] += fold(low[...].astype(F32) * mrow[0:1])
        gp_ref[...] += mm(low[...], oh[...], 1, 1)

    loop(nblk, block)


def decoder_step(shift, rvis, gvt, pix, et, ef, vec, w, wd, coef, heads):
    width, total = w.shape
    hidden = wd.shape[0]
    rows = 512
    vis = rvis.shape[0]
    per = 128 // (width // heads)
    vmem = pl.BlockSpec(memory_space=pltpu.VMEM)
    f = lambda *s: pltpu.VMEM(s, F32)
    b = lambda *s: pltpu.VMEM(s, BF16)
    return pl.pallas_call(
        functools.partial(decoder_kernel, coef, heads),
        out_shape=(
            jax.ShapeDtypeStruct((width, total), F32),
            jax.ShapeDtypeStruct((hidden, width), F32),
            jax.ShapeDtypeStruct((7, width, 128), F32),
            jax.ShapeDtypeStruct((width, vis), F32),
            jax.ShapeDtypeStruct((8, 128), F32),
        ),
        in_specs=[pl.BlockSpec(memory_space=pltpu.SMEM)] + [vmem] * 8,
        out_specs=(vmem,) * 5,
        scratch_shapes=[
            b(total, width), b(width, hidden), f(width, rows), f(width, rows), f(width, rows), f(width, rows), f(width, rows),
            b(width, rows), b(width, rows), b(width, rows), f(24, rows),
            b(3 * width, rows), b(width, rows), b(hidden, rows), f(hidden, rows),
            f(rows // 128 * (width // 128), 32, 128 * per), b(3 * width, rows), b(hidden, rows), b(width, rows),
            b(vis, rows), f(8, rows), f(32, 128 * per), b(128, 128 * per), b(128, 128 * per),
        ],
        compiler_params=pltpu.CompilerParams(vmem_limit_bytes=63 * 2**20),
        name="decoder",
    )(shift, rvis, gvt, pix, et, ef, vec, w, wd)


CHUNK = 768


def lane(i):
    return pl.ds(i * 128 if isinstance(i, int) else pl.multiple_of(i * 128, 128), 128)


def part(i, base=0):
    return pl.ds(pl.multiple_of(base + i * CHUNK, 128), CHUNK)


def encoder_clips(seg_ref, own, others):
    clip = lax.broadcasted_iota(jnp.int32, own.shape, 0) == seg_ref[0:1]
    own[...] = jnp.where(clip, 1.0, 0.0).astype(BF16)
    others[...] = jnp.where(clip, 0.0, -1e31).astype(BF16)


def encoder_scores(q, k, scale):
    c = mm(k, q)
    e = jnp.exp2((c - jnp.max(c, axis=0, keepdims=True)) * (scale * 1.4426950408889634))
    return e * (1.0 / jnp.sum(e, axis=0, keepdims=True))


def encoder_forward_kernel(
    heads, seen_ref, pos_ref, grid_pos_ref, seg_ref, vec_ref, we_ref, wi_ref, wd_ref,
    grid_ref, seen_t_ref, xh1_ref, n1_ref, qkv_ref, att_ref, xh2_ref, n2_ref, act_ref, dgel_ref, xh3_ref, fin_ref, rs_ref,
    we, wi, wd, res, own, others, seen_t, xh1, n1, qkv, att, xh2, n2, act, dgel, xh3, fin, rs, w_sem, o_sem,
):
    width, hidden = we.shape[1], wd.shape[0]
    rows = res.shape[1]
    size = width // heads
    scale = size ** -0.5
    c_out, c_up, c_proj = 3 * width, 4 * width, 4 * width + hidden
    total = wi.shape[1]
    loads = [pltpu.make_async_copy(we_ref, we, w_sem.at[0])]
    for i, (lo, hi) in enumerate(((0, c_out), (c_out, c_up), (c_up, c_proj), (c_proj, total))):
        at = pl.ds(lo, hi - lo)
        loads.append(pltpu.make_async_copy(wi_ref.at[:, at], wi.at[:, at], w_sem.at[1 + i]))
    loads.insert(4, pltpu.make_async_copy(wd_ref, wd, w_sem.at[5]))
    for load in loads:
        load.start()
    pairs = (
        (seen_t, seen_t_ref), (xh1, xh1_ref), (n1, n1_ref), (qkv, qkv_ref), (att, att_ref), (xh2, xh2_ref),
        (n2, n2_ref), (act, act_ref), (dgel, dgel_ref), (xh3, xh3_ref), (fin, fin_ref), (rs, rs_ref),
    )
    saves = [pltpu.make_async_copy(a, b, o_sem.at[i]) for i, (a, b) in enumerate(pairs)]

    def ln_forward(k, xh, out):
        def body(i):
            x = res[:, lane(i)]
            centre = x - jnp.mean(x, axis=0, keepdims=True)
            r = lax.rsqrt(jnp.mean(centre * centre, axis=0, keepdims=True) + 1e-06)
            xhat = centre * r
            xh[:, lane(i)] = xhat
            rs[8 * k : 8 * k + 8, lane(i)] = jnp.broadcast_to(r, (8, 128))
            out[:, lane(i)] = (xhat * vec_ref[2 * k] + vec_ref[2 * k + 1]).astype(BF16)
        for i in range(rows // 128):
            body(i)

    seen_t[...] = seen_ref[...].T
    saves[0].start()
    encoder_clips(seg_ref, own, others)
    loads[0].wait()
    res[...] = mm(we[...], seen_t[...], 0, 0) + pos_ref[...]
    ln_forward(0, xh1, n1)
    saves[1].start()
    saves[2].start()
    loads[1].wait()

    def qkv_part(i):
        qkv[part(i), :] = mm(wi[:, part(i)], n1[...], 0, 0).astype(BF16)
    loop(3, qkv_part, 3)
    saves[3].start()

    def attend(h):
        f0 = pl.multiple_of(h * size, size)
        k = jnp.concatenate([qkv[pl.ds(width + f0, size), :], others[...]], axis=0).T
        v = qkv[pl.ds(2 * width + f0, size), :]
        for i in range(rows // 128):
            q = jnp.concatenate([qkv[pl.ds(f0, size), lane(i)], own[:, lane(i)]], axis=0)
            p = encoder_scores(q, k, scale)
            att[pl.ds(f0, size), lane(i)] = mm(v, p.astype(BF16)).astype(BF16)
    loop(heads, attend, 4)
    saves[4].start()
    loads[2].wait()
    res[...] += mm(wi[:, c_out:c_up], att[...], 0, 0)
    ln_forward(1, xh2, n2)
    saves[5].start()
    saves[6].start()
    loads[3].wait()

    def up_part(i):
        u = mm(wi[:, part(i, c_up)], n2[...], 0, 0)
        square = u * u
        hp = 0.5 + 0.5 * jnp.tanh(u * (GELU_C + (GELU_C * 0.044715) * square))
        v = u * hp
        act[part(i), :] = v.astype(BF16)
        dgel[part(i), :] = hp + (v - v * hp) * ((2 * GELU_C) + (6 * GELU_C * 0.044715) * square)
    loop(hidden // CHUNK, up_part, 4)
    saves[7].start()
    saves[8].start()
    loads[4].wait()
    res[...] += mm(wd[...], act[...], 0, 0)
    ln_forward(2, xh3, fin)
    for i in (9, 10, 11):
        saves[i].start()
    loads[5].wait()
    grid_ref[...] = (mm(wi[:, c_proj:], fin[...], 0, 0) + grid_pos_ref[...]).astype(BF16)
    for save in saves:
        save.wait()


def encoder_forward(seen, pos, grid_pos, seg, vec, we, wi, wd, heads):
    rows, patch = seen.shape
    width, total = wi.shape
    hidden = wd.shape[0]
    any_, vmem = pl.BlockSpec(memory_space=pl.ANY), pl.BlockSpec(memory_space=pltpu.VMEM)
    saved = (
        ((patch, rows), BF16), ((width, rows), F32), ((width, rows), BF16), ((3 * width, rows), BF16),
        ((width, rows), BF16), ((width, rows), F32), ((width, rows), BF16), ((hidden, rows), BF16), ((hidden, rows), F32),
        ((width, rows), F32), ((width, rows), BF16), ((24, rows), F32),
    )
    return pl.pallas_call(
        functools.partial(encoder_forward_kernel, heads),
        out_shape=(jax.ShapeDtypeStruct((grid_pos.shape[0], rows), BF16),) + tuple(jax.ShapeDtypeStruct(*s) for s in saved),
        in_specs=[vmem] * 5 + [any_] * 3,
        out_specs=(vmem,) + (any_,) * len(saved),
        scratch_shapes=[pltpu.VMEM(we.shape, BF16), pltpu.VMEM(wi.shape, BF16), pltpu.VMEM(wd.shape, BF16), pltpu.VMEM((width, rows), F32)]
        + [pltpu.VMEM((16, rows), BF16)] * 2 + [pltpu.VMEM(*s) for s in saved] + [pltpu.SemaphoreType.DMA((6,)), pltpu.SemaphoreType.DMA((len(saved),))],
        compiler_params=pltpu.CompilerParams(vmem_limit_bytes=62 * 2**20),
        name="encode",
    )(seen, pos, grid_pos, seg, vec, we, wi, wd)


def encoder_backward_kernel(
    heads, gp_ref, vec_ref, seg_ref, wi_ref, wd_ref,
    seen_t_ref, xh1_ref, n1_ref, qkv_ref, att_ref, xh2_ref, n2_ref, act_ref, dgel_ref, xh3_ref, fin_ref, rs_ref,
    gin_ref, gdown_ref, gembed_ref, gvec_ref,
    wi, wd, res, tmp, low, dqkv, probs, dscores, stage, own, others, seen_t, xh1, n1, qkv, att, xh2, n2, act, dgel, rs, i_sem, s_sem,
):
    width, hidden = wi.shape[0], wd.shape[0]
    rows = res.shape[1]
    size = width // heads
    scale = size ** -0.5
    c_out, c_up, c_proj = 3 * width, 4 * width, 4 * width + hidden
    total = wi.shape[1]
    n_proj = total - c_proj

    def load(i, src, dst):
        return pltpu.make_async_copy(src, dst, i_sem.at[i])

    def columns(i, lo, hi):
        at = pl.ds(lo, hi - lo)
        return load(i, wi_ref.at[:, at], wi.at[:, at])

    first = [load(0, fin_ref, n1), columns(1, c_proj, total), load(2, xh3_ref, xh1), load(3, rs_ref, rs)]
    mlp = [load(4, wd_ref, wd), load(5, dgel_ref, dgel), load(6, act_ref, act), load(7, n2_ref, n2)]
    second = [columns(8, c_up, c_proj), load(9, xh2_ref, xh2), columns(10, c_out, c_up), load(11, att_ref, att)]
    attention = [load(12, qkv_ref, qkv), columns(14, 0, c_out), load(15, seen_t_ref, seen_t)]
    again = [load(16, xh1_ref, xh1), load(17, n1_ref, n1)]
    for group in (first, mlp, second, attention):
        for copy in group:
            copy.start()
    gvec_ref[...] = jnp.zeros_like(gvec_ref)
    encoder_clips(seg_ref, own, others)

    open_copies = [None, None]
    turn = [0]

    def leave(value, dst):
        slot = turn[0] % 2
        if open_copies[slot] is not None:
            open_copies[slot].wait()
        height, length = value.shape
        stage[slot, :height, :length] = value
        copy = pltpu.make_async_copy(stage.at[slot, pl.ds(0, height), pl.ds(0, length)], dst, s_sem.at[slot])
        copy.start()
        open_copies[slot] = copy
        turn[0] += 1

    def ln_backward(k, xh, add):
        for i in range(rows // 128):
            d = tmp[:, lane(i)]
            xhat = xh[:, lane(i)]
            gvec_ref[2 * k] += d * xhat
            gvec_ref[2 * k + 1] += d
            dx = d * vec_ref[2 * k]
            m1 = jnp.mean(dx, axis=0, keepdims=True)
            m2 = jnp.mean(dx * xhat, axis=0, keepdims=True)
            g = rs[8 * k : 8 * k + 1, lane(i)] * (dx - m1 - xhat * m2)
            if add:
                g = g + res[:, lane(i)]
            res[:, lane(i)] = g
            low[:, lane(i)] = g.astype(BF16)

    for copy in first:
        copy.wait()
    gp = gp_ref[...].astype(BF16)
    leave(mm(n1[...], gp, 1, 1), gin_ref.at[:, pl.ds(c_proj, n_proj)])
    tmp[...] = mm(wi[:, c_proj:], gp)
    ln_backward(2, xh1, False)
    for copy in again:
        copy.start()
    for copy in mlp:
        copy.wait()
    for i in range(hidden // CHUNK):
        at = pl.ds(i * CHUNK, CHUNK)
        d = (mm(wd[at, :], low[...]) * dgel[at, :]).astype(BF16)
        leave(mm(act[at, :], low[...], 1, 1), gdown_ref.at[at, :])
        act[at, :] = d
        leave(mm(n2[...], d, 1, 1), gin_ref.at[:, pl.ds(c_up + i * CHUNK, CHUNK)])
    for copy in second:
        copy.wait()
    tmp[...] = mm(wi[:, c_up:c_proj], act[...])
    ln_backward(1, xh2, True)
    leave(mm(att[...], low[...], 1, 1), gin_ref.at[:, pl.ds(c_out, width)])
    att[...] = mm(wi[:, c_out:c_up], low[...]).astype(BF16)
    for copy in attention:
        copy.wait()

    def attend_back(h):
        f0 = pl.multiple_of(h * size, size)
        mine = pl.ds(f0, size)
        q = qkv[mine, :]
        k = qkv[pl.ds(width + f0, size), :]
        v = qkv[pl.ds(2 * width + f0, size), :]
        do = att[mine, :]
        keys = jnp.concatenate([k, others[...]], axis=0).T
        values = v.T
        for i in range(rows // 128):
            part_q = jnp.concatenate([q[:, 128 * i : 128 * i + 128], own[:, lane(i)]], axis=0)
            p = encoder_scores(part_q, keys, scale)
            dp = mm(values, do[:, 128 * i : 128 * i + 128])
            ds = p * (dp - jnp.sum(dp * p, axis=0, keepdims=True))
            probs[:, lane(i)] = p.astype(BF16)
            dscores[:, lane(i)] = (ds * scale).astype(BF16)
        dqkv[mine, :] = mm(k, dscores[...]).astype(BF16)
        dqkv[pl.ds(width + f0, size), :] = mm(q, dscores[...], 1, 1).astype(BF16)
        dqkv[pl.ds(2 * width + f0, size), :] = mm(do, probs[...], 1, 1).astype(BF16)
    loop(heads, attend_back, 3)
    for copy in again:
        copy.wait()
    for i in range(3 * width // CHUNK):
        at = pl.ds(i * CHUNK, CHUNK)
        leave(mm(n1[...], dqkv[at, :], 1, 1), gin_ref.at[:, at])
    tmp[...] = mm(wi[:, :c_out], dqkv[...])
    ln_backward(0, xh1, True)
    leave(mm(seen_t[...], low[...], 1, 1), gembed_ref)
    for copy in open_copies:
        copy.wait()


def encoder_backward(gp, vec, seg, wi, wd, saved, patch, heads):
    rows = gp.shape[1]
    width, total = wi.shape
    hidden = wd.shape[0]
    any_, vmem = pl.BlockSpec(memory_space=pl.ANY), pl.BlockSpec(memory_space=pltpu.VMEM)
    f = lambda *s: pltpu.VMEM(s, F32)
    b = lambda *s: pltpu.VMEM(s, BF16)
    shape = lambda *s: jax.ShapeDtypeStruct(s, F32)
    return pl.pallas_call(
        functools.partial(encoder_backward_kernel, heads),
        out_shape=(shape(width, total), shape(hidden, width), shape(patch, width), shape(6, width, 128)),
        in_specs=[vmem] * 3 + [any_] * (2 + len(saved)),
        out_specs=(any_,) * 3 + (vmem,),
        scratch_shapes=[
            b(*wi.shape), b(*wd.shape), f(width, rows), f(width, rows), b(width, rows), b(3 * width, rows), b(rows, rows), b(rows, rows),
            f(2, CHUNK, CHUNK), b(16, rows), b(16, rows), b(patch, rows), f(width, rows), b(width, rows), b(3 * width, rows), b(width, rows),
            f(width, rows), b(width, rows), b(hidden, rows), f(hidden, rows), f(24, rows),
            pltpu.SemaphoreType.DMA((18,)), pltpu.SemaphoreType.DMA((2,)),
        ],
        compiler_params=pltpu.CompilerParams(vmem_limit_bytes=63 * 2**20),
        name="encode_back",
    )(gp, vec, seg, wi, wd, *saved)


def place():
    clip, band = lax.axis_index("clip"), lax.axis_index("band")
    return clip // 2, clip % 2, band // 2, band % 2


def device(z, x, y, c):
    return (z * 2 + x, y * 2 + c)


def greet(z, x, y, c):
    barrier = pltpu.get_barrier_semaphore()
    others = [device(z, x, y, 1 - c), device(z, 1 - x, y, c), device(z, x, 1 - y, c)]
    others += [device((z + k) % 4, x, y, c) for k in (1, 2, 3)]
    for other in others:
        pl.semaphore_signal(barrier, inc=1, device_id=other, device_id_type=pl.DeviceIdType.MESH)
    pl.semaphore_wait(barrier, len(others))


def remote(src, dst, send, recv, to):
    return pltpu.make_async_remote_copy(
        src_ref=src, dst_ref=dst, send_sem=send, recv_sem=recv, device_id=to, device_id_type=pl.DeviceIdType.MESH
    )


def reduce_kernel(widths, n, *refs):
    grads, small, before = refs[:n], refs[n], refs[n + 1]
    outs, small_out, squares = refs[n + 2 : 2 * n + 2], refs[2 * n + 2], refs[2 * n + 3]
    rest = refs[2 * n + 4 :]
    sums, r0 = rest[:n], rest[n : 2 * n]
    coded = {1 + i: rest[(2 + i) * n : (3 + i) * n] for i in range(5)}
    came = {1 + i: rest[(7 + i) * n : (8 + i) * n] for i in range(5)}
    step_out = {1 + i: rest[(12 + i) * n : (13 + i) * n] for i in range(5)}
    step_in = {1 + i: rest[(17 + i) * n : (18 + i) * n] for i in range(5)}
    s_buf, s_sum, q_buf, q_sum, send, recv, near, t_send, t_recv, s_send, s_recv = rest[22 * n :]
    z, x, y, c = place()
    greet(z, x, y, c)

    def at_z(k):
        return (z + k) % 4

    def columns(t, core):
        half = sums[t].shape[4]
        return pl.ds(pl.multiple_of(core * half, 128), half)

    def local(t, k):
        zk = at_z(k)
        return pltpu.make_async_copy(grads[t].at[zk, :, :, :, columns(t, c)], sums[t].at[zk], near.at[t, k])

    def target(stage, k):
        return {
            1: lambda: device(z, 1 - x, y, c),
            2: lambda: device(z, x, 1 - y, c),
            3: lambda: device(z, x, 1 - y, c),
            4: lambda: device(z, 1 - x, y, c),
            5: lambda: device(at_z(k), x, y, c),
        }[stage]()

    def copy(stage, t, k):
        if stage == 0:
            src, dst, to = grads[t].at[at_z(k), :, :, :, columns(t, 1 - c)], r0[t].at[at_z(k)], device(z, x, y, 1 - c)
        elif stage == 6:
            src, dst, to = sums[t].at[z, x, y], outs[t].at[y, :, columns(t, c)], device(z, x, 1 - y, c)
        elif stage == 7:
            src = outs[t].at[:, :, columns(t, c)]
            dst, to = src, device(z, x, y, 1 - c)
        else:
            src, dst, to = coded[stage][t].at[k], came[stage][t].at[k], target(stage, k)
        return remote(src, dst, send.at[t, stage, k], recv.at[t, stage, k], to)

    def steps(stage, t, k):
        src, dst = step_out[stage][t].at[k], step_in[stage][t].at[k]
        return remote(src, dst, t_send.at[t, stage, k], t_recv.at[t, stage, k], target(stage, k))

    def keep(t):
        return pltpu.make_async_copy(sums[t].at[z, x, y], outs[t].at[y, :, columns(t, c)], near.at[t, 4])

    def each(lo, hi, body):
        def one(k, carry):
            body(k)
            return carry
        lax.fori_loop(lo, hi, one, 0)

    def slab(i, height):
        return pl.ds(pl.multiple_of(i * height, height), height)

    def part(stage, t):
        w = widths[t]
        return slice(0, w) if stage in (1, 3) else slice(w, None) if stage in (2, 4) else slice(None)

    def encode(stage, t, k, parts, read):
        rows = sums[t].shape[3]
        zk, width = at_z(k), coded[stage][t].shape[-1]
        block = lambda p: coded[stage][t].at[(k, p) if parts > 1 else k]
        per = rows // 8
        def peak(i, most):
            return jnp.maximum(most, jnp.abs(read(zk, i // per, slab(i % per, 8))))
        most = lax.fori_loop(0, parts * per, peak, jnp.zeros((8, width), F32))
        most = jnp.maximum(jnp.max(most, axis=0, keepdims=True), 1e-30)
        step_out[stage][t][k] = most * (1.0 / 32767.0)
        steps(stage, t, k).start()
        scale = 32767.0 / most
        half = rows // 16
        def one(i):
            values = jnp.round(read(zk, i // half, slab(i % half, 16)) * scale).astype(jnp.int32).astype(jnp.int16)
            block(i // half)[slab(i % half, 16)] = values
        each(0, parts * half, one)
        copy(stage, t, k).start()

    def landed(stage, t, k):
        steps(stage, t, k).wait_recv()
        copy(stage, t, k).wait_recv()

    def decoded(stage, t, k, p, rows, parts):
        values = came[stage][t][(k, p, rows) if parts > 1 else (k, rows)]
        return values.astype(jnp.int32).astype(F32) * step_in[stage][t][k]

    order = (2, 1, 3, 0)
    for t in range(n):
        for k in order:
            copy(0, t, k).start()
            local(t, k).start()

    def hop(total, buffer, first, stage, to):
        return remote(total, buffer.at[stage], s_send.at[first + stage], s_recv.at[first + stage], to)

    def advance(total, buffer, first, stage):
        neighbours = (device(z, x, y, 1 - c), device(z, 1 - x, y, c), device(z, x, 1 - y, c))
        if stage:
            hop(total, buffer, first, stage - 1, neighbours[stage - 1]).wait()
            total[...] += buffer[stage - 1]
        if stage < 3:
            hop(total, buffer, first, stage, neighbours[stage]).start()
        else:
            for k in (1, 2, 3):
                last_hop(total, buffer, first, k).start()
            buffer[3 + z] = total[...]

    def last_hop(total, buffer, first, k):
        return remote(total, buffer.at[3 + z], s_send.at[first + 2 + k], s_recv.at[first + 2 + k], device(at_z(k), x, y, c))

    def finish_sum(total, buffer, first, out):
        for k in (1, 2, 3):
            last_hop(total, buffer, first, k).wait()
        out[...] = (buffer[3] + buffer[4]) + (buffer[5] + buffer[6])

    s_sum[...] = small[...]

    def first_sum(t, k):
        zk = at_z(k)
        copy(0, t, k).wait_recv()
        local(t, k).wait()
        per = sums[t].shape[3] // 16
        def one(i):
            p, r = i // per, slab(i % per, 16)
            sums[t][zk, p // 2, p % 2, r] += r0[t][zk, p // 2, p % 2, r]
        each(0, 4 * per, one)
        encode(1, t, k, 2, lambda zk, p, r: sums[t][zk, 1 - x, p, r, part(1, t)])
        encode(2, t, k, 2, lambda zk, p, r: sums[t][zk, p, 1 - y, r, part(2, t)])

    def second_sum(t, k):
        zk = at_z(k)
        per = sums[t].shape[3] // 16
        landed(1, t, k)
        def one(i):
            p, r = i // per, slab(i % per, 16)
            sums[t][zk, x, p, r, part(1, t)] += decoded(1, t, k, p, r, 2)
        each(0, 2 * per, one)
        encode(3, t, k, 1, lambda zk, p, r: sums[t][zk, x, 1 - y, r, part(3, t)])
        landed(2, t, k)
        def two(i):
            p, r = i // per, slab(i % per, 16)
            sums[t][zk, p, y, r, part(2, t)] += decoded(2, t, k, p, r, 2)
        each(0, 2 * per, two)
        encode(4, t, k, 1, lambda zk, p, r: sums[t][zk, 1 - x, y, r, part(4, t)])

    def third_sum(t, k):
        zk = at_z(k)
        landed(3, t, k)
        landed(4, t, k)
        def one(i):
            r = slab(i, 16)
            sums[t][zk, x, y, r, part(3, t)] += decoded(3, t, k, 0, r, 1)
            sums[t][zk, x, y, r, part(4, t)] += decoded(4, t, k, 0, r, 1)
        each(0, sums[t].shape[3] // 16, one)
        if k:
            encode(5, t, k, 1, lambda zk, p, r: sums[t][zk, x, y, r])

    def last_sum(t, total):
        for k in (1, 2, 3):
            landed(5, t, k)
        half = sums[t].shape[4]
        def one(i, acc):
            r = slab(i, 16)
            value = sums[t][z, x, y, r]
            for k in (1, 2, 3):
                value = value + decoded(5, t, k, 0, r, 1)
            sums[t][z, x, y, r] = value
            value = value * value
            value = value[:8] + value[8:]
            for j in range(half // 128):
                acc = acc + value[:, 128 * j : 128 * j + 128]
            return acc
        total = lax.fori_loop(0, sums[t].shape[3] // 16, one, total)
        copy(6, t, 0).start()
        keep(t).start()
        return total

    def share(t):
        copy(6, t, 0).wait_recv()
        keep(t).wait()
        copy(7, t, 0).start()

    blocks = [(t, k) for t in range(n) for k in order]
    total = before[...]
    for i in range(len(blocks) + 2):
        if i < len(blocks):
            first_sum(*blocks[i])
        if 0 <= i - 1 < len(blocks):
            second_sum(*blocks[i - 1])
        if 0 <= i - 2:
            third_sum(*blocks[i - 2])
        if i < 4:
            advance(s_sum, s_buf, 0, i)
        for t in range(n - 1):
            if i == 4 * t + 7:
                total = last_sum(t, total)
            if i == 4 * t + 9:
                share(t)
    total = last_sum(n - 1, total)
    finish_sum(s_sum, s_buf, 0, small_out)
    late = [t for t in range(n) if t == n - 1 or 4 * t + 9 >= len(blocks) + 2]
    for t in late[:-1]:
        share(t)
    q_sum[...] = total
    if q_buf.shape[0] > 1:
        for stage in range(4):
            advance(q_sum, q_buf, 6, stage)
        finish_sum(q_sum, q_buf, 6, squares)
    else:
        squares[...] = total
    share(late[-1])

    def finish(k):
        for t in range(n):
            copy(0, t, k).wait_send()
            for stage in range(1, 5):
                copy(stage, t, k).wait_send()
                steps(stage, t, k).wait_send()
    each(0, 4, finish)
    def finish_z(k):
        for t in range(n):
            copy(5, t, k).wait_send()
            steps(5, t, k).wait_send()
    each(1, 4, finish_z)
    for t in range(n):
        copy(6, t, 0).wait_send()
        copy(7, t, 0).wait()


def reduce_grads(grads, small, before, last, ident):
    n = len(grads)
    views, widths = [], []
    scratch = [[] for _ in range(22)]
    f = lambda *s: pltpu.VMEM(s, F32)
    q = lambda *s: pltpu.VMEM(s, jnp.int16)
    for grad in grads:
        rows, cols = grad.shape
        r2, half = rows // 16, cols // 2
        w = (half // 128 * 7 + 5) // 10 * 128
        views.append(grad.reshape(4, 2, 2, r2, cols))
        widths.append(w)
        blocks = [(4, 2, r2, w), (4, 2, r2, half - w), (4, r2, w), (4, r2, half - w), (4, r2, half)]
        for i, s in enumerate([f(4, 2, 2, r2, half)] * 2 + [q(*b) for b in blocks * 2] + [f(4, 1, b[-1]) for b in blocks * 2]):
            scratch[i].append(s)
    anywhere, vmem = pl.BlockSpec(memory_space=pl.ANY), pl.BlockSpec(memory_space=pltpu.VMEM)
    dma = pltpu.SemaphoreType.DMA
    square = jax.ShapeDtypeStruct((8, 128), F32)
    out = pl.pallas_call(
        functools.partial(reduce_kernel, tuple(widths), n),
        out_shape=tuple(jax.ShapeDtypeStruct((2, v.shape[3], v.shape[4]), F32) for v in views)
        + (jax.ShapeDtypeStruct(small.shape, F32), square),
        in_specs=[anywhere] * n + [vmem] * 2,
        out_specs=(anywhere,) * n + (vmem,) * 2,
        scratch_shapes=sum(scratch, []) + [
            f(7, *small.shape), f(*small.shape), f(7 if last else 1, 8, 128), f(8, 128),
            dma((n, 8, 4)), dma((n, 8, 4)), dma((n, 5)), dma((n, 6, 4)), dma((n, 6, 4)), dma((12,)), dma((12,)),
        ],
        compiler_params=pltpu.CompilerParams(
            collective_id=ident, has_side_effects=True, vmem_limit_bytes=60 * 2**20
        ),
        name="reduce",
    )(*views, small, before)
    return [o.reshape(-1, o.shape[2]) for o in out[:n]], out[n], out[n + 1]


def gather_kernel(chunks, n, *refs):
    shards, vector, results, vectors = refs[:n], refs[n], refs[n + 1 : 2 * n + 1], refs[2 * n + 1]
    outs = refs[2 * n + 2 : 3 * n + 2]
    send, recv, near, v_send, v_recv = refs[3 * n + 2 :]
    z, x, y, c = place()
    greet(z, x, y, c)

    def at_z(k):
        return (z + k) % 4

    def own(t):
        return pltpu.make_async_copy(shards[t], outs[t].at[z, x], near.at[t])

    def copy(stage, i, k):
        t, r0, nr, c0, both, split = chunks[i]
        half = shards[t].shape[2] // 2
        columns = lambda lo, size: pl.ds(pl.multiple_of(c * half + lo, 128), size)
        wide, narrow, whole = columns(c0, both), columns(c0 + both, split), columns(c0, both + split)
        rows = pl.ds(r0, nr)
        mine = isinstance(k, int) and k == 0
        o, src_z = outs[t], (z + 4 - k) % 4
        if stage == 0:
            src, dst, to = shards[t].at[:, rows, wide], o.at[z, x, :, rows, wide], device(at_z(k), x, y, c)
        elif stage == 1:
            src, dst, to = shards[t].at[y, rows, narrow], o.at[z, x, y, rows, narrow], device(at_z(k), x, y, c)
        elif stage == 2:
            dst, to = o.at[src_z, x, :, rows, wide], device(z, 1 - x, y, c)
            src = shards[t].at[:, rows, wide] if mine else dst
        elif stage == 3:
            dst, to = o.at[src_z, x, y, rows, narrow], device(z, 1 - x, y, c)
            src = shards[t].at[y, rows, narrow] if mine else dst
        elif stage == 4:
            src = o.at[src_z, 1 - x, y, rows, narrow] if mine else o.at[src_z, :, y, rows, narrow]
            dst, to = src, device(z, x, 1 - y, c)
        else:
            src = o.at[src_z, 1 - x, :, rows, whole] if mine else o.at[src_z, :, :, rows, whole]
            dst, to = src, device(z, x, y, 1 - c)
        return remote(src, dst, send.at[i, stage, k], recv.at[i, stage, k], to)

    def leave(t):
        return pltpu.make_async_copy(outs[t], results[t], near.at[n + t])

    def vector_copy(stage, k):
        src_z = (z + 4 - k) % 4
        if stage == 0:
            return remote(vector, vectors.at[z, x], v_send.at[k], v_recv.at[k], device(at_z(k), x, y, c))
        src = vector if k == 0 else vectors.at[src_z, x]
        return remote(src, vectors.at[src_z, x], v_send.at[4 + k], v_recv.at[4 + k], device(z, 1 - x, y, c))

    def each(lo, hi, body):
        def step(k, carry):
            body(k)
            return carry
        lax.fori_loop(lo, hi, step, 0)

    def along_z(i):
        def one(k):
            copy(0, i, k).start()
            copy(1, i, k).start()
        each(1, 4, one)
        copy(2, i, 0).start()
        copy(3, i, 0).start()

    def along_x(i):
        def one(k):
            copy(0, i, k).wait_recv()
            copy(2, i, k).start()
            copy(1, i, k).wait_recv()
            copy(3, i, k).start()
        each(1, 4, one)

    def along_y(i):
        copy(3, i, 0).wait_recv()
        copy(4, i, 0).start()
        def one(k):
            copy(3, i, k).wait_recv()
            copy(4, i, k).start()
        each(1, 4, one)

    def across(i):
        def one(k):
            copy(2, i, k).wait_recv()
            copy(4, i, k).wait_recv()
            copy(5, i, k).start()
        one(0)
        each(1, 4, one)

    vectors[z, x] = vector[...]
    for k in (1, 2, 3):
        vector_copy(0, k).start()
    vector_copy(1, 0).start()
    along_z(0)
    for t in range(n):
        own(t).start()
    count = len(chunks)
    for i in range(count + 3):
        if i + 1 < count:
            along_z(i + 1)
        if i < count:
            along_x(i)
        if i == 0:
            for t in range(n):
                own(t).wait()
        if i == 1:
            for k in (1, 2, 3):
                vector_copy(0, k).wait_recv()
                vector_copy(1, k).start()
        if 0 <= i - 1 < count:
            along_y(i - 1)
        if 0 <= i - 2 < count:
            across(i - 2)
        if 0 <= i - 3:
            copy(5, i - 3, 0).wait_recv()
            each(1, 4, lambda k, i=i: copy(5, i - 3, k).wait_recv())
            if i - 2 == count or chunks[i - 2][0] != chunks[i - 3][0]:
                leave(chunks[i - 3][0]).start()

    for i in range(count):
        for stage in (2, 3, 4, 5):
            copy(stage, i, 0).wait_send()
        def finish(k, i=i):
            for stage in range(6):
                copy(stage, i, k).wait_send()
        each(1, 4, finish)
    for t in range(n):
        leave(t).wait()
    vector_copy(1, 0).wait()
    for k in (1, 2, 3):
        vector_copy(0, k).wait_send()
        vector_copy(1, k).wait()


def chunks_of(shards, largest):
    chunks = []
    for t, shard in enumerate(shards):
        rows, tiles = shard.shape[0] // 2, shard.shape[1] // 256
        size = rows * tiles * 128
        parts = -(-size // largest)
        by_rows = rows // parts % 16 == 0 and tiles < 2 * parts
        if by_rows:
            for p in range(parts):
                both = max(1, tiles // 3) if tiles > 1 else 0
                chunks.append((t, rows // parts * p, rows // parts, 0, both * 128, (tiles - both) * 128))
        else:
            cuts = [tiles * p // parts for p in range(parts + 1)]
            for lo, hi in zip(cuts, cuts[1:]):
                both = max(1, (hi - lo) // 3)
                chunks.append((t, 0, rows, lo * 128, both * 128, (hi - lo - both) * 128))
    return tuple(chunks)


def gather_weights(shards, vector, ident):
    n = len(shards)
    views = [shard.reshape(2, shard.shape[0] // 2, shard.shape[1]) for shard in shards]
    chunks = chunks_of(shards, 75000)
    anywhere, vmem = pl.BlockSpec(memory_space=pl.ANY), pl.BlockSpec(memory_space=pltpu.VMEM)
    dma = pltpu.SemaphoreType.DMA
    out = pl.pallas_call(
        functools.partial(gather_kernel, chunks, n),
        out_shape=tuple(jax.ShapeDtypeStruct((4, 2) + v.shape, BF16) for v in views)
        + (jax.ShapeDtypeStruct((4, 2, 8, 128), F32),),
        in_specs=[vmem] * n + [vmem],
        out_specs=(anywhere,) * n + (vmem,),
        scratch_shapes=[pltpu.VMEM((4, 2) + v.shape, BF16) for v in views]
        + [dma((len(chunks), 6, 4)), dma((len(chunks), 6, 4)), dma((2 * n,)), dma((8,)), dma((8,))],
        compiler_params=pltpu.CompilerParams(collective_id=ident, has_side_effects=True, vmem_limit_bytes=60 * 2**20),
        name="gather",
    )(*views, vector.reshape(8, 128))
    return [o.reshape(-1, o.shape[4]) for o in out[:n]], out[n].reshape(-1)


def clip_of(column, clip_lengths, clip_shifts):
    columns = clip_lengths // 8
    ends = jnp.cumsum(columns)
    clip_id = jnp.sum((column[:, None] >= ends[None, :]).astype(jnp.int32), axis=1)
    onehot = (clip_id[:, None] == jnp.arange(clip_lengths.shape[0], dtype=jnp.int32)[None, :]).astype(jnp.int32)

    def select(values):
        return jnp.sum(onehot * values[None, :], axis=1)

    return clip_id, select(ends - columns), select(columns), select(clip_shifts[:, 0]), select(clip_shifts[:, 1])


def half_table(position, width):
    quarter = width // 4
    omega = 1.0 / 10000.0 ** (jnp.arange(quarter, dtype=jnp.float32) / quarter)
    angle = omega[:, None] * position.astype(jnp.float32)[None, :]
    return jnp.concatenate([jnp.sin(angle), jnp.cos(angle)])


def adam_update(weight, first, second, grad, decay):
    first = BETA_ONE * first + (1.0 - BETA_ONE) * grad
    second = BETA_TWO * second + (1.0 - BETA_TWO) * grad * grad
    first_hat = first / (1.0 - BETA_ONE**STEP)
    second_hat = second / (1.0 - BETA_TWO**STEP)
    weight = weight - LEARN_RATE * (first_hat / (jnp.sqrt(second_hat) + EPSILON) + decay * weight)
    return (weight, first, second)


def shards(
    pixels,
    lengths,
    shifts,
    visible,
    patch_embed,
    encoder_in,
    encoder_down,
    decoder_in,
    decoder_down,
    norm_vectors,
    first_embed,
    first_encoder_in,
    first_encoder_down,
    first_decoder_in,
    first_decoder_down,
    first_vectors,
    second_embed,
    second_encoder_in,
    second_encoder_down,
    second_decoder_in,
    second_decoder_down,
    second_vectors,
):
    masters = (patch_embed, encoder_in, encoder_down, decoder_in, decoder_down, norm_vectors)
    firsts = (
        first_embed,
        first_encoder_in,
        first_encoder_down,
        first_decoder_in,
        first_decoder_down,
        first_vectors,
    )
    seconds = (
        second_embed,
        second_encoder_in,
        second_encoder_down,
        second_decoder_in,
        second_decoder_down,
        second_vectors,
    )
    direct = lax.axis_size("clip") == 8 and lax.axis_size("band") == 4
    low_shards = [master.astype(jnp.bfloat16) for master in masters]
    if direct:
        (w_embed, w_enc, w_enc_down, w_dec, w_dec_down), vectors = gather_weights(
            low_shards[:5], lax.reduce_precision(norm_vectors, exponent_bits=8, mantissa_bits=7), 0
        )
    else:
        w_embed, w_enc, w_enc_down, w_dec, w_dec_down, gathered_vectors = (
            lax.all_gather(shard, "clip", axis=0, tiled=True) for shard in low_shards
        )
        vectors = gathered_vectors.astype(jnp.float32)
    enc_width, dec_width = (w_enc.shape[0], w_dec.shape[0])
    patch_dev, n_visible = pixels.shape[0], visible.shape[0]
    padded = -(-n_visible // 128) * 128
    enc_gains = vectors[: 6 * enc_width].reshape(6, enc_width, 1)
    dec_gains = vectors[6 * enc_width :].reshape(7, dec_width, 1)
    enc_gains = jnp.broadcast_to(enc_gains, (6, enc_width, 128))
    dec_gains = jnp.broadcast_to(dec_gains, (7, dec_width, 128))
    turned = jnp.arange(patch_dev // 8, dtype=jnp.int32)
    _, start, size, shift_time, shift_band = clip_of(turned, lengths[0], shifts[0])
    turned_time = (turned - start - shift_time) % size
    decoder_pixels = pixels.reshape(patch_dev // 8, 8, -1)[start + turned_time].reshape(pixels.shape)
    time_table = half_table(turned_time, dec_width).T
    band_table = jnp.tile(half_table(jnp.arange(8, dtype=jnp.int32), dec_width), (1, 16))
    spots = jnp.pad(visible, (0, padded - n_visible))
    real = jnp.arange(padded, dtype=jnp.int32) < n_visible
    seen = pixels[spots]
    column, band = spots // 8, spots % 8
    segment, seen_start, seen_size, seen_shift, _ = clip_of(column, lengths[0], shifts[0])
    segment = jnp.where(real, segment, 15).astype(jnp.int32)
    segment = jnp.broadcast_to(segment[None, :], (8, padded))
    seen_time = column - seen_start
    decoder_row = jnp.where(real, 8 * (seen_start + (seen_time + seen_shift) % seen_size) + band, -1)
    decoder_row = jnp.broadcast_to(decoder_row[:, None], (padded, 128)).astype(jnp.int32)

    def positions(width):
        return jnp.concatenate([half_table(seen_time, width), half_table(band, width)])

    grid_seen, *saved = encoder_forward(
        seen,
        positions(enc_width),
        positions(dec_width),
        segment,
        enc_gains,
        w_embed,
        w_enc,
        w_enc_down,
        HEADS_ENC,
    )
    masked_count = 13.0 * (patch_dev // 16) * lax.axis_size("clip") * lax.axis_size("band")
    g_dec_in, g_dec_down, g_dec_vectors, grad_grid, loss = decoder_step(
        shift_band[::64],
        decoder_row,
        grid_seen,
        decoder_pixels,
        time_table,
        band_table,
        dec_gains,
        w_dec,
        w_dec_down,
        2.0 / (pixels.shape[1] * masked_count),
        HEADS_DEC,
    )
    local_loss = jnp.sum(loss[0])
    g_enc_in, g_enc_down, g_embed, g_enc_vectors = encoder_backward(
        grad_grid, enc_gains, segment, w_enc, w_enc_down, saved, pixels.shape[1], HEADS_ENC
    )
    g_vectors = jnp.concatenate(
        [jnp.sum(g_enc_vectors, axis=2).reshape(-1), jnp.sum(g_dec_vectors, axis=2).reshape(-1)]
    )
    if direct:
        small = jnp.concatenate([g_vectors.reshape(-1, 128), jnp.full((8, 128), local_loss)])
        nothing = jnp.zeros((8, 128), jnp.float32)
        dec_shards, _, squares = reduce_grads([g_dec_in, g_dec_down], nothing, nothing, False, 1)
        enc_shards, summed, squares = reduce_grads(
            [g_enc_in, g_enc_down, g_embed], small, squares, True, 2
        )
        rows = norm_vectors.shape[0]
        vector_sums = summed[:-8].reshape(-1)
        own = lax.dynamic_slice(vector_sums, (lax.axis_index("clip") * rows,), (rows,))
        reduced = (enc_shards[2], enc_shards[0], enc_shards[1], *dec_shards, own)
        loss_sum = summed[-1, 0]
        norm_squared = jnp.sum(squares) + jnp.sum(vector_sums * vector_sums)
    else:
        reduced = lax.psum(
            tuple(
                lax.psum_scatter(grad, "clip", scatter_dimension=0, tiled=True)
                for grad in (g_embed, g_enc_in, g_enc_down, g_dec_in, g_dec_down, g_vectors)
            ),
            "band",
        )
        loss_sum = lax.psum(local_loss, ("clip", "band"))
        norm_squared = lax.psum(sum(jnp.sum(grad * grad) for grad in reduced), "clip")
    grad_norm = jnp.sqrt(norm_squared)
    factor = jnp.minimum(1.0, CLIP_LIMIT / (grad_norm + 1e-06))
    results = []
    for index in range(6):
        decay = DECAY_RATE if index < 5 else 0.0
        results.append(
            adam_update(
                masters[index], firsts[index], seconds[index], reduced[index] * factor, decay
            )
        )
    return (
        loss_sum,
        grad_norm,
        results[0][0],
        results[1][0],
        results[2][0],
        results[3][0],
        results[4][0],
        results[5][0],
        results[0][1],
        results[1][1],
        results[2][1],
        results[3][1],
        results[4][1],
        results[5][1],
        results[0][2],
        results[1][2],
        results[2][2],
        results[3][2],
        results[4][2],
        results[5][2],
    )


def solution(mesh):
    in_specs = (
        P(("clip", "band"), None),
        P(("clip", "band"), None),
        P(("clip", "band"), None, None),
        P(("clip", "band")),
        P("clip", None),
        P("clip", None),
        P("clip", None),
        P("clip", None),
        P("clip", None),
        P("clip"),
        P("clip", None),
        P("clip", None),
        P("clip", None),
        P("clip", None),
        P("clip", None),
        P("clip"),
        P("clip", None),
        P("clip", None),
        P("clip", None),
        P("clip", None),
        P("clip", None),
        P("clip"),
    )
    out_specs = (
        P(),
        P(),
        P("clip", None),
        P("clip", None),
        P("clip", None),
        P("clip", None),
        P("clip", None),
        P("clip"),
        P("clip", None),
        P("clip", None),
        P("clip", None),
        P("clip", None),
        P("clip", None),
        P("clip"),
        P("clip", None),
        P("clip", None),
        P("clip", None),
        P("clip", None),
        P("clip", None),
        P("clip"),
    )
    return jax.shard_map(shards, mesh=mesh, in_specs=in_specs, out_specs=out_specs, check_vma=False)
```

```python
import functools

import jax
import jax.numpy as jnp
from jax import lax
from jax.experimental import pallas as pl
from jax.experimental.pallas import tpu as pltpu
from jax.sharding import PartitionSpec as P

HEADS_ENC = 12
HEADS_DEC = 16
STEP = 10


LEARN_RATE = 0.02
BETA_ONE = 0.9
BETA_TWO = 0.95
EPSILON = 1e-08
DECAY_RATE = 0.05
CLIP_LIMIT = 0.001


F32, BF16 = jnp.float32, jnp.bfloat16
GELU_C = 0.7978845608028654


def mm(a, b, ca=1, cb=0):
    return lax.dot_general(a, b, (((ca,), (cb,)), ((), ())), preferred_element_type=F32)


def wide(v, n):
    return jnp.concatenate([v] * (n // 128), axis=1)


def loop(n, body, unroll=1):
    def step(i, carry):
        for k in range(unroll):
            body(i * unroll + k)
        return carry
    lax.fori_loop(0, n // unroll, step, 0)


def fold(v):
    total = v[:, :128]
    for i in range(1, v.shape[1] // 128):
        total = total + v[:, 128 * i : 128 * (i + 1)]
    return total


def decoder_kernel(
    coef, heads, shift_ref, rvis_ref, gvt_ref, pix_ref, et_ref, ef_ref, vec_ref, w_ref, wd_ref,
    gin_ref, gdown_ref, gvec_ref, gp_ref, loss_ref,
    wt_ref, wdt_ref, res, xh1, xh2, xh3, tmp, n1, n2, fin, rs, qkv, att, act, dgel, probs, dqkv, dup, low, oh, mrow, hb, hm, wm,
):
    width = w_ref.shape[0]
    hidden = wd_ref.shape[0]
    rows = res.shape[1]
    size = width // heads
    per = 128 // size
    scale = size ** -0.5
    groups = width // 128
    c_out, c_up, c_head = 3 * width, 4 * width, 4 * width + hidden
    pixels = w_ref.shape[1] - c_head
    cols = rows // 8
    nblk = pix_ref.shape[0] // rows
    chunk = 512

    def turn_in(i):
        at = pl.ds(pl.multiple_of(i * 256, 256), 256)
        wt_ref[at, :] = w_ref[:, at].T
    loop(w_ref.shape[1] // 256, turn_in)

    def turn_down(i):
        at = pl.ds(pl.multiple_of(i * 256, 256), 256)
        wdt_ref[:, at] = wd_ref[at, :].T
    loop(hidden // 256, turn_down)
    gin_ref[...] = jnp.zeros_like(gin_ref)
    gdown_ref[...] = jnp.zeros_like(gdown_ref)
    gvec_ref[...] = jnp.zeros_like(gvec_ref)
    gp_ref[...] = jnp.zeros_like(gp_ref)
    loss_ref[...] = jnp.zeros_like(loss_ref)
    f_id = lax.broadcasted_iota(jnp.int32, (128, 128 * per), 0)
    q_id = lax.broadcasted_iota(jnp.int32, (128, 128 * per), 1)
    hm[...] = jnp.where(f_id // size == q_id // 128, 1.0, 0.0).astype(BF16)
    wm[...] = jnp.where(f_id // 32 == (q_id % 128) // 32, 1.0, 0.0).astype(BF16)

    def lane(i):
        return pl.ds(pl.multiple_of(i * 128, 128), 128)

    def ln_forward(k, xh, out):
        def body(i):
            x = res[:, lane(i)]
            centre = x - jnp.mean(x, axis=0, keepdims=True)
            r = lax.rsqrt(jnp.mean(centre * centre, axis=0, keepdims=True) + 1e-06)
            xhat = centre * r
            xh[:, lane(i)] = xhat
            rs[8 * k : 8 * k + 8, lane(i)] = jnp.broadcast_to(r, (8, 128))
            out[:, lane(i)] = (xhat * vec_ref[2 * k] + vec_ref[2 * k + 1]).astype(BF16)
        loop(rows // 128, body, 4)

    def ln_backward(k, xh, add):
        def body(i):
            d = tmp[:, lane(i)]
            xhat = xh[:, lane(i)]
            gvec_ref[2 * k] += d * xhat
            gvec_ref[2 * k + 1] += d
            dx = d * vec_ref[2 * k]
            m1 = jnp.mean(dx, axis=0, keepdims=True)
            m2 = jnp.mean(dx * xhat, axis=0, keepdims=True)
            g = rs[8 * k : 8 * k + 1, lane(i)] * (dx - m1 - xhat * m2)
            if add:
                g = g + res[:, lane(i)]
            res[:, lane(i)] = g
            low[:, lane(i)] = g.astype(BF16)
        loop(rows // 128, body, 4)

    def block(j):
        first = pl.multiple_of(j * rows, rows)
        turn = shift_ref[j]
        spot = lax.broadcasted_iota(jnp.int32, (rvis_ref.shape[0], rows), 1) + first
        hot = jnp.where(wide(rvis_ref[...], rows) == spot, 1.0, 0.0)
        oh[...] = hot.astype(BF16)
        masked = 1.0 - jnp.sum(hot, axis=0, keepdims=True)
        mrow[...] = jnp.broadcast_to(masked, (8, rows))
        et = et_ref[pl.ds(pl.multiple_of(j * cols, cols), cols), :]
        e_hi = et.astype(BF16)
        rest = et - e_hi.astype(F32)
        e_mid = rest.astype(BF16)
        e_lo = (rest - e_mid.astype(F32)).astype(BF16)
        spread = jnp.where(
            lax.broadcasted_iota(jnp.int32, (cols, rows), 1) // 8 == lax.broadcasted_iota(jnp.int32, (cols, rows), 0), 1.0, 0.0
        ).astype(BF16)
        e_t = mm(e_hi, spread, 0, 0) + (mm(e_mid, spread, 0, 0) + mm(e_lo, spread, 0, 0))
        half = width // 2
        keep = masked > 0.5
        placed = mm(gvt_ref[...], oh[...])
        top = (wide(vec_ref[6, :half], rows) + e_t).astype(BF16).astype(F32)
        res[:half] = jnp.where(keep, top, placed[:half])
        bottom = wide((vec_ref[6, half:] + ef_ref[...]).astype(BF16).astype(F32), rows)
        res[half:] = jnp.where(keep, bottom, placed[half:])
        k_half = (lax.broadcasted_iota(jnp.int32, (32, 128 * per), 0) % 8 + turn) % 8 // 4
        q_half = (lax.broadcasted_iota(jnp.int32, (32, 128 * per), 1) % 8 + turn) % 8 // 4
        hb[...] = jnp.where(k_half == q_half, 0.0, -1e30)

        ln_forward(0, xh1, n1)

        def qkv_part(i):
            part = pl.ds(pl.multiple_of(i * chunk, chunk), chunk)
            qkv[part, :] = mm(wt_ref[part, :], n1[...]).astype(BF16)
        loop(3 * width // chunk, qkv_part, 3)

        q_group = (lax.broadcasted_iota(jnp.int32, (32, 128 * per), 1) % 128) // 32

        def compact(s):
            c = s[96:128]
            for i in (2, 1, 0):
                c = jnp.where(q_group == i, s[32 * i : 32 * i + 32], c)
            return c

        def attend(i):
            sb, g = i // groups, i % groups
            at = lane(sb)
            f0 = pl.multiple_of(g * 128, 128)
            q = qkv[pl.ds(f0, 128), at]
            k = qkv[pl.ds(width + f0, 128), at]
            v = qkv[pl.ds(2 * width + f0, 128), at]
            s = jnp.concatenate([mm(k[size * h : size * h + size], q[size * h : size * h + size], 0, 0) for h in range(per)], axis=1)
            c = compact(s) * scale + hb[...]
            e = jnp.exp(c - jnp.max(c, axis=0, keepdims=True))
            p = e * (1.0 / jnp.sum(e, axis=0, keepdims=True))
            probs[i] = p
            p_low = p.astype(BF16)
            p_all = jnp.concatenate([p_low] * 4, axis=0) * wm[...]
            for h in range(per):
                o = mm(v[size * h : size * h + size], p_all[:, 128 * h : 128 * h + 128])
                att[pl.ds(f0 + size * h, size), at] = o.astype(BF16)
        loop(rows // 128 * groups, attend, 16)

        res[...] += mm(wt_ref[c_out : c_out + width], att[...])
        ln_forward(1, xh2, n2)

        def up_part(i):
            part = pl.ds(pl.multiple_of(i * chunk, chunk), chunk)
            u = mm(wt_ref[pl.ds(pl.multiple_of(c_up + i * chunk, chunk), chunk), :], n2[...])
            square = u * u
            hp = 0.5 + 0.5 * jnp.tanh(u * (GELU_C + (GELU_C * 0.044715) * square))
            v = u * hp
            act[part, :] = v.astype(BF16)
            dgel[part, :] = hp + (v - v * hp) * ((2 * GELU_C) + (6 * GELU_C * 0.044715) * square)
        loop(hidden // chunk, up_part, 4)

        res[...] += mm(wdt_ref[...], act[...])
        ln_forward(2, xh3, fin)
        pred = mm(wt_ref[c_head:], fin[...])
        pix = pix_ref[pl.ds(first, rows), :].astype(F32).T
        centre = pix - jnp.mean(pix, axis=0, keepdims=True)
        target = (centre * lax.rsqrt(jnp.mean(centre * centre, axis=0, keepdims=True) + 1e-06)).astype(BF16).astype(F32)
        err = pred - target
        loss_ref[...] += fold(mrow[...] * jnp.mean(err * err, axis=0, keepdims=True))
        gpred = (mrow[0:1] * err * coef).astype(BF16)

        gin_ref[:, c_head:] += mm(fin[...], gpred, 1, 1)
        tmp[...] = mm(w_ref[:, c_head:], gpred)
        ln_backward(2, xh3, False)

        def mlp_back(i):
            part = pl.ds(pl.multiple_of(i * chunk, chunk), chunk)
            there = pl.ds(pl.multiple_of(c_up + i * chunk, chunk), chunk)
            d = (mm(wd_ref[part, :], low[...]) * dgel[part, :]).astype(BF16)
            dup[part, :] = d
            gdown_ref[part, :] += mm(act[part, :], low[...], 1, 1)
            gin_ref[:, there] += mm(n2[...], d, 1, 1)
        loop(hidden // chunk, mlp_back, 4)
        tmp[...] = mm(w_ref[:, c_up:c_head], dup[...])
        ln_backward(1, xh2, True)
        gin_ref[:, c_out:c_up] += mm(att[...], low[...], 1, 1)
        fin[...] = mm(w_ref[:, c_out:c_up], low[...]).astype(BF16)

        def attend_back(i):
            sb, g = i // groups, i % groups
            at = lane(sb)
            f0 = pl.multiple_of(g * 128, 128)
            q = qkv[pl.ds(f0, 128), at]
            k = qkv[pl.ds(width + f0, 128), at]
            v = qkv[pl.ds(2 * width + f0, 128), at]
            do = fin[pl.ds(f0, 128), at]
            do_all = wide(do, 128 * per) * hm[...]
            dp = compact(jnp.concatenate([mm(v[size * h : size * h + size], do[size * h : size * h + size], 0, 0) for h in range(per)], axis=1))
            p = probs[i]
            ds = p * (dp - jnp.sum(dp * p, axis=0, keepdims=True))
            p_all = jnp.concatenate([p.astype(BF16)] * 4, axis=0) * wm[...]
            ds_all = jnp.concatenate([(ds * scale).astype(BF16)] * 4, axis=0) * wm[...]
            tall = jnp.concatenate([ds_all[:, 128 * h : 128 * h + 128] for h in range(per)], axis=0)
            dqkv[pl.ds(f0, 128), at] = mm(wide(k, 128 * per) * hm[...], tall).astype(BF16)
            dqkv[pl.ds(width + f0, 128), at] = mm(wide(q, 128 * per) * hm[...], ds_all, 1, 1).astype(BF16)
            dqkv[pl.ds(2 * width + f0, 128), at] = mm(do_all, p_all, 1, 1).astype(BF16)
        loop(rows // 128 * groups, attend_back, 8)

        def qkv_back(i):
            part = pl.ds(pl.multiple_of(i * chunk, chunk), chunk)
            gin_ref[:, part] += mm(n1[...], dqkv[part, :], 1, 1)
        loop(3 * width // chunk, qkv_back, 3)
        tmp[...] = mm(w_ref[:, :c_out], dqkv[...])
        ln_backward(0, xh1, True)
        gvec_ref[6] += fold(low[...].astype(F32) * mrow[0:1])
        gp_ref[...] += mm(low[...], oh[...], 1, 1)

    loop(nblk, block)


def decoder_step(shift, rvis, gvt, pix, et, ef, vec, w, wd, coef, heads):
    width, total = w.shape
    hidden = wd.shape[0]
    rows = 512
    vis = rvis.shape[0]
    per = 128 // (width // heads)
    vmem = pl.BlockSpec(memory_space=pltpu.VMEM)
    f = lambda *s: pltpu.VMEM(s, F32)
    b = lambda *s: pltpu.VMEM(s, BF16)
    return pl.pallas_call(
        functools.partial(decoder_kernel, coef, heads),
        out_shape=(
            jax.ShapeDtypeStruct((width, total), F32),
            jax.ShapeDtypeStruct((hidden, width), F32),
            jax.ShapeDtypeStruct((7, width, 128), F32),
            jax.ShapeDtypeStruct((width, vis), F32),
            jax.ShapeDtypeStruct((8, 128), F32),
        ),
        in_specs=[pl.BlockSpec(memory_space=pltpu.SMEM)] + [vmem] * 8,
        out_specs=(vmem,) * 5,
        scratch_shapes=[
            b(total, width), b(width, hidden), f(width, rows), f(width, rows), f(width, rows), f(width, rows), f(width, rows),
            b(width, rows), b(width, rows), b(width, rows), f(24, rows),
            b(3 * width, rows), b(width, rows), b(hidden, rows), f(hidden, rows),
            f(rows // 128 * (width // 128), 32, 128 * per), b(3 * width, rows), b(hidden, rows), b(width, rows),
            b(vis, rows), f(8, rows), f(32, 128 * per), b(128, 128 * per), b(128, 128 * per),
        ],
        compiler_params=pltpu.CompilerParams(vmem_limit_bytes=63 * 2**20),
        name="decoder",
    )(shift, rvis, gvt, pix, et, ef, vec, w, wd)


CHUNK = 768


def lane(i):
    return pl.ds(i * 128 if isinstance(i, int) else pl.multiple_of(i * 128, 128), 128)


def part(i, base=0):
    return pl.ds(pl.multiple_of(base + i * CHUNK, 128), CHUNK)


def encoder_clips(seg_ref, own, others):
    clip = lax.broadcasted_iota(jnp.int32, own.shape, 0) == seg_ref[0:1]
    own[...] = jnp.where(clip, 1.0, 0.0).astype(BF16)
    others[...] = jnp.where(clip, 0.0, -1e31).astype(BF16)


def encoder_scores(q, k, scale):
    c = mm(k, q)
    e = jnp.exp2((c - jnp.max(c, axis=0, keepdims=True)) * (scale * 1.4426950408889634))
    return e * (1.0 / jnp.sum(e, axis=0, keepdims=True))


def encoder_forward_kernel(
    heads, seen_ref, pos_ref, grid_pos_ref, seg_ref, vec_ref, we_ref, wi_ref, wd_ref,
    grid_ref, seen_t_ref, xh1_ref, n1_ref, qkv_ref, att_ref, xh2_ref, n2_ref, act_ref, dgel_ref, xh3_ref, fin_ref, rs_ref,
    we, wi, wd, res, own, others, seen_t, xh1, n1, qkv, att, xh2, n2, act, dgel, xh3, fin, rs, w_sem, o_sem,
):
    width, hidden = we.shape[1], wd.shape[0]
    rows = res.shape[1]
    size = width // heads
    scale = size ** -0.5
    c_out, c_up, c_proj = 3 * width, 4 * width, 4 * width + hidden
    total = wi.shape[1]
    loads = [pltpu.make_async_copy(we_ref, we, w_sem.at[0])]
    for i, (lo, hi) in enumerate(((0, c_out), (c_out, c_up), (c_up, c_proj), (c_proj, total))):
        at = pl.ds(lo, hi - lo)
        loads.append(pltpu.make_async_copy(wi_ref.at[:, at], wi.at[:, at], w_sem.at[1 + i]))
    loads.insert(4, pltpu.make_async_copy(wd_ref, wd, w_sem.at[5]))
    for load in loads:
        load.start()
    pairs = (
        (seen_t, seen_t_ref), (xh1, xh1_ref), (n1, n1_ref), (qkv, qkv_ref), (att, att_ref), (xh2, xh2_ref),
        (n2, n2_ref), (act, act_ref), (dgel, dgel_ref), (xh3, xh3_ref), (fin, fin_ref), (rs, rs_ref),
    )
    saves = [pltpu.make_async_copy(a, b, o_sem.at[i]) for i, (a, b) in enumerate(pairs)]

    def ln_forward(k, xh, out):
        def body(i):
            x = res[:, lane(i)]
            centre = x - jnp.mean(x, axis=0, keepdims=True)
            r = lax.rsqrt(jnp.mean(centre * centre, axis=0, keepdims=True) + 1e-06)
            xhat = centre * r
            xh[:, lane(i)] = xhat
            rs[8 * k : 8 * k + 8, lane(i)] = jnp.broadcast_to(r, (8, 128))
            out[:, lane(i)] = (xhat * vec_ref[2 * k] + vec_ref[2 * k + 1]).astype(BF16)
        for i in range(rows // 128):
            body(i)

    seen_t[...] = seen_ref[...].T
    saves[0].start()
    encoder_clips(seg_ref, own, others)
    loads[0].wait()
    res[...] = mm(we[...], seen_t[...], 0, 0) + pos_ref[...]
    ln_forward(0, xh1, n1)
    saves[1].start()
    saves[2].start()
    loads[1].wait()

    def qkv_part(i):
        qkv[part(i), :] = mm(wi[:, part(i)], n1[...], 0, 0).astype(BF16)
    loop(3, qkv_part, 3)
    saves[3].start()

    def attend(h):
        f0 = pl.multiple_of(h * size, size)
        k = jnp.concatenate([qkv[pl.ds(width + f0, size), :], others[...]], axis=0).T
        v = qkv[pl.ds(2 * width + f0, size), :]
        for i in range(rows // 128):
            q = jnp.concatenate([qkv[pl.ds(f0, size), lane(i)], own[:, lane(i)]], axis=0)
            p = encoder_scores(q, k, scale)
            att[pl.ds(f0, size), lane(i)] = mm(v, p.astype(BF16)).astype(BF16)
    loop(heads, attend, 4)
    saves[4].start()
    loads[2].wait()
    res[...] += mm(wi[:, c_out:c_up], att[...], 0, 0)
    ln_forward(1, xh2, n2)
    saves[5].start()
    saves[6].start()
    loads[3].wait()

    def up_part(i):
        u = mm(wi[:, part(i, c_up)], n2[...], 0, 0)
        square = u * u
        hp = 0.5 + 0.5 * jnp.tanh(u * (GELU_C + (GELU_C * 0.044715) * square))
        v = u * hp
        act[part(i), :] = v.astype(BF16)
        dgel[part(i), :] = hp + (v - v * hp) * ((2 * GELU_C) + (6 * GELU_C * 0.044715) * square)
    loop(hidden // CHUNK, up_part, 4)
    saves[7].start()
    saves[8].start()
    loads[4].wait()
    res[...] += mm(wd[...], act[...], 0, 0)
    ln_forward(2, xh3, fin)
    for i in (9, 10, 11):
        saves[i].start()
    loads[5].wait()
    grid_ref[...] = (mm(wi[:, c_proj:], fin[...], 0, 0) + grid_pos_ref[...]).astype(BF16)
    for save in saves:
        save.wait()


def encoder_forward(seen, pos, grid_pos, seg, vec, we, wi, wd, heads):
    rows, patch = seen.shape
    width, total = wi.shape
    hidden = wd.shape[0]
    any_, vmem = pl.BlockSpec(memory_space=pl.ANY), pl.BlockSpec(memory_space=pltpu.VMEM)
    saved = (
        ((patch, rows), BF16), ((width, rows), F32), ((width, rows), BF16), ((3 * width, rows), BF16),
        ((width, rows), BF16), ((width, rows), F32), ((width, rows), BF16), ((hidden, rows), BF16), ((hidden, rows), F32),
        ((width, rows), F32), ((width, rows), BF16), ((24, rows), F32),
    )
    return pl.pallas_call(
        functools.partial(encoder_forward_kernel, heads),
        out_shape=(jax.ShapeDtypeStruct((grid_pos.shape[0], rows), BF16),) + tuple(jax.ShapeDtypeStruct(*s) for s in saved),
        in_specs=[vmem] * 5 + [any_] * 3,
        out_specs=(vmem,) + (any_,) * len(saved),
        scratch_shapes=[pltpu.VMEM(we.shape, BF16), pltpu.VMEM(wi.shape, BF16), pltpu.VMEM(wd.shape, BF16), pltpu.VMEM((width, rows), F32)]
        + [pltpu.VMEM((16, rows), BF16)] * 2 + [pltpu.VMEM(*s) for s in saved] + [pltpu.SemaphoreType.DMA((6,)), pltpu.SemaphoreType.DMA((len(saved),))],
        compiler_params=pltpu.CompilerParams(vmem_limit_bytes=62 * 2**20),
        name="encode",
    )(seen, pos, grid_pos, seg, vec, we, wi, wd)


def encoder_backward_kernel(
    heads, gp_ref, vec_ref, seg_ref, wi_ref, wd_ref,
    seen_t_ref, xh1_ref, n1_ref, qkv_ref, att_ref, xh2_ref, n2_ref, act_ref, dgel_ref, xh3_ref, fin_ref, rs_ref,
    gin_ref, gdown_ref, gembed_ref, gvec_ref,
    wi, wd, res, tmp, low, dqkv, probs, dscores, stage, own, others, seen_t, xh1, n1, qkv, att, xh2, n2, act, dgel, rs, i_sem, s_sem,
):
    width, hidden = wi.shape[0], wd.shape[0]
    rows = res.shape[1]
    size = width // heads
    scale = size ** -0.5
    c_out, c_up, c_proj = 3 * width, 4 * width, 4 * width + hidden
    total = wi.shape[1]
    n_proj = total - c_proj

    def load(i, src, dst):
        return pltpu.make_async_copy(src, dst, i_sem.at[i])

    def columns(i, lo, hi):
        at = pl.ds(lo, hi - lo)
        return load(i, wi_ref.at[:, at], wi.at[:, at])

    first = [load(0, fin_ref, n1), columns(1, c_proj, total), load(2, xh3_ref, xh1), load(3, rs_ref, rs)]
    mlp = [load(4, wd_ref, wd), load(5, dgel_ref, dgel), load(6, act_ref, act), load(7, n2_ref, n2)]
    second = [columns(8, c_up, c_proj), load(9, xh2_ref, xh2), columns(10, c_out, c_up), load(11, att_ref, att)]
    attention = [load(12, qkv_ref, qkv), columns(14, 0, c_out), load(15, seen_t_ref, seen_t)]
    again = [load(16, xh1_ref, xh1), load(17, n1_ref, n1)]
    for group in (first, mlp, second, attention):
        for copy in group:
            copy.start()
    gvec_ref[...] = jnp.zeros_like(gvec_ref)
    encoder_clips(seg_ref, own, others)

    open_copies = [None, None]
    turn = [0]

    def leave(value, dst):
        slot = turn[0] % 2
        if open_copies[slot] is not None:
            open_copies[slot].wait()
        height, length = value.shape
        stage[slot, :height, :length] = value
        copy = pltpu.make_async_copy(stage.at[slot, pl.ds(0, height), pl.ds(0, length)], dst, s_sem.at[slot])
        copy.start()
        open_copies[slot] = copy
        turn[0] += 1

    def ln_backward(k, xh, add):
        for i in range(rows // 128):
            d = tmp[:, lane(i)]
            xhat = xh[:, lane(i)]
            gvec_ref[2 * k] += d * xhat
            gvec_ref[2 * k + 1] += d
            dx = d * vec_ref[2 * k]
            m1 = jnp.mean(dx, axis=0, keepdims=True)
            m2 = jnp.mean(dx * xhat, axis=0, keepdims=True)
            g = rs[8 * k : 8 * k + 1, lane(i)] * (dx - m1 - xhat * m2)
            if add:
                g = g + res[:, lane(i)]
            res[:, lane(i)] = g
            low[:, lane(i)] = g.astype(BF16)

    for copy in first:
        copy.wait()
    gp = gp_ref[...].astype(BF16)
    leave(mm(n1[...], gp, 1, 1), gin_ref.at[:, pl.ds(c_proj, n_proj)])
    tmp[...] = mm(wi[:, c_proj:], gp)
    ln_backward(2, xh1, False)
    for copy in again:
        copy.start()
    for copy in mlp:
        copy.wait()
    for i in range(hidden // CHUNK):
        at = pl.ds(i * CHUNK, CHUNK)
        d = (mm(wd[at, :], low[...]) * dgel[at, :]).astype(BF16)
        leave(mm(act[at, :], low[...], 1, 1), gdown_ref.at[at, :])
        act[at, :] = d
        leave(mm(n2[...], d, 1, 1), gin_ref.at[:, pl.ds(c_up + i * CHUNK, CHUNK)])
    for copy in second:
        copy.wait()
    tmp[...] = mm(wi[:, c_up:c_proj], act[...])
    ln_backward(1, xh2, True)
    leave(mm(att[...], low[...], 1, 1), gin_ref.at[:, pl.ds(c_out, width)])
    att[...] = mm(wi[:, c_out:c_up], low[...]).astype(BF16)
    for copy in attention:
        copy.wait()

    def attend_back(h):
        f0 = pl.multiple_of(h * size, size)
        mine = pl.ds(f0, size)
        q = qkv[mine, :]
        k = qkv[pl.ds(width + f0, size), :]
        v = qkv[pl.ds(2 * width + f0, size), :]
        do = att[mine, :]
        keys = jnp.concatenate([k, others[...]], axis=0).T
        values = v.T
        for i in range(rows // 128):
            part_q = jnp.concatenate([q[:, 128 * i : 128 * i + 128], own[:, lane(i)]], axis=0)
            p = encoder_scores(part_q, keys, scale)
            dp = mm(values, do[:, 128 * i : 128 * i + 128])
            ds = p * (dp - jnp.sum(dp * p, axis=0, keepdims=True))
            probs[:, lane(i)] = p.astype(BF16)
            dscores[:, lane(i)] = (ds * scale).astype(BF16)
        dqkv[mine, :] = mm(k, dscores[...]).astype(BF16)
        dqkv[pl.ds(width + f0, size), :] = mm(q, dscores[...], 1, 1).astype(BF16)
        dqkv[pl.ds(2 * width + f0, size), :] = mm(do, probs[...], 1, 1).astype(BF16)
    loop(heads, attend_back, 3)
    for copy in again:
        copy.wait()
    for i in range(3 * width // CHUNK):
        at = pl.ds(i * CHUNK, CHUNK)
        leave(mm(n1[...], dqkv[at, :], 1, 1), gin_ref.at[:, at])
    tmp[...] = mm(wi[:, :c_out], dqkv[...])
    ln_backward(0, xh1, True)
    leave(mm(seen_t[...], low[...], 1, 1), gembed_ref)
    for copy in open_copies:
        copy.wait()


def encoder_backward(gp, vec, seg, wi, wd, saved, patch, heads):
    rows = gp.shape[1]
    width, total = wi.shape
    hidden = wd.shape[0]
    any_, vmem = pl.BlockSpec(memory_space=pl.ANY), pl.BlockSpec(memory_space=pltpu.VMEM)
    f = lambda *s: pltpu.VMEM(s, F32)
    b = lambda *s: pltpu.VMEM(s, BF16)
    shape = lambda *s: jax.ShapeDtypeStruct(s, F32)
    return pl.pallas_call(
        functools.partial(encoder_backward_kernel, heads),
        out_shape=(shape(width, total), shape(hidden, width), shape(patch, width), shape(6, width, 128)),
        in_specs=[vmem] * 3 + [any_] * (2 + len(saved)),
        out_specs=(any_,) * 3 + (vmem,),
        scratch_shapes=[
            b(*wi.shape), b(*wd.shape), f(width, rows), f(width, rows), b(width, rows), b(3 * width, rows), b(rows, rows), b(rows, rows),
            f(2, CHUNK, CHUNK), b(16, rows), b(16, rows), b(patch, rows), f(width, rows), b(width, rows), b(3 * width, rows), b(width, rows),
            f(width, rows), b(width, rows), b(hidden, rows), f(hidden, rows), f(24, rows),
            pltpu.SemaphoreType.DMA((18,)), pltpu.SemaphoreType.DMA((2,)),
        ],
        compiler_params=pltpu.CompilerParams(vmem_limit_bytes=63 * 2**20),
        name="encode_back",
    )(gp, vec, seg, wi, wd, *saved)


def place():
    clip, band = lax.axis_index("clip"), lax.axis_index("band")
    return clip // 2, clip % 2, band // 2, band % 2


def device(z, x, y, c):
    return (z * 2 + x, y * 2 + c)


def greet(z, x, y, c):
    barrier = pltpu.get_barrier_semaphore()
    others = [device(z, x, y, 1 - c), device(z, 1 - x, y, c), device(z, x, 1 - y, c)]
    others += [device((z + k) % 4, x, y, c) for k in (1, 2, 3)]
    for other in others:
        pl.semaphore_signal(barrier, inc=1, device_id=other, device_id_type=pl.DeviceIdType.MESH)
    pl.semaphore_wait(barrier, len(others))


def remote(src, dst, send, recv, to):
    return pltpu.make_async_remote_copy(
        src_ref=src, dst_ref=dst, send_sem=send, recv_sem=recv, device_id=to, device_id_type=pl.DeviceIdType.MESH
    )


def reduce_kernel(widths, n, *refs):
    grads, small = refs[:n], refs[n]
    outs, small_out, squares = refs[n + 1 : 2 * n + 1], refs[2 * n + 1], refs[2 * n + 2]
    rest = refs[2 * n + 3 :]
    sums, r0 = rest[:n], rest[n : 2 * n]
    coded = {1 + i: rest[(2 + i) * n : (3 + i) * n] for i in range(5)}
    came = {1 + i: rest[(7 + i) * n : (8 + i) * n] for i in range(5)}
    step_out = {1 + i: rest[(12 + i) * n : (13 + i) * n] for i in range(5)}
    step_in = {1 + i: rest[(17 + i) * n : (18 + i) * n] for i in range(5)}
    s_buf, s_sum, q_buf, q_sum, send, recv, near, t_send, t_recv, s_send, s_recv = rest[22 * n :]
    z, x, y, c = place()
    greet(z, x, y, c)

    def at_z(k):
        return (z + k) % 4

    def columns(t, core):
        half = sums[t].shape[4]
        return pl.ds(pl.multiple_of(core * half, 128), half)

    def local(t, k):
        zk = at_z(k)
        return pltpu.make_async_copy(grads[t].at[zk, :, :, :, columns(t, c)], sums[t].at[zk], near.at[t, k])

    def target(stage, k):
        return {
            1: lambda: device(z, 1 - x, y, c),
            2: lambda: device(z, x, 1 - y, c),
            3: lambda: device(z, x, 1 - y, c),
            4: lambda: device(z, 1 - x, y, c),
            5: lambda: device(at_z(k), x, y, c),
        }[stage]()

    def slot(stage, k):
        return k - 1 if stage == 5 else k

    def copy(stage, t, k):
        if stage == 0:
            src, dst, to = grads[t].at[at_z(k), :, :, :, columns(t, 1 - c)], r0[t].at[at_z(k)], device(z, x, y, 1 - c)
        elif stage == 6:
            src, dst, to = sums[t].at[z, x, y], outs[t].at[y, :, columns(t, c)], device(z, x, 1 - y, c)
        elif stage == 7:
            src = outs[t].at[:, :, columns(t, c)]
            dst, to = src, device(z, x, y, 1 - c)
        else:
            src, dst, to = coded[stage][t].at[slot(stage, k)], came[stage][t].at[slot(stage, k)], target(stage, k)
        return remote(src, dst, send.at[t, stage, k], recv.at[t, stage, k], to)

    def steps(stage, t, k):
        src, dst = step_out[stage][t].at[k], step_in[stage][t].at[k]
        return remote(src, dst, t_send.at[t, stage, k], t_recv.at[t, stage, k], target(stage, k))

    def keep(t):
        return pltpu.make_async_copy(sums[t].at[z, x, y], outs[t].at[y, :, columns(t, c)], near.at[t, 4])

    def each(lo, hi, body):
        def one(k, carry):
            body(k)
            return carry
        lax.fori_loop(lo, hi, one, 0)

    def slab(i, height):
        return pl.ds(pl.multiple_of(i * height, height), height)

    def part(stage, t):
        w = widths[t]
        return slice(0, w) if stage in (1, 3) else slice(w, None) if stage in (2, 4) else slice(None)

    def encode(stage, t, k, parts, read):
        rows = sums[t].shape[3]
        zk, width = at_z(k), coded[stage][t].shape[-1]
        block = lambda p: coded[stage][t].at[(k, p) if parts > 1 else slot(stage, k)]
        per = rows // 8
        def peak(i, most):
            return jnp.maximum(most, jnp.abs(read(zk, i // per, slab(i % per, 8))))
        most = lax.fori_loop(0, parts * per, peak, jnp.zeros((8, width), F32))
        most = jnp.maximum(jnp.max(most, axis=0, keepdims=True), 1e-30)
        step_out[stage][t][k] = most * (1.0 / 32767.0)
        steps(stage, t, k).start()
        scale = 32767.0 / most
        half = rows // 16
        def one(i):
            values = jnp.round(read(zk, i // half, slab(i % half, 16)) * scale).astype(jnp.int32).astype(jnp.int16)
            block(i // half)[slab(i % half, 16)] = values
        each(0, parts * half, one)
        copy(stage, t, k).start()

    def landed(stage, t, k):
        steps(stage, t, k).wait_recv()
        copy(stage, t, k).wait_recv()

    def decoded(stage, t, k, p, rows, parts):
        values = came[stage][t][(k, p, rows) if parts > 1 else (slot(stage, k), rows)]
        return values.astype(jnp.int32).astype(F32) * step_in[stage][t][k]

    order = (2, 1, 3, 0)
    for t in range(n):
        for k in order:
            copy(0, t, k).start()
            local(t, k).start()

    def hop(total, buffer, first, stage, to):
        return remote(total, buffer.at[stage], s_send.at[first + stage], s_recv.at[first + stage], to)

    def advance(total, buffer, first, stage):
        neighbours = (device(z, x, y, 1 - c), device(z, 1 - x, y, c), device(z, x, 1 - y, c))
        if stage:
            hop(total, buffer, first, stage - 1, neighbours[stage - 1]).wait()
            total[...] += buffer[stage - 1]
        if stage < 3:
            hop(total, buffer, first, stage, neighbours[stage]).start()
        else:
            for k in (1, 2, 3):
                last_hop(total, buffer, first, k).start()
            buffer[3 + z] = total[...]

    def last_hop(total, buffer, first, k):
        return remote(total, buffer.at[3 + z], s_send.at[first + 2 + k], s_recv.at[first + 2 + k], device(at_z(k), x, y, c))

    def finish_sum(total, buffer, first, out):
        for k in (1, 2, 3):
            last_hop(total, buffer, first, k).wait()
        out[...] = (buffer[3] + buffer[4]) + (buffer[5] + buffer[6])

    s_sum[...] = small[...]

    def first_sum(t, k):
        zk = at_z(k)
        copy(0, t, k).wait_recv()
        local(t, k).wait()
        per = sums[t].shape[3] // 16
        def one(i):
            p, r = i // per, slab(i % per, 16)
            sums[t][zk, p // 2, p % 2, r] += r0[t][zk, p // 2, p % 2, r]
        each(0, 4 * per, one)
        encode(1, t, k, 2, lambda zk, p, r: sums[t][zk, 1 - x, p, r, part(1, t)])
        encode(2, t, k, 2, lambda zk, p, r: sums[t][zk, p, 1 - y, r, part(2, t)])

    def second_sum(t, k):
        zk = at_z(k)
        per = sums[t].shape[3] // 16
        landed(1, t, k)
        def one(i):
            p, r = i // per, slab(i % per, 16)
            sums[t][zk, x, p, r, part(1, t)] += decoded(1, t, k, p, r, 2)
        each(0, 2 * per, one)
        encode(3, t, k, 1, lambda zk, p, r: sums[t][zk, x, 1 - y, r, part(3, t)])
        landed(2, t, k)
        def two(i):
            p, r = i // per, slab(i % per, 16)
            sums[t][zk, p, y, r, part(2, t)] += decoded(2, t, k, p, r, 2)
        each(0, 2 * per, two)
        encode(4, t, k, 1, lambda zk, p, r: sums[t][zk, 1 - x, y, r, part(4, t)])

    def third_sum(t, k):
        zk = at_z(k)
        landed(3, t, k)
        landed(4, t, k)
        def one(i):
            r = slab(i, 16)
            sums[t][zk, x, y, r, part(3, t)] += decoded(3, t, k, 0, r, 1)
            sums[t][zk, x, y, r, part(4, t)] += decoded(4, t, k, 0, r, 1)
        each(0, sums[t].shape[3] // 16, one)
        if k:
            encode(5, t, k, 1, lambda zk, p, r: sums[t][zk, x, y, r])

    def last_sum(t, total):
        for k in (1, 2, 3):
            landed(5, t, k)
        half = sums[t].shape[4]
        def one(i, acc):
            r = slab(i, 16)
            value = sums[t][z, x, y, r]
            for k in (1, 2, 3):
                value = value + decoded(5, t, k, 0, r, 1)
            sums[t][z, x, y, r] = value
            value = value * value
            value = value[:8] + value[8:]
            for j in range(half // 128):
                acc = acc + value[:, 128 * j : 128 * j + 128]
            return acc
        total = lax.fori_loop(0, sums[t].shape[3] // 16, one, total)
        copy(6, t, 0).start()
        keep(t).start()
        return total

    def share(t):
        copy(6, t, 0).wait_recv()
        keep(t).wait()
        copy(7, t, 0).start()

    blocks = [(t, k) for t in range(n) for k in order]
    total = jnp.zeros((8, 128), F32)
    for i in range(len(blocks) + 2):
        if i < len(blocks):
            first_sum(*blocks[i])
        if 0 <= i - 1 < len(blocks):
            second_sum(*blocks[i - 1])
        if 0 <= i - 2:
            third_sum(*blocks[i - 2])
        if i < 4:
            advance(s_sum, s_buf, 0, i)
        for t in range(n - 1):
            if i == 4 * t + 7:
                total = last_sum(t, total)
            if i == 4 * t + 9:
                share(t)
    total = last_sum(n - 1, total)
    finish_sum(s_sum, s_buf, 0, small_out)
    late = [t for t in range(n) if t == n - 1 or 4 * t + 9 >= len(blocks) + 2]
    for t in late[:-1]:
        share(t)
    q_sum[...] = total
    for stage in range(4):
        advance(q_sum, q_buf, 6, stage)
    finish_sum(q_sum, q_buf, 6, squares)
    share(late[-1])

    def finish(k):
        for t in range(n):
            copy(0, t, k).wait_send()
            for stage in range(1, 5):
                copy(stage, t, k).wait_send()
                steps(stage, t, k).wait_send()
    each(0, 4, finish)
    def finish_z(k):
        for t in range(n):
            copy(5, t, k).wait_send()
            steps(5, t, k).wait_send()
    each(1, 4, finish_z)
    for t in range(n):
        copy(6, t, 0).wait_send()
        copy(7, t, 0).wait()


def reduce_grads(grads, small, ident):
    n = len(grads)
    views, widths = [], []
    scratch = [[] for _ in range(22)]
    f = lambda *s: pltpu.VMEM(s, F32)
    q = lambda *s: pltpu.VMEM(s, jnp.int16)
    for grad in grads:
        rows, cols = grad.shape
        r2, half = rows // 16, cols // 2
        w = (half // 128 * 60 + 50) // 100 * 128
        views.append(grad.reshape(4, 2, 2, r2, cols))
        widths.append(w)
        blocks = [(4, 2, r2, w), (4, 2, r2, half - w), (4, r2, w), (4, r2, half - w), (3, r2, half)]
        for i, s in enumerate([f(4, 2, 2, r2, half)] * 2 + [q(*b) for b in blocks * 2] + [f(4, 1, b[-1]) for b in blocks * 2]):
            scratch[i].append(s)
    anywhere, vmem = pl.BlockSpec(memory_space=pl.ANY), pl.BlockSpec(memory_space=pltpu.VMEM)
    dma = pltpu.SemaphoreType.DMA
    square = jax.ShapeDtypeStruct((8, 128), F32)
    out = pl.pallas_call(
        functools.partial(reduce_kernel, tuple(widths), n),
        out_shape=tuple(jax.ShapeDtypeStruct((2, v.shape[3], v.shape[4]), F32) for v in views)
        + (jax.ShapeDtypeStruct(small.shape, F32), square),
        in_specs=[anywhere] * n + [vmem],
        out_specs=(anywhere,) * n + (vmem,) * 2,
        scratch_shapes=sum(scratch, []) + [
            f(7, *small.shape), f(*small.shape), f(7, 8, 128), f(8, 128),
            dma((n, 8, 4)), dma((n, 8, 4)), dma((n, 5)), dma((n, 6, 4)), dma((n, 6, 4)), dma((12,)), dma((12,)),
        ],
        compiler_params=pltpu.CompilerParams(
            collective_id=ident, has_side_effects=True, vmem_limit_bytes=63 * 2**20
        ),
        name="reduce",
    )(*views, small)
    return [o.reshape(-1, o.shape[2]) for o in out[:n]], out[n], out[n + 1]


def gather_kernel(chunks, n, *refs):
    shards, vector, results, vectors = refs[:n], refs[n], refs[n + 1 : 2 * n + 1], refs[2 * n + 1]
    outs = refs[2 * n + 2 : 3 * n + 2]
    send, recv, near, v_send, v_recv = refs[3 * n + 2 :]
    z, x, y, c = place()
    greet(z, x, y, c)

    def at_z(k):
        return (z + k) % 4

    def own(t):
        return pltpu.make_async_copy(shards[t], outs[t].at[z, x], near.at[t])

    def copy(stage, i, k):
        t, r0, nr, c0, both, split = chunks[i]
        half = shards[t].shape[2] // 2
        columns = lambda lo, size: pl.ds(pl.multiple_of(c * half + lo, 128), size)
        wide, narrow, whole = columns(c0, both), columns(c0 + both, split), columns(c0, both + split)
        rows = pl.ds(r0, nr)
        mine = isinstance(k, int) and k == 0
        o, src_z = outs[t], (z + 4 - k) % 4
        if stage == 0:
            src, dst, to = shards[t].at[:, rows, wide], o.at[z, x, :, rows, wide], device(at_z(k), x, y, c)
        elif stage == 1:
            src, dst, to = shards[t].at[y, rows, narrow], o.at[z, x, y, rows, narrow], device(at_z(k), x, y, c)
        elif stage == 2:
            dst, to = o.at[src_z, x, :, rows, wide], device(z, 1 - x, y, c)
            src = shards[t].at[:, rows, wide] if mine else dst
        elif stage == 3:
            dst, to = o.at[src_z, x, y, rows, narrow], device(z, 1 - x, y, c)
            src = shards[t].at[y, rows, narrow] if mine else dst
        elif stage == 4:
            src = o.at[src_z, 1 - x, y, rows, narrow] if mine else o.at[src_z, :, y, rows, narrow]
            dst, to = src, device(z, x, 1 - y, c)
        else:
            src = o.at[src_z, 1 - x, :, rows, whole] if mine else o.at[src_z, :, :, rows, whole]
            dst, to = src, device(z, x, y, 1 - c)
        return remote(src, dst, send.at[i, stage, k], recv.at[i, stage, k], to)

    def leave(t):
        return pltpu.make_async_copy(outs[t], results[t], near.at[n + t])

    def vector_copy(stage, k):
        src_z = (z + 4 - k) % 4
        if stage == 0:
            return remote(vector, vectors.at[z, x], v_send.at[k], v_recv.at[k], device(at_z(k), x, y, c))
        src = vector if k == 0 else vectors.at[src_z, x]
        return remote(src, vectors.at[src_z, x], v_send.at[4 + k], v_recv.at[4 + k], device(z, 1 - x, y, c))

    def each(lo, hi, body):
        def step(k, carry):
            body(k)
            return carry
        lax.fori_loop(lo, hi, step, 0)

    def along_z(i):
        def one(k):
            copy(0, i, k).start()
            copy(1, i, k).start()
        each(1, 4, one)
        copy(2, i, 0).start()
        copy(3, i, 0).start()

    def along_x(i):
        def one(k):
            copy(0, i, k).wait_recv()
            copy(2, i, k).start()
            copy(1, i, k).wait_recv()
            copy(3, i, k).start()
        each(1, 4, one)

    def along_y(i):
        copy(3, i, 0).wait_recv()
        copy(4, i, 0).start()
        def one(k):
            copy(3, i, k).wait_recv()
            copy(4, i, k).start()
        each(1, 4, one)

    def across(i):
        def one(k):
            copy(2, i, k).wait_recv()
            copy(4, i, k).wait_recv()
            copy(5, i, k).start()
        one(0)
        each(1, 4, one)

    vectors[z, x] = vector[...]
    for k in (1, 2, 3):
        vector_copy(0, k).start()
    vector_copy(1, 0).start()
    along_z(0)
    for t in range(n):
        own(t).start()
    count = len(chunks)
    for i in range(count + 3):
        if i + 1 < count:
            along_z(i + 1)
        if i < count:
            along_x(i)
        if i == 0:
            for t in range(n):
                own(t).wait()
        if i == 1:
            for k in (1, 2, 3):
                vector_copy(0, k).wait_recv()
                vector_copy(1, k).start()
        if 0 <= i - 1 < count:
            along_y(i - 1)
        if 0 <= i - 2 < count:
            across(i - 2)
        if 0 <= i - 3:
            copy(5, i - 3, 0).wait_recv()
            each(1, 4, lambda k, i=i: copy(5, i - 3, k).wait_recv())
            if i - 2 == count or chunks[i - 2][0] != chunks[i - 3][0]:
                leave(chunks[i - 3][0]).start()

    for i in range(count):
        for stage in (2, 3, 4, 5):
            copy(stage, i, 0).wait_send()
        def finish(k, i=i):
            for stage in range(6):
                copy(stage, i, k).wait_send()
        each(1, 4, finish)
    for t in range(n):
        leave(t).wait()
    vector_copy(1, 0).wait()
    for k in (1, 2, 3):
        vector_copy(0, k).wait_send()
        vector_copy(1, k).wait()


def chunks_of(shards, largest):
    chunks = []
    for t, shard in enumerate(shards):
        rows, tiles = shard.shape[0] // 2, shard.shape[1] // 256
        size = rows * tiles * 128
        parts = -(-size // largest)
        by_rows = rows // parts % 16 == 0 and tiles < 2 * parts
        if by_rows:
            for p in range(parts):
                both = max(1, tiles // 3) if tiles > 1 else 0
                chunks.append((t, rows // parts * p, rows // parts, 0, both * 128, (tiles - both) * 128))
        else:
            cuts = [tiles * p // parts for p in range(parts + 1)]
            for lo, hi in zip(cuts, cuts[1:]):
                both = max(1, (hi - lo) // 3)
                chunks.append((t, 0, rows, lo * 128, both * 128, (hi - lo - both) * 128))
    return tuple(chunks)


def gather_weights(shards, vector, ident):
    n = len(shards)
    views = [shard.reshape(2, shard.shape[0] // 2, shard.shape[1]) for shard in shards]
    chunks = chunks_of(shards, 75000)
    anywhere, vmem = pl.BlockSpec(memory_space=pl.ANY), pl.BlockSpec(memory_space=pltpu.VMEM)
    dma = pltpu.SemaphoreType.DMA
    out = pl.pallas_call(
        functools.partial(gather_kernel, chunks, n),
        out_shape=tuple(jax.ShapeDtypeStruct((4, 2) + v.shape, BF16) for v in views)
        + (jax.ShapeDtypeStruct((4, 2, 8, 128), F32),),
        in_specs=[vmem] * n + [vmem],
        out_specs=(anywhere,) * n + (vmem,),
        scratch_shapes=[pltpu.VMEM((4, 2) + v.shape, BF16) for v in views]
        + [dma((len(chunks), 6, 4)), dma((len(chunks), 6, 4)), dma((2 * n,)), dma((8,)), dma((8,))],
        compiler_params=pltpu.CompilerParams(collective_id=ident, has_side_effects=True, vmem_limit_bytes=60 * 2**20),
        name="gather",
    )(*views, vector.reshape(8, 128))
    return [o.reshape(-1, o.shape[4]) for o in out[:n]], out[n].reshape(-1)


def clip_of(column, clip_lengths, clip_shifts):
    columns = clip_lengths // 8
    ends = jnp.cumsum(columns)
    clip_id = jnp.sum((column[:, None] >= ends[None, :]).astype(jnp.int32), axis=1)
    onehot = (clip_id[:, None] == jnp.arange(clip_lengths.shape[0], dtype=jnp.int32)[None, :]).astype(jnp.int32)

    def select(values):
        return jnp.sum(onehot * values[None, :], axis=1)

    return clip_id, select(ends - columns), select(columns), select(clip_shifts[:, 0]), select(clip_shifts[:, 1])


def half_table(position, width):
    quarter = width // 4
    omega = 1.0 / 10000.0 ** (jnp.arange(quarter, dtype=jnp.float32) / quarter)
    angle = omega[:, None] * position.astype(jnp.float32)[None, :]
    return jnp.concatenate([jnp.sin(angle), jnp.cos(angle)])


def adam_update(weight, first, second, grad, decay):
    first = BETA_ONE * first + (1.0 - BETA_ONE) * grad
    second = BETA_TWO * second + (1.0 - BETA_TWO) * grad * grad
    first_hat = first / (1.0 - BETA_ONE**STEP)
    second_hat = second / (1.0 - BETA_TWO**STEP)
    weight = weight - LEARN_RATE * (first_hat / (jnp.sqrt(second_hat) + EPSILON) + decay * weight)
    return (weight, first, second)


def shards(
    pixels,
    lengths,
    shifts,
    visible,
    patch_embed,
    encoder_in,
    encoder_down,
    decoder_in,
    decoder_down,
    norm_vectors,
    first_embed,
    first_encoder_in,
    first_encoder_down,
    first_decoder_in,
    first_decoder_down,
    first_vectors,
    second_embed,
    second_encoder_in,
    second_encoder_down,
    second_decoder_in,
    second_decoder_down,
    second_vectors,
):
    masters = (patch_embed, encoder_in, encoder_down, decoder_in, decoder_down, norm_vectors)
    firsts = (
        first_embed,
        first_encoder_in,
        first_encoder_down,
        first_decoder_in,
        first_decoder_down,
        first_vectors,
    )
    seconds = (
        second_embed,
        second_encoder_in,
        second_encoder_down,
        second_decoder_in,
        second_decoder_down,
        second_vectors,
    )
    direct = lax.axis_size("clip") == 8 and lax.axis_size("band") == 4
    low_shards = [master.astype(jnp.bfloat16) for master in masters]
    if direct:
        (w_embed, w_enc, w_enc_down, w_dec, w_dec_down), vectors = gather_weights(
            low_shards[:5], lax.reduce_precision(norm_vectors, exponent_bits=8, mantissa_bits=7), 0
        )
    else:
        w_embed, w_enc, w_enc_down, w_dec, w_dec_down, gathered_vectors = (
            lax.all_gather(shard, "clip", axis=0, tiled=True) for shard in low_shards
        )
        vectors = gathered_vectors.astype(jnp.float32)
    enc_width, dec_width = (w_enc.shape[0], w_dec.shape[0])
    patch_dev, n_visible = pixels.shape[0], visible.shape[0]
    padded = -(-n_visible // 128) * 128
    enc_gains = vectors[: 6 * enc_width].reshape(6, enc_width, 1)
    dec_gains = vectors[6 * enc_width :].reshape(7, dec_width, 1)
    enc_gains = jnp.broadcast_to(enc_gains, (6, enc_width, 128))
    dec_gains = jnp.broadcast_to(dec_gains, (7, dec_width, 128))
    turned = jnp.arange(patch_dev // 8, dtype=jnp.int32)
    _, start, size, shift_time, shift_band = clip_of(turned, lengths[0], shifts[0])
    turned_time = (turned - start - shift_time) % size
    decoder_pixels = pixels.reshape(patch_dev // 8, 8, -1)[start + turned_time].reshape(pixels.shape)
    time_table = half_table(turned_time, dec_width).T
    band_table = jnp.tile(half_table(jnp.arange(8, dtype=jnp.int32), dec_width), (1, 16))
    spots = jnp.pad(visible, (0, padded - n_visible))
    real = jnp.arange(padded, dtype=jnp.int32) < n_visible
    seen = pixels[spots]
    column, band = spots // 8, spots % 8
    segment, seen_start, seen_size, seen_shift, _ = clip_of(column, lengths[0], shifts[0])
    segment = jnp.where(real, segment, 15).astype(jnp.int32)
    segment = jnp.broadcast_to(segment[None, :], (8, padded))
    seen_time = column - seen_start
    decoder_row = jnp.where(real, 8 * (seen_start + (seen_time + seen_shift) % seen_size) + band, -1)
    decoder_row = jnp.broadcast_to(decoder_row[:, None], (padded, 128)).astype(jnp.int32)

    def positions(width):
        return jnp.concatenate([half_table(seen_time, width), half_table(band, width)])

    grid_seen, *saved = encoder_forward(
        seen,
        positions(enc_width),
        positions(dec_width),
        segment,
        enc_gains,
        w_embed,
        w_enc,
        w_enc_down,
        HEADS_ENC,
    )
    masked_count = 13.0 * (patch_dev // 16) * lax.axis_size("clip") * lax.axis_size("band")
    g_dec_in, g_dec_down, g_dec_vectors, grad_grid, loss = decoder_step(
        shift_band[::64],
        decoder_row,
        grid_seen,
        decoder_pixels,
        time_table,
        band_table,
        dec_gains,
        w_dec,
        w_dec_down,
        2.0 / (pixels.shape[1] * masked_count),
        HEADS_DEC,
    )
    local_loss = jnp.sum(loss[0])
    g_enc_in, g_enc_down, g_embed, g_enc_vectors = encoder_backward(
        grad_grid, enc_gains, segment, w_enc, w_enc_down, saved, pixels.shape[1], HEADS_ENC
    )
    g_vectors = jnp.concatenate(
        [jnp.sum(g_enc_vectors, axis=2).reshape(-1), jnp.sum(g_dec_vectors, axis=2).reshape(-1)]
    )
    if direct:
        small = jnp.concatenate([g_vectors.reshape(-1, 128), jnp.full((8, 128), local_loss)])
        shard_sums, summed, squares = reduce_grads(
            [g_enc_in, g_dec_in, g_enc_down, g_dec_down, g_embed], small, 1
        )
        rows = norm_vectors.shape[0]
        vector_sums = summed[:-8].reshape(-1)
        own = lax.dynamic_slice(vector_sums, (lax.axis_index("clip") * rows,), (rows,))
        reduced = (shard_sums[4], shard_sums[0], shard_sums[2], shard_sums[1], shard_sums[3], own)
        loss_sum = summed[-1, 0]
        norm_squared = jnp.sum(squares) + jnp.sum(vector_sums * vector_sums)
    else:
        reduced = lax.psum(
            tuple(
                lax.psum_scatter(grad, "clip", scatter_dimension=0, tiled=True)
                for grad in (g_embed, g_enc_in, g_enc_down, g_dec_in, g_dec_down, g_vectors)
            ),
            "band",
        )
        loss_sum = lax.psum(local_loss, ("clip", "band"))
        norm_squared = lax.psum(sum(jnp.sum(grad * grad) for grad in reduced), "clip")
    grad_norm = jnp.sqrt(norm_squared)
    factor = jnp.minimum(1.0, CLIP_LIMIT / (grad_norm + 1e-06))
    results = []
    for index in range(6):
        decay = DECAY_RATE if index < 5 else 0.0
        results.append(
            adam_update(
                masters[index], firsts[index], seconds[index], reduced[index] * factor, decay
            )
        )
    return (
        loss_sum,
        grad_norm,
        results[0][0],
        results[1][0],
        results[2][0],
        results[3][0],
        results[4][0],
        results[5][0],
        results[0][1],
        results[1][1],
        results[2][1],
        results[3][1],
        results[4][1],
        results[5][1],
        results[0][2],
        results[1][2],
        results[2][2],
        results[3][2],
        results[4][2],
        results[5][2],
    )


def solution(mesh):
    in_specs = (
        P(("clip", "band"), None),
        P(("clip", "band"), None),
        P(("clip", "band"), None, None),
        P(("clip", "band")),
        P("clip", None),
        P("clip", None),
        P("clip", None),
        P("clip", None),
        P("clip", None),
        P("clip"),
        P("clip", None),
        P("clip", None),
        P("clip", None),
        P("clip", None),
        P("clip", None),
        P("clip"),
        P("clip", None),
        P("clip", None),
        P("clip", None),
        P("clip", None),
        P("clip", None),
        P("clip"),
    )
    out_specs = (
        P(),
        P(),
        P("clip", None),
        P("clip", None),
        P("clip", None),
        P("clip", None),
        P("clip", None),
        P("clip"),
        P("clip", None),
        P("clip", None),
        P("clip", None),
        P("clip", None),
        P("clip", None),
        P("clip"),
        P("clip", None),
        P("clip", None),
        P("clip", None),
        P("clip", None),
        P("clip", None),
        P("clip"),
    )
    return jax.shard_map(shards, mesh=mesh, in_specs=in_specs, out_specs=out_specs, check_vma=False)
```

```python
import functools

import jax
import jax.numpy as jnp
from jax import lax
from jax.experimental import pallas as pl
from jax.experimental.pallas import tpu as pltpu
from jax.sharding import PartitionSpec as P

HEADS_ENC = 12
HEADS_DEC = 16
STEP = 10


LEARN_RATE = 0.02
BETA_ONE = 0.9
BETA_TWO = 0.95
EPSILON = 1e-08
DECAY_RATE = 0.05
CLIP_LIMIT = 0.001


F32, BF16 = jnp.float32, jnp.bfloat16
GELU_C = 0.7978845608028654


def mm(a, b, ca=1, cb=0):
    return lax.dot_general(a, b, (((ca,), (cb,)), ((), ())), preferred_element_type=F32)


def wide(v, n):
    return jnp.concatenate([v] * (n // 128), axis=1)


def loop(n, body, unroll=1):
    def step(i, carry):
        for k in range(unroll):
            body(i * unroll + k)
        return carry
    lax.fori_loop(0, n // unroll, step, 0)


def fold(v):
    total = v[:, :128]
    for i in range(1, v.shape[1] // 128):
        total = total + v[:, 128 * i : 128 * (i + 1)]
    return total


def decoder_kernel(
    coef, heads, shift_ref, rvis_ref, gvt_ref, pix_ref, et_ref, ef_ref, vec_ref, w_ref, wd_ref,
    gin_ref, gdown_ref, gvec_ref, gp_ref, loss_ref,
    wt_ref, wdt_ref, res, xh1, xh2, xh3, tmp, n1, n2, fin, rs, qkv, att, act, dgel, probs, dqkv, dup, low, oh, mrow, hb, hm, wm,
):
    width = w_ref.shape[0]
    hidden = wd_ref.shape[0]
    rows = res.shape[1]
    size = width // heads
    per = 128 // size
    scale = size ** -0.5
    groups = width // 128
    c_out, c_up, c_head = 3 * width, 4 * width, 4 * width + hidden
    pixels = w_ref.shape[1] - c_head
    cols = rows // 8
    nblk = pix_ref.shape[0] // rows
    chunk = 512

    def turn_in(i):
        at = pl.ds(pl.multiple_of(i * 256, 256), 256)
        wt_ref[at, :] = w_ref[:, at].T
    loop(w_ref.shape[1] // 256, turn_in)

    def turn_down(i):
        at = pl.ds(pl.multiple_of(i * 256, 256), 256)
        wdt_ref[:, at] = wd_ref[at, :].T
    loop(hidden // 256, turn_down)
    gin_ref[...] = jnp.zeros_like(gin_ref)
    gdown_ref[...] = jnp.zeros_like(gdown_ref)
    gvec_ref[...] = jnp.zeros_like(gvec_ref)
    gp_ref[...] = jnp.zeros_like(gp_ref)
    loss_ref[...] = jnp.zeros_like(loss_ref)
    f_id = lax.broadcasted_iota(jnp.int32, (128, 128 * per), 0)
    q_id = lax.broadcasted_iota(jnp.int32, (128, 128 * per), 1)
    hm[...] = jnp.where(f_id // size == q_id // 128, 1.0, 0.0).astype(BF16)
    wm[...] = jnp.where(f_id // 32 == (q_id % 128) // 32, 1.0, 0.0).astype(BF16)

    def lane(i):
        return pl.ds(pl.multiple_of(i * 128, 128), 128)

    def ln_forward(k, xh, out):
        def body(i):
            x = res[:, lane(i)]
            centre = x - jnp.mean(x, axis=0, keepdims=True)
            r = lax.rsqrt(jnp.mean(centre * centre, axis=0, keepdims=True) + 1e-06)
            xhat = centre * r
            xh[:, lane(i)] = xhat
            rs[8 * k : 8 * k + 8, lane(i)] = jnp.broadcast_to(r, (8, 128))
            out[:, lane(i)] = (xhat * vec_ref[2 * k] + vec_ref[2 * k + 1]).astype(BF16)
        loop(rows // 128, body, 4)

    def ln_backward(k, xh, add):
        def body(i):
            d = tmp[:, lane(i)]
            xhat = xh[:, lane(i)]
            gvec_ref[2 * k] += d * xhat
            gvec_ref[2 * k + 1] += d
            dx = d * vec_ref[2 * k]
            m1 = jnp.mean(dx, axis=0, keepdims=True)
            m2 = jnp.mean(dx * xhat, axis=0, keepdims=True)
            g = rs[8 * k : 8 * k + 1, lane(i)] * (dx - m1 - xhat * m2)
            if add:
                g = g + res[:, lane(i)]
            res[:, lane(i)] = g
            low[:, lane(i)] = g.astype(BF16)
        loop(rows // 128, body, 4)

    def block(j):
        first = pl.multiple_of(j * rows, rows)
        turn = shift_ref[j]
        spot = lax.broadcasted_iota(jnp.int32, (rvis_ref.shape[0], rows), 1) + first
        hot = jnp.where(wide(rvis_ref[...], rows) == spot, 1.0, 0.0)
        oh[...] = hot.astype(BF16)
        masked = 1.0 - jnp.sum(hot, axis=0, keepdims=True)
        mrow[...] = jnp.broadcast_to(masked, (8, rows))
        et = et_ref[pl.ds(pl.multiple_of(j * cols, cols), cols), :]
        e_hi = et.astype(BF16)
        rest = et - e_hi.astype(F32)
        e_mid = rest.astype(BF16)
        e_lo = (rest - e_mid.astype(F32)).astype(BF16)
        spread = jnp.where(
            lax.broadcasted_iota(jnp.int32, (cols, rows), 1) // 8 == lax.broadcasted_iota(jnp.int32, (cols, rows), 0), 1.0, 0.0
        ).astype(BF16)
        e_t = mm(e_hi, spread, 0, 0) + (mm(e_mid, spread, 0, 0) + mm(e_lo, spread, 0, 0))
        half = width // 2
        keep = masked > 0.5
        placed = mm(gvt_ref[...], oh[...])
        top = (wide(vec_ref[6, :half], rows) + e_t).astype(BF16).astype(F32)
        res[:half] = jnp.where(keep, top, placed[:half])
        bottom = wide((vec_ref[6, half:] + ef_ref[...]).astype(BF16).astype(F32), rows)
        res[half:] = jnp.where(keep, bottom, placed[half:])
        k_half = (lax.broadcasted_iota(jnp.int32, (32, 128 * per), 0) % 8 + turn) % 8 // 4
        q_half = (lax.broadcasted_iota(jnp.int32, (32, 128 * per), 1) % 8 + turn) % 8 // 4
        hb[...] = jnp.where(k_half == q_half, 0.0, -1e30)

        ln_forward(0, xh1, n1)

        def qkv_part(i):
            part = pl.ds(pl.multiple_of(i * chunk, chunk), chunk)
            qkv[part, :] = mm(wt_ref[part, :], n1[...]).astype(BF16)
        loop(3 * width // chunk, qkv_part, 3)

        q_group = (lax.broadcasted_iota(jnp.int32, (32, 128 * per), 1) % 128) // 32

        def compact(s):
            c = s[96:128]
            for i in (2, 1, 0):
                c = jnp.where(q_group == i, s[32 * i : 32 * i + 32], c)
            return c

        def attend(i):
            sb, g = i // groups, i % groups
            at = lane(sb)
            f0 = pl.multiple_of(g * 128, 128)
            q = qkv[pl.ds(f0, 128), at]
            k = qkv[pl.ds(width + f0, 128), at]
            v = qkv[pl.ds(2 * width + f0, 128), at]
            s = jnp.concatenate([mm(k[size * h : size * h + size], q[size * h : size * h + size], 0, 0) for h in range(per)], axis=1)
            c = compact(s) * scale + hb[...]
            e = jnp.exp(c - jnp.max(c, axis=0, keepdims=True))
            p = e * (1.0 / jnp.sum(e, axis=0, keepdims=True))
            probs[i] = p
            p_low = p.astype(BF16)
            p_all = jnp.concatenate([p_low] * 4, axis=0) * wm[...]
            for h in range(per):
                o = mm(v[size * h : size * h + size], p_all[:, 128 * h : 128 * h + 128])
                att[pl.ds(f0 + size * h, size), at] = o.astype(BF16)
        loop(rows // 128 * groups, attend, 16)

        res[...] += mm(wt_ref[c_out : c_out + width], att[...])
        ln_forward(1, xh2, n2)

        def up_part(i):
            part = pl.ds(pl.multiple_of(i * chunk, chunk), chunk)
            u = mm(wt_ref[pl.ds(pl.multiple_of(c_up + i * chunk, chunk), chunk), :], n2[...])
            square = u * u
            hp = 0.5 + 0.5 * jnp.tanh(u * (GELU_C + (GELU_C * 0.044715) * square))
            v = u * hp
            act[part, :] = v.astype(BF16)
            dgel[part, :] = hp + (v - v * hp) * ((2 * GELU_C) + (6 * GELU_C * 0.044715) * square)
        loop(hidden // chunk, up_part, 4)

        res[...] += mm(wdt_ref[...], act[...])
        ln_forward(2, xh3, fin)
        pred = mm(wt_ref[c_head:], fin[...])
        pix = pix_ref[pl.ds(first, rows), :].astype(F32).T
        centre = pix - jnp.mean(pix, axis=0, keepdims=True)
        target = (centre * lax.rsqrt(jnp.mean(centre * centre, axis=0, keepdims=True) + 1e-06)).astype(BF16).astype(F32)
        err = pred - target
        loss_ref[...] += fold(mrow[...] * jnp.mean(err * err, axis=0, keepdims=True))
        gpred = (mrow[0:1] * err * coef).astype(BF16)

        gin_ref[:, c_head:] += mm(fin[...], gpred, 1, 1)
        tmp[...] = mm(w_ref[:, c_head:], gpred)
        ln_backward(2, xh3, False)

        def mlp_back(i):
            part = pl.ds(pl.multiple_of(i * chunk, chunk), chunk)
            there = pl.ds(pl.multiple_of(c_up + i * chunk, chunk), chunk)
            d = (mm(wd_ref[part, :], low[...]) * dgel[part, :]).astype(BF16)
            dup[part, :] = d
            gdown_ref[part, :] += mm(act[part, :], low[...], 1, 1)
            gin_ref[:, there] += mm(n2[...], d, 1, 1)
        loop(hidden // chunk, mlp_back, 4)
        tmp[...] = mm(w_ref[:, c_up:c_head], dup[...])
        ln_backward(1, xh2, True)
        gin_ref[:, c_out:c_up] += mm(att[...], low[...], 1, 1)
        fin[...] = mm(w_ref[:, c_out:c_up], low[...]).astype(BF16)

        def attend_back(i):
            sb, g = i // groups, i % groups
            at = lane(sb)
            f0 = pl.multiple_of(g * 128, 128)
            q = qkv[pl.ds(f0, 128), at]
            k = qkv[pl.ds(width + f0, 128), at]
            v = qkv[pl.ds(2 * width + f0, 128), at]
            do = fin[pl.ds(f0, 128), at]
            do_all = wide(do, 128 * per) * hm[...]
            dp = compact(jnp.concatenate([mm(v[size * h : size * h + size], do[size * h : size * h + size], 0, 0) for h in range(per)], axis=1))
            p = probs[i]
            ds = p * (dp - jnp.sum(dp * p, axis=0, keepdims=True))
            p_all = jnp.concatenate([p.astype(BF16)] * 4, axis=0) * wm[...]
            ds_all = jnp.concatenate([(ds * scale).astype(BF16)] * 4, axis=0) * wm[...]
            tall = jnp.concatenate([ds_all[:, 128 * h : 128 * h + 128] for h in range(per)], axis=0)
            dqkv[pl.ds(f0, 128), at] = mm(wide(k, 128 * per) * hm[...], tall).astype(BF16)
            dqkv[pl.ds(width + f0, 128), at] = mm(wide(q, 128 * per) * hm[...], ds_all, 1, 1).astype(BF16)
            dqkv[pl.ds(2 * width + f0, 128), at] = mm(do_all, p_all, 1, 1).astype(BF16)
        loop(rows // 128 * groups, attend_back, 8)

        def qkv_back(i):
            part = pl.ds(pl.multiple_of(i * chunk, chunk), chunk)
            gin_ref[:, part] += mm(n1[...], dqkv[part, :], 1, 1)
        loop(3 * width // chunk, qkv_back, 3)
        tmp[...] = mm(w_ref[:, :c_out], dqkv[...])
        ln_backward(0, xh1, True)
        gvec_ref[6] += fold(low[...].astype(F32) * mrow[0:1])
        gp_ref[...] += mm(low[...], oh[...], 1, 1)

    loop(nblk, block)


def decoder_step(shift, rvis, gvt, pix, et, ef, vec, w, wd, coef, heads):
    width, total = w.shape
    hidden = wd.shape[0]
    rows = 512
    vis = rvis.shape[0]
    per = 128 // (width // heads)
    vmem = pl.BlockSpec(memory_space=pltpu.VMEM)
    f = lambda *s: pltpu.VMEM(s, F32)
    b = lambda *s: pltpu.VMEM(s, BF16)
    return pl.pallas_call(
        functools.partial(decoder_kernel, coef, heads),
        out_shape=(
            jax.ShapeDtypeStruct((width, total), F32),
            jax.ShapeDtypeStruct((hidden, width), F32),
            jax.ShapeDtypeStruct((7, width, 128), F32),
            jax.ShapeDtypeStruct((width, vis), F32),
            jax.ShapeDtypeStruct((8, 128), F32),
        ),
        in_specs=[pl.BlockSpec(memory_space=pltpu.SMEM)] + [vmem] * 8,
        out_specs=(vmem,) * 5,
        scratch_shapes=[
            b(total, width), b(width, hidden), f(width, rows), f(width, rows), f(width, rows), f(width, rows), f(width, rows),
            b(width, rows), b(width, rows), b(width, rows), f(24, rows),
            b(3 * width, rows), b(width, rows), b(hidden, rows), f(hidden, rows),
            f(rows // 128 * (width // 128), 32, 128 * per), b(3 * width, rows), b(hidden, rows), b(width, rows),
            b(vis, rows), f(8, rows), f(32, 128 * per), b(128, 128 * per), b(128, 128 * per),
        ],
        compiler_params=pltpu.CompilerParams(vmem_limit_bytes=63 * 2**20),
        name="decoder",
    )(shift, rvis, gvt, pix, et, ef, vec, w, wd)


CHUNK = 768


def lane(i):
    return pl.ds(i * 128 if isinstance(i, int) else pl.multiple_of(i * 128, 128), 128)


def part(i, base=0):
    return pl.ds(pl.multiple_of(base + i * CHUNK, 128), CHUNK)


def encoder_clips(seg_ref, own, others):
    clip = lax.broadcasted_iota(jnp.int32, own.shape, 0) == seg_ref[0:1]
    own[...] = jnp.where(clip, 1.0, 0.0).astype(BF16)
    others[...] = jnp.where(clip, 0.0, -1e31).astype(BF16)


def encoder_scores(q, k, scale):
    c = mm(k, q)
    e = jnp.exp2((c - jnp.max(c, axis=0, keepdims=True)) * (scale * 1.4426950408889634))
    return e * (1.0 / jnp.sum(e, axis=0, keepdims=True))


def encoder_forward_kernel(
    heads, seen_ref, pos_ref, grid_pos_ref, seg_ref, vec_ref, we_ref, wi_ref, wd_ref,
    grid_ref, seen_t_ref, xh1_ref, n1_ref, qkv_ref, att_ref, xh2_ref, n2_ref, act_ref, dgel_ref, xh3_ref, fin_ref, rs_ref,
    we, wi, wd, res, own, others, seen_t, xh1, n1, qkv, att, xh2, n2, act, dgel, xh3, fin, rs, w_sem, o_sem,
):
    width, hidden = we.shape[1], wd.shape[0]
    rows = res.shape[1]
    size = width // heads
    scale = size ** -0.5
    c_out, c_up, c_proj = 3 * width, 4 * width, 4 * width + hidden
    total = wi.shape[1]
    loads = [pltpu.make_async_copy(we_ref, we, w_sem.at[0])]
    for i, (lo, hi) in enumerate(((0, c_out), (c_out, c_up), (c_up, c_proj), (c_proj, total))):
        at = pl.ds(lo, hi - lo)
        loads.append(pltpu.make_async_copy(wi_ref.at[:, at], wi.at[:, at], w_sem.at[1 + i]))
    loads.insert(4, pltpu.make_async_copy(wd_ref, wd, w_sem.at[5]))
    for load in loads:
        load.start()
    pairs = (
        (seen_t, seen_t_ref), (xh1, xh1_ref), (n1, n1_ref), (qkv, qkv_ref), (att, att_ref), (xh2, xh2_ref),
        (n2, n2_ref), (act, act_ref), (dgel, dgel_ref), (xh3, xh3_ref), (fin, fin_ref), (rs, rs_ref),
    )
    saves = [pltpu.make_async_copy(a, b, o_sem.at[i]) for i, (a, b) in enumerate(pairs)]

    def ln_forward(k, xh, out):
        def body(i):
            x = res[:, lane(i)]
            centre = x - jnp.mean(x, axis=0, keepdims=True)
            r = lax.rsqrt(jnp.mean(centre * centre, axis=0, keepdims=True) + 1e-06)
            xhat = centre * r
            xh[:, lane(i)] = xhat
            rs[8 * k : 8 * k + 8, lane(i)] = jnp.broadcast_to(r, (8, 128))
            out[:, lane(i)] = (xhat * vec_ref[2 * k] + vec_ref[2 * k + 1]).astype(BF16)
        for i in range(rows // 128):
            body(i)

    seen_t[...] = seen_ref[...].T
    saves[0].start()
    encoder_clips(seg_ref, own, others)
    loads[0].wait()
    res[...] = mm(we[...], seen_t[...], 0, 0) + pos_ref[...]
    ln_forward(0, xh1, n1)
    saves[1].start()
    saves[2].start()
    loads[1].wait()

    def qkv_part(i):
        qkv[part(i), :] = mm(wi[:, part(i)], n1[...], 0, 0).astype(BF16)
    loop(3, qkv_part, 3)
    saves[3].start()

    def attend(h):
        f0 = pl.multiple_of(h * size, size)
        k = jnp.concatenate([qkv[pl.ds(width + f0, size), :], others[...]], axis=0).T
        v = qkv[pl.ds(2 * width + f0, size), :]
        for lo in range(0, rows, 640):
            at = pl.ds(lo, min(640, rows - lo))
            q = jnp.concatenate([qkv[pl.ds(f0, size), at], own[:, at]], axis=0)
            p = encoder_scores(q, k, scale)
            att[pl.ds(f0, size), at] = mm(v, p.astype(BF16)).astype(BF16)
    loop(heads, attend, 2)
    saves[4].start()
    loads[2].wait()
    res[...] += mm(wi[:, c_out:c_up], att[...], 0, 0)
    ln_forward(1, xh2, n2)
    saves[5].start()
    saves[6].start()
    loads[3].wait()

    def up_part(i):
        u = mm(wi[:, part(i, c_up)], n2[...], 0, 0)
        square = u * u
        hp = 0.5 + 0.5 * jnp.tanh(u * (GELU_C + (GELU_C * 0.044715) * square))
        v = u * hp
        act[part(i), :] = v.astype(BF16)
        dgel[part(i), :] = hp + (v - v * hp) * ((2 * GELU_C) + (6 * GELU_C * 0.044715) * square)
    loop(hidden // CHUNK, up_part, 4)
    saves[7].start()
    saves[8].start()
    loads[4].wait()
    res[...] += mm(wd[...], act[...], 0, 0)
    ln_forward(2, xh3, fin)
    for i in (9, 10, 11):
        saves[i].start()
    loads[5].wait()
    grid_ref[...] = (mm(wi[:, c_proj:], fin[...], 0, 0) + grid_pos_ref[...]).astype(BF16)
    for save in saves:
        save.wait()


def encoder_forward(seen, pos, grid_pos, seg, vec, we, wi, wd, heads):
    rows, patch = seen.shape
    width, total = wi.shape
    hidden = wd.shape[0]
    any_, vmem = pl.BlockSpec(memory_space=pl.ANY), pl.BlockSpec(memory_space=pltpu.VMEM)
    saved = (
        ((patch, rows), BF16), ((width, rows), F32), ((width, rows), BF16), ((3 * width, rows), BF16),
        ((width, rows), BF16), ((width, rows), F32), ((width, rows), BF16), ((hidden, rows), BF16), ((hidden, rows), F32),
        ((width, rows), F32), ((width, rows), BF16), ((24, rows), F32),
    )
    return pl.pallas_call(
        functools.partial(encoder_forward_kernel, heads),
        out_shape=(jax.ShapeDtypeStruct((grid_pos.shape[0], rows), BF16),) + tuple(jax.ShapeDtypeStruct(*s) for s in saved),
        in_specs=[vmem] * 5 + [any_] * 3,
        out_specs=(vmem,) + (any_,) * len(saved),
        scratch_shapes=[pltpu.VMEM(we.shape, BF16), pltpu.VMEM(wi.shape, BF16), pltpu.VMEM(wd.shape, BF16), pltpu.VMEM((width, rows), F32)]
        + [pltpu.VMEM((16, rows), BF16)] * 2 + [pltpu.VMEM(*s) for s in saved] + [pltpu.SemaphoreType.DMA((6,)), pltpu.SemaphoreType.DMA((len(saved),))],
        compiler_params=pltpu.CompilerParams(vmem_limit_bytes=62 * 2**20),
        name="encode",
    )(seen, pos, grid_pos, seg, vec, we, wi, wd)


def encoder_backward_kernel(
    heads, gp_ref, vec_ref, seg_ref, wi_ref, wd_ref,
    seen_t_ref, xh1_ref, n1_ref, qkv_ref, att_ref, xh2_ref, n2_ref, act_ref, dgel_ref, xh3_ref, fin_ref, rs_ref,
    gin_ref, gdown_ref, gembed_ref, gvec_ref,
    wi, wd, res, tmp, low, dqkv, probs, dscores, stage, own, others, seen_t, xh1, n1, qkv, att, xh2, n2, act, dgel, rs, i_sem, s_sem,
):
    width, hidden = wi.shape[0], wd.shape[0]
    rows = res.shape[1]
    size = width // heads
    scale = size ** -0.5
    c_out, c_up, c_proj = 3 * width, 4 * width, 4 * width + hidden
    total = wi.shape[1]
    n_proj = total - c_proj

    def load(i, src, dst):
        return pltpu.make_async_copy(src, dst, i_sem.at[i])

    def columns(i, lo, hi):
        at = pl.ds(lo, hi - lo)
        return load(i, wi_ref.at[:, at], wi.at[:, at])

    first = [load(0, fin_ref, n1), columns(1, c_proj, total), load(2, xh3_ref, xh1), load(3, rs_ref, rs)]
    mlp = [load(4, wd_ref, wd), load(5, dgel_ref, dgel), load(6, act_ref, act), load(7, n2_ref, n2)]
    second = [columns(8, c_up, c_proj), load(9, xh2_ref, xh2), columns(10, c_out, c_up), load(11, att_ref, att)]
    attention = [load(12, qkv_ref, qkv), columns(14, 0, c_out), load(15, seen_t_ref, seen_t)]
    again = [load(16, xh1_ref, xh1), load(17, n1_ref, n1)]
    for group in (first, mlp, second, attention):
        for copy in group:
            copy.start()
    gvec_ref[...] = jnp.zeros_like(gvec_ref)
    encoder_clips(seg_ref, own, others)

    open_copies = [None, None]
    turn = [0]

    def leave(value, dst):
        slot = turn[0] % 2
        if open_copies[slot] is not None:
            open_copies[slot].wait()
        height, length = value.shape
        stage[slot, :height, :length] = value
        copy = pltpu.make_async_copy(stage.at[slot, pl.ds(0, height), pl.ds(0, length)], dst, s_sem.at[slot])
        copy.start()
        open_copies[slot] = copy
        turn[0] += 1

    def ln_backward(k, xh, add):
        for i in range(rows // 128):
            d = tmp[:, lane(i)]
            xhat = xh[:, lane(i)]
            gvec_ref[2 * k] += d * xhat
            gvec_ref[2 * k + 1] += d
            dx = d * vec_ref[2 * k]
            m1 = jnp.mean(dx, axis=0, keepdims=True)
            m2 = jnp.mean(dx * xhat, axis=0, keepdims=True)
            g = rs[8 * k : 8 * k + 1, lane(i)] * (dx - m1 - xhat * m2)
            if add:
                g = g + res[:, lane(i)]
            res[:, lane(i)] = g
            low[:, lane(i)] = g.astype(BF16)

    for copy in first:
        copy.wait()
    gp = gp_ref[...].astype(BF16)
    leave(mm(n1[...], gp, 1, 1), gin_ref.at[:, pl.ds(c_proj, n_proj)])
    tmp[...] = mm(wi[:, c_proj:], gp)
    ln_backward(2, xh1, False)
    for copy in again:
        copy.start()
    for copy in mlp:
        copy.wait()
    for i in range(hidden // CHUNK):
        at = pl.ds(i * CHUNK, CHUNK)
        d = (mm(wd[at, :], low[...]) * dgel[at, :]).astype(BF16)
        leave(mm(act[at, :], low[...], 1, 1), gdown_ref.at[at, :])
        act[at, :] = d
        leave(mm(n2[...], d, 1, 1), gin_ref.at[:, pl.ds(c_up + i * CHUNK, CHUNK)])
    for copy in second:
        copy.wait()
    tmp[...] = mm(wi[:, c_up:c_proj], act[...])
    ln_backward(1, xh2, True)
    leave(mm(att[...], low[...], 1, 1), gin_ref.at[:, pl.ds(c_out, width)])
    att[...] = mm(wi[:, c_out:c_up], low[...]).astype(BF16)
    for copy in attention:
        copy.wait()

    def attend_back(h):
        f0 = pl.multiple_of(h * size, size)
        mine = pl.ds(f0, size)
        q = qkv[mine, :]
        k = qkv[pl.ds(width + f0, size), :]
        v = qkv[pl.ds(2 * width + f0, size), :]
        do = att[mine, :]
        keys = jnp.concatenate([k, others[...]], axis=0).T
        values = v.T
        for lo in range(0, rows, 640):
            at = pl.ds(lo, min(640, rows - lo))
            hi = min(lo + 640, rows)
            part_q = jnp.concatenate([q[:, lo:hi], own[:, at]], axis=0)
            p = encoder_scores(part_q, keys, scale)
            dp = mm(values, do[:, lo:hi])
            ds = p * (dp - jnp.sum(dp * p, axis=0, keepdims=True))
            probs[:, at] = p.astype(BF16)
            dscores[:, at] = (ds * scale).astype(BF16)
        dqkv[mine, :] = mm(k, dscores[...]).astype(BF16)
        dqkv[pl.ds(width + f0, size), :] = mm(q, dscores[...], 1, 1).astype(BF16)
        dqkv[pl.ds(2 * width + f0, size), :] = mm(do, probs[...], 1, 1).astype(BF16)
    loop(heads, attend_back, 2)
    for copy in again:
        copy.wait()
    for i in range(3 * width // CHUNK):
        at = pl.ds(i * CHUNK, CHUNK)
        leave(mm(n1[...], dqkv[at, :], 1, 1), gin_ref.at[:, at])
    tmp[...] = mm(wi[:, :c_out], dqkv[...])
    ln_backward(0, xh1, True)
    leave(mm(seen_t[...], low[...], 1, 1), gembed_ref)
    for copy in open_copies:
        copy.wait()


def encoder_backward(gp, vec, seg, wi, wd, saved, patch, heads):
    rows = gp.shape[1]
    width, total = wi.shape
    hidden = wd.shape[0]
    any_, vmem = pl.BlockSpec(memory_space=pl.ANY), pl.BlockSpec(memory_space=pltpu.VMEM)
    f = lambda *s: pltpu.VMEM(s, F32)
    b = lambda *s: pltpu.VMEM(s, BF16)
    shape = lambda *s: jax.ShapeDtypeStruct(s, F32)
    return pl.pallas_call(
        functools.partial(encoder_backward_kernel, heads),
        out_shape=(shape(width, total), shape(hidden, width), shape(patch, width), shape(6, width, 128)),
        in_specs=[vmem] * 3 + [any_] * (2 + len(saved)),
        out_specs=(any_,) * 3 + (vmem,),
        scratch_shapes=[
            b(*wi.shape), b(*wd.shape), f(width, rows), f(width, rows), b(width, rows), b(3 * width, rows), b(rows, rows), b(rows, rows),
            f(2, CHUNK, CHUNK), b(16, rows), b(16, rows), b(patch, rows), f(width, rows), b(width, rows), b(3 * width, rows), b(width, rows),
            f(width, rows), b(width, rows), b(hidden, rows), f(hidden, rows), f(24, rows),
            pltpu.SemaphoreType.DMA((18,)), pltpu.SemaphoreType.DMA((2,)),
        ],
        compiler_params=pltpu.CompilerParams(vmem_limit_bytes=63 * 2**20),
        name="encode_back",
    )(gp, vec, seg, wi, wd, *saved)


def place():
    clip, band = lax.axis_index("clip"), lax.axis_index("band")
    return clip // 2, clip % 2, band // 2, band % 2


def device(z, x, y, c):
    return (z * 2 + x, y * 2 + c)


def greet(z, x, y, c):
    barrier = pltpu.get_barrier_semaphore()
    others = [device(z, x, y, 1 - c), device(z, 1 - x, y, c), device(z, x, 1 - y, c)]
    others += [device((z + k) % 4, x, y, c) for k in (1, 2, 3)]
    for other in others:
        pl.semaphore_signal(barrier, inc=1, device_id=other, device_id_type=pl.DeviceIdType.MESH)
    pl.semaphore_wait(barrier, len(others))


def remote(src, dst, send, recv, to):
    return pltpu.make_async_remote_copy(
        src_ref=src, dst_ref=dst, send_sem=send, recv_sem=recv, device_id=to, device_id_type=pl.DeviceIdType.MESH
    )


def reduce_kernel(widths, n, *refs):
    grads, small = refs[:n], refs[n]
    outs, small_out, squares = refs[n + 1 : 2 * n + 1], refs[2 * n + 1], refs[2 * n + 2]
    rest = refs[2 * n + 3 :]
    sums, r0 = rest[:n], rest[n : 2 * n]
    coded = {1 + i: rest[(2 + i) * n : (3 + i) * n] for i in range(5)}
    came = {1 + i: rest[(7 + i) * n : (8 + i) * n] for i in range(5)}
    step_out = {1 + i: rest[(12 + i) * n : (13 + i) * n] for i in range(5)}
    step_in = {1 + i: rest[(17 + i) * n : (18 + i) * n] for i in range(5)}
    s_buf, s_sum, q_buf, q_sum, send, recv, near, t_send, t_recv, s_send, s_recv = rest[22 * n :]
    z, x, y, c = place()
    greet(z, x, y, c)

    def at_z(k):
        return (z + k) % 4

    def columns(t, core):
        half = sums[t].shape[4]
        return pl.ds(pl.multiple_of(core * half, 128), half)

    def local(t, k):
        zk = at_z(k)
        return pltpu.make_async_copy(grads[t].at[zk, :, :, :, columns(t, c)], sums[t].at[zk], near.at[t, k])

    def target(stage, k):
        return {
            1: lambda: device(z, 1 - x, y, c),
            2: lambda: device(z, x, 1 - y, c),
            3: lambda: device(z, x, 1 - y, c),
            4: lambda: device(z, 1 - x, y, c),
            5: lambda: device(at_z(k), x, y, c),
        }[stage]()

    def slot(stage, k):
        return k - 1 if stage == 5 else k

    def copy(stage, t, k):
        if stage == 0:
            src, dst, to = grads[t].at[at_z(k), :, :, :, columns(t, 1 - c)], r0[t].at[at_z(k)], device(z, x, y, 1 - c)
        elif stage == 6:
            src, dst, to = sums[t].at[z, x, y], outs[t].at[y, :, columns(t, c)], device(z, x, 1 - y, c)
        elif stage == 7:
            src = outs[t].at[:, :, columns(t, c)]
            dst, to = src, device(z, x, y, 1 - c)
        else:
            src, dst, to = coded[stage][t].at[slot(stage, k)], came[stage][t].at[slot(stage, k)], target(stage, k)
        return remote(src, dst, send.at[t, stage, k], recv.at[t, stage, k], to)

    def steps(stage, t, k):
        src, dst = step_out[stage][t].at[k], step_in[stage][t].at[k]
        return remote(src, dst, t_send.at[t, stage, k], t_recv.at[t, stage, k], target(stage, k))

    def keep(t):
        return pltpu.make_async_copy(sums[t].at[z, x, y], outs[t].at[y, :, columns(t, c)], near.at[t, 4])

    def each(lo, hi, body):
        def one(k, carry):
            body(k)
            return carry
        lax.fori_loop(lo, hi, one, 0)

    def slab(i, height):
        return pl.ds(pl.multiple_of(i * height, height), height)

    def part(stage, t):
        w = widths[t]
        return slice(0, w) if stage in (1, 3) else slice(w, None) if stage in (2, 4) else slice(None)

    def encode(stage, t, k, parts, read):
        rows = sums[t].shape[3]
        zk, width = at_z(k), coded[stage][t].shape[-1]
        block = lambda p: coded[stage][t].at[(k, p) if parts > 1 else slot(stage, k)]
        per = rows // 8
        def peak(i, most):
            return jnp.maximum(most, jnp.abs(read(zk, i // per, slab(i % per, 8))))
        most = lax.fori_loop(0, parts * per, peak, jnp.zeros((8, width), F32))
        most = jnp.maximum(jnp.max(most, axis=0, keepdims=True), 1e-30)
        step_out[stage][t][k] = most * (1.0 / 32767.0)
        steps(stage, t, k).start()
        scale = 32767.0 / most
        half = rows // 16
        def one(i):
            values = jnp.round(read(zk, i // half, slab(i % half, 16)) * scale).astype(jnp.int32).astype(jnp.int16)
            block(i // half)[slab(i % half, 16)] = values
        each(0, parts * half, one)
        copy(stage, t, k).start()

    def landed(stage, t, k):
        steps(stage, t, k).wait_recv()
        copy(stage, t, k).wait_recv()

    def decoded(stage, t, k, p, rows, parts):
        values = came[stage][t][(k, p, rows) if parts > 1 else (slot(stage, k), rows)]
        return values.astype(jnp.int32).astype(F32) * step_in[stage][t][k]

    order = (2, 1, 3, 0)
    for t in range(n):
        for k in order:
            copy(0, t, k).start()
            local(t, k).start()

    def hop(total, buffer, first, stage, to):
        return remote(total, buffer.at[stage], s_send.at[first + stage], s_recv.at[first + stage], to)

    def advance(total, buffer, first, stage):
        neighbours = (device(z, x, y, 1 - c), device(z, 1 - x, y, c), device(z, x, 1 - y, c))
        if stage:
            hop(total, buffer, first, stage - 1, neighbours[stage - 1]).wait()
            total[...] += buffer[stage - 1]
        if stage < 3:
            hop(total, buffer, first, stage, neighbours[stage]).start()
        else:
            for k in (1, 2, 3):
                last_hop(total, buffer, first, k).start()
            buffer[3 + z] = total[...]

    def last_hop(total, buffer, first, k):
        return remote(total, buffer.at[3 + z], s_send.at[first + 2 + k], s_recv.at[first + 2 + k], device(at_z(k), x, y, c))

    def finish_sum(total, buffer, first, out):
        for k in (1, 2, 3):
            last_hop(total, buffer, first, k).wait()
        out[...] = (buffer[3] + buffer[4]) + (buffer[5] + buffer[6])

    s_sum[...] = small[...]

    def first_sum(t, k):
        zk = at_z(k)
        copy(0, t, k).wait_recv()
        local(t, k).wait()
        per = sums[t].shape[3] // 16
        def one(i):
            p, r = i // per, slab(i % per, 16)
            sums[t][zk, p // 2, p % 2, r] += r0[t][zk, p // 2, p % 2, r]
        each(0, 4 * per, one)
        encode(1, t, k, 2, lambda zk, p, r: sums[t][zk, 1 - x, p, r, part(1, t)])
        encode(2, t, k, 2, lambda zk, p, r: sums[t][zk, p, 1 - y, r, part(2, t)])

    def second_sum(t, k):
        zk = at_z(k)
        per = sums[t].shape[3] // 16
        landed(1, t, k)
        def one(i):
            p, r = i // per, slab(i % per, 16)
            sums[t][zk, x, p, r, part(1, t)] += decoded(1, t, k, p, r, 2)
        each(0, 2 * per, one)
        encode(3, t, k, 1, lambda zk, p, r: sums[t][zk, x, 1 - y, r, part(3, t)])
        landed(2, t, k)
        def two(i):
            p, r = i // per, slab(i % per, 16)
            sums[t][zk, p, y, r, part(2, t)] += decoded(2, t, k, p, r, 2)
        each(0, 2 * per, two)
        encode(4, t, k, 1, lambda zk, p, r: sums[t][zk, 1 - x, y, r, part(4, t)])

    def third_sum(t, k):
        zk = at_z(k)
        landed(3, t, k)
        landed(4, t, k)
        def one(i):
            r = slab(i, 16)
            sums[t][zk, x, y, r, part(3, t)] += decoded(3, t, k, 0, r, 1)
            sums[t][zk, x, y, r, part(4, t)] += decoded(4, t, k, 0, r, 1)
        each(0, sums[t].shape[3] // 16, one)
        if k:
            encode(5, t, k, 1, lambda zk, p, r: sums[t][zk, x, y, r])

    def last_sum(t, total):
        for k in (1, 2, 3):
            landed(5, t, k)
        half = sums[t].shape[4]
        def one(i, acc):
            r = slab(i, 16)
            value = sums[t][z, x, y, r]
            for k in (1, 2, 3):
                value = value + decoded(5, t, k, 0, r, 1)
            sums[t][z, x, y, r] = value
            value = value * value
            value = value[:8] + value[8:]
            for j in range(half // 128):
                acc = acc + value[:, 128 * j : 128 * j + 128]
            return acc
        total = lax.fori_loop(0, sums[t].shape[3] // 16, one, total)
        copy(6, t, 0).start()
        keep(t).start()
        return total

    def share(t):
        copy(6, t, 0).wait_recv()
        keep(t).wait()
        copy(7, t, 0).start()

    blocks = [(t, k) for t in range(n) for k in order]
    total = jnp.zeros((8, 128), F32)
    for i in range(len(blocks) + 2):
        if i < len(blocks):
            first_sum(*blocks[i])
        if 0 <= i - 1 < len(blocks):
            second_sum(*blocks[i - 1])
        if 0 <= i - 2:
            third_sum(*blocks[i - 2])
        if i < 4:
            advance(s_sum, s_buf, 0, i)
        for t in range(n - 1):
            if i == 4 * t + 7:
                total = last_sum(t, total)
            if i == 4 * t + 9:
                share(t)
    total = last_sum(n - 1, total)
    finish_sum(s_sum, s_buf, 0, small_out)
    late = [t for t in range(n) if t == n - 1 or 4 * t + 9 >= len(blocks) + 2]
    for t in late[:-1]:
        share(t)
    q_sum[...] = total
    for stage in range(4):
        advance(q_sum, q_buf, 6, stage)
    finish_sum(q_sum, q_buf, 6, squares)
    share(late[-1])

    def finish(k):
        for t in range(n):
            copy(0, t, k).wait_send()
            for stage in range(1, 5):
                copy(stage, t, k).wait_send()
                steps(stage, t, k).wait_send()
    each(0, 4, finish)
    def finish_z(k):
        for t in range(n):
            copy(5, t, k).wait_send()
            steps(5, t, k).wait_send()
    each(1, 4, finish_z)
    for t in range(n):
        copy(6, t, 0).wait_send()
        copy(7, t, 0).wait()


def reduce_grads(grads, small, ident):
    n = len(grads)
    views, widths = [], []
    scratch = [[] for _ in range(22)]
    f = lambda *s: pltpu.VMEM(s, F32)
    q = lambda *s: pltpu.VMEM(s, jnp.int16)
    for grad in grads:
        rows, cols = grad.shape
        r2, half = rows // 16, cols // 2
        w = (half // 128 * 60 + 50) // 100 * 128
        views.append(grad.reshape(4, 2, 2, r2, cols))
        widths.append(w)
        blocks = [(4, 2, r2, w), (4, 2, r2, half - w), (4, r2, w), (4, r2, half - w), (3, r2, half)]
        for i, s in enumerate([f(4, 2, 2, r2, half)] * 2 + [q(*b) for b in blocks * 2] + [f(4, 1, b[-1]) for b in blocks * 2]):
            scratch[i].append(s)
    anywhere, vmem = pl.BlockSpec(memory_space=pl.ANY), pl.BlockSpec(memory_space=pltpu.VMEM)
    dma = pltpu.SemaphoreType.DMA
    square = jax.ShapeDtypeStruct((8, 128), F32)
    out = pl.pallas_call(
        functools.partial(reduce_kernel, tuple(widths), n),
        out_shape=tuple(jax.ShapeDtypeStruct((2, v.shape[3], v.shape[4]), F32) for v in views)
        + (jax.ShapeDtypeStruct(small.shape, F32), square),
        in_specs=[anywhere] * n + [vmem],
        out_specs=(anywhere,) * n + (vmem,) * 2,
        scratch_shapes=sum(scratch, []) + [
            f(7, *small.shape), f(*small.shape), f(7, 8, 128), f(8, 128),
            dma((n, 8, 4)), dma((n, 8, 4)), dma((n, 5)), dma((n, 6, 4)), dma((n, 6, 4)), dma((12,)), dma((12,)),
        ],
        compiler_params=pltpu.CompilerParams(
            collective_id=ident, has_side_effects=True, vmem_limit_bytes=63 * 2**20
        ),
        name="reduce",
    )(*views, small)
    return [o.reshape(-1, o.shape[2]) for o in out[:n]], out[n], out[n + 1]


def gather_kernel(chunks, n, *refs):
    shards, vector, results, vectors = refs[:n], refs[n], refs[n + 1 : 2 * n + 1], refs[2 * n + 1]
    outs = refs[2 * n + 2 : 3 * n + 2]
    send, recv, near, v_send, v_recv = refs[3 * n + 2 :]
    z, x, y, c = place()
    greet(z, x, y, c)

    def at_z(k):
        return (z + k) % 4

    def own(t):
        return pltpu.make_async_copy(shards[t], outs[t].at[z, x], near.at[t])

    def copy(stage, i, k):
        t, r0, nr, c0, both, split = chunks[i]
        half = shards[t].shape[2] // 2
        columns = lambda lo, size: pl.ds(pl.multiple_of(c * half + lo, 128), size)
        wide, narrow, whole = columns(c0, both), columns(c0 + both, split), columns(c0, both + split)
        rows = pl.ds(r0, nr)
        mine = isinstance(k, int) and k == 0
        o, src_z = outs[t], (z + 4 - k) % 4
        if stage == 0:
            src, dst, to = shards[t].at[:, rows, wide], o.at[z, x, :, rows, wide], device(at_z(k), x, y, c)
        elif stage == 1:
            src, dst, to = shards[t].at[y, rows, narrow], o.at[z, x, y, rows, narrow], device(at_z(k), x, y, c)
        elif stage == 2:
            dst, to = o.at[src_z, x, :, rows, wide], device(z, 1 - x, y, c)
            src = shards[t].at[:, rows, wide] if mine else dst
        elif stage == 3:
            dst, to = o.at[src_z, x, y, rows, narrow], device(z, 1 - x, y, c)
            src = shards[t].at[y, rows, narrow] if mine else dst
        elif stage == 4:
            src = o.at[src_z, 1 - x, y, rows, narrow] if mine else o.at[src_z, :, y, rows, narrow]
            dst, to = src, device(z, x, 1 - y, c)
        else:
            src = o.at[src_z, 1 - x, :, rows, whole] if mine else o.at[src_z, :, :, rows, whole]
            dst, to = src, device(z, x, y, 1 - c)
        return remote(src, dst, send.at[i, stage, k], recv.at[i, stage, k], to)

    def leave(t):
        return pltpu.make_async_copy(outs[t], results[t], near.at[n + t])

    def vector_copy(stage, k):
        src_z = (z + 4 - k) % 4
        if stage == 0:
            return remote(vector, vectors.at[z, x], v_send.at[k], v_recv.at[k], device(at_z(k), x, y, c))
        src = vector if k == 0 else vectors.at[src_z, x]
        return remote(src, vectors.at[src_z, x], v_send.at[4 + k], v_recv.at[4 + k], device(z, 1 - x, y, c))

    def each(lo, hi, body):
        def step(k, carry):
            body(k)
            return carry
        lax.fori_loop(lo, hi, step, 0)

    def along_z(i):
        def one(k):
            copy(0, i, k).start()
            copy(1, i, k).start()
        each(1, 4, one)
        copy(2, i, 0).start()
        copy(3, i, 0).start()

    def along_x(i):
        def one(k):
            copy(0, i, k).wait_recv()
            copy(2, i, k).start()
            copy(1, i, k).wait_recv()
            copy(3, i, k).start()
        each(1, 4, one)

    def along_y(i):
        copy(3, i, 0).wait_recv()
        copy(4, i, 0).start()
        def one(k):
            copy(3, i, k).wait_recv()
            copy(4, i, k).start()
        each(1, 4, one)

    def across(i):
        def one(k):
            copy(2, i, k).wait_recv()
            copy(4, i, k).wait_recv()
            copy(5, i, k).start()
        one(0)
        each(1, 4, one)

    vectors[z, x] = vector[...]
    for k in (1, 2, 3):
        vector_copy(0, k).start()
    vector_copy(1, 0).start()
    along_z(0)
    for t in range(n):
        own(t).start()
    count = len(chunks)
    for i in range(count + 3):
        if i + 1 < count:
            along_z(i + 1)
        if i < count:
            along_x(i)
        if i == 0:
            for t in range(n):
                own(t).wait()
        if i == 1:
            for k in (1, 2, 3):
                vector_copy(0, k).wait_recv()
                vector_copy(1, k).start()
        if 0 <= i - 1 < count:
            along_y(i - 1)
        if 0 <= i - 2 < count:
            across(i - 2)
        if 0 <= i - 3:
            copy(5, i - 3, 0).wait_recv()
            each(1, 4, lambda k, i=i: copy(5, i - 3, k).wait_recv())
            if i - 2 == count or chunks[i - 2][0] != chunks[i - 3][0]:
                leave(chunks[i - 3][0]).start()

    for i in range(count):
        for stage in (2, 3, 4, 5):
            copy(stage, i, 0).wait_send()
        def finish(k, i=i):
            for stage in range(6):
                copy(stage, i, k).wait_send()
        each(1, 4, finish)
    for t in range(n):
        leave(t).wait()
    vector_copy(1, 0).wait()
    for k in (1, 2, 3):
        vector_copy(0, k).wait_send()
        vector_copy(1, k).wait()


def chunks_of(shards, largest):
    chunks = []
    for t, shard in enumerate(shards):
        rows, tiles = shard.shape[0] // 2, shard.shape[1] // 256
        size = rows * tiles * 128
        parts = -(-size // largest)
        by_rows = rows // parts % 16 == 0 and tiles < 2 * parts
        if by_rows:
            for p in range(parts):
                both = max(1, tiles // 3) if tiles > 1 else 0
                chunks.append((t, rows // parts * p, rows // parts, 0, both * 128, (tiles - both) * 128))
        else:
            cuts = [tiles * p // parts for p in range(parts + 1)]
            for lo, hi in zip(cuts, cuts[1:]):
                both = max(1, (hi - lo) // 3)
                chunks.append((t, 0, rows, lo * 128, both * 128, (hi - lo - both) * 128))
    return tuple(chunks)


def gather_weights(shards, vector, ident):
    n = len(shards)
    views = [shard.reshape(2, shard.shape[0] // 2, shard.shape[1]) for shard in shards]
    chunks = chunks_of(shards, 75000)
    anywhere, vmem = pl.BlockSpec(memory_space=pl.ANY), pl.BlockSpec(memory_space=pltpu.VMEM)
    dma = pltpu.SemaphoreType.DMA
    out = pl.pallas_call(
        functools.partial(gather_kernel, chunks, n),
        out_shape=tuple(jax.ShapeDtypeStruct((4, 2) + v.shape, BF16) for v in views)
        + (jax.ShapeDtypeStruct((4, 2, 8, 128), F32),),
        in_specs=[vmem] * n + [vmem],
        out_specs=(anywhere,) * n + (vmem,),
        scratch_shapes=[pltpu.VMEM((4, 2) + v.shape, BF16) for v in views]
        + [dma((len(chunks), 6, 4)), dma((len(chunks), 6, 4)), dma((2 * n,)), dma((8,)), dma((8,))],
        compiler_params=pltpu.CompilerParams(collective_id=ident, has_side_effects=True, vmem_limit_bytes=60 * 2**20),
        name="gather",
    )(*views, vector.reshape(8, 128))
    return [o.reshape(-1, o.shape[4]) for o in out[:n]], out[n].reshape(-1)


def clip_of(column, clip_lengths, clip_shifts):
    columns = clip_lengths // 8
    ends = jnp.cumsum(columns)
    clip_id = jnp.sum((column[:, None] >= ends[None, :]).astype(jnp.int32), axis=1)
    onehot = (clip_id[:, None] == jnp.arange(clip_lengths.shape[0], dtype=jnp.int32)[None, :]).astype(jnp.int32)

    def select(values):
        return jnp.sum(onehot * values[None, :], axis=1)

    return clip_id, select(ends - columns), select(columns), select(clip_shifts[:, 0]), select(clip_shifts[:, 1])


def half_table(position, width):
    quarter = width // 4
    omega = 1.0 / 10000.0 ** (jnp.arange(quarter, dtype=jnp.float32) / quarter)
    angle = omega[:, None] * position.astype(jnp.float32)[None, :]
    return jnp.concatenate([jnp.sin(angle), jnp.cos(angle)])


def adam_update(weight, first, second, grad, decay):
    first = BETA_ONE * first + (1.0 - BETA_ONE) * grad
    second = BETA_TWO * second + (1.0 - BETA_TWO) * grad * grad
    first_hat = first / (1.0 - BETA_ONE**STEP)
    second_hat = second / (1.0 - BETA_TWO**STEP)
    weight = weight - LEARN_RATE * (first_hat / (jnp.sqrt(second_hat) + EPSILON) + decay * weight)
    return (weight, first, second)


def shards(
    pixels,
    lengths,
    shifts,
    visible,
    patch_embed,
    encoder_in,
    encoder_down,
    decoder_in,
    decoder_down,
    norm_vectors,
    first_embed,
    first_encoder_in,
    first_encoder_down,
    first_decoder_in,
    first_decoder_down,
    first_vectors,
    second_embed,
    second_encoder_in,
    second_encoder_down,
    second_decoder_in,
    second_decoder_down,
    second_vectors,
):
    masters = (patch_embed, encoder_in, encoder_down, decoder_in, decoder_down, norm_vectors)
    firsts = (
        first_embed,
        first_encoder_in,
        first_encoder_down,
        first_decoder_in,
        first_decoder_down,
        first_vectors,
    )
    seconds = (
        second_embed,
        second_encoder_in,
        second_encoder_down,
        second_decoder_in,
        second_decoder_down,
        second_vectors,
    )
    direct = lax.axis_size("clip") == 8 and lax.axis_size("band") == 4
    low_shards = [master.astype(jnp.bfloat16) for master in masters]
    if direct:
        (w_embed, w_enc, w_enc_down, w_dec, w_dec_down), vectors = gather_weights(
            low_shards[:5], lax.reduce_precision(norm_vectors, exponent_bits=8, mantissa_bits=7), 0
        )
    else:
        w_embed, w_enc, w_enc_down, w_dec, w_dec_down, gathered_vectors = (
            lax.all_gather(shard, "clip", axis=0, tiled=True) for shard in low_shards
        )
        vectors = gathered_vectors.astype(jnp.float32)
    enc_width, dec_width = (w_enc.shape[0], w_dec.shape[0])
    patch_dev, n_visible = pixels.shape[0], visible.shape[0]
    padded = -(-n_visible // 128) * 128
    enc_gains = vectors[: 6 * enc_width].reshape(6, enc_width, 1)
    dec_gains = vectors[6 * enc_width :].reshape(7, dec_width, 1)
    enc_gains = jnp.broadcast_to(enc_gains, (6, enc_width, 128))
    dec_gains = jnp.broadcast_to(dec_gains, (7, dec_width, 128))
    turned = jnp.arange(patch_dev // 8, dtype=jnp.int32)
    _, start, size, shift_time, shift_band = clip_of(turned, lengths[0], shifts[0])
    turned_time = (turned - start - shift_time) % size
    decoder_pixels = pixels.reshape(patch_dev // 8, 8, -1)[start + turned_time].reshape(pixels.shape)
    time_table = half_table(turned_time, dec_width).T
    band_table = jnp.tile(half_table(jnp.arange(8, dtype=jnp.int32), dec_width), (1, 16))
    spots = jnp.pad(visible, (0, padded - n_visible))
    real = jnp.arange(padded, dtype=jnp.int32) < n_visible
    seen = pixels[spots]
    column, band = spots // 8, spots % 8
    segment, seen_start, seen_size, seen_shift, _ = clip_of(column, lengths[0], shifts[0])
    segment = jnp.where(real, segment, 15).astype(jnp.int32)
    segment = jnp.broadcast_to(segment[None, :], (8, padded))
    seen_time = column - seen_start
    decoder_row = jnp.where(real, 8 * (seen_start + (seen_time + seen_shift) % seen_size) + band, -1)
    decoder_row = jnp.broadcast_to(decoder_row[:, None], (padded, 128)).astype(jnp.int32)

    def positions(width):
        return jnp.concatenate([half_table(seen_time, width), half_table(band, width)])

    grid_seen, *saved = encoder_forward(
        seen,
        positions(enc_width),
        positions(dec_width),
        segment,
        enc_gains,
        w_embed,
        w_enc,
        w_enc_down,
        HEADS_ENC,
    )
    masked_count = 13.0 * (patch_dev // 16) * lax.axis_size("clip") * lax.axis_size("band")
    g_dec_in, g_dec_down, g_dec_vectors, grad_grid, loss = decoder_step(
        shift_band[::64],
        decoder_row,
        grid_seen,
        decoder_pixels,
        time_table,
        band_table,
        dec_gains,
        w_dec,
        w_dec_down,
        2.0 / (pixels.shape[1] * masked_count),
        HEADS_DEC,
    )
    local_loss = jnp.sum(loss[0])
    g_enc_in, g_enc_down, g_embed, g_enc_vectors = encoder_backward(
        grad_grid, enc_gains, segment, w_enc, w_enc_down, saved, pixels.shape[1], HEADS_ENC
    )
    g_vectors = jnp.concatenate(
        [jnp.sum(g_enc_vectors, axis=2).reshape(-1), jnp.sum(g_dec_vectors, axis=2).reshape(-1)]
    )
    if direct:
        small = jnp.concatenate([g_vectors.reshape(-1, 128), jnp.full((8, 128), local_loss)])
        shard_sums, summed, squares = reduce_grads(
            [g_enc_in, g_dec_in, g_enc_down, g_dec_down, g_embed], small, 1
        )
        rows = norm_vectors.shape[0]
        vector_sums = summed[:-8].reshape(-1)
        own = lax.dynamic_slice(vector_sums, (lax.axis_index("clip") * rows,), (rows,))
        reduced = (shard_sums[4], shard_sums[0], shard_sums[2], shard_sums[1], shard_sums[3], own)
        loss_sum = summed[-1, 0]
        norm_squared = jnp.sum(squares) + jnp.sum(vector_sums * vector_sums)
    else:
        reduced = lax.psum(
            tuple(
                lax.psum_scatter(grad, "clip", scatter_dimension=0, tiled=True)
                for grad in (g_embed, g_enc_in, g_enc_down, g_dec_in, g_dec_down, g_vectors)
            ),
            "band",
        )
        loss_sum = lax.psum(local_loss, ("clip", "band"))
        norm_squared = lax.psum(sum(jnp.sum(grad * grad) for grad in reduced), "clip")
    grad_norm = jnp.sqrt(norm_squared)
    factor = jnp.minimum(1.0, CLIP_LIMIT / (grad_norm + 1e-06))
    results = []
    for index in range(6):
        decay = DECAY_RATE if index < 5 else 0.0
        results.append(
            adam_update(
                masters[index], firsts[index], seconds[index], reduced[index] * factor, decay
            )
        )
    return (
        loss_sum,
        grad_norm,
        results[0][0],
        results[1][0],
        results[2][0],
        results[3][0],
        results[4][0],
        results[5][0],
        results[0][1],
        results[1][1],
        results[2][1],
        results[3][1],
        results[4][1],
        results[5][1],
        results[0][2],
        results[1][2],
        results[2][2],
        results[3][2],
        results[4][2],
        results[5][2],
    )


def solution(mesh):
    in_specs = (
        P(("clip", "band"), None),
        P(("clip", "band"), None),
        P(("clip", "band"), None, None),
        P(("clip", "band")),
        P("clip", None),
        P("clip", None),
        P("clip", None),
        P("clip", None),
        P("clip", None),
        P("clip"),
        P("clip", None),
        P("clip", None),
        P("clip", None),
        P("clip", None),
        P("clip", None),
        P("clip"),
        P("clip", None),
        P("clip", None),
        P("clip", None),
        P("clip", None),
        P("clip", None),
        P("clip"),
    )
    out_specs = (
        P(),
        P(),
        P("clip", None),
        P("clip", None),
        P("clip", None),
        P("clip", None),
        P("clip", None),
        P("clip"),
        P("clip", None),
        P("clip", None),
        P("clip", None),
        P("clip", None),
        P("clip", None),
        P("clip"),
        P("clip", None),
        P("clip", None),
        P("clip", None),
        P("clip", None),
        P("clip", None),
        P("clip"),
    )
    return jax.shard_map(shards, mesh=mesh, in_specs=in_specs, out_specs=out_specs, check_vma=False)
```

```python
import functools

import jax
import jax.numpy as jnp
from jax import lax
from jax.experimental import pallas as pl
from jax.experimental.pallas import tpu as pltpu
from jax.sharding import PartitionSpec as P

HEADS_ENC = 12
HEADS_DEC = 16
STEP = 10


LEARN_RATE = 0.02
BETA_ONE = 0.9
BETA_TWO = 0.95
EPSILON = 1e-08
DECAY_RATE = 0.05
CLIP_LIMIT = 0.001


F32, BF16 = jnp.float32, jnp.bfloat16
GELU_C = 0.7978845608028654


def mm(a, b, ca=1, cb=0):
    return lax.dot_general(a, b, (((ca,), (cb,)), ((), ())), preferred_element_type=F32)


def wide(v, n):
    return jnp.concatenate([v] * (n // 128), axis=1)


def loop(n, body, unroll=1):
    def step(i, carry):
        for k in range(unroll):
            body(i * unroll + k)
        return carry
    lax.fori_loop(0, n // unroll, step, 0)


def fold(v):
    total = v[:, :128]
    for i in range(1, v.shape[1] // 128):
        total = total + v[:, 128 * i : 128 * (i + 1)]
    return total


def decoder_kernel(
    coef, heads, shift_ref, rvis_ref, gvt_ref, pix_ref, et_ref, ef_ref, vec_ref, w_ref, wd_ref,
    gin_ref, gdown_ref, gvec_ref, gp_ref, loss_ref,
    wt_ref, wdt_ref, res, xh1, xh2, xh3, tmp, n1, n2, fin, rs, qkv, att, act, dgel, probs, dqkv, dup, low, oh, mrow, hb, hm, wm,
):
    width = w_ref.shape[0]
    hidden = wd_ref.shape[0]
    rows = res.shape[1]
    size = width // heads
    per = 128 // size
    scale = size ** -0.5
    groups = width // 128
    c_out, c_up, c_head = 3 * width, 4 * width, 4 * width + hidden
    pixels = w_ref.shape[1] - c_head
    cols = rows // 8
    nblk = pix_ref.shape[0] // rows
    chunk = 512

    def turn_in(i):
        at = pl.ds(pl.multiple_of(i * 256, 256), 256)
        wt_ref[at, :] = w_ref[:, at].T
    loop(w_ref.shape[1] // 256, turn_in)

    def turn_down(i):
        at = pl.ds(pl.multiple_of(i * 256, 256), 256)
        wdt_ref[:, at] = wd_ref[at, :].T
    loop(hidden // 256, turn_down)
    gin_ref[...] = jnp.zeros_like(gin_ref)
    gdown_ref[...] = jnp.zeros_like(gdown_ref)
    gvec_ref[...] = jnp.zeros_like(gvec_ref)
    gp_ref[...] = jnp.zeros_like(gp_ref)
    loss_ref[...] = jnp.zeros_like(loss_ref)
    f_id = lax.broadcasted_iota(jnp.int32, (128, 128 * per), 0)
    q_id = lax.broadcasted_iota(jnp.int32, (128, 128 * per), 1)
    hm[...] = jnp.where(f_id // size == q_id // 128, 1.0, 0.0).astype(BF16)
    wm[...] = jnp.where(f_id // 32 == (q_id % 128) // 32, 1.0, 0.0).astype(BF16)

    def lane(i):
        return pl.ds(pl.multiple_of(i * 128, 128), 128)

    def ln_forward(k, xh, out):
        def body(i):
            x = res[:, lane(i)]
            centre = x - jnp.mean(x, axis=0, keepdims=True)
            r = lax.rsqrt(jnp.mean(centre * centre, axis=0, keepdims=True) + 1e-06)
            xhat = centre * r
            xh[:, lane(i)] = xhat
            rs[8 * k : 8 * k + 8, lane(i)] = jnp.broadcast_to(r, (8, 128))
            out[:, lane(i)] = (xhat * vec_ref[2 * k] + vec_ref[2 * k + 1]).astype(BF16)
        loop(rows // 128, body, 4)

    def ln_backward(k, xh, add):
        def body(i):
            d = tmp[:, lane(i)]
            xhat = xh[:, lane(i)]
            gvec_ref[2 * k] += d * xhat
            gvec_ref[2 * k + 1] += d
            dx = d * vec_ref[2 * k]
            m1 = jnp.mean(dx, axis=0, keepdims=True)
            m2 = jnp.mean(dx * xhat, axis=0, keepdims=True)
            g = rs[8 * k : 8 * k + 1, lane(i)] * (dx - m1 - xhat * m2)
            if add:
                g = g + res[:, lane(i)]
            res[:, lane(i)] = g
            low[:, lane(i)] = g.astype(BF16)
        loop(rows // 128, body, 4)

    def block(j):
        first = pl.multiple_of(j * rows, rows)
        turn = shift_ref[j]
        spot = lax.broadcasted_iota(jnp.int32, (rvis_ref.shape[0], rows), 1) + first
        hot = jnp.where(wide(rvis_ref[...], rows) == spot, 1.0, 0.0)
        oh[...] = hot.astype(BF16)
        masked = 1.0 - jnp.sum(hot, axis=0, keepdims=True)
        mrow[...] = jnp.broadcast_to(masked, (8, rows))
        et = et_ref[pl.ds(pl.multiple_of(j * cols, cols), cols), :]
        e_hi = et.astype(BF16)
        rest = et - e_hi.astype(F32)
        e_mid = rest.astype(BF16)
        e_lo = (rest - e_mid.astype(F32)).astype(BF16)
        spread = jnp.where(
            lax.broadcasted_iota(jnp.int32, (cols, rows), 1) // 8 == lax.broadcasted_iota(jnp.int32, (cols, rows), 0), 1.0, 0.0
        ).astype(BF16)
        e_t = mm(e_hi, spread, 0, 0) + (mm(e_mid, spread, 0, 0) + mm(e_lo, spread, 0, 0))
        half = width // 2
        keep = masked > 0.5
        placed = mm(gvt_ref[...], oh[...])
        top = (wide(vec_ref[6, :half], rows) + e_t).astype(BF16).astype(F32)
        res[:half] = jnp.where(keep, top, placed[:half])
        bottom = wide((vec_ref[6, half:] + ef_ref[...]).astype(BF16).astype(F32), rows)
        res[half:] = jnp.where(keep, bottom, placed[half:])
        k_half = (lax.broadcasted_iota(jnp.int32, (32, 128 * per), 0) % 8 + turn) % 8 // 4
        q_half = (lax.broadcasted_iota(jnp.int32, (32, 128 * per), 1) % 8 + turn) % 8 // 4
        hb[...] = jnp.where(k_half == q_half, 0.0, -1e30)

        ln_forward(0, xh1, n1)

        def qkv_part(i):
            part = pl.ds(pl.multiple_of(i * chunk, chunk), chunk)
            qkv[part, :] = mm(wt_ref[part, :], n1[...]).astype(BF16)
        loop(3 * width // chunk, qkv_part, 3)

        q_group = (lax.broadcasted_iota(jnp.int32, (32, 128 * per), 1) % 128) // 32

        def compact(s):
            c = s[96:128]
            for i in (2, 1, 0):
                c = jnp.where(q_group == i, s[32 * i : 32 * i + 32], c)
            return c

        def attend(i):
            sb, g = i // groups, i % groups
            at = lane(sb)
            f0 = pl.multiple_of(g * 128, 128)
            q = qkv[pl.ds(f0, 128), at]
            k = qkv[pl.ds(width + f0, 128), at]
            v = qkv[pl.ds(2 * width + f0, 128), at]
            s = jnp.concatenate([mm(k[size * h : size * h + size], q[size * h : size * h + size], 0, 0) for h in range(per)], axis=1)
            c = compact(s) * scale + hb[...]
            e = jnp.exp(c - jnp.max(c, axis=0, keepdims=True))
            p = e * (1.0 / jnp.sum(e, axis=0, keepdims=True))
            probs[i] = p
            p_low = p.astype(BF16)
            p_all = jnp.concatenate([p_low] * 4, axis=0) * wm[...]
            for h in range(per):
                o = mm(v[size * h : size * h + size], p_all[:, 128 * h : 128 * h + 128])
                att[pl.ds(f0 + size * h, size), at] = o.astype(BF16)
        loop(rows // 128 * groups, attend, 16)

        res[...] += mm(wt_ref[c_out : c_out + width], att[...])
        ln_forward(1, xh2, n2)

        def up_part(i):
            part = pl.ds(pl.multiple_of(i * chunk, chunk), chunk)
            u = mm(wt_ref[pl.ds(pl.multiple_of(c_up + i * chunk, chunk), chunk), :], n2[...])
            square = u * u
            hp = 0.5 + 0.5 * jnp.tanh(u * (GELU_C + (GELU_C * 0.044715) * square))
            v = u * hp
            act[part, :] = v.astype(BF16)
            dgel[part, :] = hp + (v - v * hp) * ((2 * GELU_C) + (6 * GELU_C * 0.044715) * square)
        loop(hidden // chunk, up_part, 4)

        res[...] += mm(wdt_ref[...], act[...])
        ln_forward(2, xh3, fin)
        pred = mm(wt_ref[c_head:], fin[...])
        pix = pix_ref[pl.ds(first, rows), :].astype(F32).T
        centre = pix - jnp.mean(pix, axis=0, keepdims=True)
        target = (centre * lax.rsqrt(jnp.mean(centre * centre, axis=0, keepdims=True) + 1e-06)).astype(BF16).astype(F32)
        err = pred - target
        loss_ref[...] += fold(mrow[...] * jnp.mean(err * err, axis=0, keepdims=True))
        gpred = (mrow[0:1] * err * coef).astype(BF16)

        gin_ref[:, c_head:] += mm(fin[...], gpred, 1, 1)
        tmp[...] = mm(w_ref[:, c_head:], gpred)
        ln_backward(2, xh3, False)

        def mlp_back(i):
            part = pl.ds(pl.multiple_of(i * chunk, chunk), chunk)
            there = pl.ds(pl.multiple_of(c_up + i * chunk, chunk), chunk)
            d = (mm(wd_ref[part, :], low[...]) * dgel[part, :]).astype(BF16)
            dup[part, :] = d
            gdown_ref[part, :] += mm(act[part, :], low[...], 1, 1)
            gin_ref[:, there] += mm(n2[...], d, 1, 1)
        loop(hidden // chunk, mlp_back, 4)
        tmp[...] = mm(w_ref[:, c_up:c_head], dup[...])
        ln_backward(1, xh2, True)
        gin_ref[:, c_out:c_up] += mm(att[...], low[...], 1, 1)
        fin[...] = mm(w_ref[:, c_out:c_up], low[...]).astype(BF16)

        def attend_back(i):
            sb, g = i // groups, i % groups
            at = lane(sb)
            f0 = pl.multiple_of(g * 128, 128)
            q = qkv[pl.ds(f0, 128), at]
            k = qkv[pl.ds(width + f0, 128), at]
            v = qkv[pl.ds(2 * width + f0, 128), at]
            do = fin[pl.ds(f0, 128), at]
            do_all = wide(do, 128 * per) * hm[...]
            dp = compact(jnp.concatenate([mm(v[size * h : size * h + size], do[size * h : size * h + size], 0, 0) for h in range(per)], axis=1))
            p = probs[i]
            ds = p * (dp - jnp.sum(dp * p, axis=0, keepdims=True))
            p_all = jnp.concatenate([p.astype(BF16)] * 4, axis=0) * wm[...]
            ds_all = jnp.concatenate([(ds * scale).astype(BF16)] * 4, axis=0) * wm[...]
            tall = jnp.concatenate([ds_all[:, 128 * h : 128 * h + 128] for h in range(per)], axis=0)
            dqkv[pl.ds(f0, 128), at] = mm(wide(k, 128 * per) * hm[...], tall).astype(BF16)
            dqkv[pl.ds(width + f0, 128), at] = mm(wide(q, 128 * per) * hm[...], ds_all, 1, 1).astype(BF16)
            dqkv[pl.ds(2 * width + f0, 128), at] = mm(do_all, p_all, 1, 1).astype(BF16)
        loop(rows // 128 * groups, attend_back, 16)

        def qkv_back(i):
            part = pl.ds(pl.multiple_of(i * chunk, chunk), chunk)
            gin_ref[:, part] += mm(n1[...], dqkv[part, :], 1, 1)
        loop(3 * width // chunk, qkv_back, 3)
        tmp[...] = mm(w_ref[:, :c_out], dqkv[...])
        ln_backward(0, xh1, True)
        gvec_ref[6] += fold(low[...].astype(F32) * mrow[0:1])
        gp_ref[...] += mm(low[...], oh[...], 1, 1)

    loop(nblk, block)


def decoder_step(shift, rvis, gvt, pix, et, ef, vec, w, wd, coef, heads):
    width, total = w.shape
    hidden = wd.shape[0]
    rows = 512
    vis = rvis.shape[0]
    per = 128 // (width // heads)
    vmem = pl.BlockSpec(memory_space=pltpu.VMEM)
    f = lambda *s: pltpu.VMEM(s, F32)
    b = lambda *s: pltpu.VMEM(s, BF16)
    return pl.pallas_call(
        functools.partial(decoder_kernel, coef, heads),
        out_shape=(
            jax.ShapeDtypeStruct((width, total), F32),
            jax.ShapeDtypeStruct((hidden, width), F32),
            jax.ShapeDtypeStruct((7, width, 128), F32),
            jax.ShapeDtypeStruct((width, vis), F32),
            jax.ShapeDtypeStruct((8, 128), F32),
        ),
        in_specs=[pl.BlockSpec(memory_space=pltpu.SMEM)] + [vmem] * 8,
        out_specs=(vmem,) * 5,
        scratch_shapes=[
            b(total, width), b(width, hidden), f(width, rows), f(width, rows), f(width, rows), f(width, rows), f(width, rows),
            b(width, rows), b(width, rows), b(width, rows), f(24, rows),
            b(3 * width, rows), b(width, rows), b(hidden, rows), f(hidden, rows),
            f(rows // 128 * (width // 128), 32, 128 * per), b(3 * width, rows), b(hidden, rows), b(width, rows),
            b(vis, rows), f(8, rows), f(32, 128 * per), b(128, 128 * per), b(128, 128 * per),
        ],
        compiler_params=pltpu.CompilerParams(vmem_limit_bytes=63 * 2**20),
        name="decoder",
    )(shift, rvis, gvt, pix, et, ef, vec, w, wd)


CHUNK = 768


def lane(i):
    return pl.ds(i * 128 if isinstance(i, int) else pl.multiple_of(i * 128, 128), 128)


def part(i, base=0):
    return pl.ds(pl.multiple_of(base + i * CHUNK, 128), CHUNK)


def encoder_clips(seg_ref, own, others):
    clip = lax.broadcasted_iota(jnp.int32, own.shape, 0) == seg_ref[0:1]
    own[...] = jnp.where(clip, 1.0, 0.0).astype(BF16)
    others[...] = jnp.where(clip, 0.0, -1e31).astype(BF16)


def encoder_scores(q, k, scale):
    c = mm(k, q)
    e = jnp.exp2((c - jnp.max(c, axis=0, keepdims=True)) * (scale * 1.4426950408889634))
    return e * (1.0 / jnp.sum(e, axis=0, keepdims=True))


def encoder_forward_kernel(
    heads, seen_ref, pos_ref, grid_pos_ref, seg_ref, vec_ref, we_ref, wi_ref, wd_ref,
    grid_ref, seen_t_ref, xh1_ref, n1_ref, qkv_ref, att_ref, xh2_ref, n2_ref, act_ref, dgel_ref, xh3_ref, fin_ref, rs_ref,
    we, wi, wd, res, own, others, seen_t, xh1, n1, qkv, att, xh2, n2, act, dgel, xh3, fin, rs, w_sem, o_sem,
):
    width, hidden = we.shape[1], wd.shape[0]
    rows = res.shape[1]
    size = width // heads
    scale = size ** -0.5
    c_out, c_up, c_proj = 3 * width, 4 * width, 4 * width + hidden
    total = wi.shape[1]
    loads = [pltpu.make_async_copy(we_ref, we, w_sem.at[0])]
    for i, (lo, hi) in enumerate(((0, c_out), (c_out, c_up), (c_up, c_proj), (c_proj, total))):
        at = pl.ds(lo, hi - lo)
        loads.append(pltpu.make_async_copy(wi_ref.at[:, at], wi.at[:, at], w_sem.at[1 + i]))
    loads.insert(4, pltpu.make_async_copy(wd_ref, wd, w_sem.at[5]))
    for load in loads:
        load.start()
    pairs = (
        (seen_t, seen_t_ref), (xh1, xh1_ref), (n1, n1_ref), (qkv, qkv_ref), (att, att_ref), (xh2, xh2_ref),
        (n2, n2_ref), (act, act_ref), (dgel, dgel_ref), (xh3, xh3_ref), (fin, fin_ref), (rs, rs_ref),
    )
    saves = [pltpu.make_async_copy(a, b, o_sem.at[i]) for i, (a, b) in enumerate(pairs)]

    def ln_forward(k, xh, out):
        def body(i):
            x = res[:, lane(i)]
            centre = x - jnp.mean(x, axis=0, keepdims=True)
            r = lax.rsqrt(jnp.mean(centre * centre, axis=0, keepdims=True) + 1e-06)
            xhat = centre * r
            xh[:, lane(i)] = xhat
            rs[8 * k : 8 * k + 8, lane(i)] = jnp.broadcast_to(r, (8, 128))
            out[:, lane(i)] = (xhat * vec_ref[2 * k] + vec_ref[2 * k + 1]).astype(BF16)
        for i in range(rows // 128):
            body(i)

    seen_t[...] = seen_ref[...].T
    saves[0].start()
    encoder_clips(seg_ref, own, others)
    loads[0].wait()
    res[...] = mm(we[...], seen_t[...], 0, 0) + pos_ref[...]
    ln_forward(0, xh1, n1)
    saves[1].start()
    saves[2].start()
    loads[1].wait()

    def qkv_part(i):
        qkv[part(i), :] = mm(wi[:, part(i)], n1[...], 0, 0).astype(BF16)
    loop(3, qkv_part, 3)
    saves[3].start()

    def attend(h):
        f0 = pl.multiple_of(h * size, size)
        k = jnp.concatenate([qkv[pl.ds(width + f0, size), :], others[...]], axis=0).T
        v = qkv[pl.ds(2 * width + f0, size), :]
        for lo in range(0, rows, 640):
            at = pl.ds(lo, min(640, rows - lo))
            q = jnp.concatenate([qkv[pl.ds(f0, size), at], own[:, at]], axis=0)
            p = encoder_scores(q, k, scale)
            att[pl.ds(f0, size), at] = mm(v, p.astype(BF16)).astype(BF16)
    loop(heads, attend, 3)
    saves[4].start()
    loads[2].wait()
    res[...] += mm(wi[:, c_out:c_up], att[...], 0, 0)
    ln_forward(1, xh2, n2)
    saves[5].start()
    saves[6].start()
    loads[3].wait()

    def up_part(i):
        u = mm(wi[:, part(i, c_up)], n2[...], 0, 0)
        square = u * u
        hp = 0.5 + 0.5 * jnp.tanh(u * (GELU_C + (GELU_C * 0.044715) * square))
        v = u * hp
        act[part(i), :] = v.astype(BF16)
        dgel[part(i), :] = hp + (v - v * hp) * ((2 * GELU_C) + (6 * GELU_C * 0.044715) * square)
    loop(hidden // CHUNK, up_part, 4)
    saves[7].start()
    saves[8].start()
    loads[4].wait()
    res[...] += mm(wd[...], act[...], 0, 0)
    ln_forward(2, xh3, fin)
    for i in (9, 10, 11):
        saves[i].start()
    loads[5].wait()
    grid_ref[...] = (mm(wi[:, c_proj:], fin[...], 0, 0) + grid_pos_ref[...]).astype(BF16)
    for save in saves:
        save.wait()


def encoder_forward(seen, pos, grid_pos, seg, vec, we, wi, wd, heads):
    rows, patch = seen.shape
    width, total = wi.shape
    hidden = wd.shape[0]
    any_, vmem = pl.BlockSpec(memory_space=pl.ANY), pl.BlockSpec(memory_space=pltpu.VMEM)
    saved = (
        ((patch, rows), BF16), ((width, rows), F32), ((width, rows), BF16), ((3 * width, rows), BF16),
        ((width, rows), BF16), ((width, rows), F32), ((width, rows), BF16), ((hidden, rows), BF16), ((hidden, rows), F32),
        ((width, rows), F32), ((width, rows), BF16), ((24, rows), F32),
    )
    return pl.pallas_call(
        functools.partial(encoder_forward_kernel, heads),
        out_shape=(jax.ShapeDtypeStruct((grid_pos.shape[0], rows), BF16),) + tuple(jax.ShapeDtypeStruct(*s) for s in saved),
        in_specs=[vmem] * 5 + [any_] * 3,
        out_specs=(vmem,) + (any_,) * len(saved),
        scratch_shapes=[pltpu.VMEM(we.shape, BF16), pltpu.VMEM(wi.shape, BF16), pltpu.VMEM(wd.shape, BF16), pltpu.VMEM((width, rows), F32)]
        + [pltpu.VMEM((16, rows), BF16)] * 2 + [pltpu.VMEM(*s) for s in saved] + [pltpu.SemaphoreType.DMA((6,)), pltpu.SemaphoreType.DMA((len(saved),))],
        compiler_params=pltpu.CompilerParams(vmem_limit_bytes=62 * 2**20),
        name="encode",
    )(seen, pos, grid_pos, seg, vec, we, wi, wd)


def encoder_backward_kernel(
    heads, gp_ref, vec_ref, seg_ref, wi_ref, wd_ref,
    seen_t_ref, xh1_ref, n1_ref, qkv_ref, att_ref, xh2_ref, n2_ref, act_ref, dgel_ref, xh3_ref, fin_ref, rs_ref,
    gin_ref, gdown_ref, gembed_ref, gvec_ref,
    wi, wd, res, tmp, low, dqkv, probs, dscores, stage, own, others, seen_t, xh1, n1, qkv, att, xh2, n2, act, dgel, rs, i_sem, s_sem,
):
    width, hidden = wi.shape[0], wd.shape[0]
    rows = res.shape[1]
    size = width // heads
    scale = size ** -0.5
    c_out, c_up, c_proj = 3 * width, 4 * width, 4 * width + hidden
    total = wi.shape[1]
    n_proj = total - c_proj

    def load(i, src, dst):
        return pltpu.make_async_copy(src, dst, i_sem.at[i])

    def columns(i, lo, hi):
        at = pl.ds(lo, hi - lo)
        return load(i, wi_ref.at[:, at], wi.at[:, at])

    first = [load(0, fin_ref, n1), columns(1, c_proj, total), load(2, xh3_ref, xh1), load(3, rs_ref, rs)]
    mlp = [load(4, wd_ref, wd), load(5, dgel_ref, dgel), load(6, act_ref, act), load(7, n2_ref, n2)]
    second = [columns(8, c_up, c_proj), load(9, xh2_ref, xh2), columns(10, c_out, c_up), load(11, att_ref, att)]
    attention = [load(12, qkv_ref, qkv), columns(14, 0, c_out), load(15, seen_t_ref, seen_t)]
    again = [load(16, xh1_ref, xh1), load(17, n1_ref, n1)]
    for group in (first, mlp, second, attention):
        for copy in group:
            copy.start()
    gvec_ref[...] = jnp.zeros_like(gvec_ref)
    encoder_clips(seg_ref, own, others)

    open_copies = [None, None]
    turn = [0]

    def leave(value, dst):
        slot = turn[0] % 2
        if open_copies[slot] is not None:
            open_copies[slot].wait()
        height, length = value.shape
        stage[slot, :height, :length] = value
        copy = pltpu.make_async_copy(stage.at[slot, pl.ds(0, height), pl.ds(0, length)], dst, s_sem.at[slot])
        copy.start()
        open_copies[slot] = copy
        turn[0] += 1

    def ln_backward(k, xh, add):
        for i in range(rows // 128):
            d = tmp[:, lane(i)]
            xhat = xh[:, lane(i)]
            gvec_ref[2 * k] += d * xhat
            gvec_ref[2 * k + 1] += d
            dx = d * vec_ref[2 * k]
            m1 = jnp.mean(dx, axis=0, keepdims=True)
            m2 = jnp.mean(dx * xhat, axis=0, keepdims=True)
            g = rs[8 * k : 8 * k + 1, lane(i)] * (dx - m1 - xhat * m2)
            if add:
                g = g + res[:, lane(i)]
            res[:, lane(i)] = g
            low[:, lane(i)] = g.astype(BF16)

    for copy in first:
        copy.wait()
    gp = gp_ref[...].astype(BF16)
    leave(mm(n1[...], gp, 1, 1), gin_ref.at[:, pl.ds(c_proj, n_proj)])
    tmp[...] = mm(wi[:, c_proj:], gp)
    ln_backward(2, xh1, False)
    for copy in again:
        copy.start()
    for copy in mlp:
        copy.wait()
    for i in range(hidden // CHUNK):
        at = pl.ds(i * CHUNK, CHUNK)
        d = (mm(wd[at, :], low[...]) * dgel[at, :]).astype(BF16)
        leave(mm(act[at, :], low[...], 1, 1), gdown_ref.at[at, :])
        act[at, :] = d
        leave(mm(n2[...], d, 1, 1), gin_ref.at[:, pl.ds(c_up + i * CHUNK, CHUNK)])
    for copy in second:
        copy.wait()
    tmp[...] = mm(wi[:, c_up:c_proj], act[...])
    ln_backward(1, xh2, True)
    leave(mm(att[...], low[...], 1, 1), gin_ref.at[:, pl.ds(c_out, width)])
    att[...] = mm(wi[:, c_out:c_up], low[...]).astype(BF16)
    for copy in attention:
        copy.wait()

    def attend_back(h):
        f0 = pl.multiple_of(h * size, size)
        mine = pl.ds(f0, size)
        q = qkv[mine, :]
        k = qkv[pl.ds(width + f0, size), :]
        v = qkv[pl.ds(2 * width + f0, size), :]
        do = att[mine, :]
        keys = jnp.concatenate([k, others[...]], axis=0).T
        values = v.T
        for lo in range(0, rows, 640):
            at = pl.ds(lo, min(640, rows - lo))
            hi = min(lo + 640, rows)
            part_q = jnp.concatenate([q[:, lo:hi], own[:, at]], axis=0)
            p = encoder_scores(part_q, keys, scale)
            dp = mm(values, do[:, lo:hi])
            ds = p * (dp - jnp.sum(dp * p, axis=0, keepdims=True))
            probs[:, at] = p.astype(BF16)
            dscores[:, at] = (ds * scale).astype(BF16)
        dqkv[mine, :] = mm(k, dscores[...]).astype(BF16)
        dqkv[pl.ds(width + f0, size), :] = mm(q, dscores[...], 1, 1).astype(BF16)
        dqkv[pl.ds(2 * width + f0, size), :] = mm(do, probs[...], 1, 1).astype(BF16)
    loop(heads, attend_back, 2)
    for copy in again:
        copy.wait()
    for i in range(3 * width // CHUNK):
        at = pl.ds(i * CHUNK, CHUNK)
        leave(mm(n1[...], dqkv[at, :], 1, 1), gin_ref.at[:, at])
    tmp[...] = mm(wi[:, :c_out], dqkv[...])
    ln_backward(0, xh1, True)
    leave(mm(seen_t[...], low[...], 1, 1), gembed_ref)
    for copy in open_copies:
        copy.wait()


def encoder_backward(gp, vec, seg, wi, wd, saved, patch, heads):
    rows = gp.shape[1]
    width, total = wi.shape
    hidden = wd.shape[0]
    any_, vmem = pl.BlockSpec(memory_space=pl.ANY), pl.BlockSpec(memory_space=pltpu.VMEM)
    f = lambda *s: pltpu.VMEM(s, F32)
    b = lambda *s: pltpu.VMEM(s, BF16)
    shape = lambda *s: jax.ShapeDtypeStruct(s, F32)
    return pl.pallas_call(
        functools.partial(encoder_backward_kernel, heads),
        out_shape=(shape(width, total), shape(hidden, width), shape(patch, width), shape(6, width, 128)),
        in_specs=[vmem] * 3 + [any_] * (2 + len(saved)),
        out_specs=(any_,) * 3 + (vmem,),
        scratch_shapes=[
            b(*wi.shape), b(*wd.shape), f(width, rows), f(width, rows), b(width, rows), b(3 * width, rows), b(rows, rows), b(rows, rows),
            f(2, CHUNK, CHUNK), b(16, rows), b(16, rows), b(patch, rows), f(width, rows), b(width, rows), b(3 * width, rows), b(width, rows),
            f(width, rows), b(width, rows), b(hidden, rows), f(hidden, rows), f(24, rows),
            pltpu.SemaphoreType.DMA((18,)), pltpu.SemaphoreType.DMA((2,)),
        ],
        compiler_params=pltpu.CompilerParams(vmem_limit_bytes=63 * 2**20),
        name="encode_back",
    )(gp, vec, seg, wi, wd, *saved)


def place():
    clip, band = lax.axis_index("clip"), lax.axis_index("band")
    return clip // 2, clip % 2, band // 2, band % 2


def device(z, x, y, c):
    return (z * 2 + x, y * 2 + c)


def greet(z, x, y, c):
    barrier = pltpu.get_barrier_semaphore()
    others = [device(z, x, y, 1 - c), device(z, 1 - x, y, c), device(z, x, 1 - y, c)]
    others += [device((z + k) % 4, x, y, c) for k in (1, 2, 3)]
    for other in others:
        pl.semaphore_signal(barrier, inc=1, device_id=other, device_id_type=pl.DeviceIdType.MESH)
    pl.semaphore_wait(barrier, len(others))


def remote(src, dst, send, recv, to):
    return pltpu.make_async_remote_copy(
        src_ref=src, dst_ref=dst, send_sem=send, recv_sem=recv, device_id=to, device_id_type=pl.DeviceIdType.MESH
    )


def reduce_kernel(widths, n, *refs):
    grads, small = refs[:n], refs[n]
    outs, small_out, squares = refs[n + 1 : 2 * n + 1], refs[2 * n + 1], refs[2 * n + 2]
    rest = refs[2 * n + 3 :]
    sums, r0 = rest[:n], rest[n : 2 * n]
    coded = {1 + i: rest[(2 + i) * n : (3 + i) * n] for i in range(5)}
    came = {1 + i: rest[(7 + i) * n : (8 + i) * n] for i in range(5)}
    step_out = {1 + i: rest[(12 + i) * n : (13 + i) * n] for i in range(5)}
    step_in = {1 + i: rest[(17 + i) * n : (18 + i) * n] for i in range(5)}
    s_buf, s_sum, q_buf, q_sum, send, recv, near, t_send, t_recv, s_send, s_recv = rest[22 * n :]
    z, x, y, c = place()
    greet(z, x, y, c)

    def at_z(k):
        return (z + k) % 4

    def columns(t, core):
        half = sums[t].shape[4]
        return pl.ds(pl.multiple_of(core * half, 128), half)

    def local(t, k):
        zk = at_z(k)
        return pltpu.make_async_copy(grads[t].at[zk, :, :, :, columns(t, c)], sums[t].at[zk], near.at[t, k])

    def target(stage, k):
        return {
            1: lambda: device(z, 1 - x, y, c),
            2: lambda: device(z, x, 1 - y, c),
            3: lambda: device(z, x, 1 - y, c),
            4: lambda: device(z, 1 - x, y, c),
            5: lambda: device(at_z(k), x, y, c),
        }[stage]()

    def slot(stage, k):
        return k - 1 if stage == 5 else k

    def copy(stage, t, k):
        if stage == 0:
            src, dst, to = grads[t].at[at_z(k), :, :, :, columns(t, 1 - c)], r0[t].at[at_z(k)], device(z, x, y, 1 - c)
        elif stage == 6:
            src, dst, to = sums[t].at[z, x, y], outs[t].at[y, :, columns(t, c)], device(z, x, 1 - y, c)
        elif stage == 7:
            src = outs[t].at[:, :, columns(t, c)]
            dst, to = src, device(z, x, y, 1 - c)
        else:
            src, dst, to = coded[stage][t].at[slot(stage, k)], came[stage][t].at[slot(stage, k)], target(stage, k)
        return remote(src, dst, send.at[t, stage, k], recv.at[t, stage, k], to)

    def steps(stage, t, k):
        src, dst = step_out[stage][t].at[k], step_in[stage][t].at[k]
        return remote(src, dst, t_send.at[t, stage, k], t_recv.at[t, stage, k], target(stage, k))

    def keep(t):
        return pltpu.make_async_copy(sums[t].at[z, x, y], outs[t].at[y, :, columns(t, c)], near.at[t, 4])

    def each(lo, hi, body):
        def one(k, carry):
            body(k)
            return carry
        lax.fori_loop(lo, hi, one, 0)

    def slab(i, height):
        return pl.ds(pl.multiple_of(i * height, height), height)

    def part(stage, t):
        w = widths[t]
        return slice(0, w) if stage in (1, 3) else slice(w, None) if stage in (2, 4) else slice(None)

    def encode(stage, t, k, parts, read):
        rows = sums[t].shape[3]
        zk, width = at_z(k), coded[stage][t].shape[-1]
        block = lambda p: coded[stage][t].at[(k, p) if parts > 1 else slot(stage, k)]
        per = rows // 8
        def peak(i, most):
            return jnp.maximum(most, jnp.abs(read(zk, i // per, slab(i % per, 8))))
        most = lax.fori_loop(0, parts * per, peak, jnp.zeros((8, width), F32))
        most = jnp.maximum(jnp.max(most, axis=0, keepdims=True), 1e-30)
        step_out[stage][t][k] = most * (1.0 / 32767.0)
        steps(stage, t, k).start()
        scale = 32767.0 / most
        half = rows // 16
        def one(i):
            values = jnp.round(read(zk, i // half, slab(i % half, 16)) * scale).astype(jnp.int32).astype(jnp.int16)
            block(i // half)[slab(i % half, 16)] = values
        each(0, parts * half, one)
        copy(stage, t, k).start()

    def landed(stage, t, k):
        steps(stage, t, k).wait_recv()
        copy(stage, t, k).wait_recv()

    def decoded(stage, t, k, p, rows, parts):
        values = came[stage][t][(k, p, rows) if parts > 1 else (slot(stage, k), rows)]
        return values.astype(jnp.int32).astype(F32) * step_in[stage][t][k]

    order = (2, 1, 3, 0)
    for t in range(n):
        for k in order:
            copy(0, t, k).start()
            local(t, k).start()

    def hop(total, buffer, first, stage, to):
        return remote(total, buffer.at[stage], s_send.at[first + stage], s_recv.at[first + stage], to)

    def advance(total, buffer, first, stage):
        neighbours = (device(z, x, y, 1 - c), device(z, 1 - x, y, c), device(z, x, 1 - y, c))
        if stage:
            hop(total, buffer, first, stage - 1, neighbours[stage - 1]).wait()
            total[...] += buffer[stage - 1]
        if stage < 3:
            hop(total, buffer, first, stage, neighbours[stage]).start()
        else:
            for k in (1, 2, 3):
                last_hop(total, buffer, first, k).start()
            buffer[3 + z] = total[...]

    def last_hop(total, buffer, first, k):
        return remote(total, buffer.at[3 + z], s_send.at[first + 2 + k], s_recv.at[first + 2 + k], device(at_z(k), x, y, c))

    def finish_sum(total, buffer, first, out):
        for k in (1, 2, 3):
            last_hop(total, buffer, first, k).wait()
        out[...] = (buffer[3] + buffer[4]) + (buffer[5] + buffer[6])

    s_sum[...] = small[...]

    def first_sum(t, k):
        zk = at_z(k)
        copy(0, t, k).wait_recv()
        local(t, k).wait()
        per = sums[t].shape[3] // 16
        def one(i):
            p, r = i // per, slab(i % per, 16)
            sums[t][zk, p // 2, p % 2, r] += r0[t][zk, p // 2, p % 2, r]
        each(0, 4 * per, one)
        encode(1, t, k, 2, lambda zk, p, r: sums[t][zk, 1 - x, p, r, part(1, t)])
        encode(2, t, k, 2, lambda zk, p, r: sums[t][zk, p, 1 - y, r, part(2, t)])

    def second_sum(t, k):
        zk = at_z(k)
        per = sums[t].shape[3] // 16
        landed(1, t, k)
        def one(i):
            p, r = i // per, slab(i % per, 16)
            sums[t][zk, x, p, r, part(1, t)] += decoded(1, t, k, p, r, 2)
        each(0, 2 * per, one)
        encode(3, t, k, 1, lambda zk, p, r: sums[t][zk, x, 1 - y, r, part(3, t)])
        landed(2, t, k)
        def two(i):
            p, r = i // per, slab(i % per, 16)
            sums[t][zk, p, y, r, part(2, t)] += decoded(2, t, k, p, r, 2)
        each(0, 2 * per, two)
        encode(4, t, k, 1, lambda zk, p, r: sums[t][zk, 1 - x, y, r, part(4, t)])

    def third_sum(t, k):
        zk = at_z(k)
        landed(3, t, k)
        landed(4, t, k)
        def one(i):
            r = slab(i, 16)
            sums[t][zk, x, y, r, part(3, t)] += decoded(3, t, k, 0, r, 1)
            sums[t][zk, x, y, r, part(4, t)] += decoded(4, t, k, 0, r, 1)
        each(0, sums[t].shape[3] // 16, one)
        if k:
            encode(5, t, k, 1, lambda zk, p, r: sums[t][zk, x, y, r])

    def last_sum(t, total):
        for k in (1, 2, 3):
            landed(5, t, k)
        half = sums[t].shape[4]
        def one(i, acc):
            r = slab(i, 16)
            value = sums[t][z, x, y, r]
            for k in (1, 2, 3):
                value = value + decoded(5, t, k, 0, r, 1)
            sums[t][z, x, y, r] = value
            value = value * value
            value = value[:8] + value[8:]
            for j in range(half // 128):
                acc = acc + value[:, 128 * j : 128 * j + 128]
            return acc
        total = lax.fori_loop(0, sums[t].shape[3] // 16, one, total)
        copy(6, t, 0).start()
        keep(t).start()
        return total

    def share(t):
        copy(6, t, 0).wait_recv()
        keep(t).wait()
        copy(7, t, 0).start()

    blocks = [(t, k) for t in range(n) for k in order]
    total = jnp.zeros((8, 128), F32)
    for i in range(len(blocks) + 2):
        if i < len(blocks):
            first_sum(*blocks[i])
        if 0 <= i - 1 < len(blocks):
            second_sum(*blocks[i - 1])
        if 0 <= i - 2:
            third_sum(*blocks[i - 2])
        if i < 4:
            advance(s_sum, s_buf, 0, i)
        for t in range(n - 1):
            if i == 4 * t + 7:
                total = last_sum(t, total)
            if i == 4 * t + 9:
                share(t)
    total = last_sum(n - 1, total)
    finish_sum(s_sum, s_buf, 0, small_out)
    late = [t for t in range(n) if t == n - 1 or 4 * t + 9 >= len(blocks) + 2]
    for t in late[:-1]:
        share(t)
    q_sum[...] = total
    for stage in range(4):
        advance(q_sum, q_buf, 6, stage)
    finish_sum(q_sum, q_buf, 6, squares)
    share(late[-1])

    def finish(k):
        for t in range(n):
            copy(0, t, k).wait_send()
            for stage in range(1, 5):
                copy(stage, t, k).wait_send()
                steps(stage, t, k).wait_send()
    each(0, 4, finish)
    def finish_z(k):
        for t in range(n):
            copy(5, t, k).wait_send()
            steps(5, t, k).wait_send()
    each(1, 4, finish_z)
    for t in range(n):
        copy(6, t, 0).wait_send()
        copy(7, t, 0).wait()


def reduce_grads(grads, small, ident):
    n = len(grads)
    views, widths = [], []
    scratch = [[] for _ in range(22)]
    f = lambda *s: pltpu.VMEM(s, F32)
    q = lambda *s: pltpu.VMEM(s, jnp.int16)
    for grad in grads:
        rows, cols = grad.shape
        r2, half = rows // 16, cols // 2
        w = (half // 128 * 60 + 50) // 100 * 128
        views.append(grad.reshape(4, 2, 2, r2, cols))
        widths.append(w)
        blocks = [(4, 2, r2, w), (4, 2, r2, half - w), (4, r2, w), (4, r2, half - w), (3, r2, half)]
        for i, s in enumerate([f(4, 2, 2, r2, half)] * 2 + [q(*b) for b in blocks * 2] + [f(4, 1, b[-1]) for b in blocks * 2]):
            scratch[i].append(s)
    anywhere, vmem = pl.BlockSpec(memory_space=pl.ANY), pl.BlockSpec(memory_space=pltpu.VMEM)
    dma = pltpu.SemaphoreType.DMA
    square = jax.ShapeDtypeStruct((8, 128), F32)
    out = pl.pallas_call(
        functools.partial(reduce_kernel, tuple(widths), n),
        out_shape=tuple(jax.ShapeDtypeStruct((2, v.shape[3], v.shape[4]), F32) for v in views)
        + (jax.ShapeDtypeStruct(small.shape, F32), square),
        in_specs=[anywhere] * n + [vmem],
        out_specs=(anywhere,) * n + (vmem,) * 2,
        scratch_shapes=sum(scratch, []) + [
            f(7, *small.shape), f(*small.shape), f(7, 8, 128), f(8, 128),
            dma((n, 8, 4)), dma((n, 8, 4)), dma((n, 5)), dma((n, 6, 4)), dma((n, 6, 4)), dma((12,)), dma((12,)),
        ],
        compiler_params=pltpu.CompilerParams(
            collective_id=ident, has_side_effects=True, vmem_limit_bytes=63 * 2**20
        ),
        name="reduce",
    )(*views, small)
    return [o.reshape(-1, o.shape[2]) for o in out[:n]], out[n], out[n + 1]


def gather_kernel(chunks, n, *refs):
    shards, vector, results, vectors = refs[:n], refs[n], refs[n + 1 : 2 * n + 1], refs[2 * n + 1]
    outs = refs[2 * n + 2 : 3 * n + 2]
    send, recv, near, v_send, v_recv = refs[3 * n + 2 :]
    z, x, y, c = place()
    greet(z, x, y, c)

    def at_z(k):
        return (z + k) % 4

    def own(t):
        return pltpu.make_async_copy(shards[t], outs[t].at[z, x], near.at[t])

    def copy(stage, i, k):
        t, r0, nr, c0, both, split = chunks[i]
        half = shards[t].shape[2] // 2
        columns = lambda lo, size: pl.ds(pl.multiple_of(c * half + lo, 128), size)
        wide, narrow, whole = columns(c0, both), columns(c0 + both, split), columns(c0, both + split)
        rows = pl.ds(r0, nr)
        mine = isinstance(k, int) and k == 0
        o, src_z = outs[t], (z + 4 - k) % 4
        if stage == 0:
            src, dst, to = shards[t].at[:, rows, wide], o.at[z, x, :, rows, wide], device(at_z(k), x, y, c)
        elif stage == 1:
            src, dst, to = shards[t].at[y, rows, narrow], o.at[z, x, y, rows, narrow], device(at_z(k), x, y, c)
        elif stage == 2:
            dst, to = o.at[src_z, x, :, rows, wide], device(z, 1 - x, y, c)
            src = shards[t].at[:, rows, wide] if mine else dst
        elif stage == 3:
            dst, to = o.at[src_z, x, y, rows, narrow], device(z, 1 - x, y, c)
            src = shards[t].at[y, rows, narrow] if mine else dst
        elif stage == 4:
            src = o.at[src_z, 1 - x, y, rows, narrow] if mine else o.at[src_z, :, y, rows, narrow]
            dst, to = src, device(z, x, 1 - y, c)
        else:
            src = o.at[src_z, 1 - x, :, rows, whole] if mine else o.at[src_z, :, :, rows, whole]
            dst, to = src, device(z, x, y, 1 - c)
        return remote(src, dst, send.at[i, stage, k], recv.at[i, stage, k], to)

    def leave(t):
        return pltpu.make_async_copy(outs[t], results[t], near.at[n + t])

    def vector_copy(stage, k):
        src_z = (z + 4 - k) % 4
        if stage == 0:
            return remote(vector, vectors.at[z, x], v_send.at[k], v_recv.at[k], device(at_z(k), x, y, c))
        src = vector if k == 0 else vectors.at[src_z, x]
        return remote(src, vectors.at[src_z, x], v_send.at[4 + k], v_recv.at[4 + k], device(z, 1 - x, y, c))

    def each(lo, hi, body):
        def step(k, carry):
            body(k)
            return carry
        lax.fori_loop(lo, hi, step, 0)

    def along_z(i):
        def one(k):
            copy(0, i, k).start()
            copy(1, i, k).start()
        each(1, 4, one)
        copy(2, i, 0).start()
        copy(3, i, 0).start()

    def along_x(i):
        def one(k):
            copy(0, i, k).wait_recv()
            copy(2, i, k).start()
            copy(1, i, k).wait_recv()
            copy(3, i, k).start()
        each(1, 4, one)

    def along_y(i):
        copy(3, i, 0).wait_recv()
        copy(4, i, 0).start()
        def one(k):
            copy(3, i, k).wait_recv()
            copy(4, i, k).start()
        each(1, 4, one)

    def across(i):
        def one(k):
            copy(2, i, k).wait_recv()
            copy(4, i, k).wait_recv()
            copy(5, i, k).start()
        one(0)
        each(1, 4, one)

    vectors[z, x] = vector[...]
    for k in (1, 2, 3):
        vector_copy(0, k).start()
    vector_copy(1, 0).start()
    along_z(0)
    for t in range(n):
        own(t).start()
    count = len(chunks)
    for i in range(count + 3):
        if i + 1 < count:
            along_z(i + 1)
        if i < count:
            along_x(i)
        if i == 0:
            for t in range(n):
                own(t).wait()
        if i == 1:
            for k in (1, 2, 3):
                vector_copy(0, k).wait_recv()
                vector_copy(1, k).start()
        if 0 <= i - 1 < count:
            along_y(i - 1)
        if 0 <= i - 2 < count:
            across(i - 2)
        if 0 <= i - 3:
            copy(5, i - 3, 0).wait_recv()
            each(1, 4, lambda k, i=i: copy(5, i - 3, k).wait_recv())
            if i - 2 == count or chunks[i - 2][0] != chunks[i - 3][0]:
                leave(chunks[i - 3][0]).start()

    for i in range(count):
        for stage in (2, 3, 4, 5):
            copy(stage, i, 0).wait_send()
        def finish(k, i=i):
            for stage in range(6):
                copy(stage, i, k).wait_send()
        each(1, 4, finish)
    for t in range(n):
        leave(t).wait()
    vector_copy(1, 0).wait()
    for k in (1, 2, 3):
        vector_copy(0, k).wait_send()
        vector_copy(1, k).wait()


def chunks_of(shards, largest):
    chunks = []
    for t, shard in enumerate(shards):
        rows, tiles = shard.shape[0] // 2, shard.shape[1] // 256
        size = rows * tiles * 128
        parts = -(-size // largest)
        by_rows = rows // parts % 16 == 0 and tiles < 2 * parts
        if by_rows:
            for p in range(parts):
                both = max(1, tiles // 3) if tiles > 1 else 0
                chunks.append((t, rows // parts * p, rows // parts, 0, both * 128, (tiles - both) * 128))
        else:
            cuts = [tiles * p // parts for p in range(parts + 1)]
            for lo, hi in zip(cuts, cuts[1:]):
                both = max(1, (hi - lo) // 3)
                chunks.append((t, 0, rows, lo * 128, both * 128, (hi - lo - both) * 128))
    return tuple(chunks)


def gather_weights(shards, vector, ident):
    n = len(shards)
    views = [shard.reshape(2, shard.shape[0] // 2, shard.shape[1]) for shard in shards]
    chunks = chunks_of(shards, 75000)
    anywhere, vmem = pl.BlockSpec(memory_space=pl.ANY), pl.BlockSpec(memory_space=pltpu.VMEM)
    dma = pltpu.SemaphoreType.DMA
    out = pl.pallas_call(
        functools.partial(gather_kernel, chunks, n),
        out_shape=tuple(jax.ShapeDtypeStruct((4, 2) + v.shape, BF16) for v in views)
        + (jax.ShapeDtypeStruct((4, 2, 8, 128), F32),),
        in_specs=[vmem] * n + [vmem],
        out_specs=(anywhere,) * n + (vmem,),
        scratch_shapes=[pltpu.VMEM((4, 2) + v.shape, BF16) for v in views]
        + [dma((len(chunks), 6, 4)), dma((len(chunks), 6, 4)), dma((2 * n,)), dma((8,)), dma((8,))],
        compiler_params=pltpu.CompilerParams(collective_id=ident, has_side_effects=True, vmem_limit_bytes=60 * 2**20),
        name="gather",
    )(*views, vector.reshape(8, 128))
    return [o.reshape(-1, o.shape[4]) for o in out[:n]], out[n].reshape(-1)


def clip_of(column, clip_lengths, clip_shifts):
    columns = clip_lengths // 8
    ends = jnp.cumsum(columns)
    clip_id = jnp.sum((column[:, None] >= ends[None, :]).astype(jnp.int32), axis=1)
    onehot = (clip_id[:, None] == jnp.arange(clip_lengths.shape[0], dtype=jnp.int32)[None, :]).astype(jnp.int32)

    def select(values):
        return jnp.sum(onehot * values[None, :], axis=1)

    return clip_id, select(ends - columns), select(columns), select(clip_shifts[:, 0]), select(clip_shifts[:, 1])


def half_table(position, width):
    quarter = width // 4
    omega = 1.0 / 10000.0 ** (jnp.arange(quarter, dtype=jnp.float32) / quarter)
    angle = omega[:, None] * position.astype(jnp.float32)[None, :]
    return jnp.concatenate([jnp.sin(angle), jnp.cos(angle)])


def adam_update(weight, first, second, grad, decay):
    first = BETA_ONE * first + (1.0 - BETA_ONE) * grad
    second = BETA_TWO * second + (1.0 - BETA_TWO) * grad * grad
    first_hat = first / (1.0 - BETA_ONE**STEP)
    second_hat = second / (1.0 - BETA_TWO**STEP)
    weight = weight - LEARN_RATE * (first_hat / (jnp.sqrt(second_hat) + EPSILON) + decay * weight)
    return (weight, first, second)


def shards(
    pixels,
    lengths,
    shifts,
    visible,
    patch_embed,
    encoder_in,
    encoder_down,
    decoder_in,
    decoder_down,
    norm_vectors,
    first_embed,
    first_encoder_in,
    first_encoder_down,
    first_decoder_in,
    first_decoder_down,
    first_vectors,
    second_embed,
    second_encoder_in,
    second_encoder_down,
    second_decoder_in,
    second_decoder_down,
    second_vectors,
):
    masters = (patch_embed, encoder_in, encoder_down, decoder_in, decoder_down, norm_vectors)
    firsts = (
        first_embed,
        first_encoder_in,
        first_encoder_down,
        first_decoder_in,
        first_decoder_down,
        first_vectors,
    )
    seconds = (
        second_embed,
        second_encoder_in,
        second_encoder_down,
        second_decoder_in,
        second_decoder_down,
        second_vectors,
    )
    direct = lax.axis_size("clip") == 8 and lax.axis_size("band") == 4
    low_shards = [master.astype(jnp.bfloat16) for master in masters]
    if direct:
        (w_embed, w_enc, w_enc_down, w_dec, w_dec_down), vectors = gather_weights(
            low_shards[:5], lax.reduce_precision(norm_vectors, exponent_bits=8, mantissa_bits=7), 0
        )
    else:
        w_embed, w_enc, w_enc_down, w_dec, w_dec_down, gathered_vectors = (
            lax.all_gather(shard, "clip", axis=0, tiled=True) for shard in low_shards
        )
        vectors = gathered_vectors.astype(jnp.float32)
    enc_width, dec_width = (w_enc.shape[0], w_dec.shape[0])
    patch_dev, n_visible = pixels.shape[0], visible.shape[0]
    padded = -(-n_visible // 128) * 128
    enc_gains = vectors[: 6 * enc_width].reshape(6, enc_width, 1)
    dec_gains = vectors[6 * enc_width :].reshape(7, dec_width, 1)
    enc_gains = jnp.broadcast_to(enc_gains, (6, enc_width, 128))
    dec_gains = jnp.broadcast_to(dec_gains, (7, dec_width, 128))
    turned = jnp.arange(patch_dev // 8, dtype=jnp.int32)
    _, start, size, shift_time, shift_band = clip_of(turned, lengths[0], shifts[0])
    turned_time = (turned - start - shift_time) % size
    decoder_pixels = pixels.reshape(patch_dev // 8, 8, -1)[start + turned_time].reshape(pixels.shape)
    time_table = half_table(turned_time, dec_width).T
    band_table = jnp.tile(half_table(jnp.arange(8, dtype=jnp.int32), dec_width), (1, 16))
    spots = jnp.pad(visible, (0, padded - n_visible))
    real = jnp.arange(padded, dtype=jnp.int32) < n_visible
    seen = pixels[spots]
    column, band = spots // 8, spots % 8
    segment, seen_start, seen_size, seen_shift, _ = clip_of(column, lengths[0], shifts[0])
    segment = jnp.where(real, segment, 15).astype(jnp.int32)
    segment = jnp.broadcast_to(segment[None, :], (8, padded))
    seen_time = column - seen_start
    decoder_row = jnp.where(real, 8 * (seen_start + (seen_time + seen_shift) % seen_size) + band, -1)
    decoder_row = jnp.broadcast_to(decoder_row[:, None], (padded, 128)).astype(jnp.int32)

    def positions(width):
        return jnp.concatenate([half_table(seen_time, width), half_table(band, width)])

    grid_seen, *saved = encoder_forward(
        seen,
        positions(enc_width),
        positions(dec_width),
        segment,
        enc_gains,
        w_embed,
        w_enc,
        w_enc_down,
        HEADS_ENC,
    )
    masked_count = 13.0 * (patch_dev // 16) * lax.axis_size("clip") * lax.axis_size("band")
    g_dec_in, g_dec_down, g_dec_vectors, grad_grid, loss = decoder_step(
        shift_band[::64],
        decoder_row,
        grid_seen,
        decoder_pixels,
        time_table,
        band_table,
        dec_gains,
        w_dec,
        w_dec_down,
        2.0 / (pixels.shape[1] * masked_count),
        HEADS_DEC,
    )
    local_loss = jnp.sum(loss[0])
    g_enc_in, g_enc_down, g_embed, g_enc_vectors = encoder_backward(
        grad_grid, enc_gains, segment, w_enc, w_enc_down, saved, pixels.shape[1], HEADS_ENC
    )
    g_vectors = jnp.concatenate(
        [jnp.sum(g_enc_vectors, axis=2).reshape(-1), jnp.sum(g_dec_vectors, axis=2).reshape(-1)]
    )
    if direct:
        small = jnp.concatenate([g_vectors.reshape(-1, 128), jnp.full((8, 128), local_loss)])
        shard_sums, summed, squares = reduce_grads(
            [g_enc_in, g_dec_in, g_enc_down, g_dec_down, g_embed], small, 1
        )
        rows = norm_vectors.shape[0]
        vector_sums = summed[:-8].reshape(-1)
        own = lax.dynamic_slice(vector_sums, (lax.axis_index("clip") * rows,), (rows,))
        reduced = (shard_sums[4], shard_sums[0], shard_sums[2], shard_sums[1], shard_sums[3], own)
        loss_sum = summed[-1, 0]
        norm_squared = jnp.sum(squares) + jnp.sum(vector_sums * vector_sums)
    else:
        reduced = lax.psum(
            tuple(
                lax.psum_scatter(grad, "clip", scatter_dimension=0, tiled=True)
                for grad in (g_embed, g_enc_in, g_enc_down, g_dec_in, g_dec_down, g_vectors)
            ),
            "band",
        )
        loss_sum = lax.psum(local_loss, ("clip", "band"))
        norm_squared = lax.psum(sum(jnp.sum(grad * grad) for grad in reduced), "clip")
    grad_norm = jnp.sqrt(norm_squared)
    factor = jnp.minimum(1.0, CLIP_LIMIT / (grad_norm + 1e-06))
    results = []
    for index in range(6):
        decay = DECAY_RATE if index < 5 else 0.0
        results.append(
            adam_update(
                masters[index], firsts[index], seconds[index], reduced[index] * factor, decay
            )
        )
    return (
        loss_sum,
        grad_norm,
        results[0][0],
        results[1][0],
        results[2][0],
        results[3][0],
        results[4][0],
        results[5][0],
        results[0][1],
        results[1][1],
        results[2][1],
        results[3][1],
        results[4][1],
        results[5][1],
        results[0][2],
        results[1][2],
        results[2][2],
        results[3][2],
        results[4][2],
        results[5][2],
    )


def solution(mesh):
    in_specs = (
        P(("clip", "band"), None),
        P(("clip", "band"), None),
        P(("clip", "band"), None, None),
        P(("clip", "band")),
        P("clip", None),
        P("clip", None),
        P("clip", None),
        P("clip", None),
        P("clip", None),
        P("clip"),
        P("clip", None),
        P("clip", None),
        P("clip", None),
        P("clip", None),
        P("clip", None),
        P("clip"),
        P("clip", None),
        P("clip", None),
        P("clip", None),
        P("clip", None),
        P("clip", None),
        P("clip"),
    )
    out_specs = (
        P(),
        P(),
        P("clip", None),
        P("clip", None),
        P("clip", None),
        P("clip", None),
        P("clip", None),
        P("clip"),
        P("clip", None),
        P("clip", None),
        P("clip", None),
        P("clip", None),
        P("clip", None),
        P("clip"),
        P("clip", None),
        P("clip", None),
        P("clip", None),
        P("clip", None),
        P("clip", None),
        P("clip"),
    )
    return jax.shard_map(shards, mesh=mesh, in_specs=in_specs, out_specs=out_specs, check_vma=False)
```
